32 devices in a mesh: dp: 8 (over y, x, core), rows: 4 (over z).
Axes of the slice: x: 2, y: 2, z: 4, core: 2. Of those that a mesh axis runs over, the one named last changes fastest.
Arguments:
- inputs: float32 [64, 8, 44, 512], P('rows', 'dp'), may hold values from -60 to 60
- image_ids: int32 [64, 8, 44], P('rows', 'dp'), may hold values from -1 to 6, as said below
- first_norm_gain: float32 [512], replicated, may hold values from 0.5 to 1.5
- first_norm_bias: float32 [512], replicated, may hold values from -0.5 to 0.5
- point_one: float32 [512, 512], replicated, may hold values from -0.25 to 0.25
- kernel_big: float32 [27, 27, 512], replicated, may hold values from -0.21875 to 0.21875
- kernel_small: float32 [5, 5, 512], replicated, may hold values from -1.25 to 1.25
- second_norm_gain: float32 [512], replicated, may hold values from 0.5 to 1.5
- second_norm_bias: float32 [512], replicated, may hold values from -0.5 to 0.5
- point_two: float32 [512, 512], replicated, may hold values from -0.25 to 0.25
- feedforward_norm_gain: float32 [512], replicated, may hold values from 0.5 to 1.5
- feedforward_norm_bias: float32 [512], replicated, may hold values from -0.5 to 0.5
- w_up: float32 [512, 2048], P(None, 'rows'), may hold values from -0.25 to 0.25
- w_down: float32 [2048, 512], P('rows'), may hold values from -0.125 to 0.125
- out_grad: float32 [64, 8, 44, 512], P('rows', 'dp'), may hold values from -6 to 6
Outputs:
- output: float32 [64, 8, 44, 512], P('rows', 'dp')
- grad_input: float32 [64, 8, 44, 512], P('rows', 'dp')
- grad_gain_one: float32 [512], replicated
- grad_bias_one: float32 [512], replicated
- grad_point_one: float32 [512, 512], replicated
- grad_kernel_big: float32 [27, 27, 512], replicated
- grad_kernel_small: float32 [5, 5, 512], replicated
- grad_gain_two: float32 [512], replicated
- grad_bias_two: float32 [512], replicated
- grad_point_two: float32 [512, 512], replicated
- grad_gain_three: float32 [512], replicated
- grad_bias_three: float32 [512], replicated
- grad_w_up: float32 [512, 2048], P(None, 'rows')
- grad_w_down: float32 [2048, 512], P('rows')
The draws below stay inside these ranges and needn't reach their ends.
Inputs may be any that keep to these rules, and one draw needn't show every extreme that they name: `image_ids`: each canvas packs three square maps of sides 24, 24 and 14 stacked in its left columns and four 14 x 14 maps stacked to their right; ids 0 to 2 name the first three, 3 to 6 the others; -1 marks unused pixels.
All inputs are finite; a program needn't handle non-finite values.
Results may differ from the reference program's by a relative error of at most 0.0003.
Values sent between devices are 32-bit elements; how exact they have to be, the bound alone decides.
A program may use at most 192 MiB of HBM per device.

```python
import math
import jax
import jax.numpy as jnp
from jax import lax

C = 512
FF = 2048
HEIGHT = 64
WIDTH = 44
KS = 27
KSMALL = 5
CANVAS = 8


def draw_image_ids(key, part):
    key = jax.random.fold_in(key, 1)

    def one_canvas(canvas_key):
        order_key, left_key, right_key, shift_key = jax.random.split(canvas_key, 4)
        order = jax.random.permutation(order_key, 3).astype(jnp.int32)
        sides = jnp.array([24, 24, 14], jnp.int32)[order]
        left_top = jax.random.randint(left_key, (), 0, 3)
        right_top = jax.random.randint(right_key, (), 0, 9)
        right_left = 24 + jax.random.randint(shift_key, (), 0, 7)
        rows_index = jnp.arange(HEIGHT, dtype=jnp.int32)[:, None]
        cols_index = jnp.arange(WIDTH, dtype=jnp.int32)[None, :]
        labels = jnp.full((HEIGHT, WIDTH), -1, jnp.int32)
        top_row = left_top
        for slot in range(3):
            inside = (rows_index >= top_row) & (rows_index < top_row + sides[slot]) & (cols_index < sides[slot])
            labels = jnp.where(inside, order[slot], labels)
            top_row = top_row + sides[slot]
        for slot in range(4):
            first_row = right_top + 14 * slot
            inside = (rows_index >= first_row) & (rows_index < first_row + 14) & (cols_index >= right_left) & (cols_index < right_left + 14)
            labels = jnp.where(inside, 3 + slot, labels)
        return labels
    canvas_keys = jax.random.split(key, CANVAS)
    labels_all = jax.vmap(one_canvas)(canvas_keys)
    return jnp.transpose(labels_all, (1, 0, 2))


def draw_inputs(key, part):
    key = jax.random.fold_in(key, 2)
    noise_key, shift_key = jax.random.split(key)
    shape_all = (HEIGHT, CANVAS, WIDTH, C)
    noise = jnp.clip(jax.random.normal(noise_key, shape_all, jnp.float32), -5.0, 5.0)
    shift = jax.random.uniform(shift_key, (C,), jnp.float32, -1.0, 1.0)
    row_rise = jnp.exp(math.log(3.0) * jnp.arange(HEIGHT, dtype=jnp.float32) / HEIGHT)
    canvas_rise = jnp.exp(math.log(3.0) * jnp.arange(CANVAS, dtype=jnp.float32) / CANVAS)
    scale_all = row_rise[:, None, None, None] * canvas_rise[None, :, None, None]
    return scale_all * (noise + shift)


def levels(key, dims, pieces, smallest, top_value):
    gain, own = 1.0, jax.random.fold_in(key, 6)
    for position, parts in pieces:
        heights = jnp.exp(jax.random.uniform(jax.random.fold_in(own, position), (parts,), jnp.float32, smallest / len(pieces), top_value / len(pieces)))
        gain = gain * jnp.repeat(heights, dims[position] // parts).reshape([-1 if axis == position else 1 for axis in range(len(dims))])
    return gain


def scatter_about(rng, dims, scale, limit, pieces=(), kind=jnp.bfloat16):
    drawn = scale * jax.random.normal(rng, dims, jnp.float32)
    if pieces:
        drawn = drawn * levels(rng, dims, pieces, -0.22, 0.18)
    return jnp.clip(drawn, -limit, limit).astype(kind)


def setup_inputs(seed: int = 0) -> dict:
    key_list = jax.random.split(jax.random.key(seed), 16)
    return {
        "inputs": draw_inputs(jax.random.fold_in(key_list[15], 71), 0),
        "image_ids": draw_image_ids(jax.random.fold_in(key_list[15], 71), 0),
        "first_norm_gain": jnp.clip(1.0 + 0.1 * jax.random.normal(key_list[2], (C,), jnp.float32), 0.5, 1.5),
        "first_norm_bias": jnp.clip(jax.random.uniform(key_list[3], (C,), jnp.float32, -0.5, 0.5), -0.5, 0.5),
        "point_one": scatter_about(key_list[4], (C, C), C ** -0.5, 0.25, (), jnp.float32),
        "kernel_big": scatter_about(key_list[5], (KS, KS, C), (KS * KS) ** -0.5, 0.21875, (), jnp.float32),
        "kernel_small": scatter_about(key_list[6], (KSMALL, KSMALL, C), (KSMALL * KSMALL) ** -0.5, 1.25, (), jnp.float32),
        "second_norm_gain": jnp.clip(1.0 + 0.1 * jax.random.normal(key_list[7], (C,), jnp.float32), 0.5, 1.5),
        "second_norm_bias": jnp.clip(jax.random.uniform(key_list[8], (C,), jnp.float32, -0.5, 0.5), -0.5, 0.5),
        "point_two": scatter_about(key_list[9], (C, C), C ** -0.5, 0.25, (), jnp.float32),
        "feedforward_norm_gain": jnp.clip(1.0 + 0.1 * jax.random.normal(key_list[10], (C,), jnp.float32), 0.5, 1.5),
        "feedforward_norm_bias": jnp.clip(jax.random.uniform(key_list[11], (C,), jnp.float32, -0.5, 0.5), -0.5, 0.5),
        "w_up": scatter_about(key_list[12], (C, FF), C ** -0.5, 0.25, ((1, 4),), jnp.float32),
        "w_down": scatter_about(key_list[13], (FF, C), FF ** -0.5, 0.125, ((0, 4),), jnp.float32),
        "out_grad": scatter_about(key_list[14], (HEIGHT, CANVAS, WIDTH, C), 1.0, 6.0, ((0, 4), (1, 8)), jnp.float32),
    }


@jax.custom_vjp
def low(v):
    return lax.optimization_barrier(v.astype(jnp.bfloat16)).astype(jnp.float32)

@jax.custom_vjp
def low_back(v):
    return v

def low_keep(v):
    return (low(v), None)

def low_pass(kept, grad):
    return (grad,)

def back_keep(v):
    return (v, None)

def back_low(kept, grad):
    return (low(grad),)
low.defvjp(low_keep, low_pass)
low_back.defvjp(back_keep, back_low)
EPSILON = 1e-05
HIGHEST = lax.Precision.HIGHEST

def product(left, right):
    return jnp.dot(left, right, precision=HIGHEST, preferred_element_type=jnp.float32)

def apply_layer_norm(field, gain_vec, bias_vec, valid_mask, canvas_pixel_count):
    total_sum = lax.optimization_barrier(jnp.sum(field * valid_mask, axis=(0, 1, 2)))
    square_sum = lax.optimization_barrier(jnp.sum(field * field * valid_mask, axis=(0, 1, 2)))
    channel_mean = total_sum / canvas_pixel_count
    variance = square_sum / canvas_pixel_count - channel_mean * channel_mean
    return ((field - channel_mean) * lax.rsqrt(variance + EPSILON) * gain_vec + bias_vec) * valid_mask

def depthwise(padded, id_padded, image_ids, kernel):
    row_count = image_ids.shape[0]
    width_count = image_ids.shape[2]
    kernel_span = kernel.shape[0]

    def row_step(running, offset):
        row_slab = lax.dynamic_slice_in_dim(padded, offset, row_count, 0)
        id_slab = lax.dynamic_slice_in_dim(id_padded, offset, row_count, 0)
        weights = lax.dynamic_index_in_dim(kernel, offset, 0, keepdims=False)
        for column in range(kernel_span):
            same_image = (id_slab[:, :, column:column + width_count] == image_ids)[..., None]
            running = running + jnp.where(same_image, row_slab[:, :, column:column + width_count], 0.0) * weights[column]
        return (running, None)
    start_sum = jnp.zeros(image_ids.shape + (kernel.shape[2],), jnp.float32)
    result, ignored_value = lax.scan(jax.checkpoint(row_step), start_sum, jnp.arange(kernel_span, dtype=jnp.int32))
    return result

def reference(inputs, image_ids, first_norm_gain, first_norm_bias, point_one, kernel_big, kernel_small, second_norm_gain, second_norm_bias, point_two, feedforward_norm_gain, feedforward_norm_bias, w_up, w_down, out_grad):
    valid_mask = (image_ids >= 0).astype(jnp.float32)[..., None]
    canvas_pixel_count = jnp.sum(valid_mask)
    kernel_reach = kernel_big.shape[0] // 2
    small_start = kernel_reach - kernel_small.shape[0] // 2
    id_padded = jnp.pad(image_ids, ((kernel_reach, kernel_reach), (0, 0), (kernel_reach, kernel_reach)), constant_values=-2)

    def forward(inputs, first_norm_gain, first_norm_bias, point_one, kernel_big, kernel_small, second_norm_gain, second_norm_bias, point_two, feedforward_norm_gain, feedforward_norm_bias, w_up, w_down):
        first_normed_output = apply_layer_norm(inputs, first_norm_gain, first_norm_bias, valid_mask, canvas_pixel_count)
        act_one = jax.nn.gelu(product(first_normed_output, point_one))
        kernel = kernel_big + jnp.pad(kernel_small, ((small_start, small_start), (small_start, small_start), (0, 0)))
        act_padded = jnp.pad(act_one, ((kernel_reach, kernel_reach), (0, 0), (kernel_reach, kernel_reach), (0, 0)))
        depthwise_output = depthwise(act_padded, id_padded, image_ids, kernel) * valid_mask
        second_normed_output = apply_layer_norm(depthwise_output, second_norm_gain, second_norm_bias, valid_mask, canvas_pixel_count)
        mixed_output = inputs + product(jax.nn.gelu(second_normed_output), point_two)
        third_normed_output = apply_layer_norm(mixed_output, feedforward_norm_gain, feedforward_norm_bias, valid_mask, canvas_pixel_count)
        return mixed_output + product(jax.nn.gelu(product(third_normed_output, w_up)), w_down)
    output, pullback = jax.vjp(forward, inputs, first_norm_gain, first_norm_bias, point_one, kernel_big, kernel_small, second_norm_gain, second_norm_bias, point_two, feedforward_norm_gain, feedforward_norm_bias, w_up, w_down)
    grads_all = pullback(out_grad)
    return (output, grads_all[0], grads_all[1], grads_all[2], grads_all[3], grads_all[4], grads_all[5], grads_all[6], grads_all[7], grads_all[8], grads_all[9], grads_all[10], grads_all[11], grads_all[12])
```

```python
import functools

import jax
import jax.numpy as jnp
import numpy as np
from jax import lax
from jax.experimental import pallas as pl
from jax.experimental.pallas import tpu as pltpu
from jax.sharding import PartitionSpec as P

EPSILON = 1e-05
HIGHEST = lax.Precision.HIGHEST
HIGH = lax.Precision.HIGH
MESH = pl.DeviceIdType.MESH
F32 = jnp.float32
BF16 = jnp.bfloat16

LEFT, RIGHT = 24, 16
SLOTS = LEFT + RIGHT
LEFT_IDS = 3
LEFT_N, RIGHT_N = 37, 27
LEFT_F, RIGHT_F = 24, 16
FREQ = 2 * LEFT_F + 2 * RIGHT_F
REACH = 13
SPAN = 2 * REACH + 1
SPAN_PAD = 32


def forward_transform(length, padded, positions, columns):
    count = length // 2 + 1
    out = np.zeros((2 * padded, columns))
    angle = 2 * np.pi * np.outer(np.arange(count), positions) / length
    out[:count, : len(positions)] = np.cos(angle)
    out[padded : padded + count, : len(positions)] = -np.sin(angle)
    return out


def backward_transform(length, padded, positions, rows):
    count = length // 2 + 1
    out = np.zeros((rows, 2 * padded))
    twice = np.where(np.arange(count) == 0, 1.0, 2.0)
    angle = 2 * np.pi * np.outer(positions, np.arange(count)) / length
    out[: len(positions), :count] = np.cos(angle) * twice / length
    out[: len(positions), padded : padded + count] = -np.sin(angle) * twice / length
    return out


def slots_to_freq():
    out = np.zeros((FREQ, SLOTS))
    out[: 2 * LEFT_F, :LEFT] = forward_transform(LEFT_N, LEFT_F, np.arange(LEFT), LEFT)
    out[2 * LEFT_F :, LEFT:] = forward_transform(RIGHT_N, RIGHT_F, np.arange(RIGHT), RIGHT)
    return out


def freq_to_slots():
    out = np.zeros((SLOTS, FREQ))
    out[:LEFT, : 2 * LEFT_F] = backward_transform(LEFT_N, LEFT_F, np.arange(LEFT), LEFT)
    out[LEFT:, 2 * LEFT_F :] = backward_transform(RIGHT_N, RIGHT_F, np.arange(RIGHT), RIGHT)
    return out


def taps_to_freq():
    taps = np.arange(SPAN) - REACH
    return np.concatenate(
        [
            forward_transform(LEFT_N, LEFT_F, taps, SPAN_PAD),
            forward_transform(RIGHT_N, RIGHT_F, taps, SPAN_PAD),
        ]
    )


def freq_to_taps():
    taps = np.arange(SPAN) - REACH
    return np.concatenate(
        [
            backward_transform(LEFT_N, LEFT_F, taps, SPAN_PAD),
            backward_transform(RIGHT_N, RIGHT_F, taps, SPAN_PAD),
        ],
        axis=1,
    )


def split_constant(matrix, group):
    whole = np.kron(np.eye(group), matrix).astype(np.float32)
    high = whole.astype(jnp.bfloat16)
    low = (whole - high.astype(np.float32)).astype(jnp.bfloat16)
    return np.concatenate([high, high, low], axis=1)


def split_stack(value):
    high = value.astype(BF16)
    low = (value - high.astype(F32)).astype(BF16)
    return jnp.concatenate([high, low, high], axis=0)


def product_split(constant_ref, value):
    return jnp.dot(constant_ref[...], split_stack(value), preferred_element_type=F32)


GROUP_IN = 6
GROUP_OUT = 4
GROUP_TAP = 7
GROUP_GRAD = 4


def transform_window(rows, window, to_freq_ref, out_ref):
    for first in range(0, rows, GROUP_IN):
        part = window[first * SLOTS : (first + GROUP_IN) * SLOTS, :]
        freq = product_split(to_freq_ref, part)
        out_ref[first : first + GROUP_IN] = freq.reshape(GROUP_IN, FREQ, freq.shape[-1])


def fill_window(window, top_ref, own_ref, bottom_ref):
    at = 0
    for ref in (top_ref, own_ref, bottom_ref):
        rows = ref.shape[0]
        window[at : at + rows * SLOTS, :] = ref[...].reshape(rows * SLOTS, ref.shape[-1])
        at += rows * SLOTS


def sum_rows(bounds, rows, x_ref, k_ref, y_ref, flipped, conjugate):
    width = x_ref.shape[-1]
    for side, (start, size) in enumerate(((0, LEFT_F), (2 * LEFT_F, RIGHT_F))):
        real, imag = pl.ds(start, size), pl.ds(start + size, size)

        def one_row(row, carry):
            def tap(w, total):
                index = row + SPAN - 1 - w if flipped else w - row
                xr, xi = x_ref[w, real, :], x_ref[w, imag, :]
                kr, ki = k_ref[index, real, :], k_ref[index, imag, :]
                if conjugate:
                    return (total[0] + kr * xr + ki * xi, total[1] + kr * xi - ki * xr)
                return (total[0] + kr * xr - ki * xi, total[1] + kr * xi + ki * xr)

            zero = jnp.zeros((size, width), F32)
            low, high = bounds[2 * side, row], bounds[2 * side + 1, row]
            yr, yi = lax.fori_loop(low, high, tap, (zero, zero))
            y_ref[row, real, :] = yr
            y_ref[row, imag, :] = yi
            return carry

        lax.fori_loop(0, rows, one_row, 0)


def rows_to_slots(rows, y_ref, to_slots_ref, mask_ref, out_ref):
    for first in range(0, rows, GROUP_OUT):
        freq = y_ref[first : first + GROUP_OUT].reshape(GROUP_OUT * FREQ, y_ref.shape[-1])
        cells = product_split(to_slots_ref, freq).reshape(GROUP_OUT, SLOTS, y_ref.shape[-1])
        out_ref[first : first + GROUP_OUT] = cells * mask_ref[first : first + GROUP_OUT]


def conv_forward_kernel(
    bounds, top, own, bottom, taps, mask, to_freq, taps_freq, to_slots, out, xf, kf, stats, window, yf
):
    rows = own.shape[0]
    fill_window(window, top, own, bottom)
    transform_window(rows + 2 * REACH, window, to_freq, xf)
    for first in range(0, kf.shape[0], GROUP_TAP):
        part = taps[first : first + GROUP_TAP].reshape(GROUP_TAP * SPAN_PAD, taps.shape[-1])
        freq = product_split(taps_freq, part)
        kf[first : first + GROUP_TAP] = freq.reshape(GROUP_TAP, FREQ, freq.shape[-1])
    sum_rows(bounds, rows, xf, kf, yf, False, True)
    rows_to_slots(rows, yf, to_slots, mask, out)
    cells = out[...].reshape(rows * SLOTS, out.shape[-1])
    stats[0:1, :] = jnp.sum(cells, axis=0, keepdims=True)
    stats[1:2, :] = jnp.sum(cells * cells, axis=0, keepdims=True)
    stats[2:8, :] = jnp.zeros((6, stats.shape[-1]), F32)


def conv_backward_kernel(
    bounds, top, own, bottom, xf, kf, mask, to_freq, to_slots, to_taps, out, grad, window, df, yf, gf
):
    rows = own.shape[0]
    width = own.shape[-1]
    fill_window(window, top, own, bottom)
    transform_window(rows + 2 * REACH, window, to_freq, df)
    sum_rows(bounds, rows, df, kf, yf, True, False)
    rows_to_slots(rows, yf, to_slots, mask, out)
    gf[...] = jnp.zeros(gf.shape, F32)
    for side, (start, size) in enumerate(((0, LEFT_F), (2 * LEFT_F, RIGHT_F))):
        real, imag = pl.ds(start, size), pl.ds(start + size, size)

        def one_row(row, carry):
            dr, di = df[row + REACH, real, :], df[row + REACH, imag, :]

            def tap(w, inner):
                xr, xi = xf[w, real, :], xf[w, imag, :]
                gf[w - row, real, :] += dr * xr + di * xi
                gf[w - row, imag, :] += dr * xi - di * xr
                return inner

            lax.fori_loop(bounds[2 * side, row], bounds[2 * side + 1, row], tap, 0)
            return carry

        lax.fori_loop(0, rows, one_row, 0)
    for first in range(0, gf.shape[0], GROUP_GRAD):
        freq = gf[first : first + GROUP_GRAD].reshape(GROUP_GRAD * FREQ, width)
        cells = product_split(to_taps, freq).reshape(GROUP_GRAD, SPAN_PAD, width)
        grad[first : first + GROUP_GRAD] = cells


CHUNK = 256
TAP_ROWS = 28


def chunked(leading):
    return pl.BlockSpec(leading + (CHUNK,), lambda c, *_: (0,) * len(leading) + (c,))


def whole(array):
    return pl.BlockSpec(array.shape, lambda c, *_: (0,) * array.ndim)


def conv_forward(bounds, top, own, bottom, taps, mask):
    rows, _, channels = own.shape
    window = rows + 2 * REACH
    constants = [
        jnp.asarray(split_constant(slots_to_freq(), GROUP_IN)),
        jnp.asarray(split_constant(taps_to_freq(), GROUP_TAP)),
        jnp.asarray(split_constant(freq_to_slots(), GROUP_OUT)),
    ]
    return pl.pallas_call(
        conv_forward_kernel,
        grid_spec=pltpu.PrefetchScalarGridSpec(
            num_scalar_prefetch=1,
            grid=(channels // CHUNK,),
            in_specs=[
                chunked((REACH, SLOTS)),
                chunked((rows, SLOTS)),
                chunked((REACH, SLOTS)),
                chunked((TAP_ROWS, SPAN_PAD)),
                pl.BlockSpec((rows, SLOTS, CHUNK), lambda c, *_: (0, 0, 0)),
            ]
            + [whole(c) for c in constants],
            out_specs=[
                chunked((rows, SLOTS)),
                chunked((window, FREQ)),
                chunked((TAP_ROWS, FREQ)),
                chunked((8,)),
            ],
            scratch_shapes=[
                pltpu.VMEM((window * SLOTS, CHUNK), F32),
                pltpu.VMEM((rows, FREQ, CHUNK), F32),
            ],
        ),
        out_shape=[
            jax.ShapeDtypeStruct((rows, SLOTS, channels), F32),
            jax.ShapeDtypeStruct((window, FREQ, channels), F32),
            jax.ShapeDtypeStruct((TAP_ROWS, FREQ, channels), F32),
            jax.ShapeDtypeStruct((8, channels), F32),
        ],
        compiler_params=pltpu.CompilerParams(vmem_limit_bytes=56 << 20),
        name="conv_forward",
    )(bounds, top, own, bottom, taps, mask, *constants)


def conv_backward(bounds, top, own, bottom, xf, kf, mask):
    rows, _, channels = own.shape
    window = rows + 2 * REACH
    constants = [
        jnp.asarray(split_constant(slots_to_freq(), GROUP_IN)),
        jnp.asarray(split_constant(freq_to_slots(), GROUP_OUT)),
        jnp.asarray(split_constant(freq_to_taps(), GROUP_GRAD)),
    ]
    return pl.pallas_call(
        conv_backward_kernel,
        grid_spec=pltpu.PrefetchScalarGridSpec(
            num_scalar_prefetch=1,
            grid=(channels // CHUNK,),
            in_specs=[
                chunked((REACH, SLOTS)),
                chunked((rows, SLOTS)),
                chunked((REACH, SLOTS)),
                chunked((window, FREQ)),
                chunked((TAP_ROWS, FREQ)),
                pl.BlockSpec((rows, SLOTS, CHUNK), lambda c, *_: (0, 0, 0)),
            ]
            + [whole(c) for c in constants],
            out_specs=[chunked((rows, SLOTS)), chunked((TAP_ROWS, SPAN_PAD))],
            scratch_shapes=[
                pltpu.VMEM((window * SLOTS, CHUNK), F32),
                pltpu.VMEM((window, FREQ, CHUNK), F32),
                pltpu.VMEM((rows, FREQ, CHUNK), F32),
                pltpu.VMEM((TAP_ROWS, FREQ, CHUNK), F32),
            ],
        ),
        out_shape=[
            jax.ShapeDtypeStruct((rows, SLOTS, channels), F32),
            jax.ShapeDtypeStruct((TAP_ROWS, SPAN_PAD, channels), F32),
        ],
        compiler_params=pltpu.CompilerParams(vmem_limit_bytes=56 << 20),
        name="conv_backward",
    )(bounds, top, own, bottom, xf, kf, mask, *constants)


def all_sum_kernel(dp, rows, x_ref, out_ref, slots, own_sem, send_sem, recv_sem):
    count = dp * rows
    me = lax.axis_index("dp") * rows + lax.axis_index("rows")
    barrier = pltpu.get_barrier_semaphore()

    def place(step):
        other = lax.rem(me + step, count)
        return (other // rows, lax.rem(other, rows))

    def greet(step, carry):
        pl.semaphore_signal(barrier, inc=1, device_id=place(step), device_id_type=MESH)
        return carry

    lax.fori_loop(1, count, greet, 0)
    own = pltpu.make_async_copy(x_ref, slots.at[me], own_sem)
    own.start()
    pl.semaphore_wait(barrier, count - 1)

    def send(step, carry):
        pltpu.make_async_remote_copy(
            src_ref=x_ref,
            dst_ref=slots.at[me],
            send_sem=send_sem,
            recv_sem=recv_sem,
            device_id=place(step),
            device_id_type=MESH,
        ).start()
        return carry

    lax.fori_loop(1, count, send, 0)
    own.wait()
    others = slots.at[pl.ds(0, count - 1)]
    pltpu.make_async_copy(others, others, recv_sem).wait()
    pltpu.make_async_copy(others, others, send_sem).wait()
    total = slots[0]
    for index in range(1, count):
        total = total + slots[index]
    out_ref[...] = total


def all_sum(value, dp, rows, collective_id):
    return pl.pallas_call(
        functools.partial(all_sum_kernel, dp, rows),
        out_shape=jax.ShapeDtypeStruct(value.shape, F32),
        in_specs=[pl.BlockSpec(memory_space=pltpu.VMEM)],
        out_specs=pl.BlockSpec(memory_space=pltpu.VMEM),
        scratch_shapes=[
            pltpu.VMEM((dp * rows,) + value.shape, F32),
            pltpu.SemaphoreType.DMA,
            pltpu.SemaphoreType.DMA,
            pltpu.SemaphoreType.DMA,
        ],
        compiler_params=pltpu.CompilerParams(
            collective_id=collective_id, has_side_effects=True, vmem_limit_bytes=32 << 20
        ),
        name="all_sum",
    )(value)


def neighbours(cells, width):
    count = lax.axis_size("rows")
    down = [(i, i + 1) for i in range(count - 1)]
    up = [(i + 1, i) for i in range(count - 1)]
    return (
        lax.ppermute(cells[-width:], "rows", down),
        lax.ppermute(cells[:width], "rows", up),
    )


def gelu_parts(x):
    scale, cubic = 0.7978845608028654, 0.044715
    square = x * x
    t = jnp.tanh(scale * (x + cubic * (x * square)))
    half = 0.5 * (1.0 + t)
    return (x * half, half + 0.5 * x * (1.0 - t * t) * (scale * (1.0 + 3.0 * cubic * square)))


def product(left, right):
    return jnp.dot(left, right, precision=HIGH, preferred_element_type=F32)


def product_t(left, right):
    return lax.dot_general(left, right, (((1,), (1,)), ((), ())), precision=HIGH, preferred_element_type=F32)


def contract(left, right):
    return lax.dot_general(left, right, (((0,), (0,)), ((), ())), precision=HIGH, preferred_element_type=F32)


def shards(
    dp,
    devices_rows,
    inputs,
    image_ids,
    first_norm_gain,
    first_norm_bias,
    point_one,
    kernel_big,
    kernel_small,
    second_norm_gain,
    second_norm_bias,
    point_two,
    feedforward_norm_gain,
    feedforward_norm_bias,
    w_up,
    w_down,
    out_grad,
):
    rows, canvases, columns, channels = inputs.shape
    assert canvases == 1 and kernel_big.shape[0] == SPAN
    pixels = rows * SLOTS
    ids = image_ids[:, 0]
    w_up_all = lax.all_gather(w_up, "rows")
    w_down_all = lax.all_gather(w_down, "rows")

    place = jnp.arange(columns, dtype=jnp.int32)[None, :]
    is_left = (ids >= 0) & (ids < LEFT_IDS)
    is_right = ids >= LEFT_IDS

    def side(member, width):
        name = jnp.max(jnp.where(member, ids, -1), axis=1)
        first = jnp.min(jnp.where(member, place, columns), axis=1)
        return name, jnp.minimum(first, columns - width)

    left_id, left_at = side(is_left, LEFT)
    right_id, right_at = side(is_right, RIGHT)
    slot_column = jnp.concatenate(
        [
            left_at[:, None] + jnp.arange(LEFT, dtype=jnp.int32)[None, :],
            right_at[:, None] + jnp.arange(RIGHT, dtype=jnp.int32)[None, :],
        ],
        axis=1,
    )
    slot_id = jnp.concatenate(
        [
            jnp.broadcast_to(left_id[:, None], (rows, LEFT)),
            jnp.broadcast_to(right_id[:, None], (rows, RIGHT)),
        ],
        axis=1,
    )
    hit = (slot_column[:, :, None] == place[:, None, :]) & (ids[:, None, :] == slot_id[:, :, None])
    hit = hit & (slot_id[:, :, None] >= 0)
    pick = hit.astype(F32)
    slot_mask = jnp.max(pick, axis=2)
    valid = (ids >= 0).astype(F32)

    names = jnp.stack([left_id, right_id], axis=1) + 1
    above, below = neighbours(names, REACH)
    window_names = jnp.concatenate([above, names, below], axis=0)
    window_rows = rows + 2 * REACH
    w_index = jnp.arange(window_rows, dtype=jnp.int32)[None, :]
    r_index = jnp.arange(rows, dtype=jnp.int32)[:, None]
    near = (w_index >= r_index) & (w_index <= r_index + 2 * REACH)
    bounds = []
    for which in range(2):
        same = near & (names[:, which][:, None] == window_names[:, which][None, :]) & (names[:, which][:, None] > 0)
        low = jnp.min(jnp.where(same, w_index, window_rows), axis=1)
        high = jnp.max(jnp.where(same, w_index + 1, 0), axis=1)
        bounds += [jnp.minimum(low, high), high]
    bounds = jnp.stack(bounds).astype(jnp.int32)

    def compact(field):
        out = lax.dot_general(
            pick, field[:, 0], (((2,), (1,)), ((0,), (0,))), precision=HIGHEST, preferred_element_type=F32
        )
        return out.reshape(pixels, channels)

    def expand(cells):
        return lax.dot_general(
            pick,
            cells.reshape(rows, SLOTS, channels),
            (((1,), (1,)), ((0,), (0,))),
            precision=HIGHEST,
            preferred_element_type=F32,
        )[:, None]

    mask = slot_mask.reshape(pixels, 1)
    mask_wide = jnp.broadcast_to(slot_mask[:, :, None], (rows, SLOTS, CHUNK))

    def stack_rows(*rows_list):
        pad = jnp.zeros((8 - len(rows_list), channels), F32)
        return jnp.concatenate([row.reshape(1, channels) for row in rows_list] + [pad], axis=0)

    x = compact(inputs)
    gy = compact(out_grad)

    def sums(field):
        return jnp.sum(field, axis=0), jnp.sum(field * field, axis=0)

    total = all_sum(
        stack_rows(*sums(x), jnp.full((channels,), jnp.sum(valid))), dp, devices_rows, 0
    )
    count = total[2, 0]

    def norm_scale(total):
        mean = total[0] / count
        return mean, lax.rsqrt(total[1] / count - mean * mean + EPSILON)

    mean_one, inv_one = norm_scale(total)
    xhat_one = (x - mean_one) * inv_one
    u1 = (xhat_one * first_norm_gain + first_norm_bias) * mask
    h1 = product(u1, point_one)
    act, act_slope = gelu_parts(h1)
    act = act.reshape(rows, SLOTS, channels)
    small_start = REACH - kernel_small.shape[0] // 2
    edge = (small_start, small_start)
    kernel = kernel_big + jnp.pad(kernel_small, (edge, edge, (0, 0)))
    taps = jnp.pad(kernel, ((0, TAP_ROWS - SPAN), (0, SPAN_PAD - SPAN), (0, 0)))
    act_above, act_below = neighbours(act, REACH)
    conv, xf, kf, conv_sums = conv_forward(bounds, act_above, act, act_below, taps, mask_wide)
    conv = conv.reshape(pixels, channels)
    mean_two, inv_two = norm_scale(all_sum(conv_sums, dp, devices_rows, 1))
    xhat_two = (conv - mean_two) * inv_two
    u2 = (xhat_two * second_norm_gain + second_norm_bias) * mask
    act2, act2_slope = gelu_parts(u2)
    mixed = x + product(act2, point_two)
    mixed_masked = mixed * mask
    mean_three, inv_three = norm_scale(
        all_sum(stack_rows(*sums(mixed_masked)), dp, devices_rows, 2)
    )
    xhat_three = (mixed - mean_three) * inv_three
    u3 = (xhat_three * feedforward_norm_gain + feedforward_norm_bias) * mask

    ffn = jnp.zeros((pixels, channels), F32)
    du3 = jnp.zeros((pixels, channels), F32)
    grad_up, grad_down = [], []
    for part in range(devices_rows):
        up, down = w_up_all[part], w_down_all[part]
        hid, slope = gelu_parts(product(u3, up))
        ffn = ffn + product(hid, down)
        dpre = product_t(gy, down) * slope
        du3 = du3 + product_t(dpre, up)
        grad_up.append(contract(u3, dpre))
        grad_down.append(contract(hid, gy))
    grad_w = lax.psum_scatter(
        jnp.stack([jnp.stack(grad_up), jnp.stack(grad_down)], axis=1), "rows", scatter_dimension=0, tiled=False
    )
    grad_w = lax.psum(grad_w, "dp")

    def norm_back(dy, xhat, inv, gain, number):
        masked = dy * mask
        total = all_sum(
            stack_rows(jnp.sum(masked, axis=0), jnp.sum(masked * xhat, axis=0)), dp, devices_rows, number
        )
        grad_bias, grad_gain = total[0], total[1]
        field = mask * gain * inv * (masked - grad_bias / count - xhat * (grad_gain / count))
        return field, grad_gain, grad_bias

    back_three, grad_gain_three, grad_bias_three = norm_back(
        du3, xhat_three, inv_three, feedforward_norm_gain, 3
    )
    dmixed = gy + back_three
    grad_point_two = contract(act2, dmixed)
    du2 = product_t(dmixed, point_two) * act2_slope
    dconv, grad_gain_two, grad_bias_two = norm_back(du2, xhat_two, inv_two, second_norm_gain, 4)
    dconv = dconv.reshape(rows, SLOTS, channels)
    d_above, d_below = neighbours(dconv, REACH)
    dact, grad_taps = conv_backward(bounds, d_above, dconv, d_below, xf, kf, mask_wide)
    dh1 = dact.reshape(pixels, channels) * act_slope
    grad_point_one = contract(u1, dh1)
    du1 = product_t(dh1, point_one)
    back_one, grad_gain_one, grad_bias_one = norm_back(du1, xhat_one, inv_one, first_norm_gain, 5)
    grad_cells = back_three + back_one
    output = inputs + expand((mixed - x) + ffn)
    grad_input = out_grad + expand(grad_cells)
    grad_point_one, grad_point_two, grad_kernel = lax.psum(
        (grad_point_one, grad_point_two, grad_taps[:SPAN, :SPAN]), ("dp", "rows")
    )
    small_end = small_start + kernel_small.shape[0]
    grad_small = grad_kernel[small_start:small_end, small_start:small_end]
    return (
        output,
        grad_input,
        grad_gain_one,
        grad_bias_one,
        grad_point_one,
        grad_kernel,
        grad_small,
        grad_gain_two,
        grad_bias_two,
        grad_point_two,
        grad_gain_three,
        grad_bias_three,
        grad_w[0],
        grad_w[1],
    )


def solution(mesh):
    field = P("rows", "dp", None, None)
    everywhere = P()
    up, down = P(None, "rows"), P("rows", None)
    return jax.shard_map(
        functools.partial(shards, mesh.shape["dp"], mesh.shape["rows"]),
        mesh=mesh,
        in_specs=(field, P("rows", "dp", None)) + (everywhere,) * 10 + (up, down, field),
        out_specs=(field, field) + (everywhere,) * 10 + (up, down),
        check_vma=False,
    )
```

```python
import functools

import jax
import jax.numpy as jnp
import numpy as np
from jax import lax
from jax.experimental import pallas as pl
from jax.experimental.pallas import tpu as pltpu
from jax.sharding import PartitionSpec as P

EPSILON = 1e-05
HIGHEST = lax.Precision.HIGHEST
HIGH = lax.Precision.HIGH
MESH = pl.DeviceIdType.MESH
F32 = jnp.float32
BF16 = jnp.bfloat16

LEFT, RIGHT = 24, 16
SLOTS = LEFT + RIGHT
LEFT_IDS = 3
LEFT_N, RIGHT_N = 37, 27
LEFT_F, RIGHT_F = 24, 16
FREQ = 2 * LEFT_F + 2 * RIGHT_F
REACH = 13
SPAN = 2 * REACH + 1
SPAN_PAD = 32
LANES = 128


def forward_transform(length, padded, positions, columns):
    count = length // 2 + 1
    out = np.zeros((2 * padded, columns))
    angle = 2 * np.pi * np.outer(np.arange(count), positions) / length
    out[:count, : len(positions)] = np.cos(angle)
    out[padded : padded + count, : len(positions)] = -np.sin(angle)
    return out


def backward_transform(length, padded, positions, rows):
    count = length // 2 + 1
    out = np.zeros((rows, 2 * padded))
    twice = np.where(np.arange(count) == 0, 1.0, 2.0)
    angle = 2 * np.pi * np.outer(positions, np.arange(count)) / length
    out[: len(positions), :count] = np.cos(angle) * twice / length
    out[: len(positions), padded : padded + count] = -np.sin(angle) * twice / length
    return out


def slots_to_freq():
    out = np.zeros((FREQ, SLOTS))
    out[: 2 * LEFT_F, :LEFT] = forward_transform(LEFT_N, LEFT_F, np.arange(LEFT), LEFT)
    out[2 * LEFT_F :, LEFT:] = forward_transform(RIGHT_N, RIGHT_F, np.arange(RIGHT), RIGHT)
    return out


def freq_to_slots():
    out = np.zeros((SLOTS, FREQ))
    out[:LEFT, : 2 * LEFT_F] = backward_transform(LEFT_N, LEFT_F, np.arange(LEFT), LEFT)
    out[LEFT:, 2 * LEFT_F :] = backward_transform(RIGHT_N, RIGHT_F, np.arange(RIGHT), RIGHT)
    return out


def taps_to_freq():
    taps = np.arange(SPAN) - REACH
    return np.concatenate(
        [
            forward_transform(LEFT_N, LEFT_F, taps, SPAN_PAD),
            forward_transform(RIGHT_N, RIGHT_F, taps, SPAN_PAD),
        ]
    )


def freq_to_taps():
    taps = np.arange(SPAN) - REACH
    return np.concatenate(
        [
            backward_transform(LEFT_N, LEFT_F, taps, SPAN_PAD),
            backward_transform(RIGHT_N, RIGHT_F, taps, SPAN_PAD),
        ],
        axis=1,
    )


def split_constant(matrix, group):
    whole = np.kron(np.eye(group), matrix).astype(np.float32)
    high = whole.astype(jnp.bfloat16)
    low = (whole - high.astype(np.float32)).astype(jnp.bfloat16)
    return np.concatenate([high, high, low], axis=1)


def split_stack(value):
    high = value.astype(BF16)
    low = (value - high.astype(F32)).astype(BF16)
    return jnp.concatenate([high, low, high], axis=0)


def product_split(constant_ref, value):
    return jnp.dot(constant_ref[...], split_stack(value), preferred_element_type=F32)


GROUP_IN = 6
GROUP_OUT = 4
GROUP_TAP = 7
GROUP_GRAD = 4


def transform_window(window, to_freq_ref, out_ref):
    for first in range(0, window.shape[0], GROUP_IN):
        part = window[first : first + GROUP_IN].reshape(GROUP_IN * SLOTS, window.shape[-1])
        freq = product_split(to_freq_ref, part)
        out_ref[first : first + GROUP_IN] = freq.reshape(GROUP_IN, FREQ, freq.shape[-1])


def sum_rows(bounds, rows, x_ref, k_ref, y_ref, flipped, conjugate):
    width = x_ref.shape[-1]
    for side, (start, size) in enumerate(((0, LEFT_F), (2 * LEFT_F, RIGHT_F))):
        real, imag = pl.ds(start, size), pl.ds(start + size, size)

        def one_row(row, carry):
            def tap(w, total):
                index = row + SPAN - 1 - w if flipped else w - row
                xr, xi = x_ref[w, real, :], x_ref[w, imag, :]
                kr, ki = k_ref[index, real, :], k_ref[index, imag, :]
                if conjugate:
                    return (total[0] + kr * xr + ki * xi, total[1] + kr * xi - ki * xr)
                return (total[0] + kr * xr - ki * xi, total[1] + kr * xi + ki * xr)

            zero = jnp.zeros((size, width), F32)
            low, high = bounds[2 * side, row], bounds[2 * side + 1, row]
            yr, yi = lax.fori_loop(low, high, tap, (zero, zero))
            y_ref[row, real, :] = yr
            y_ref[row, imag, :] = yi
            return carry

        lax.fori_loop(0, rows, one_row, 0)


def rows_to_slots(rows, y_ref, to_slots_ref, mask_ref, out_ref):
    for first in range(0, rows, GROUP_OUT):
        freq = y_ref[first : first + GROUP_OUT].reshape(GROUP_OUT * FREQ, y_ref.shape[-1])
        cells = product_split(to_slots_ref, freq).reshape(GROUP_OUT, SLOTS, y_ref.shape[-1])
        out_ref[first : first + GROUP_OUT] = cells * mask_ref[first : first + GROUP_OUT]


def conv_forward_kernel(
    bounds, window, taps, mask, to_freq, taps_freq, to_slots, out, xf, kf, stats, yf
):
    rows = out.shape[0]
    transform_window(window, to_freq, xf)
    for first in range(0, kf.shape[0], GROUP_TAP):
        part = taps[first : first + GROUP_TAP].reshape(GROUP_TAP * SPAN_PAD, taps.shape[-1])
        freq = product_split(taps_freq, part)
        kf[first : first + GROUP_TAP] = freq.reshape(GROUP_TAP, FREQ, freq.shape[-1])
    sum_rows(bounds, rows, xf, kf, yf, False, True)
    rows_to_slots(rows, yf, to_slots, mask, out)
    cells = out[...].reshape(rows * SLOTS, out.shape[-1])
    stats[0:1, :] = jnp.sum(cells, axis=0, keepdims=True)
    stats[1:2, :] = jnp.sum(cells * cells, axis=0, keepdims=True)
    stats[2:8, :] = jnp.zeros((6, stats.shape[-1]), F32)


def conv_backward_kernel(
    bounds, window, xf, kf, mask, to_freq, to_slots, to_taps, out, grad, df, yf, gf
):
    rows = out.shape[0]
    width = out.shape[-1]
    transform_window(window, to_freq, df)
    sum_rows(bounds, rows, df, kf, yf, True, False)
    rows_to_slots(rows, yf, to_slots, mask, out)
    gf[...] = jnp.zeros(gf.shape, F32)
    for side, (start, size) in enumerate(((0, LEFT_F), (2 * LEFT_F, RIGHT_F))):
        real, imag = pl.ds(start, size), pl.ds(start + size, size)

        def one_row(row, carry):
            dr, di = df[row + REACH, real, :], df[row + REACH, imag, :]

            def tap(w, inner):
                xr, xi = xf[w, real, :], xf[w, imag, :]
                gf[w - row, real, :] += dr * xr + di * xi
                gf[w - row, imag, :] += dr * xi - di * xr
                return inner

            lax.fori_loop(bounds[2 * side, row], bounds[2 * side + 1, row], tap, 0)
            return carry

        lax.fori_loop(0, rows, one_row, 0)
    for first in range(0, gf.shape[0], GROUP_GRAD):
        freq = gf[first : first + GROUP_GRAD].reshape(GROUP_GRAD * FREQ, width)
        cells = product_split(to_taps, freq).reshape(GROUP_GRAD, SPAN_PAD, width)
        grad[first : first + GROUP_GRAD] = cells


CHUNK = 256
TAP_ROWS = 28


def chunked(leading):
    return pl.BlockSpec(leading + (CHUNK,), lambda c, *_: (0,) * len(leading) + (c,))


def whole(array):
    return pl.BlockSpec(array.shape, lambda c, *_: (0,) * array.ndim)


def conv_forward(bounds, field, taps, mask):
    window, _, channels = field.shape
    rows = window - 2 * REACH
    constants = [
        jnp.asarray(split_constant(slots_to_freq(), GROUP_IN)),
        jnp.asarray(split_constant(taps_to_freq(), GROUP_TAP)),
        jnp.asarray(split_constant(freq_to_slots(), GROUP_OUT)),
    ]
    return pl.pallas_call(
        conv_forward_kernel,
        grid_spec=pltpu.PrefetchScalarGridSpec(
            num_scalar_prefetch=1,
            grid=(channels // CHUNK,),
            in_specs=[
                chunked((window, SLOTS)),
                chunked((TAP_ROWS, SPAN_PAD)),
                pl.BlockSpec((rows, SLOTS, CHUNK), lambda c, *_: (0, 0, 0)),
            ]
            + [whole(c) for c in constants],
            out_specs=[
                chunked((rows, SLOTS)),
                chunked((window, FREQ)),
                chunked((TAP_ROWS, FREQ)),
                chunked((8,)),
            ],
            scratch_shapes=[
                pltpu.VMEM((rows, FREQ, CHUNK), F32),
            ],
        ),
        out_shape=[
            jax.ShapeDtypeStruct((rows, SLOTS, channels), F32),
            jax.ShapeDtypeStruct((window, FREQ, channels), F32),
            jax.ShapeDtypeStruct((TAP_ROWS, FREQ, channels), F32),
            jax.ShapeDtypeStruct((8, channels), F32),
        ],
        compiler_params=pltpu.CompilerParams(vmem_limit_bytes=56 << 20),
        name="conv_forward",
    )(bounds, field, taps, mask, *constants)


def conv_backward(bounds, field, xf, kf, mask):
    window, _, channels = field.shape
    rows = window - 2 * REACH
    constants = [
        jnp.asarray(split_constant(slots_to_freq(), GROUP_IN)),
        jnp.asarray(split_constant(freq_to_slots(), GROUP_OUT)),
        jnp.asarray(split_constant(freq_to_taps(), GROUP_GRAD)),
    ]
    return pl.pallas_call(
        conv_backward_kernel,
        grid_spec=pltpu.PrefetchScalarGridSpec(
            num_scalar_prefetch=1,
            grid=(channels // CHUNK,),
            in_specs=[
                chunked((window, SLOTS)),
                chunked((window, FREQ)),
                chunked((TAP_ROWS, FREQ)),
                pl.BlockSpec((rows, SLOTS, CHUNK), lambda c, *_: (0, 0, 0)),
            ]
            + [whole(c) for c in constants],
            out_specs=[chunked((rows, SLOTS)), chunked((TAP_ROWS, SPAN_PAD))],
            scratch_shapes=[
                pltpu.VMEM((window, FREQ, CHUNK), F32),
                pltpu.VMEM((rows, FREQ, CHUNK), F32),
                pltpu.VMEM((TAP_ROWS, FREQ, CHUNK), F32),
            ],
        ),
        out_shape=[
            jax.ShapeDtypeStruct((rows, SLOTS, channels), F32),
            jax.ShapeDtypeStruct((TAP_ROWS, SPAN_PAD, channels), F32),
        ],
        compiler_params=pltpu.CompilerParams(vmem_limit_bytes=56 << 20),
        name="conv_backward",
    )(bounds, field, xf, kf, mask, *constants)


class Net:
    def __init__(self, dp, rows, send_sem, recv_sem):
        self.count, self.rows = dp, rows
        self.send_sem, self.recv_sem, self.used = send_sem, recv_sem, 0
        self.dp = lax.axis_index("dp")
        self.z = lax.axis_index("rows")
        self.bits = list(range(1, dp.bit_length() - 1))

    def bit(self, index):
        return lax.rem(self.dp // (1 << index), 2)

    def across(self, index):
        return (self.dp + (1 << index) * (1 - 2 * self.bit(index)), self.z)

    def line(self, step):
        return (self.dp, lax.rem(self.z + step, self.rows))

    def layer(self, step):
        return (lax.rem(self.dp + step, self.count), self.z)

    def greet(self):
        barrier = pltpu.get_barrier_semaphore()

        def greet_line(step, carry):
            pl.semaphore_signal(barrier, inc=1, device_id=self.line(step), device_id_type=MESH)
            return carry

        def greet_layer(step, carry):
            pl.semaphore_signal(barrier, inc=1, device_id=self.layer(step), device_id_type=MESH)
            return carry

        lax.fori_loop(1, self.rows, greet_line, 0)
        lax.fori_loop(1, self.count, greet_layer, 0)

    def ready(self):
        pl.semaphore_wait(pltpu.get_barrier_semaphore(), self.rows + self.count - 2)

    def copy(self, src, dst, device):
        made = pltpu.make_async_remote_copy(
            src_ref=src,
            dst_ref=dst,
            send_sem=self.send_sem.at[self.used],
            recv_sem=self.recv_sem.at[self.used],
            device_id=device,
            device_id_type=MESH,
        )
        self.used += 1
        return made

    def own(self, src, dst):
        made = pltpu.make_async_copy(src, dst, self.recv_sem.at[self.used])
        self.used += 1
        return made


def all_sum_job(net, value, out, line_slots, part, layer_slots):
    own = net.own(value, line_slots.at[net.z])
    own.start()
    sent = [net.copy(value, line_slots.at[net.z], net.line(s)) for s in range(1, net.rows)]
    for one in sent:
        one.start()
    yield
    own.wait()
    for one in sent:
        one.wait()
    total = line_slots[0]
    for index in range(1, net.rows):
        total = total + line_slots[index]
    part[...] = total
    own = net.own(part, layer_slots.at[net.dp])
    own.start()
    sent = [net.copy(part, layer_slots.at[net.dp], net.layer(s)) for s in range(1, net.count)]
    for one in sent:
        one.start()
    yield
    own.wait()
    for one in sent:
        one.wait()
    total = layer_slots[0]
    for index in range(1, net.count):
        total = total + layer_slots[index]
    out[...] = total


def aligned(value, unit):
    return pl.multiple_of(value, unit)


def halving(net, order, rows):
    base, steps = 0, []
    for bit in order:
        steps.append((bit, base, rows))
        rows //= 2
        base = base + net.bit(bit) * rows
    return steps, base, rows


def add_rows(dst, src, count, step):
    def one(i, carry):
        at = aligned(i * step, step)
        to, of = dst(at), src(at)
        to[...] = to[...] + of[...]
        return carry

    lax.fori_loop(0, count // step, one, 0)


def run(*jobs):
    jobs = list(jobs)
    while jobs:
        jobs = [job for job in jobs if next(job, StopIteration) is not StopIteration]


def line_gather_job(net, value, out):
    own = net.own(value, out.at[net.z])
    own.start()
    sent = [net.copy(value, out.at[net.z], net.line(s)) for s in range(1, net.rows)]
    for one in sent:
        one.start()
    yield
    own.wait()
    for one in sent:
        one.wait()


def sides(net, rows):
    core = net.bit(0)
    return [
        (pl.ds(aligned((2 * core + side) * LANES, LANES), LANES), *halving(net, order, rows))
        for side, order in enumerate((net.bits, net.bits[::-1]))
    ]


def weights_line_job(net, up, down, wall):
    own = [net.own(up, wall.at[net.z, 0]), net.own(down, wall.at[net.z, 1])]
    for one in own:
        one.start()
    for one in own:
        one.wait()
    last = net.rows - 1
    for step in range(1, net.rows):
        moves = []
        for lanes, _, base, rows in sides(net, up.shape[0]):
            for way in (1, -1):
                shard = net.z - way * (step - 1)
                going = (net.z >= step - 1) & (net.z < last) if way > 0 else (net.z <= last - (step - 1)) & (net.z > 0)
                coming = net.z >= step if way > 0 else net.z <= last - step
                shard = lax.rem(shard + net.rows, net.rows)
                piece = wall.at[shard, :, pl.ds(aligned(base, 8), rows), lanes]
                one = net.copy(piece, piece, net.line(way % net.rows))
                pl.when(going)(one.start)
                moves.append((one, going, coming))
        yield
        for one, going, coming in moves:
            pl.when(coming)(one.wait_recv)
            pl.when(going)(one.wait_send)


def weights_layer_job(net, wall):
    parts = sides(net, wall.shape[2])
    for back in range(1, len(net.bits) + 1):
        moves = []
        for lanes, steps, _, _ in parts:
            bit, base, rows = steps[-back]
            mine = pl.ds(aligned(base + net.bit(bit) * (rows // 2), 8), rows // 2)
            for step in range(1, net.rows):
                piece = wall.at[lax.rem(net.z + step, net.rows), :, mine, lanes]
                moves.append(net.copy(piece, piece, net.across(bit)))
        for one in moves:
            one.start()
        yield
        for one in moves:
            one.wait()


def weights_pair_job(net, wall):
    half = wall.shape[3] // 2
    lanes = pl.ds(aligned(net.bit(0) * half, LANES), half)
    moves = []
    for step in range(1, net.rows):
        piece = wall.at[lax.rem(net.z + step, net.rows), :, :, lanes]
        moves.append(net.copy(piece, piece, net.across(0)))
    for one in moves:
        one.start()
    yield
    for one in moves:
        one.wait()


def halo_job(net, field, window, zeros):
    rows = field.shape[0]
    own = net.own(field, window.at[pl.ds(REACH, rows)])
    own.start()
    has_above, has_below = net.z > 0, net.z < net.rows - 1
    down = net.copy(field.at[pl.ds(rows - REACH, REACH)], window.at[pl.ds(0, REACH)], net.line(1))
    up = net.copy(field.at[pl.ds(0, REACH)], window.at[pl.ds(REACH + rows, REACH)], net.line(net.rows - 1))
    pl.when(has_below)(down.start)
    pl.when(has_above)(up.start)
    zeros[...] = jnp.zeros(zeros.shape, F32)
    top = net.own(zeros, window.at[pl.ds(0, REACH)])
    bottom = net.own(zeros, window.at[pl.ds(REACH + rows, REACH)])
    pl.when(jnp.logical_not(has_above))(top.start)
    pl.when(jnp.logical_not(has_below))(bottom.start)
    yield
    own.wait()
    pl.when(jnp.logical_not(has_above))(top.wait)
    pl.when(jnp.logical_not(has_below))(bottom.wait)
    pl.when(has_above)(down.wait_recv)
    pl.when(has_below)(down.wait_send)
    pl.when(has_below)(up.wait_recv)
    pl.when(has_above)(up.wait_send)


def reduce_layer_job(net, source, acc, got_pair, got, out):
    lead, rows, width = source.shape
    half = width // 2
    core = net.bit(0)
    mine = pl.ds(aligned(core * half, LANES), half)
    other = pl.ds(aligned((1 - core) * half, LANES), half)
    own = [net.own(source.at[k, :, mine], acc.at[k]) for k in range(lead)]
    sent = [net.copy(source.at[k, :, other], got_pair.at[k], net.across(0)) for k in range(lead)]
    for one in own + sent:
        one.start()
    yield
    for k in range(lead):
        own[k].wait()
        sent[k].wait()
        add_rows(lambda at: acc.at[k, pl.ds(at, 32)], lambda at: got_pair.at[k, pl.ds(at, 32)], rows, 32)
    parts = sides(net, rows)
    for index in range(len(net.bits)):
        moves = []
        for side, (_, steps, _, _) in enumerate(parts):
            bit, base, size = steps[index]
            size //= 2
            give = base + (1 - net.bit(bit)) * size
            keep = base + net.bit(bit) * size
            lanes = pl.ds(side * LANES, LANES)
            place = got.at[side, :, pl.ds(rows - 2 * size, size)]
            one = net.copy(acc.at[:, pl.ds(aligned(give, 8), size), lanes], place, net.across(bit))
            one.start()
            moves.append((one, keep, size, lanes, side))
        yield
        for one, keep, size, lanes, side in moves:
            one.wait()
            for k in range(lead):
                add_rows(
                    lambda at: acc.at[k, pl.ds(aligned(keep + at, 8), 8), lanes],
                    lambda at: got.at[side, k, pl.ds(rows - 2 * size + at, 8)],
                    size,
                    8,
                )
    if out is not None:
        for side, (_, _, base, size) in enumerate(parts):
            out[side] = acc[:, pl.ds(aligned(base, 8), size), pl.ds(side * LANES, LANES)]


def scatter_line_job(net, part, got, out):
    own = net.own(part.at[:, net.z], got.at[net.z])
    own.start()
    sent = []
    for step in range(1, net.rows):
        other = lax.rem(net.z + step, net.rows)
        sent.append(net.copy(part.at[:, other], got.at[net.z], net.line(step)))
        sent[-1].start()
    yield
    own.wait()
    for one in sent:
        one.wait()
    total = got[0]
    for index in range(1, net.rows):
        total = total + got[index]
    out[...] = total


def gather_layer_job(net, out):
    parts = sides(net, out.shape[0])
    for back in range(1, len(net.bits) + 1):
        moves = []
        for lanes, steps, _, _ in parts:
            bit, base, rows = steps[-back]
            mine = pl.ds(aligned(base + net.bit(bit) * (rows // 2), 8), rows // 2)
            piece = out.at[mine, lanes]
            one = net.copy(piece, piece, net.across(bit))
            one.start()
            moves.append(one)
        yield
        for one in moves:
            one.wait()
    half = out.shape[1] // 2
    piece = out.at[:, pl.ds(aligned(net.bit(0) * half, LANES), half)]
    one = net.copy(piece, piece, net.across(0))
    one.start()
    yield
    one.wait()


def place_then_gather_job(net, part, out):
    own = []
    for side, (lanes, _, base, rows) in enumerate(sides(net, out.shape[0])):
        own.append(net.own(part.at[side], out.at[pl.ds(aligned(base, 8), rows), lanes]))
        own[-1].start()
    for one in own:
        one.wait()
    yield from gather_layer_job(net, out)


def reduce_all_job(net, source, acc, got_pair, got, got_line, out):
    yield from reduce_layer_job(net, source, acc, got_pair, got, None)
    parts = sides(net, source.shape[1])
    moves, own = [], []
    for side, (_, _, base, rows) in enumerate(parts):
        rows //= net.rows
        inner = pl.ds(side * LANES, LANES)
        own.append(net.own(acc.at[0, pl.ds(aligned(base + net.z * rows, 8), rows), inner], got_line.at[side, net.z]))
        for step in range(1, net.rows):
            other = lax.rem(net.z + step, net.rows)
            piece = acc.at[0, pl.ds(aligned(base + other * rows, 8), rows), inner]
            moves.append(net.copy(piece, got_line.at[side, net.z], net.line(step)))
    for one in own + moves:
        one.start()
    yield
    for one in own + moves:
        one.wait()
    moves = []
    for side, (lanes, _, base, rows) in enumerate(parts):
        rows //= net.rows
        total = got_line[side, 0]
        for index in range(1, net.rows):
            total = total + got_line[side, index]
        piece = out.at[pl.ds(aligned(base + net.z * rows, 8), rows), lanes]
        out[pl.ds(aligned(base + net.z * rows, 8), rows), lanes] = total
        for step in range(1, net.rows):
            moves.append(net.copy(piece, piece, net.line(step)))
            moves[-1].start()
    yield
    for one in moves:
        one.wait()
    yield from gather_layer_job(net, out)


VMEM = pl.BlockSpec(memory_space=pltpu.VMEM)
HBM = pl.BlockSpec(memory_space=pltpu.HBM)
COPIES = 96


def shape(*dims):
    return jax.ShapeDtypeStruct(dims, F32)


def exchange(name, number, mesh, body, args, in_specs, outs, out_specs, scratch, aliases=None):
    dp, rows = mesh

    def kernel(*refs):
        *refs, send_sem, recv_sem = refs
        net = Net(dp, rows, send_sem, recv_sem)
        net.greet()
        net.ready()
        body(net, *refs)
        assert net.used <= COPIES

    return pl.pallas_call(
        kernel,
        out_shape=outs,
        in_specs=in_specs,
        out_specs=out_specs,
        scratch_shapes=scratch + [pltpu.SemaphoreType.DMA((COPIES,))] * 2,
        input_output_aliases=aliases or {},
        compiler_params=pltpu.CompilerParams(
            collective_id=number, has_side_effects=True, vmem_limit_bytes=48 << 20
        ),
        name=name,
    )(*args)


def sum_scratch(mesh, height):
    dp, rows = mesh
    return [pltpu.VMEM((rows, height, LANES), F32), pltpu.VMEM((height, LANES), F32), pltpu.VMEM((dp, height, LANES), F32)]


def sums_names_weights(mesh, value, names, up, down):
    rows = mesh[1]

    def body(net, value, names, up, down, total, all_names, wall, *slots):
        run(
            all_sum_job(net, value, total, *slots),
            line_gather_job(net, names, all_names),
            weights_line_job(net, up, down, wall),
        )

    return exchange(
        "sums_one",
        0,
        mesh,
        body,
        (value, names, up, down),
        [VMEM, VMEM, HBM, HBM],
        [
            shape(*value.shape),
            jax.ShapeDtypeStruct((rows,) + names.shape, jnp.int32),
            shape(rows, 2, *up.shape),
        ],
        [VMEM, VMEM, HBM],
        sum_scratch(mesh, value.shape[0]),
    )


def halo_weights(mesh, field, wall):
    rows = field.shape[0]

    def body(net, field, wall_in, window, wall, zeros):
        run(halo_job(net, field, window, zeros), weights_layer_job(net, wall))

    return exchange(
        "halo_act",
        1,
        mesh,
        body,
        (field, wall),
        [HBM, HBM],
        [shape(rows + 2 * REACH, *field.shape[1:]), shape(*wall.shape)],
        [HBM, HBM],
        [pltpu.VMEM((REACH,) + field.shape[1:], F32)],
        {1: 1},
    )


def sums_weights(mesh, value, wall):
    def body(net, value, wall_in, total, wall, *slots):
        run(all_sum_job(net, value, total, *slots), weights_pair_job(net, wall))

    return exchange(
        "sums_two",
        2,
        mesh,
        body,
        (value, wall),
        [VMEM, HBM],
        [shape(*value.shape), shape(*wall.shape)],
        [VMEM, HBM],
        sum_scratch(mesh, value.shape[0]),
        {1: 1},
    )


def sums_only(mesh, name, number, value):
    def body(net, value, total, *slots):
        run(all_sum_job(net, value, total, *slots))

    return exchange(
        name, number, mesh, body, (value,), [VMEM], shape(*value.shape), VMEM, sum_scratch(mesh, value.shape[0])
    )


def layer_scratch(lead, rows, width):
    return [
        pltpu.VMEM((lead, rows, width // 2), F32),
        pltpu.VMEM((lead, rows, width // 2), F32),
        pltpu.VMEM((2, lead, rows, LANES), F32),
    ]


def sums_grads(mesh, value, grads):
    lead, rows, width = grads.shape

    def body(net, value, grads, total, part, line, mid, layer, acc, got_pair, got):
        run(
            all_sum_job(net, value, total, line, mid, layer),
            reduce_layer_job(net, grads, acc, got_pair, got, part),
        )

    return exchange(
        "sums_four",
        4,
        mesh,
        body,
        (value, grads),
        [VMEM, HBM],
        [shape(*value.shape), shape(2, lead, 2 * rows // mesh[0], LANES)],
        [VMEM, VMEM],
        sum_scratch(mesh, value.shape[0]) + layer_scratch(lead, rows, width),
    )


def sums_scatter(mesh, value, part):
    def body(net, value, part, total, mine, line, mid, layer, got):
        run(all_sum_job(net, value, total, line, mid, layer), scatter_line_job(net, part, got, mine))

    piece = (2,) + part.shape[2:]
    return exchange(
        "sums_five",
        5,
        mesh,
        body,
        (value, part),
        [VMEM, VMEM],
        [shape(*value.shape), shape(*piece)],
        [VMEM, VMEM],
        sum_scratch(mesh, value.shape[0]) + [pltpu.VMEM((mesh[1],) + piece, F32)],
    )


def halo_grads(mesh, field, part, height, width):
    rows = field.shape[0]

    def body(net, field, part, window, grads, zeros):
        run(halo_job(net, field, window, zeros), place_then_gather_job(net, part, grads))

    return exchange(
        "halo_grad",
        6,
        mesh,
        body,
        (field, part),
        [HBM, VMEM],
        [shape(rows + 2 * REACH, *field.shape[1:]), shape(height, width)],
        [HBM, VMEM],
        [pltpu.VMEM((REACH,) + field.shape[1:], F32)],
    )


def sums_all_grads(mesh, value, grads):
    rows, width = grads.shape
    piece = 2 * rows // mesh[0] // mesh[1]

    def body(net, value, grads, total, out, line, mid, layer, acc, got_pair, got, got_line):
        run(
            all_sum_job(net, value, total, line, mid, layer),
            reduce_all_job(net, grads, acc, got_pair, got, got_line, out),
        )

    return exchange(
        "sums_six",
        7,
        mesh,
        body,
        (value, grads.reshape(1, rows, width)),
        [VMEM, HBM],
        [shape(*value.shape), shape(rows, width)],
        [VMEM, VMEM],
        sum_scratch(mesh, value.shape[0])
        + layer_scratch(1, rows, width)
        + [pltpu.VMEM((2, mesh[1], piece, LANES), F32)],
    )


def gelu_parts(x):
    scale, cubic = 0.7978845608028654, 0.044715
    square = x * x
    t = jnp.tanh(scale * (x + cubic * (x * square)))
    half = 0.5 * (1.0 + t)
    return (x * half, half + 0.5 * x * (1.0 - t * t) * (scale * (1.0 + 3.0 * cubic * square)))


def product(left, right):
    return jnp.dot(left, right, precision=HIGH, preferred_element_type=F32)


def product_t(left, right):
    return lax.dot_general(left, right, (((1,), (1,)), ((), ())), precision=HIGH, preferred_element_type=F32)


def contract(left, right):
    return lax.dot_general(left, right, (((0,), (0,)), ((), ())), precision=HIGH, preferred_element_type=F32)


def shards(
    dp,
    devices_rows,
    inputs,
    image_ids,
    first_norm_gain,
    first_norm_bias,
    point_one,
    kernel_big,
    kernel_small,
    second_norm_gain,
    second_norm_bias,
    point_two,
    feedforward_norm_gain,
    feedforward_norm_bias,
    w_up,
    w_down,
    out_grad,
):
    rows, canvases, columns, channels = inputs.shape
    assert canvases == 1 and kernel_big.shape[0] == SPAN
    pixels = rows * SLOTS
    ids = image_ids[:, 0]
    mesh = (dp, devices_rows)

    place = jnp.arange(columns, dtype=jnp.int32)[None, :]
    is_left = (ids >= 0) & (ids < LEFT_IDS)
    is_right = ids >= LEFT_IDS

    def side(member, width):
        name = jnp.max(jnp.where(member, ids, -1), axis=1)
        first = jnp.min(jnp.where(member, place, columns), axis=1)
        return name, jnp.minimum(first, columns - width)

    left_id, left_at = side(is_left, LEFT)
    right_id, right_at = side(is_right, RIGHT)
    slot_column = jnp.concatenate(
        [
            left_at[:, None] + jnp.arange(LEFT, dtype=jnp.int32)[None, :],
            right_at[:, None] + jnp.arange(RIGHT, dtype=jnp.int32)[None, :],
        ],
        axis=1,
    )
    slot_id = jnp.concatenate(
        [
            jnp.broadcast_to(left_id[:, None], (rows, LEFT)),
            jnp.broadcast_to(right_id[:, None], (rows, RIGHT)),
        ],
        axis=1,
    )
    hit = (slot_column[:, :, None] == place[:, None, :]) & (ids[:, None, :] == slot_id[:, :, None])
    hit = hit & (slot_id[:, :, None] >= 0)
    pick = hit.astype(F32)
    slot_mask = jnp.max(pick, axis=2)
    valid = (ids >= 0).astype(F32)

    def compact(field):
        out = lax.dot_general(
            pick, field[:, 0], (((2,), (1,)), ((0,), (0,))), precision=HIGHEST, preferred_element_type=F32
        )
        return out.reshape(pixels, channels)

    def expand(cells):
        return lax.dot_general(
            pick,
            cells.reshape(rows, SLOTS, channels),
            (((1,), (1,)), ((0,), (0,))),
            precision=HIGHEST,
            preferred_element_type=F32,
        )[:, None]

    def pack(first, second):
        return jnp.stack([first, second]).reshape(2 * channels // LANES, LANES)

    def sums(field):
        return jnp.sum(field, axis=0), jnp.sum(field * field, axis=0)

    names = jnp.stack([left_id, right_id], axis=1) + 1
    names_tile = jnp.pad(names.reshape(1, 2 * rows), ((0, 7), (0, LANES - 2 * rows)))
    x = compact(inputs)
    gy = compact(out_grad)
    total, all_names, wall = sums_names_weights(
        mesh,
        jnp.concatenate([pack(*sums(x)), pack(jnp.full((channels,), jnp.sum(valid)), jnp.zeros((channels,)))]),
        names_tile,
        w_up,
        w_down,
    )
    count = total[8, 0]
    total = total[:8].reshape(2, channels)
    all_names = jnp.pad(all_names[:, 0, : 2 * rows].reshape(devices_rows * rows, 2), ((REACH, REACH), (0, 0)))
    window_rows = rows + 2 * REACH
    window_names = lax.dynamic_slice_in_dim(all_names, lax.axis_index("rows") * rows, window_rows, 0)
    w_index = jnp.arange(window_rows, dtype=jnp.int32)[None, :]
    r_index = jnp.arange(rows, dtype=jnp.int32)[:, None]
    near = (w_index >= r_index) & (w_index <= r_index + 2 * REACH)
    bounds = []
    for which in range(2):
        same = near & (names[:, which][:, None] == window_names[:, which][None, :]) & (names[:, which][:, None] > 0)
        low = jnp.min(jnp.where(same, w_index, window_rows), axis=1)
        high = jnp.max(jnp.where(same, w_index + 1, 0), axis=1)
        bounds += [jnp.minimum(low, high), high]
    bounds = jnp.stack(bounds).astype(jnp.int32)

    mask = slot_mask.reshape(pixels, 1)
    mask_wide = jnp.broadcast_to(slot_mask[:, :, None], (rows, SLOTS, CHUNK))

    def norm_scale(total):
        mean = total[0] / count
        return mean, lax.rsqrt(total[1] / count - mean * mean + EPSILON)

    mean_one, inv_one = norm_scale(total)
    xhat_one = (x - mean_one) * inv_one
    u1 = (xhat_one * first_norm_gain + first_norm_bias) * mask
    h1 = product(u1, point_one)
    act, act_slope = gelu_parts(h1)
    act = act.reshape(rows, SLOTS, channels)
    small_start = REACH - kernel_small.shape[0] // 2
    edge = (small_start, small_start)
    kernel = kernel_big + jnp.pad(kernel_small, (edge, edge, (0, 0)))
    taps = jnp.pad(kernel, ((0, TAP_ROWS - SPAN), (0, SPAN_PAD - SPAN), (0, 0)))
    act_window, wall = halo_weights(mesh, act, wall)
    conv, xf, kf, conv_sums = conv_forward(bounds, act_window, taps, mask_wide)
    conv = conv.reshape(pixels, channels)
    total, wall = sums_weights(mesh, conv_sums[:2].reshape(8, LANES), wall)
    mean_two, inv_two = norm_scale(total.reshape(2, channels))
    xhat_two = (conv - mean_two) * inv_two
    u2 = (xhat_two * second_norm_gain + second_norm_bias) * mask
    act2, act2_slope = gelu_parts(u2)
    mixed = x + product(act2, point_two)
    mixed_masked = mixed * mask
    total = sums_only(mesh, "sums_three", 3, pack(*sums(mixed_masked)))
    mean_three, inv_three = norm_scale(total.reshape(2, channels))
    xhat_three = (mixed - mean_three) * inv_three
    u3 = (xhat_three * feedforward_norm_gain + feedforward_norm_bias) * mask

    ffn = jnp.zeros((pixels, channels), F32)
    du3 = jnp.zeros((pixels, channels), F32)
    grad_up, grad_down = [], []
    for part in range(devices_rows):
        up, down = wall[part, 0], wall[part, 1]
        hid, slope = gelu_parts(product(u3, up))
        ffn = ffn + product(hid, down)
        dpre = product_t(gy, down) * slope
        du3 = du3 + product_t(dpre, up)
        grad_up.append(contract(u3, dpre))
        grad_down.append(contract(hid, gy))
    grads_ffn = jnp.stack([jnp.stack(grad_up), jnp.stack(grad_down)], axis=1)
    grads_ffn = grads_ffn.reshape(devices_rows, 2 * channels, grads_ffn.shape[-1])

    def back_sums(dy, xhat):
        masked = dy * mask
        return masked, pack(jnp.sum(masked, axis=0), jnp.sum(masked * xhat, axis=0))

    def norm_back(masked, total, xhat, inv, gain):
        grad_bias, grad_gain = total.reshape(2, channels)
        field = mask * gain * inv * (masked - grad_bias / count - xhat * (grad_gain / count))
        return field, grad_gain, grad_bias

    du3, total = back_sums(du3, xhat_three)
    total, part = sums_grads(mesh, total, grads_ffn)
    back_three, grad_gain_three, grad_bias_three = norm_back(
        du3, total, xhat_three, inv_three, feedforward_norm_gain
    )
    dmixed = gy + back_three
    grad_point_two = contract(act2, dmixed)
    du2, total = back_sums(product_t(dmixed, point_two) * act2_slope, xhat_two)
    total, part = sums_scatter(mesh, total, part)
    dconv, grad_gain_two, grad_bias_two = norm_back(du2, total, xhat_two, inv_two, second_norm_gain)
    d_window, grad_w = halo_grads(
        mesh, dconv.reshape(rows, SLOTS, channels), part, grads_ffn.shape[1], grads_ffn.shape[2]
    )
    dact, grad_taps = conv_backward(bounds, d_window, xf, kf, mask_wide)
    dh1 = dact.reshape(pixels, channels) * act_slope
    grad_point_one = contract(u1, dh1)
    du1, total = back_sums(product_t(dh1, point_one), xhat_one)
    grads_all = jnp.concatenate(
        [grad_point_one, grad_point_two, grad_taps[:SPAN, :SPAN].reshape(SPAN * SPAN, channels)]
    )
    unit = 4 * dp * devices_rows
    grads_all = jnp.pad(grads_all, ((0, -grads_all.shape[0] % unit), (0, 0)))
    total, grads_all = sums_all_grads(mesh, total, grads_all)
    back_one, grad_gain_one, grad_bias_one = norm_back(du1, total, xhat_one, inv_one, first_norm_gain)
    output = inputs + expand((mixed - x) + ffn)
    grad_input = out_grad + expand(back_three + back_one)
    grad_kernel = grads_all[2 * channels : 2 * channels + SPAN * SPAN].reshape(SPAN, SPAN, channels)
    small_end = small_start + kernel_small.shape[0]
    grad_small = grad_kernel[small_start:small_end, small_start:small_end]
    return (
        output,
        grad_input,
        grad_gain_one,
        grad_bias_one,
        grads_all[:channels],
        grad_kernel,
        grad_small,
        grad_gain_two,
        grad_bias_two,
        grads_all[channels : 2 * channels],
        grad_gain_three,
        grad_bias_three,
        grad_w[:channels],
        grad_w[channels:],
    )


def solution(mesh):
    field = P("rows", "dp", None, None)
    everywhere = P()
    up, down = P(None, "rows"), P("rows", None)
    return jax.shard_map(
        functools.partial(shards, mesh.shape["dp"], mesh.shape["rows"]),
        mesh=mesh,
        in_specs=(field, P("rows", "dp", None)) + (everywhere,) * 10 + (up, down, field),
        out_specs=(field, field) + (everywhere,) * 10 + (up, down),
        check_vma=False,
    )
```

```python
import functools

import jax
import jax.numpy as jnp
import numpy as np
from jax import lax
from jax.experimental import pallas as pl
from jax.experimental.pallas import tpu as pltpu
from jax.sharding import PartitionSpec as P

EPSILON = 1e-05
HIGHEST = lax.Precision.HIGHEST
HIGH = lax.Precision.HIGH
MESH = pl.DeviceIdType.MESH
F32 = jnp.float32
BF16 = jnp.bfloat16

LEFT, RIGHT = 24, 16
SLOTS = LEFT + RIGHT
LEFT_IDS = 3
LEFT_N, RIGHT_N = 37, 27
LEFT_F, RIGHT_F = 24, 16
FREQ = 2 * LEFT_F + 2 * RIGHT_F
REACH = 13
SPAN = 2 * REACH + 1
SPAN_PAD = 32
LANES = 128


def forward_transform(length, padded, positions, columns):
    count = length // 2 + 1
    out = np.zeros((2 * padded, columns))
    angle = 2 * np.pi * np.outer(np.arange(count), positions) / length
    out[:count, : len(positions)] = np.cos(angle)
    out[padded : padded + count, : len(positions)] = -np.sin(angle)
    return out


def backward_transform(length, padded, positions, rows):
    count = length // 2 + 1
    out = np.zeros((rows, 2 * padded))
    twice = np.where(np.arange(count) == 0, 1.0, 2.0)
    angle = 2 * np.pi * np.outer(positions, np.arange(count)) / length
    out[: len(positions), :count] = np.cos(angle) * twice / length
    out[: len(positions), padded : padded + count] = -np.sin(angle) * twice / length
    return out


def slots_to_freq():
    out = np.zeros((FREQ, SLOTS))
    out[: 2 * LEFT_F, :LEFT] = forward_transform(LEFT_N, LEFT_F, np.arange(LEFT), LEFT)
    out[2 * LEFT_F :, LEFT:] = forward_transform(RIGHT_N, RIGHT_F, np.arange(RIGHT), RIGHT)
    return out


def freq_to_slots():
    out = np.zeros((SLOTS, FREQ))
    out[:LEFT, : 2 * LEFT_F] = backward_transform(LEFT_N, LEFT_F, np.arange(LEFT), LEFT)
    out[LEFT:, 2 * LEFT_F :] = backward_transform(RIGHT_N, RIGHT_F, np.arange(RIGHT), RIGHT)
    return out


def taps_to_freq():
    taps = np.arange(SPAN) - REACH
    return np.concatenate(
        [
            forward_transform(LEFT_N, LEFT_F, taps, SPAN_PAD),
            forward_transform(RIGHT_N, RIGHT_F, taps, SPAN_PAD),
        ]
    )


def freq_to_taps():
    taps = np.arange(SPAN) - REACH
    return np.concatenate(
        [
            backward_transform(LEFT_N, LEFT_F, taps, SPAN_PAD),
            backward_transform(RIGHT_N, RIGHT_F, taps, SPAN_PAD),
        ],
        axis=1,
    )


def split_constant(matrix, group):
    whole = np.kron(np.eye(group), matrix).astype(np.float32)
    high = whole.astype(jnp.bfloat16)
    low = (whole - high.astype(np.float32)).astype(jnp.bfloat16)
    return np.concatenate([high, high, low], axis=1)


def split_stack(value):
    high = value.astype(BF16)
    low = (value - high.astype(F32)).astype(BF16)
    return jnp.concatenate([high, low, high], axis=0)


def product_split(constant_ref, value):
    return jnp.dot(constant_ref[...], split_stack(value), preferred_element_type=F32)


GROUP_IN = 6
GROUP_OUT = 4
GROUP_TAP = 7
GROUP_GRAD = 4


def transform_window(window, to_freq_ref, out_ref):
    for first in range(0, window.shape[0], GROUP_IN):
        part = window[first : first + GROUP_IN].reshape(GROUP_IN * SLOTS, window.shape[-1])
        freq = product_split(to_freq_ref, part)
        out_ref[first : first + GROUP_IN] = freq.reshape(GROUP_IN, FREQ, freq.shape[-1])


def sum_rows(bounds, rows, x_ref, k_ref, y_ref, flipped, conjugate):
    width = x_ref.shape[-1]
    for side, (start, size) in enumerate(((0, LEFT_F), (2 * LEFT_F, RIGHT_F))):
        real, imag = pl.ds(start, size), pl.ds(start + size, size)

        def one_row(row, carry):
            def tap(w, total):
                index = row + SPAN - 1 - w if flipped else w - row
                xr, xi = x_ref[w, real, :], x_ref[w, imag, :]
                kr, ki = k_ref[index, real, :], k_ref[index, imag, :]
                if conjugate:
                    return (total[0] + kr * xr + ki * xi, total[1] + kr * xi - ki * xr)
                return (total[0] + kr * xr - ki * xi, total[1] + kr * xi + ki * xr)

            zero = jnp.zeros((size, width), F32)
            low, high = bounds[2 * side, row], bounds[2 * side + 1, row]
            yr, yi = lax.fori_loop(low, high, tap, (zero, zero))
            y_ref[row, real, :] = yr
            y_ref[row, imag, :] = yi
            return carry

        lax.fori_loop(0, rows, one_row, 0)


def rows_to_slots(rows, y_ref, to_slots_ref, mask_ref, out_ref):
    for first in range(0, rows, GROUP_OUT):
        freq = y_ref[first : first + GROUP_OUT].reshape(GROUP_OUT * FREQ, y_ref.shape[-1])
        cells = product_split(to_slots_ref, freq).reshape(GROUP_OUT, SLOTS, y_ref.shape[-1])
        out_ref[first : first + GROUP_OUT] = cells * mask_ref[first : first + GROUP_OUT]


def conv_forward_kernel(
    bounds, window, taps, mask, to_freq, taps_freq, to_slots, out, xf, kf, stats, yf
):
    rows = out.shape[0]
    transform_window(window, to_freq, xf)
    for first in range(0, kf.shape[0], GROUP_TAP):
        part = taps[first : first + GROUP_TAP].reshape(GROUP_TAP * SPAN_PAD, taps.shape[-1])
        freq = product_split(taps_freq, part)
        kf[first : first + GROUP_TAP] = freq.reshape(GROUP_TAP, FREQ, freq.shape[-1])
    sum_rows(bounds, rows, xf, kf, yf, False, True)
    rows_to_slots(rows, yf, to_slots, mask, out)
    cells = out[...].reshape(rows * SLOTS, out.shape[-1])
    stats[0:1, :] = jnp.sum(cells, axis=0, keepdims=True)
    stats[1:2, :] = jnp.sum(cells * cells, axis=0, keepdims=True)
    stats[2:8, :] = jnp.zeros((6, stats.shape[-1]), F32)


def conv_backward_kernel(
    bounds, window, xf, kf, mask, to_freq, to_slots, to_taps, out, grad, df, yf, gf
):
    rows = out.shape[0]
    width = out.shape[-1]
    transform_window(window, to_freq, df)
    sum_rows(bounds, rows, df, kf, yf, True, False)
    rows_to_slots(rows, yf, to_slots, mask, out)
    gf[...] = jnp.zeros(gf.shape, F32)
    for side, (start, size) in enumerate(((0, LEFT_F), (2 * LEFT_F, RIGHT_F))):
        real, imag = pl.ds(start, size), pl.ds(start + size, size)

        def one_row(row, carry):
            dr, di = df[row + REACH, real, :], df[row + REACH, imag, :]

            def tap(w, inner):
                xr, xi = xf[w, real, :], xf[w, imag, :]
                gf[w - row, real, :] += dr * xr + di * xi
                gf[w - row, imag, :] += dr * xi - di * xr
                return inner

            lax.fori_loop(bounds[2 * side, row], bounds[2 * side + 1, row], tap, 0)
            return carry

        lax.fori_loop(0, rows, one_row, 0)
    for first in range(0, gf.shape[0], GROUP_GRAD):
        freq = gf[first : first + GROUP_GRAD].reshape(GROUP_GRAD * FREQ, width)
        cells = product_split(to_taps, freq).reshape(GROUP_GRAD, SPAN_PAD, width)
        for row in range(first, min(first + GROUP_GRAD, SPAN)):
            grad[row * SPAN : (row + 1) * SPAN, :] = cells[row - first, :SPAN]
    grad[SPAN * SPAN :, :] = jnp.zeros((grad.shape[0] - SPAN * SPAN, width), F32)


CHUNK = 256
TAP_ROWS = 28


def chunked(leading):
    return pl.BlockSpec(leading + (CHUNK,), lambda c, *_: (0,) * len(leading) + (c,))


def whole(array):
    return pl.BlockSpec(array.shape, lambda c, *_: (0,) * array.ndim)


def conv_forward(bounds, field, taps, mask):
    window, _, channels = field.shape
    rows = window - 2 * REACH
    constants = [
        jnp.asarray(split_constant(slots_to_freq(), GROUP_IN)),
        jnp.asarray(split_constant(taps_to_freq(), GROUP_TAP)),
        jnp.asarray(split_constant(freq_to_slots(), GROUP_OUT)),
    ]
    return pl.pallas_call(
        conv_forward_kernel,
        grid_spec=pltpu.PrefetchScalarGridSpec(
            num_scalar_prefetch=1,
            grid=(channels // CHUNK,),
            in_specs=[
                chunked((window, SLOTS)),
                chunked((TAP_ROWS, SPAN_PAD)),
                pl.BlockSpec((rows, SLOTS, CHUNK), lambda c, *_: (0, 0, 0)),
            ]
            + [whole(c) for c in constants],
            out_specs=[
                chunked((rows, SLOTS)),
                chunked((window, FREQ)),
                chunked((TAP_ROWS, FREQ)),
                chunked((8,)),
            ],
            scratch_shapes=[
                pltpu.VMEM((rows, FREQ, CHUNK), F32),
            ],
        ),
        out_shape=[
            jax.ShapeDtypeStruct((rows, SLOTS, channels), F32),
            jax.ShapeDtypeStruct((window, FREQ, channels), F32),
            jax.ShapeDtypeStruct((TAP_ROWS, FREQ, channels), F32),
            jax.ShapeDtypeStruct((8, channels), F32),
        ],
        compiler_params=pltpu.CompilerParams(vmem_limit_bytes=36 << 20),
        name="conv_forward",
    )(bounds, field, taps, mask, *constants)


def conv_backward(bounds, field, xf, kf, mask, tap_rows):
    window, _, channels = field.shape
    rows = window - 2 * REACH
    constants = [
        jnp.asarray(split_constant(slots_to_freq(), GROUP_IN)),
        jnp.asarray(split_constant(freq_to_slots(), GROUP_OUT)),
        jnp.asarray(split_constant(freq_to_taps(), GROUP_GRAD)),
    ]
    return pl.pallas_call(
        conv_backward_kernel,
        grid_spec=pltpu.PrefetchScalarGridSpec(
            num_scalar_prefetch=1,
            grid=(channels // CHUNK,),
            in_specs=[
                chunked((window, SLOTS)),
                chunked((window, FREQ)),
                chunked((TAP_ROWS, FREQ)),
                pl.BlockSpec((rows, SLOTS, CHUNK), lambda c, *_: (0, 0, 0)),
            ]
            + [whole(c) for c in constants],
            out_specs=[chunked((rows, SLOTS)), chunked((tap_rows,))],
            scratch_shapes=[
                pltpu.VMEM((window, FREQ, CHUNK), F32),
                pltpu.VMEM((rows, FREQ, CHUNK), F32),
                pltpu.VMEM((TAP_ROWS, FREQ, CHUNK), F32),
            ],
        ),
        out_shape=[
            jax.ShapeDtypeStruct((rows, SLOTS, channels), F32),
            jax.ShapeDtypeStruct((tap_rows, channels), F32),
        ],
        compiler_params=pltpu.CompilerParams(vmem_limit_bytes=36 << 20),
        name="conv_backward",
    )(bounds, field, xf, kf, mask, *constants)


class Net:
    def __init__(self, dp, rows, send_sem, recv_sem):
        self.count, self.rows = dp, rows
        self.send_sem, self.recv_sem, self.used = send_sem, recv_sem, 0
        self.dp = lax.axis_index("dp")
        self.z = lax.axis_index("rows")
        self.bits = list(range(1, dp.bit_length() - 1))

    def bit(self, index):
        return lax.rem(self.dp // (1 << index), 2)

    def across(self, index):
        return (self.dp + (1 << index) * (1 - 2 * self.bit(index)), self.z)

    def line(self, step):
        return (self.dp, lax.rem(self.z + step, self.rows))

    def layer(self, step):
        return (lax.rem(self.dp + step, self.count), self.z)

    def greet(self):
        barrier = pltpu.get_barrier_semaphore()

        def greet_line(step, carry):
            pl.semaphore_signal(barrier, inc=1, device_id=self.line(step), device_id_type=MESH)
            return carry

        def greet_layer(step, carry):
            pl.semaphore_signal(barrier, inc=1, device_id=self.layer(step), device_id_type=MESH)
            return carry

        lax.fori_loop(1, self.rows, greet_line, 0)
        lax.fori_loop(1, self.count, greet_layer, 0)

    def ready(self):
        pl.semaphore_wait(pltpu.get_barrier_semaphore(), self.rows + self.count - 2)

    def copy(self, src, dst, device):
        made = pltpu.make_async_remote_copy(
            src_ref=src,
            dst_ref=dst,
            send_sem=self.send_sem.at[self.used],
            recv_sem=self.recv_sem.at[self.used],
            device_id=device,
            device_id_type=MESH,
        )
        self.used += 1
        return made

    def reserve(self, number):
        self.used += number
        return self.used - number

    def copy_at(self, index, src, dst, device):
        return pltpu.make_async_remote_copy(
            src_ref=src,
            dst_ref=dst,
            send_sem=self.send_sem.at[index],
            recv_sem=self.recv_sem.at[index],
            device_id=device,
            device_id_type=MESH,
        )

    def own(self, src, dst):
        made = pltpu.make_async_copy(src, dst, self.recv_sem.at[self.used])
        self.used += 1
        return made


def all_sum_job(net, value, out, line_slots, part, layer_slots):
    own = net.own(value, line_slots.at[net.z])
    own.start()
    sent = [net.copy(value, line_slots.at[net.z], net.line(s)) for s in range(1, net.rows)]
    for one in sent:
        one.start()
    yield
    own.wait()
    for one in sent:
        one.wait()
    total = line_slots[0]
    for index in range(1, net.rows):
        total = total + line_slots[index]
    part[...] = total
    own = net.own(part, layer_slots.at[net.dp])
    own.start()
    sent = [net.copy(part, layer_slots.at[net.dp], net.layer(s)) for s in range(1, net.count)]
    for one in sent:
        one.start()
    yield
    own.wait()
    for one in sent:
        one.wait()
    total = layer_slots[0]
    for index in range(1, net.count):
        total = total + layer_slots[index]
    out[...] = total


def aligned(value, unit):
    return pl.multiple_of(value, unit)


def halving(net, order, rows):
    base, steps = 0, []
    for bit in order:
        steps.append((bit, base, rows))
        rows //= 2
        base = base + net.bit(bit) * rows
    return steps, base, rows


def add_rows(dst, src, count, step):
    def one(i, carry):
        at = aligned(i * step, step)
        to, of = dst(at), src(at)
        to[...] = to[...] + of[...]
        return carry

    lax.fori_loop(0, count // step, one, 0)


def run(*jobs):
    jobs = list(jobs)
    while jobs:
        jobs = [job for job in jobs if next(job, StopIteration) is not StopIteration]


def line_gather_job(net, value, out):
    own = net.own(value, out.at[net.z])
    own.start()
    sent = [net.copy(value, out.at[net.z], net.line(s)) for s in range(1, net.rows)]
    for one in sent:
        one.start()
    yield
    own.wait()
    for one in sent:
        one.wait()


def sides(net, rows):
    core = net.bit(0)
    return [
        (pl.ds(aligned((2 * core + side) * LANES, LANES), LANES), *halving(net, order, rows))
        for side, order in enumerate((net.bits, net.bits[::-1]))
    ]


def weights_line_job(net, up, down, wall):
    own = [net.own(up, wall.at[net.z, 0]), net.own(down, wall.at[net.z, 1])]
    last = net.rows - 1
    for step in range(1, net.rows):
        moves = []
        for lanes, _, base, rows in sides(net, up.shape[0]):
            mine = pl.ds(aligned(base, 8), rows)
            for way in (1, -1):
                shard = net.z - way * (step - 1)
                going = (net.z >= step - 1) & (net.z < last) if way > 0 else (net.z <= last - (step - 1)) & (net.z > 0)
                coming = net.z >= step if way > 0 else net.z <= last - step
                shard = lax.rem(shard + net.rows, net.rows)
                for which, ref in enumerate((up, down)):
                    piece = wall.at[shard, which, mine, lanes]
                    one = net.copy(ref.at[mine, lanes] if step == 1 else piece, piece, net.line(way % net.rows))
                    pl.when(going)(one.start)
                    moves.append((one, going, coming))
        if step == 1:
            for one in own:
                one.start()
        yield
        for one, going, coming in moves:
            pl.when(coming)(one.wait_recv)
            pl.when(going)(one.wait_send)
    for one in own:
        one.wait()


def weights_layer_job(net, wall):
    parts = sides(net, wall.shape[2])
    for back in range(1, len(net.bits) + 1):
        moves = []
        for lanes, steps, _, _ in parts:
            bit, base, rows = steps[-back]
            mine = pl.ds(aligned(base + net.bit(bit) * (rows // 2), 8), rows // 2)
            for step in range(1, net.rows):
                piece = wall.at[lax.rem(net.z + step, net.rows), :, mine, lanes]
                moves.append(net.copy(piece, piece, net.across(bit)))
        for one in moves:
            one.start()
        yield
        for one in moves:
            one.wait()


def weights_pair_job(net, wall):
    half = wall.shape[3] // 2
    lanes = pl.ds(aligned(net.bit(0) * half, LANES), half)
    moves = []
    for step in range(1, net.rows):
        piece = wall.at[lax.rem(net.z + step, net.rows), :, :, lanes]
        moves.append(net.copy(piece, piece, net.across(0)))
    for one in moves:
        one.start()
    yield
    for one in moves:
        one.wait()


def halo_job(net, field, window, zeros):
    rows = field.shape[0]
    own = net.own(field, window.at[pl.ds(REACH, rows)])
    own.start()
    has_above, has_below = net.z > 0, net.z < net.rows - 1
    down = net.copy(field.at[pl.ds(rows - REACH, REACH)], window.at[pl.ds(0, REACH)], net.line(1))
    up = net.copy(field.at[pl.ds(0, REACH)], window.at[pl.ds(REACH + rows, REACH)], net.line(net.rows - 1))
    pl.when(has_below)(down.start)
    pl.when(has_above)(up.start)
    zeros[...] = jnp.zeros(zeros.shape, F32)
    top = net.own(zeros, window.at[pl.ds(0, REACH)])
    bottom = net.own(zeros, window.at[pl.ds(REACH + rows, REACH)])
    pl.when(jnp.logical_not(has_above))(top.start)
    pl.when(jnp.logical_not(has_below))(bottom.start)
    yield
    own.wait()
    pl.when(jnp.logical_not(has_above))(top.wait)
    pl.when(jnp.logical_not(has_below))(bottom.wait)
    pl.when(has_above)(down.wait_recv)
    pl.when(has_below)(down.wait_send)
    pl.when(has_below)(up.wait_recv)
    pl.when(has_above)(up.wait_send)


def reduce_layer_job(net, source, acc, got_pair, got, out):
    lead, rows, width = source.shape
    half = width // 2
    core = net.bit(0)
    mine = pl.ds(aligned(core * half, LANES), half)
    other = pl.ds(aligned((1 - core) * half, LANES), half)
    own = [net.own(source.at[k, :, mine], acc.at[k]) for k in range(lead)]
    sent = [net.copy(source.at[k, :, other], got_pair.at[k], net.across(0)) for k in range(lead)]
    for one in own + sent:
        one.start()
    yield
    for k in range(lead):
        own[k].wait()
        sent[k].wait()
        add_rows(lambda at: acc.at[k, pl.ds(at, 32)], lambda at: got_pair.at[k, pl.ds(at, 32)], rows, 32)
    parts = sides(net, rows)
    for index in range(len(net.bits)):
        moves = []
        for side, (_, steps, _, _) in enumerate(parts):
            bit, base, size = steps[index]
            size //= 2
            give = base + (1 - net.bit(bit)) * size
            keep = base + net.bit(bit) * size
            lanes = pl.ds(side * LANES, LANES)
            place = got.at[side, :, pl.ds(rows - 2 * size, size)]
            one = net.copy(acc.at[:, pl.ds(aligned(give, 8), size), lanes], place, net.across(bit))
            one.start()
            moves.append((one, keep, size, lanes, side))
        yield
        for one, keep, size, lanes, side in moves:
            one.wait()
            for k in range(lead):
                add_rows(
                    lambda at: acc.at[k, pl.ds(aligned(keep + at, 8), 8), lanes],
                    lambda at: got.at[side, k, pl.ds(rows - 2 * size + at, 8)],
                    size,
                    8,
                )
    if out is not None:
        for side, (_, _, base, size) in enumerate(parts):
            out[side] = acc[:, pl.ds(aligned(base, 8), size), pl.ds(side * LANES, LANES)]


def gather_layer_job(net, outs):
    rows, width = outs[0].shape
    parts = sides(net, rows)
    for back in range(1, len(net.bits) + 1):
        moves = []
        for lanes, steps, _, _ in parts:
            bit, base, size = steps[-back]
            mine = pl.ds(aligned(base + net.bit(bit) * (size // 2), 8), size // 2)
            for out in outs:
                piece = out.at[mine, lanes]
                moves.append(net.copy(piece, piece, net.across(bit)))
                moves[-1].start()
        yield
        for one in moves:
            one.wait()
    moves = []
    for out in outs:
        piece = out.at[:, pl.ds(aligned(net.bit(0) * (width // 2), LANES), width // 2)]
        moves.append(net.copy(piece, piece, net.across(0)))
        moves[-1].start()
    yield
    for one in moves:
        one.wait()


def reduce_all_job(net, source, acc, got_pair, got, got_line, out):
    yield from reduce_layer_job(net, source, acc, got_pair, got, None)
    parts = sides(net, source.shape[1])
    moves, own = [], []
    for side, (_, _, base, rows) in enumerate(parts):
        rows //= net.rows
        inner = pl.ds(side * LANES, LANES)
        own.append(net.own(acc.at[0, pl.ds(aligned(base + net.z * rows, 8), rows), inner], got_line.at[side, net.z]))
        for step in range(1, net.rows):
            other = lax.rem(net.z + step, net.rows)
            piece = acc.at[0, pl.ds(aligned(base + other * rows, 8), rows), inner]
            moves.append(net.copy(piece, got_line.at[side, net.z], net.line(step)))
    for one in own + moves:
        one.start()
    yield
    for one in own + moves:
        one.wait()
    moves = []
    for side, (lanes, _, base, rows) in enumerate(parts):
        rows //= net.rows
        total = got_line[side, 0]
        for index in range(1, net.rows):
            total = total + got_line[side, index]
        piece = out.at[pl.ds(aligned(base + net.z * rows, 8), rows), lanes]
        out[pl.ds(aligned(base + net.z * rows, 8), rows), lanes] = total
        for step in range(1, net.rows):
            moves.append(net.copy(piece, piece, net.line(step)))
            moves[-1].start()
    yield
    for one in moves:
        one.wait()
    yield from gather_layer_job(net, [out])


VMEM = pl.BlockSpec(memory_space=pltpu.VMEM)
HBM = pl.BlockSpec(memory_space=pltpu.HBM)
COPIES = 448


def shape(*dims):
    return jax.ShapeDtypeStruct(dims, F32)


def exchange(name, number, mesh, body, args, in_specs, outs, out_specs, scratch, limit, aliases=None, late=False):
    dp, rows = mesh

    def kernel(*refs):
        *refs, send_sem, recv_sem = refs
        net = Net(dp, rows, send_sem, recv_sem)
        net.greet()
        if not late:
            net.ready()
        body(net, *refs)
        assert net.used <= COPIES

    return pl.pallas_call(
        kernel,
        out_shape=outs,
        in_specs=in_specs,
        out_specs=out_specs,
        scratch_shapes=scratch + [pltpu.SemaphoreType.DMA((COPIES,))] * 2,
        input_output_aliases=aliases or {},
        compiler_params=pltpu.CompilerParams(
            collective_id=number, has_side_effects=True, vmem_limit_bytes=limit << 20
        ),
        name=name,
    )(*args)


def sum_scratch(mesh, height):
    dp, rows = mesh
    return [pltpu.VMEM((rows, height, LANES), F32), pltpu.VMEM((height, LANES), F32), pltpu.VMEM((dp, height, LANES), F32)]


def sums_names_weights(mesh, value, names, up, down):
    rows = mesh[1]

    def body(net, value, names, up, down, total, all_names, wall, *slots):
        run(
            weights_line_job(net, up, down, wall),
            line_gather_job(net, names, all_names),
            all_sum_job(net, value, total, *slots),
        )

    return exchange(
        "sums_one",
        0,
        mesh,
        body,
        (value, names, up, down),
        [VMEM] * 4,
        [
            shape(*value.shape),
            jax.ShapeDtypeStruct((rows,) + names.shape, jnp.int32),
            shape(rows, 2, *up.shape),
        ],
        [VMEM, VMEM, HBM],
        sum_scratch(mesh, value.shape[0]),
        16,
    )


def halo_weights(mesh, field, wall):
    rows = field.shape[0]

    def body(net, field, wall_in, window, wall, zeros):
        halo = halo_job(net, field, window, zeros)
        next(halo)
        run(weights_layer_job(net, wall))
        run(weights_pair_job(net, wall))
        finish(halo)

    return exchange(
        "halo_act",
        1,
        mesh,
        body,
        (field, wall),
        [VMEM, HBM],
        [shape(rows + 2 * REACH, *field.shape[1:]), shape(*wall.shape)],
        [HBM, HBM],
        [pltpu.VMEM((REACH,) + field.shape[1:], F32)],
        16,
        {1: 1},
    )


def layer_scratch(lead, rows, width):
    return [
        pltpu.VMEM((lead, rows, width // 2), F32),
        pltpu.VMEM((lead, rows, width // 2), F32),
        pltpu.VMEM((2, lead, rows, LANES), F32),
    ]


def all_scratch(mesh, rows, width):
    return layer_scratch(1, rows, width) + [pltpu.VMEM((2, mesh[1], 2 * rows // mesh[0] // mesh[1], LANES), F32)]


def sums_all_grads(mesh, value, grads, taps):
    rows, width = grads.shape
    tap_rows = taps.shape[0]

    def body(net, value, grads, taps, total, out, cube, line, mid, layer, flat, *scratch):
        run(
            reduce_all_job(net, taps, *scratch[:4], flat),
            reduce_all_job(net, grads, *scratch[4:], out),
            all_sum_job(net, value, total, line, mid, layer),
        )
        for row in range(SPAN):
            cube[row] = flat[row * SPAN : (row + 1) * SPAN, :]

    return exchange(
        "sums_six",
        7,
        mesh,
        body,
        (value, grads.reshape(1, rows, width), taps.reshape(1, tap_rows, width)),
        [VMEM] * 3,
        [shape(*value.shape), shape(rows, width), shape(SPAN, SPAN, width)],
        [VMEM, VMEM, VMEM],
        sum_scratch(mesh, value.shape[0])
        + [pltpu.VMEM((tap_rows, width), F32)]
        + all_scratch(mesh, tap_rows, width)
        + all_scratch(mesh, rows, width),
        24,
    )


def gelu_parts(x):
    scale, cubic = 0.7978845608028654, 0.044715
    square = x * x
    t = jnp.tanh(scale * (x + cubic * (x * square)))
    half = 0.5 * (1.0 + t)
    return (x * half, half + 0.5 * x * (1.0 - t * t) * (scale * (1.0 + 3.0 * cubic * square)))


NN = (((1,), (0,)), ((), ()))
NT = (((1,), (1,)), ((), ()))
TILE = 320


def split_two(value):
    high = value.astype(BF16)
    return high, (value - high.astype(F32)).astype(BF16)


def store_split(refs, where, value):
    refs[0][where], refs[1][where] = split_two(value)


def dot_split(left, right, dims=NN):
    def one(a, b):
        return lax.dot_general(a, b, dims, preferred_element_type=F32)

    return one(left[0], right[0]) + (one(left[0], right[1]) + one(left[1], right[0]))


def read_pair(refs, where=Ellipsis):
    return refs[0][where], refs[1][where]


def write_sums(value, first, second):
    for row in range(4):
        lanes = slice(row * LANES, (row + 1) * LANES)
        value[row : row + 1, :] = first[:, lanes]
        value[4 + row : 5 + row, :] = second[:, lanes]


def read_sums(total):
    return tuple(
        jnp.concatenate([total[4 * k + row : 4 * k + row + 1, :] for row in range(4)], axis=1) for k in range(2)
    )


def column_sum(value):
    return jnp.sum(value, axis=0, keepdims=True)


def norm_terms(total, count):
    first, second = read_sums(total)
    mean = first / count
    return mean, lax.rsqrt(second / count - mean * mean + EPSILON)


def finish(job):
    for _ in job:
        pass


def rem(value, unit):
    return value % unit if isinstance(value, int) else lax.rem(value, unit)


def middle_kernel(
    net,
    conv,
    conv_sums,
    x,
    gy,
    mask,
    params,
    point_two,
    wall,
    delta,
    back,
    total_four,
    total_five,
    window,
    grad_point,
    grad_up,
    grad_down,
    sums_own,
    sums_slots,
    own_sem,
    mixed,
    xhat,
    slope_two,
    act_pair,
    u_pair,
    ut_pair,
    g_pair,
    gt_pair,
    point_pair,
    up_pair,
    down_pair,
    hid_pair,
    dpre_pair,
    w_up,
    w_down,
    made,
    acc,
    got_pair,
    got_layer,
    got_line,
    down_t,
    point_grad,
    dconv,
    zeros,
    *point_scratch,
):
    pixels, channels = conv.shape
    tiles = pixels // TILE
    hidden = w_up.shape[2]
    per_shard = wall.shape[2] // hidden
    chunks = net.rows * per_shard
    core = net.bit(0)
    gain_two, bias_two, gain_three, bias_three, count = (params[row : row + 1, :] for row in range(5))

    def each_tile(body):
        def one(index, carry):
            return body(pl.ds(aligned(index * TILE, TILE), TILE), carry)

        zero = jnp.zeros((1, channels), F32)
        return lax.fori_loop(0, tiles, one, (zero, zero))

    def valid(rows):
        return jnp.concatenate([mask[rows, :]] * (channels // LANES), axis=1)

    def total_job(which, out):
        return all_sum_job(net, sums_own.at[which], out, *(slots.at[which] for slots in sums_slots))

    def shard_of(chunk):
        return lax.rem(net.z + chunk // per_shard, net.rows)

    def load(chunk):
        slot, shard, part = rem(chunk, 2), shard_of(chunk), rem(chunk, per_shard)
        span = pl.ds(aligned(part * hidden, hidden), hidden)
        return (
            pltpu.make_async_copy(wall.at[shard, 0, :, span], w_up.at[slot], own_sem.at[0, slot]),
            pltpu.make_async_copy(wall.at[shard, 1, span, :], w_down.at[slot], own_sem.at[1, slot]),
        )

    sums_own[0] = conv_sums[...]
    net.ready()
    job = total_job(0, sums_slots[1].at[0])
    next(job)
    for one in load(0):
        one.start()
    store_split(point_pair, Ellipsis, point_two[...])
    store_split(g_pair, Ellipsis, gy[...])
    next(job)
    store_split(gt_pair, Ellipsis, gy[...].T)
    finish(job)
    mean, inv_two = norm_terms(sums_slots[1].at[0], count)

    def second_norm(rows, carry):
        m = valid(rows)
        hat = (conv[rows, :] - mean) * inv_two
        act, slope = gelu_parts((hat * gain_two + bias_two) * m)
        xhat[rows, :] = hat
        slope_two[rows, :] = slope * m
        store_split(act_pair, rows, act)
        field = x[rows, :] + dot_split(read_pair(act_pair, rows), read_pair(point_pair))
        mixed[rows, :] = field
        return carry[0] + column_sum(field), carry[1] + column_sum(field * field)

    write_sums(sums_own.at[1], *each_tile(second_norm))
    job = total_job(1, sums_slots[1].at[1])
    next(job)
    next(job)
    finish(job)
    mean_three, inv_three = norm_terms(sums_slots[1].at[1], count)

    def third_norm(rows, carry):
        hat = (mixed[rows, :] - mean_three) * inv_three
        store_split(u_pair, rows, (hat * gain_three + bias_three) * valid(rows))
        delta[rows, :] = mixed[rows, :] - x[rows, :]
        back[rows, :] = jnp.zeros((TILE, channels), F32)
        return carry

    each_tile(third_norm)
    for side in range(2):
        ut_pair[side][...] = u_pair[side][...].T

    mine = pl.ds(aligned(core * LANES, LANES), LANES)
    other = pl.ds(aligned((1 - core) * LANES, LANES), LANES)
    halvings = [halving(net, order, channels) for order in (net.bits, net.bits[::-1])]
    stages = len(net.bits)
    pair_base = net.reserve(chunks)
    layer_base = net.reserve(2 * stages * chunks)
    line_base = net.reserve(2 * chunks)

    def pair_move(chunk):
        slot = rem(chunk, 2)
        return (
            net.copy_at(pair_base + chunk, made.at[slot, :, :, other], got_pair.at[chunk], net.across(0)),
            pltpu.make_async_copy(made.at[slot, :, :, mine], acc.at[chunk], own_sem.at[2, slot]),
        )

    def layer_move(stage, chunk):
        moves = []
        for side, (steps, _, _) in enumerate(halvings):
            bit, base, size = steps[stage]
            size //= 2
            give, keep = base + (1 - net.bit(bit)) * size, base + net.bit(bit) * size
            place = pl.ds(channels - 2 * size, size)
            moves.append(
                (
                    net.copy_at(
                        layer_base + (2 * stage + side) * chunks + chunk,
                        acc.at[chunk, side, pl.ds(aligned(give, 8), size), :],
                        got_layer.at[chunk, side, place, :],
                        net.across(bit),
                    ),
                    keep,
                    size,
                    side,
                )
            )
        return moves

    def line_move(chunk, remote):
        moves = []
        shard, part = shard_of(chunk), rem(chunk, per_shard)
        for side, (_, base, size) in enumerate(halvings):
            piece = acc.at[chunk, side, pl.ds(aligned(base, 8), size), :]
            place = got_line.at[net.z, part, side]
            if remote:
                moves.append(net.copy_at(line_base + 2 * chunk + side, piece, place, (net.dp, shard)))
            else:
                moves.append(pltpu.make_async_copy(piece, place, net.recv_sem.at[line_base + 2 * chunk + side]))
        return moves

    def when(test, body):
        if isinstance(test, bool):
            if test:
                body()
        else:
            pl.when(test)(body)

    def within(chunk):
        if isinstance(chunk, int):
            return 0 <= chunk < chunks
        return (chunk >= 0) & (chunk < chunks)

    def progress(step):
        def after_pair():
            chunk = step - 1
            sent, own = pair_move(chunk)
            own.wait()
            sent.wait()
            for side in range(2):
                add_rows(
                    lambda at: acc.at[chunk, side, pl.ds(at, 64), :],
                    lambda at: got_pair.at[chunk, side, pl.ds(at, 64), :],
                    channels,
                    64,
                )
            for one, *_ in layer_move(0, chunk):
                one.start()

        def after_layer(stage):
            chunk = step - 2 - stage
            for one, keep, size, side in layer_move(stage, chunk):
                one.wait()
                unit = min(size, 64)
                add_rows(
                    lambda at: acc.at[chunk, side, pl.ds(aligned(keep + at, 8), unit), :],
                    lambda at: got_layer.at[chunk, side, pl.ds(aligned(channels - 2 * size + at, 8), unit), :],
                    size,
                    unit,
                )
            if stage + 1 < stages:
                for one, *_ in layer_move(stage + 1, chunk):
                    one.start()
            else:

                def go(remote):
                    def start():
                        for one in line_move(chunk, remote):
                            one.start()

                    return start

                when(chunk >= per_shard, go(True))
                when(chunk < per_shard, go(False))

        when(within(step - 1), after_pair)
        for stage in range(stages):
            when(within(step - 2 - stage), functools.partial(after_layer, stage))

    def feed_forward(chunk, carry):
        progress(chunk)
        slot = rem(chunk, 2)
        for one in load(chunk):
            one.wait()

        @pl.when(chunk + 1 < chunks)
        def _():
            for one in load(chunk + 1):
                one.start()

        store_split(up_pair, Ellipsis, w_up[slot])
        store_split(down_pair, Ellipsis, w_down[slot])

        def first_half(rows, carry):
            hid, slope = gelu_parts(dot_split(read_pair(u_pair, rows), read_pair(up_pair)))
            store_split(hid_pair, rows, hid)
            store_split(
                dpre_pair, rows, dot_split(read_pair(g_pair, rows), read_pair(down_pair), NT) * slope
            )
            return carry

        each_tile(first_half)
        made[slot, 0] = dot_split(read_pair(ut_pair), read_pair(dpre_pair))
        made[slot, 1] = dot_split(read_pair(gt_pair), read_pair(hid_pair))
        for one in pair_move(chunk):
            one.start()

        def second_half(rows, carry):
            delta[rows, :] += dot_split(read_pair(hid_pair, rows), read_pair(down_pair))
            back[rows, :] += dot_split(read_pair(dpre_pair, rows), read_pair(up_pair), NT)
            return carry

        each_tile(second_half)
        return carry

    lax.fori_loop(0, chunks, feed_forward, 0)

    def third_sums(rows, carry):
        dy = back[rows, :] * valid(rows)
        back[rows, :] = dy
        hat = (mixed[rows, :] - mean_three) * inv_three
        return carry[0] + column_sum(dy), carry[1] + column_sum(dy * hat)

    write_sums(sums_own.at[2], *each_tile(third_sums))
    job = total_job(2, total_four)
    next(job)
    progress(chunks)
    next(job)
    progress(chunks + 1)
    finish(job)
    for step in range(chunks + 2, chunks + 1 + stages):
        progress(step)
    grad_bias, grad_gain = read_sums(total_four)

    def third_back(rows, carry):
        m = valid(rows)
        hat = (mixed[rows, :] - mean_three) * inv_three
        field = m * gain_three * inv_three * (back[rows, :] - grad_bias / count - hat * (grad_gain / count))
        back[rows, :] = field
        dmixed = gy[rows, :] + field
        store_split(g_pair, rows, dmixed)
        du = dot_split(read_pair(g_pair, rows), read_pair(point_pair), NT) * slope_two[rows, :]
        mixed[rows, :] = du
        return carry[0] + column_sum(du), carry[1] + column_sum(du * xhat[rows, :])

    write_sums(sums_own.at[3], *each_tile(third_back))
    job = total_job(3, total_five)
    next(job)
    for side in range(2):
        ut_pair[side][...] = act_pair[side][...].T
    next(job)
    point_grad[0] = dot_split(read_pair(ut_pair), read_pair(g_pair))
    finish(job)
    grad_bias_two, grad_gain_two = read_sums(total_five)

    def second_back(row, carry):
        rows = pl.ds(aligned(row * SLOTS, 8), SLOTS)
        field = mixed[rows, :] - grad_bias_two / count - xhat[rows, :] * (grad_gain_two / count)
        dconv[row] = valid(rows) * gain_two * inv_two * field
        return carry

    lax.fori_loop(0, pixels // SLOTS, second_back, 0)
    halo = halo_job(net, dconv, window, zeros)
    next(halo)
    points = reduce_all_job(net, point_grad, *point_scratch, grad_point)
    next(points)

    def gather_job():
        for chunk in range(chunks):
            for one in line_move(chunk, chunk >= per_shard):
                one.wait()
        for which, out in enumerate((grad_up, down_t)):
            _, base, size = halvings[which]
            for part in range(per_shard):
                total = got_line[0, part, which]
                for index in range(1, net.rows):
                    total = total + got_line[index, part, which]
                lanes = pl.ds(aligned(part * hidden + core * LANES, LANES), LANES)
                out[pl.ds(aligned(base, 8), size), lanes] = total
        for back_step in range(1, stages + 1):
            moves = []
            for which, out in enumerate((grad_up, down_t)):
                bit, base, size = halvings[which][0][-back_step]
                here = pl.ds(aligned(base + net.bit(bit) * (size // 2), 8), size // 2)
                for part in range(per_shard):
                    piece = out.at[here, pl.ds(aligned(part * hidden + core * LANES, LANES), LANES)]
                    moves.append(net.copy(piece, piece, net.across(bit)))
                    moves[-1].start()
            yield
            for one in moves:
                one.wait()
        moves = []
        for out in (grad_up, down_t):
            for part in range(per_shard):
                piece = out.at[:, pl.ds(aligned(part * hidden + core * LANES, LANES), LANES)]
                moves.append(net.copy(piece, piece, net.across(0)))
                moves[-1].start()
        yield
        for one in moves:
            one.wait()
        grad_down[...] = down_t[...].T

    run(points, gather_job())
    finish(halo)


def middle(mesh, conv, conv_sums, x, gy, mask, params, point_two, wall):
    dp, rows = mesh
    pixels, channels = conv.shape
    hidden = 2 * LANES
    chunks = rows * (wall.shape[2] // hidden)
    lines = pixels // SLOTS

    def pair(*dims):
        return [pltpu.VMEM(dims, BF16)] * 2

    piece = channels * 2 // dp
    scratch = [
        pltpu.VMEM((4, 8, LANES), F32),
        [pltpu.VMEM((4, rows, 8, LANES), F32), pltpu.VMEM((4, 8, LANES), F32), pltpu.VMEM((4, dp, 8, LANES), F32)],
        pltpu.SemaphoreType.DMA((3, 2)),
        pltpu.VMEM((pixels, channels), F32),
        pltpu.VMEM((pixels, channels), F32),
        pltpu.VMEM((pixels, channels), F32),
        pair(pixels, channels),
        pair(pixels, channels),
        pair(channels, pixels),
        pair(pixels, channels),
        pair(channels, pixels),
        pair(channels, channels),
        pair(channels, hidden),
        pair(hidden, channels),
        pair(pixels, hidden),
        pair(pixels, hidden),
        pltpu.VMEM((2, channels, hidden), F32),
        pltpu.VMEM((2, hidden, channels), F32),
        pltpu.VMEM((2, 2, channels, hidden), F32),
        pltpu.VMEM((chunks, 2, channels, LANES), F32),
        pltpu.VMEM((chunks, 2, channels, LANES), F32),
        pltpu.VMEM((chunks, 2, channels, LANES), F32),
        pltpu.VMEM((rows, wall.shape[2] // hidden, 2, piece, LANES), F32),
        pltpu.VMEM((channels, channels), F32),
        pltpu.VMEM((1, channels, channels), F32),
        pltpu.VMEM((lines, SLOTS, channels), F32),
        pltpu.VMEM((REACH, SLOTS, channels), F32),
    ] + all_scratch(mesh, channels, channels)
    return exchange(
        "middle",
        2,
        mesh,
        middle_kernel,
        (conv, conv_sums, x, gy, mask, params, point_two, wall),
        [VMEM] * 7 + [HBM],
        [shape(pixels, channels)] * 2
        + [shape(8, LANES)] * 2
        + [shape(lines + 2 * REACH, SLOTS, channels)]
        + [shape(channels, channels)] * 3,
        [VMEM] * 4 + [HBM] + [VMEM] * 3,
        scratch,
        56,
        late=True,
    )


def product(left, right):
    return jnp.dot(left, right, precision=HIGH, preferred_element_type=F32)


def product_t(left, right):
    return lax.dot_general(left, right, (((1,), (1,)), ((), ())), precision=HIGH, preferred_element_type=F32)


def contract(left, right):
    return lax.dot_general(left, right, (((0,), (0,)), ((), ())), precision=HIGH, preferred_element_type=F32)


def shards(
    dp,
    devices_rows,
    inputs,
    image_ids,
    first_norm_gain,
    first_norm_bias,
    point_one,
    kernel_big,
    kernel_small,
    second_norm_gain,
    second_norm_bias,
    point_two,
    feedforward_norm_gain,
    feedforward_norm_bias,
    w_up,
    w_down,
    out_grad,
):
    rows, canvases, columns, channels = inputs.shape
    assert canvases == 1 and kernel_big.shape[0] == SPAN
    pixels = rows * SLOTS
    ids = image_ids[:, 0]
    mesh = (dp, devices_rows)

    place = jnp.arange(columns, dtype=jnp.int32)[None, :]
    is_left = (ids >= 0) & (ids < LEFT_IDS)
    is_right = ids >= LEFT_IDS

    def side(member, width):
        name = jnp.max(jnp.where(member, ids, -1), axis=1)
        first = jnp.min(jnp.where(member, place, columns), axis=1)
        return name, jnp.minimum(first, columns - width)

    left_id, left_at = side(is_left, LEFT)
    right_id, right_at = side(is_right, RIGHT)
    slot_column = jnp.concatenate(
        [
            left_at[:, None] + jnp.arange(LEFT, dtype=jnp.int32)[None, :],
            right_at[:, None] + jnp.arange(RIGHT, dtype=jnp.int32)[None, :],
        ],
        axis=1,
    )
    slot_id = jnp.concatenate(
        [
            jnp.broadcast_to(left_id[:, None], (rows, LEFT)),
            jnp.broadcast_to(right_id[:, None], (rows, RIGHT)),
        ],
        axis=1,
    )
    hit = (slot_column[:, :, None] == place[:, None, :]) & (ids[:, None, :] == slot_id[:, :, None])
    hit = hit & (slot_id[:, :, None] >= 0)
    pick = hit.astype(F32)
    slot_mask = jnp.max(pick, axis=2)
    valid = (ids >= 0).astype(F32)

    def compact(field):
        out = lax.dot_general(
            pick, field[:, 0], (((2,), (1,)), ((0,), (0,))), precision=HIGHEST, preferred_element_type=F32
        )
        return out.reshape(pixels, channels)

    def expand(cells):
        return lax.dot_general(
            pick,
            cells.reshape(rows, SLOTS, channels),
            (((1,), (1,)), ((0,), (0,))),
            precision=HIGHEST,
            preferred_element_type=F32,
        )[:, None]

    def pack(first, second):
        return jnp.stack([first, second]).reshape(2 * channels // LANES, LANES)

    def sums(field):
        return jnp.sum(field, axis=0), jnp.sum(field * field, axis=0)

    names = jnp.stack([left_id, right_id], axis=1) + 1
    names_tile = jnp.pad(names.reshape(1, 2 * rows), ((0, 7), (0, LANES - 2 * rows)))
    x = compact(inputs)
    gy = compact(out_grad)
    total, all_names, wall = sums_names_weights(
        mesh,
        jnp.concatenate([pack(*sums(x)), pack(jnp.full((channels,), jnp.sum(valid)), jnp.zeros((channels,)))]),
        names_tile,
        w_up,
        w_down,
    )
    count = total[8, 0]
    total = total[:8].reshape(2, channels)
    all_names = jnp.pad(all_names[:, 0, : 2 * rows].reshape(devices_rows * rows, 2), ((REACH, REACH), (0, 0)))
    window_rows = rows + 2 * REACH
    window_names = lax.dynamic_slice_in_dim(all_names, lax.axis_index("rows") * rows, window_rows, 0)
    w_index = jnp.arange(window_rows, dtype=jnp.int32)[None, :]
    r_index = jnp.arange(rows, dtype=jnp.int32)[:, None]
    near = (w_index >= r_index) & (w_index <= r_index + 2 * REACH)
    bounds = []
    for which in range(2):
        same = near & (names[:, which][:, None] == window_names[:, which][None, :]) & (names[:, which][:, None] > 0)
        low = jnp.min(jnp.where(same, w_index, window_rows), axis=1)
        high = jnp.max(jnp.where(same, w_index + 1, 0), axis=1)
        bounds += [jnp.minimum(low, high), high]
    bounds = jnp.stack(bounds).astype(jnp.int32)

    mask = slot_mask.reshape(pixels, 1)
    mask_wide = jnp.broadcast_to(slot_mask[:, :, None], (rows, SLOTS, CHUNK))

    def norm_scale(total):
        mean = total[0] / count
        return mean, lax.rsqrt(total[1] / count - mean * mean + EPSILON)

    mean_one, inv_one = norm_scale(total)
    xhat_one = (x - mean_one) * inv_one
    u1 = (xhat_one * first_norm_gain + first_norm_bias) * mask
    h1 = product(u1, point_one)
    act, act_slope = gelu_parts(h1)
    act = act.reshape(rows, SLOTS, channels)
    small_start = REACH - kernel_small.shape[0] // 2
    edge = (small_start, small_start)
    kernel = kernel_big + jnp.pad(kernel_small, (edge, edge, (0, 0)))
    taps = jnp.pad(kernel, ((0, TAP_ROWS - SPAN), (0, SPAN_PAD - SPAN), (0, 0)))
    act_window, wall = halo_weights(mesh, act, wall)
    conv, xf, kf, conv_sums = conv_forward(bounds, act_window, taps, mask_wide)
    conv = conv.reshape(pixels, channels)
    conv_sums = conv_sums[:2].reshape(8, LANES)
    vectors = [second_norm_gain, second_norm_bias, feedforward_norm_gain, feedforward_norm_bias]
    params = jnp.stack(vectors + [jnp.full((channels,), count)] + [jnp.zeros((channels,), F32)] * 3)
    mask_lanes = jnp.broadcast_to(mask, (pixels, LANES))
    delta, back_three, total_four, total_five, d_window, grad_point_two, grad_up, grad_down = middle(
        mesh, conv, conv_sums, x, gy, mask_lanes, params, point_two, wall
    )
    grad_bias_three, grad_gain_three = total_four.reshape(2, channels)
    grad_bias_two, grad_gain_two = total_five.reshape(2, channels)

    def back_sums(dy, xhat):
        masked = dy * mask
        return masked, pack(jnp.sum(masked, axis=0), jnp.sum(masked * xhat, axis=0))

    def norm_back(masked, total, xhat, inv, gain):
        grad_bias, grad_gain = total.reshape(2, channels)
        field = mask * gain * inv * (masked - grad_bias / count - xhat * (grad_gain / count))
        return field, grad_gain, grad_bias

    unit = 4 * dp * devices_rows
    dact, grad_taps = conv_backward(bounds, d_window, xf, kf, mask_wide, -(-SPAN * SPAN // unit) * unit)
    dh1 = dact.reshape(pixels, channels) * act_slope
    grad_point_one = contract(u1, dh1)
    du1, total = back_sums(product_t(dh1, point_one), xhat_one)
    total, grad_point_one, grad_kernel = sums_all_grads(mesh, total, grad_point_one, grad_taps)
    back_one, grad_gain_one, grad_bias_one = norm_back(du1, total, xhat_one, inv_one, first_norm_gain)
    output = inputs + expand(delta)
    grad_input = out_grad + expand(back_three + back_one)
    small_end = small_start + kernel_small.shape[0]
    grad_small = grad_kernel[small_start:small_end, small_start:small_end]
    return (
        output,
        grad_input,
        grad_gain_one,
        grad_bias_one,
        grad_point_one,
        grad_kernel,
        grad_small,
        grad_gain_two,
        grad_bias_two,
        grad_point_two,
        grad_gain_three,
        grad_bias_three,
        grad_up,
        grad_down,
    )


def solution(mesh):
    field = P("rows", "dp", None, None)
    everywhere = P()
    up, down = P(None, "rows"), P("rows", None)
    return jax.shard_map(
        functools.partial(shards, mesh.shape["dp"], mesh.shape["rows"]),
        mesh=mesh,
        in_specs=(field, P("rows", "dp", None)) + (everywhere,) * 10 + (up, down, field),
        out_specs=(field, field) + (everywhere,) * 10 + (up, down),
        check_vma=False,
    )
```

```python
import functools

import jax
import jax.numpy as jnp
import numpy as np
from jax import lax
from jax.experimental import pallas as pl
from jax.experimental.pallas import tpu as pltpu
from jax.sharding import PartitionSpec as P

EPSILON = 1e-05
HIGHEST = lax.Precision.HIGHEST
HIGH = lax.Precision.HIGH
MESH = pl.DeviceIdType.MESH
F32 = jnp.float32
BF16 = jnp.bfloat16

LEFT, RIGHT = 24, 16
SLOTS = LEFT + RIGHT
LEFT_IDS = 3
LEFT_N, RIGHT_N = 37, 27
LEFT_F, RIGHT_F = 24, 16
FREQ = 2 * LEFT_F + 2 * RIGHT_F
REACH = 13
SPAN = 2 * REACH + 1
SPAN_PAD = 32
LANES = 128


def forward_transform(length, padded, positions, columns):
    count = length // 2 + 1
    out = np.zeros((2 * padded, columns))
    angle = 2 * np.pi * np.outer(np.arange(count), positions) / length
    out[:count, : len(positions)] = np.cos(angle)
    out[padded : padded + count, : len(positions)] = -np.sin(angle)
    return out


def backward_transform(length, padded, positions, rows):
    count = length // 2 + 1
    out = np.zeros((rows, 2 * padded))
    twice = np.where(np.arange(count) == 0, 1.0, 2.0)
    angle = 2 * np.pi * np.outer(positions, np.arange(count)) / length
    out[: len(positions), :count] = np.cos(angle) * twice / length
    out[: len(positions), padded : padded + count] = -np.sin(angle) * twice / length
    return out


def slots_to_freq():
    out = np.zeros((FREQ, SLOTS))
    out[: 2 * LEFT_F, :LEFT] = forward_transform(LEFT_N, LEFT_F, np.arange(LEFT), LEFT)
    out[2 * LEFT_F :, LEFT:] = forward_transform(RIGHT_N, RIGHT_F, np.arange(RIGHT), RIGHT)
    return out


def freq_to_slots():
    out = np.zeros((SLOTS, FREQ))
    out[:LEFT, : 2 * LEFT_F] = backward_transform(LEFT_N, LEFT_F, np.arange(LEFT), LEFT)
    out[LEFT:, 2 * LEFT_F :] = backward_transform(RIGHT_N, RIGHT_F, np.arange(RIGHT), RIGHT)
    return out


def taps_to_freq():
    taps = np.arange(SPAN) - REACH
    return np.concatenate(
        [
            forward_transform(LEFT_N, LEFT_F, taps, SPAN_PAD),
            forward_transform(RIGHT_N, RIGHT_F, taps, SPAN_PAD),
        ]
    )


def freq_to_taps():
    taps = np.arange(SPAN) - REACH
    return np.concatenate(
        [
            backward_transform(LEFT_N, LEFT_F, taps, SPAN_PAD),
            backward_transform(RIGHT_N, RIGHT_F, taps, SPAN_PAD),
        ],
        axis=1,
    )


def split_constant(matrix, group):
    whole = np.kron(np.eye(group), matrix).astype(np.float32)
    high = whole.astype(jnp.bfloat16)
    low = (whole - high.astype(np.float32)).astype(jnp.bfloat16)
    return np.concatenate([high, high, low], axis=1)


def split_stack(value):
    high = value.astype(BF16)
    low = (value - high.astype(F32)).astype(BF16)
    return jnp.concatenate([high, low, high], axis=0)


def product_split(constant_ref, value):
    return jnp.dot(constant_ref[...], split_stack(value), preferred_element_type=F32)


GROUP_IN = 6
GROUP_OUT = 4
GROUP_TAP = 7
GROUP_GRAD = 4


def transform_window(window, to_freq_ref, out_ref):
    for first in range(0, window.shape[0], GROUP_IN):
        part = window[first : first + GROUP_IN].reshape(GROUP_IN * SLOTS, window.shape[-1])
        freq = product_split(to_freq_ref, part)
        out_ref[first : first + GROUP_IN] = freq.reshape(GROUP_IN, FREQ, freq.shape[-1])


def sum_rows(bounds, rows, x_ref, k_ref, y_ref, flipped, conjugate):
    width = x_ref.shape[-1]
    for side, (start, size) in enumerate(((0, LEFT_F), (2 * LEFT_F, RIGHT_F))):
        real, imag = pl.ds(start, size), pl.ds(start + size, size)

        def one_row(row, carry):
            def tap(w, total):
                index = row + SPAN - 1 - w if flipped else w - row
                xr, xi = x_ref[w, real, :], x_ref[w, imag, :]
                kr, ki = k_ref[index, real, :], k_ref[index, imag, :]
                if conjugate:
                    return (total[0] + kr * xr + ki * xi, total[1] + kr * xi - ki * xr)
                return (total[0] + kr * xr - ki * xi, total[1] + kr * xi + ki * xr)

            zero = jnp.zeros((size, width), F32)
            low, high = bounds[2 * side, row], bounds[2 * side + 1, row]
            yr, yi = lax.fori_loop(low, high, tap, (zero, zero))
            y_ref[row, real, :] = yr
            y_ref[row, imag, :] = yi
            return carry

        lax.fori_loop(0, rows, one_row, 0)


def rows_to_slots(rows, y_ref, to_slots_ref, mask_ref, out_ref):
    for first in range(0, rows, GROUP_OUT):
        freq = y_ref[first : first + GROUP_OUT].reshape(GROUP_OUT * FREQ, y_ref.shape[-1])
        cells = product_split(to_slots_ref, freq).reshape(GROUP_OUT, SLOTS, y_ref.shape[-1])
        out_ref[first : first + GROUP_OUT] = cells * mask_ref[first : first + GROUP_OUT]


def conv_forward_kernel(
    bounds, window, taps, mask, to_freq, taps_freq, to_slots, out, xf, kf, stats, yf
):
    rows = out.shape[0]
    transform_window(window, to_freq, xf)
    for first in range(0, kf.shape[0], GROUP_TAP):
        part = taps[first : first + GROUP_TAP].reshape(GROUP_TAP * SPAN_PAD, taps.shape[-1])
        freq = product_split(taps_freq, part)
        kf[first : first + GROUP_TAP] = freq.reshape(GROUP_TAP, FREQ, freq.shape[-1])
    sum_rows(bounds, rows, xf, kf, yf, False, True)
    rows_to_slots(rows, yf, to_slots, mask, out)
    cells = out[...].reshape(rows * SLOTS, out.shape[-1])
    stats[0:1, :] = jnp.sum(cells, axis=0, keepdims=True)
    stats[1:2, :] = jnp.sum(cells * cells, axis=0, keepdims=True)
    stats[2:8, :] = jnp.zeros((6, stats.shape[-1]), F32)


CHUNK = 256
TAP_ROWS = 28


def chunked(leading):
    return pl.BlockSpec(leading + (CHUNK,), lambda c, *_: (0,) * len(leading) + (c,))


def whole(array):
    return pl.BlockSpec(array.shape, lambda c, *_: (0,) * array.ndim)


def conv_forward(bounds, field, taps, mask):
    window, _, channels = field.shape
    rows = window - 2 * REACH
    constants = [
        jnp.asarray(split_constant(slots_to_freq(), GROUP_IN)),
        jnp.asarray(split_constant(taps_to_freq(), GROUP_TAP)),
        jnp.asarray(split_constant(freq_to_slots(), GROUP_OUT)),
    ]
    return pl.pallas_call(
        conv_forward_kernel,
        grid_spec=pltpu.PrefetchScalarGridSpec(
            num_scalar_prefetch=1,
            grid=(channels // CHUNK,),
            in_specs=[
                chunked((window, SLOTS)),
                chunked((TAP_ROWS, SPAN_PAD)),
                pl.BlockSpec((rows, SLOTS, CHUNK), lambda c, *_: (0, 0, 0)),
            ]
            + [whole(c) for c in constants],
            out_specs=[
                chunked((rows, SLOTS)),
                chunked((window, FREQ)),
                chunked((TAP_ROWS, FREQ)),
                chunked((8,)),
            ],
            scratch_shapes=[
                pltpu.VMEM((rows, FREQ, CHUNK), F32),
            ],
        ),
        out_shape=[
            jax.ShapeDtypeStruct((rows, SLOTS, channels), F32),
            jax.ShapeDtypeStruct((window, FREQ, channels), F32),
            jax.ShapeDtypeStruct((TAP_ROWS, FREQ, channels), F32),
            jax.ShapeDtypeStruct((8, channels), F32),
        ],
        compiler_params=pltpu.CompilerParams(vmem_limit_bytes=36 << 20),
        name="conv_forward",
    )(bounds, field, taps, mask, *constants)


def all_sum_job(net, value, out, line_slots, part, layer_slots):
    own = net.own(value, line_slots.at[net.z])
    own.start()
    sent = [net.copy(value, line_slots.at[net.z], net.line(s)) for s in range(1, net.rows)]
    for one in sent:
        one.start()
    yield
    own.wait()
    for one in sent:
        one.wait()
    total = line_slots[0]
    for index in range(1, net.rows):
        total = total + line_slots[index]
    part[...] = total
    own = net.own(part, layer_slots.at[net.dp])
    own.start()
    sent = [net.copy(part, layer_slots.at[net.dp], net.layer(s)) for s in range(1, net.count)]
    for one in sent:
        one.start()
    yield
    own.wait()
    for one in sent:
        one.wait()
    total = layer_slots[0]
    for index in range(1, net.count):
        total = total + layer_slots[index]
    out[...] = total


class Net:
    def __init__(self, dp, rows, send_sem, recv_sem):
        self.count, self.rows = dp, rows
        self.send_sem, self.recv_sem, self.used = send_sem, recv_sem, 0
        self.dp = lax.axis_index("dp")
        self.z = lax.axis_index("rows")
        self.bits = list(range(1, dp.bit_length() - 1))

    def bit(self, index):
        return lax.rem(self.dp // (1 << index), 2)

    def across(self, index):
        return (self.dp + (1 << index) * (1 - 2 * self.bit(index)), self.z)

    def line(self, step):
        return (self.dp, lax.rem(self.z + step, self.rows))

    def layer(self, step):
        return (lax.rem(self.dp + step, self.count), self.z)

    def greet(self):
        barrier = pltpu.get_barrier_semaphore()

        def greet_line(step, carry):
            pl.semaphore_signal(barrier, inc=1, device_id=self.line(step), device_id_type=MESH)
            return carry

        def greet_layer(step, carry):
            pl.semaphore_signal(barrier, inc=1, device_id=self.layer(step), device_id_type=MESH)
            return carry

        lax.fori_loop(1, self.rows, greet_line, 0)
        lax.fori_loop(1, self.count, greet_layer, 0)

    def ready(self):
        pl.semaphore_wait(pltpu.get_barrier_semaphore(), self.rows + self.count - 2)

    def copy(self, src, dst, device):
        made = pltpu.make_async_remote_copy(
            src_ref=src,
            dst_ref=dst,
            send_sem=self.send_sem.at[self.used],
            recv_sem=self.recv_sem.at[self.used],
            device_id=device,
            device_id_type=MESH,
        )
        self.used += 1
        return made

    def reserve(self, number):
        self.used += number
        return self.used - number

    def copy_at(self, index, src, dst, device):
        return pltpu.make_async_remote_copy(
            src_ref=src,
            dst_ref=dst,
            send_sem=self.send_sem.at[index],
            recv_sem=self.recv_sem.at[index],
            device_id=device,
            device_id_type=MESH,
        )

    def own(self, src, dst):
        made = pltpu.make_async_copy(src, dst, self.recv_sem.at[self.used])
        self.used += 1
        return made


def all_sum_job(net, value, out, line_slots, part, layer_slots):
    own = net.own(value, line_slots.at[net.z])
    own.start()
    sent = [net.copy(value, line_slots.at[net.z], net.line(s)) for s in range(1, net.rows)]
    for one in sent:
        one.start()
    yield
    own.wait()
    for one in sent:
        one.wait()
    total = line_slots[0]
    for index in range(1, net.rows):
        total = total + line_slots[index]
    part[...] = total
    own = net.own(part, layer_slots.at[net.dp])
    own.start()
    sent = [net.copy(part, layer_slots.at[net.dp], net.layer(s)) for s in range(1, net.count)]
    for one in sent:
        one.start()
    yield
    own.wait()
    for one in sent:
        one.wait()
    total = layer_slots[0]
    for index in range(1, net.count):
        total = total + layer_slots[index]
    out[...] = total


def aligned(value, unit):
    return pl.multiple_of(value, unit)


def halving(net, order, rows):
    base, steps = 0, []
    for bit in order:
        steps.append((bit, base, rows))
        rows //= 2
        base = base + net.bit(bit) * rows
    return steps, base, rows


def add_rows(dst, src, count, step):
    def one(i, carry):
        at = aligned(i * step, step)
        to, of = dst(at), src(at)
        to[...] = to[...] + of[...]
        return carry

    lax.fori_loop(0, count // step, one, 0)


def run(*jobs):
    jobs = list(jobs)
    while jobs:
        jobs = [job for job in jobs if next(job, StopIteration) is not StopIteration]


def line_gather_job(net, value, out):
    own = net.own(value, out.at[net.z])
    own.start()
    sent = [net.copy(value, out.at[net.z], net.line(s)) for s in range(1, net.rows)]
    for one in sent:
        one.start()
    yield
    own.wait()
    for one in sent:
        one.wait()


def sides(net, rows):
    core = net.bit(0)
    return [
        (pl.ds(aligned((2 * core + side) * LANES, LANES), LANES), *halving(net, order, rows))
        for side, order in enumerate((net.bits, net.bits[::-1]))
    ]


def weights_line_job(net, up, down, wall):
    own = [net.own(up, wall.at[net.z, 0]), net.own(down, wall.at[net.z, 1])]
    last = net.rows - 1
    for step in range(1, net.rows):
        moves = []
        for lanes, _, base, rows in sides(net, up.shape[0]):
            mine = pl.ds(aligned(base, 8), rows)
            for way in (1, -1):
                shard = net.z - way * (step - 1)
                going = (net.z >= step - 1) & (net.z < last) if way > 0 else (net.z <= last - (step - 1)) & (net.z > 0)
                coming = net.z >= step if way > 0 else net.z <= last - step
                shard = lax.rem(shard + net.rows, net.rows)
                for which, ref in enumerate((up, down)):
                    piece = wall.at[shard, which, mine, lanes]
                    one = net.copy(ref.at[mine, lanes] if step == 1 else piece, piece, net.line(way % net.rows))
                    pl.when(going)(one.start)
                    moves.append((one, going, coming))
        if step == 1:
            for one in own:
                one.start()
        yield
        for one, going, coming in moves:
            pl.when(coming)(one.wait_recv)
            pl.when(going)(one.wait_send)
    for one in own:
        one.wait()


def weights_layer_job(net, wall):
    parts = sides(net, wall.shape[2])
    for back in range(1, len(net.bits) + 1):
        moves = []
        for lanes, steps, _, _ in parts:
            bit, base, rows = steps[-back]
            mine = pl.ds(aligned(base + net.bit(bit) * (rows // 2), 8), rows // 2)
            for step in range(1, net.rows):
                piece = wall.at[lax.rem(net.z + step, net.rows), :, mine, lanes]
                moves.append(net.copy(piece, piece, net.across(bit)))
        for one in moves:
            one.start()
        yield
        for one in moves:
            one.wait()


def weights_pair_job(net, wall):
    half = wall.shape[3] // 2
    lanes = pl.ds(aligned(net.bit(0) * half, LANES), half)
    moves = []
    for step in range(1, net.rows):
        piece = wall.at[lax.rem(net.z + step, net.rows), :, :, lanes]
        moves.append(net.copy(piece, piece, net.across(0)))
    for one in moves:
        one.start()
    yield
    for one in moves:
        one.wait()


def halo_job(net, field, window, zeros):
    rows = field.shape[0]
    own = net.own(field, window.at[pl.ds(REACH, rows)])
    own.start()
    has_above, has_below = net.z > 0, net.z < net.rows - 1
    down = net.copy(field.at[pl.ds(rows - REACH, REACH)], window.at[pl.ds(0, REACH)], net.line(1))
    up = net.copy(field.at[pl.ds(0, REACH)], window.at[pl.ds(REACH + rows, REACH)], net.line(net.rows - 1))
    pl.when(has_below)(down.start)
    pl.when(has_above)(up.start)
    zeros[...] = jnp.zeros(zeros.shape, F32)
    top = net.own(zeros, window.at[pl.ds(0, REACH)])
    bottom = net.own(zeros, window.at[pl.ds(REACH + rows, REACH)])
    pl.when(jnp.logical_not(has_above))(top.start)
    pl.when(jnp.logical_not(has_below))(bottom.start)
    yield
    own.wait()
    pl.when(jnp.logical_not(has_above))(top.wait)
    pl.when(jnp.logical_not(has_below))(bottom.wait)
    pl.when(has_above)(down.wait_recv)
    pl.when(has_below)(down.wait_send)
    pl.when(has_below)(up.wait_recv)
    pl.when(has_above)(up.wait_send)


def shares(net, rows, width):
    core, out = net.bit(0), []
    by_rows = width == 2 * LANES
    for side, order in enumerate((net.bits, net.bits[::-1])):
        start = side * (rows // 2) if by_rows else 0
        steps, base, size = halving(net, order, rows // 2 if by_rows else rows)
        steps = [(bit, start + first, count) for bit, first, count in steps]
        block = 0 if by_rows else side
        outer = pl.ds(aligned((core if by_rows else 2 * core + side) * LANES, LANES), LANES)
        out.append((pl.ds(block * LANES, LANES), outer, steps, start + base, size))
    return out


def reduce_all_job(net, source, acc, got_pair, got, got_line, out):
    rows, width = source.shape
    half = width // 2
    core = net.bit(0)
    own = net.own(source.at[:, pl.ds(aligned(core * half, LANES), half)], acc)
    sent = net.copy(source.at[:, pl.ds(aligned((1 - core) * half, LANES), half)], got_pair, net.across(0))
    own.start()
    sent.start()
    yield
    own.wait()
    sent.wait()
    add_rows(lambda at: acc.at[pl.ds(at, 64)], lambda at: got_pair.at[pl.ds(at, 64)], rows, 64)
    parts = shares(net, rows, width)
    for index in range(len(net.bits)):
        moves = []
        for side, (inner, _, steps, _, _) in enumerate(parts):
            bit, base, size = steps[index]
            size //= 2
            give = base + (1 - net.bit(bit)) * size
            keep = base + net.bit(bit) * size
            place = got.at[side, pl.ds(rows - 2 * size, size)]
            one = net.copy(acc.at[pl.ds(aligned(give, 8), size), inner], place, net.across(bit))
            one.start()
            moves.append((one, keep, size, inner, side))
        yield
        for one, keep, size, inner, side in moves:
            one.wait()
            unit = 64 if size % 64 == 0 else 8
            add_rows(
                lambda at: acc.at[pl.ds(aligned(keep + at, 8), unit), inner],
                lambda at: got.at[side, pl.ds(aligned(rows - 2 * size + at, 8), unit)],
                size,
                unit,
            )
    moves, own = [], []
    for side, (inner, _, _, base, size) in enumerate(parts):
        size //= net.rows
        own.append(net.own(acc.at[pl.ds(aligned(base + net.z * size, 8), size), inner], got_line.at[side, net.z]))
        for step in range(1, net.rows):
            other = lax.rem(net.z + step, net.rows)
            piece = acc.at[pl.ds(aligned(base + other * size, 8), size), inner]
            moves.append(net.copy(piece, got_line.at[side, net.z], net.line(step)))
    for one in own + moves:
        one.start()
    yield
    for one in own + moves:
        one.wait()
    moves = []
    for side, (_, outer, _, base, size) in enumerate(parts):
        size //= net.rows
        total = got_line[side, 0]
        for index in range(1, net.rows):
            total = total + got_line[side, index]
        piece = out.at[pl.ds(aligned(base + net.z * size, 8), size), outer]
        out[pl.ds(aligned(base + net.z * size, 8), size), outer] = total
        for step in range(1, net.rows):
            moves.append(net.copy(piece, piece, net.line(step)))
            moves[-1].start()
    yield
    for one in moves:
        one.wait()
    for back in range(1, len(net.bits) + 1):
        moves = []
        for _, outer, steps, _, _ in parts:
            bit, base, size = steps[-back]
            piece = out.at[pl.ds(aligned(base + net.bit(bit) * (size // 2), 8), size // 2), outer]
            moves.append(net.copy(piece, piece, net.across(bit)))
            moves[-1].start()
        yield
        for one in moves:
            one.wait()
    piece = out.at[:, pl.ds(aligned(core * half, LANES), half)]
    one = net.copy(piece, piece, net.across(0))
    one.start()
    yield
    one.wait()


VMEM = pl.BlockSpec(memory_space=pltpu.VMEM)
HBM = pl.BlockSpec(memory_space=pltpu.HBM)
COPIES = 448


def shape(*dims):
    return jax.ShapeDtypeStruct(dims, F32)


def exchange(name, number, mesh, body, args, in_specs, outs, out_specs, scratch, limit, aliases=None, late=False):
    dp, rows = mesh

    def kernel(*refs):
        *refs, send_sem, recv_sem = refs
        net = Net(dp, rows, send_sem, recv_sem)
        net.greet()
        if not late:
            net.ready()
        body(net, *refs)
        assert net.used <= COPIES

    return pl.pallas_call(
        kernel,
        out_shape=outs,
        in_specs=in_specs,
        out_specs=out_specs,
        scratch_shapes=scratch + [pltpu.SemaphoreType.DMA((COPIES,))] * 2,
        input_output_aliases=aliases or {},
        compiler_params=pltpu.CompilerParams(
            collective_id=number, has_side_effects=True, vmem_limit_bytes=limit << 20
        ),
        name=name,
    )(*args)


def sum_scratch(mesh, height):
    dp, rows = mesh
    return [pltpu.VMEM((rows, height, LANES), F32), pltpu.VMEM((height, LANES), F32), pltpu.VMEM((dp, height, LANES), F32)]


def sums_names_weights(mesh, value, names, up, down):
    rows = mesh[1]

    def body(net, value, names, up, down, total, all_names, wall, *slots):
        run(
            weights_line_job(net, up, down, wall),
            line_gather_job(net, names, all_names),
            all_sum_job(net, value, total, *slots),
        )

    return exchange(
        "sums_one",
        0,
        mesh,
        body,
        (value, names, up, down),
        [VMEM] * 4,
        [
            shape(*value.shape),
            jax.ShapeDtypeStruct((rows,) + names.shape, jnp.int32),
            shape(rows, 2, *up.shape),
        ],
        [VMEM, VMEM, HBM],
        sum_scratch(mesh, value.shape[0]),
        16,
    )


def halo_weights(mesh, field, wall):
    rows = field.shape[0]

    def body(net, field, wall_in, window, wall, zeros):
        halo = halo_job(net, field, window, zeros)
        next(halo)
        run(weights_layer_job(net, wall))
        run(weights_pair_job(net, wall))
        finish(halo)

    return exchange(
        "halo_act",
        1,
        mesh,
        body,
        (field, wall),
        [VMEM, HBM],
        [shape(rows + 2 * REACH, *field.shape[1:]), shape(*wall.shape)],
        [HBM, HBM],
        [pltpu.VMEM((REACH,) + field.shape[1:], F32)],
        16,
        {1: 1},
    )


def all_scratch(mesh, rows, width):
    size = (rows // 2 if width == 2 * LANES else rows) * 2 // mesh[0] // mesh[1]
    return [
        pltpu.VMEM((rows, width // 2), F32),
        pltpu.VMEM((rows, width // 2), F32),
        pltpu.VMEM((2, rows, LANES), F32),
        pltpu.VMEM((2, mesh[1], size, LANES), F32),
    ]


class Loads:
    def __init__(self, sems):
        self.sems, self.used, self.leaving = sems, 0, []

    def start(self, src, dst):
        one = pltpu.make_async_copy(src, dst, self.sems.at[self.used])
        self.used += 1
        one.start()
        return one

    def leave(self, src, dst):
        self.leaving.append(self.start(src, dst))

    def finish(self):
        for one in self.leaving:
            one.wait()


def gelu_parts(x):
    scale, cubic = 0.7978845608028654, 0.044715
    square = x * x
    t = jnp.tanh(scale * (x + cubic * (x * square)))
    half = 0.5 * (1.0 + t)
    return (x * half, half + 0.5 * x * (1.0 - t * t) * (scale * (1.0 + 3.0 * cubic * square)))


NN = (((1,), (0,)), ((), ()))
NT = (((1,), (1,)), ((), ()))
TILE = 320


def split_two(value):
    high = value.astype(BF16)
    return high, (value - high.astype(F32)).astype(BF16)


def store_split(refs, where, value):
    refs[0][where], refs[1][where] = split_two(value)


def dot_split(left, right, dims=NN):
    def one(a, b):
        return lax.dot_general(a, b, dims, preferred_element_type=F32)

    return one(left[0], right[0]) + (one(left[0], right[1]) + one(left[1], right[0]))


def read_pair(refs, where=Ellipsis):
    return refs[0][where], refs[1][where]


def write_sums(value, first, second):
    for row in range(4):
        lanes = slice(row * LANES, (row + 1) * LANES)
        value[row : row + 1, :] = first[:, lanes]
        value[4 + row : 5 + row, :] = second[:, lanes]


def read_sums(total):
    return tuple(
        jnp.concatenate([total[4 * k + row : 4 * k + row + 1, :] for row in range(4)], axis=1) for k in range(2)
    )


def column_sum(value):
    return jnp.sum(value, axis=0, keepdims=True)


def norm_terms(total, count):
    first, second = read_sums(total)
    mean = first / count
    return mean, lax.rsqrt(second / count - mean * mean + EPSILON)


def finish(job):
    for _ in job:
        pass


def rem(value, unit):
    return value % unit if isinstance(value, int) else lax.rem(value, unit)


def middle_kernel(
    net,
    conv,
    conv_sums,
    x,
    gy,
    mask,
    params,
    point_two,
    wall,
    delta,
    back,
    total_four,
    total_five,
    dconv,
    point_grad,
    part,
    sums_own,
    sums_slots,
    own_sem,
    mixed,
    xhat,
    slope_two,
    act_pair,
    u_pair,
    ut_pair,
    g_pair,
    gt_pair,
    point_pair,
    up_pair,
    down_pair,
    hid_pair,
    dpre_pair,
    w_up,
    w_down,
    made,
    acc,
    got_pair,
    got_layer,
    got_line,
):
    pixels, channels = conv.shape
    tiles = pixels // TILE
    hidden = w_up.shape[2]
    per_shard = wall.shape[2] // hidden
    chunks = net.rows * per_shard
    core = net.bit(0)
    gain_two, bias_two, gain_three, bias_three, count = (params[row : row + 1, :] for row in range(5))

    def each_tile(body):
        def one(index, carry):
            return body(pl.ds(aligned(index * TILE, TILE), TILE), carry)

        zero = jnp.zeros((1, channels), F32)
        return lax.fori_loop(0, tiles, one, (zero, zero))

    def valid(rows):
        return jnp.concatenate([mask[rows, :]] * (channels // LANES), axis=1)

    def total_job(which, out):
        return all_sum_job(net, sums_own.at[which], out, *(slots.at[which] for slots in sums_slots))

    def shard_of(chunk):
        return lax.rem(net.z + chunk // per_shard, net.rows)

    def load(chunk):
        slot, shard, part = rem(chunk, 2), shard_of(chunk), rem(chunk, per_shard)
        span = pl.ds(aligned(part * hidden, hidden), hidden)
        return (
            pltpu.make_async_copy(wall.at[shard, 0, :, span], w_up.at[slot], own_sem.at[0, slot]),
            pltpu.make_async_copy(wall.at[shard, 1, span, :], w_down.at[slot], own_sem.at[1, slot]),
        )

    sums_own[0] = conv_sums[...]
    net.ready()
    job = total_job(0, sums_slots[1].at[0])
    next(job)
    for one in load(0):
        one.start()
    store_split(point_pair, Ellipsis, point_two[...])
    store_split(g_pair, Ellipsis, gy[...])
    next(job)
    store_split(gt_pair, Ellipsis, gy[...].T)
    finish(job)
    mean, inv_two = norm_terms(sums_slots[1].at[0], count)

    def second_norm(rows, carry):
        m = valid(rows)
        hat = (conv[rows, :] - mean) * inv_two
        act, slope = gelu_parts((hat * gain_two + bias_two) * m)
        xhat[rows, :] = hat
        slope_two[rows, :] = slope * m
        store_split(act_pair, rows, act)
        field = x[rows, :] + dot_split(read_pair(act_pair, rows), read_pair(point_pair))
        mixed[rows, :] = field
        return carry[0] + column_sum(field), carry[1] + column_sum(field * field)

    write_sums(sums_own.at[1], *each_tile(second_norm))
    job = total_job(1, sums_slots[1].at[1])
    next(job)
    next(job)
    finish(job)
    mean_three, inv_three = norm_terms(sums_slots[1].at[1], count)

    def third_norm(rows, carry):
        hat = (mixed[rows, :] - mean_three) * inv_three
        store_split(u_pair, rows, (hat * gain_three + bias_three) * valid(rows))
        delta[rows, :] = mixed[rows, :] - x[rows, :]
        back[rows, :] = jnp.zeros((TILE, channels), F32)
        return carry

    each_tile(third_norm)
    for side in range(2):
        ut_pair[side][...] = u_pair[side][...].T

    mine = pl.ds(aligned(core * LANES, LANES), LANES)
    other = pl.ds(aligned((1 - core) * LANES, LANES), LANES)
    halvings = [halving(net, order, channels) for order in (net.bits, net.bits[::-1])]
    stages = len(net.bits)
    pair_base = net.reserve(chunks)
    layer_base = net.reserve(2 * stages * chunks)
    line_base = net.reserve(2 * chunks)

    def pair_move(chunk):
        slot = rem(chunk, 2)
        return (
            net.copy_at(pair_base + chunk, made.at[slot, :, :, other], got_pair.at[chunk], net.across(0)),
            pltpu.make_async_copy(made.at[slot, :, :, mine], acc.at[chunk], own_sem.at[2, slot]),
        )

    def layer_move(stage, chunk):
        moves = []
        for side, (steps, _, _) in enumerate(halvings):
            bit, base, size = steps[stage]
            size //= 2
            give, keep = base + (1 - net.bit(bit)) * size, base + net.bit(bit) * size
            place = pl.ds(channels - 2 * size, size)
            moves.append(
                (
                    net.copy_at(
                        layer_base + (2 * stage + side) * chunks + chunk,
                        acc.at[chunk, side, pl.ds(aligned(give, 8), size), :],
                        got_layer.at[chunk, side, place, :],
                        net.across(bit),
                    ),
                    keep,
                    size,
                    side,
                )
            )
        return moves

    def line_move(chunk, remote):
        moves = []
        shard, part = shard_of(chunk), rem(chunk, per_shard)
        for side, (_, base, size) in enumerate(halvings):
            piece = acc.at[chunk, side, pl.ds(aligned(base, 8), size), :]
            place = got_line.at[net.z, part, side]
            if remote:
                moves.append(net.copy_at(line_base + 2 * chunk + side, piece, place, (net.dp, shard)))
            else:
                moves.append(pltpu.make_async_copy(piece, place, net.recv_sem.at[line_base + 2 * chunk + side]))
        return moves

    def when(test, body):
        if isinstance(test, bool):
            if test:
                body()
        else:
            pl.when(test)(body)

    def within(chunk):
        if isinstance(chunk, int):
            return 0 <= chunk < chunks
        return (chunk >= 0) & (chunk < chunks)

    def progress(step):
        def after_pair():
            chunk = step - 1
            sent, own = pair_move(chunk)
            own.wait()
            sent.wait()
            for side in range(2):
                add_rows(
                    lambda at: acc.at[chunk, side, pl.ds(at, 64), :],
                    lambda at: got_pair.at[chunk, side, pl.ds(at, 64), :],
                    channels,
                    64,
                )
            for one, *_ in layer_move(0, chunk):
                one.start()

        def after_layer(stage):
            chunk = step - 2 - stage
            for one, keep, size, side in layer_move(stage, chunk):
                one.wait()
                unit = min(size, 64)
                add_rows(
                    lambda at: acc.at[chunk, side, pl.ds(aligned(keep + at, 8), unit), :],
                    lambda at: got_layer.at[chunk, side, pl.ds(aligned(channels - 2 * size + at, 8), unit), :],
                    size,
                    unit,
                )
            if stage + 1 < stages:
                for one, *_ in layer_move(stage + 1, chunk):
                    one.start()
            else:

                def go(remote):
                    def start():
                        for one in line_move(chunk, remote):
                            one.start()

                    return start

                when(chunk >= per_shard, go(True))
                when(chunk < per_shard, go(False))

        when(within(step - 1), after_pair)
        for stage in range(stages):
            when(within(step - 2 - stage), functools.partial(after_layer, stage))

    def feed_forward(chunk, carry):
        progress(chunk)
        slot = rem(chunk, 2)
        for one in load(chunk):
            one.wait()

        @pl.when(chunk + 1 < chunks)
        def _():
            for one in load(chunk + 1):
                one.start()

        store_split(up_pair, Ellipsis, w_up[slot])
        store_split(down_pair, Ellipsis, w_down[slot])

        def first_half(rows, carry):
            hid, slope = gelu_parts(dot_split(read_pair(u_pair, rows), read_pair(up_pair)))
            store_split(hid_pair, rows, hid)
            store_split(
                dpre_pair, rows, dot_split(read_pair(g_pair, rows), read_pair(down_pair), NT) * slope
            )
            return carry

        each_tile(first_half)
        made[slot, 0] = dot_split(read_pair(ut_pair), read_pair(dpre_pair))
        made[slot, 1] = dot_split(read_pair(gt_pair), read_pair(hid_pair))
        for one in pair_move(chunk):
            one.start()

        def second_half(rows, carry):
            delta[rows, :] += dot_split(read_pair(hid_pair, rows), read_pair(down_pair))
            back[rows, :] += dot_split(read_pair(dpre_pair, rows), read_pair(up_pair), NT)
            return carry

        each_tile(second_half)
        return carry

    lax.fori_loop(0, chunks, feed_forward, 0)

    def third_sums(rows, carry):
        dy = back[rows, :] * valid(rows)
        back[rows, :] = dy
        hat = (mixed[rows, :] - mean_three) * inv_three
        return carry[0] + column_sum(dy), carry[1] + column_sum(dy * hat)

    write_sums(sums_own.at[2], *each_tile(third_sums))
    job = total_job(2, total_four)
    next(job)
    progress(chunks)
    next(job)
    progress(chunks + 1)
    finish(job)
    for step in range(chunks + 2, chunks + 1 + stages):
        progress(step)
    grad_bias, grad_gain = read_sums(total_four)

    def third_back(rows, carry):
        m = valid(rows)
        hat = (mixed[rows, :] - mean_three) * inv_three
        field = m * gain_three * inv_three * (back[rows, :] - grad_bias / count - hat * (grad_gain / count))
        back[rows, :] = field
        dmixed = gy[rows, :] + field
        store_split(g_pair, rows, dmixed)
        du = dot_split(read_pair(g_pair, rows), read_pair(point_pair), NT) * slope_two[rows, :]
        mixed[rows, :] = du
        return carry[0] + column_sum(du), carry[1] + column_sum(du * xhat[rows, :])

    write_sums(sums_own.at[3], *each_tile(third_back))
    job = total_job(3, total_five)
    next(job)
    for side in range(2):
        ut_pair[side][...] = act_pair[side][...].T
    next(job)
    point_grad[...] = dot_split(read_pair(ut_pair), read_pair(g_pair))
    finish(job)
    grad_bias_two, grad_gain_two = read_sums(total_five)

    def second_back(row, carry):
        rows = pl.ds(aligned(row * SLOTS, 8), SLOTS)
        field = mixed[rows, :] - grad_bias_two / count - xhat[rows, :] * (grad_gain_two / count)
        dconv[row] = valid(rows) * gain_two * inv_two * field
        return carry

    lax.fori_loop(0, pixels // SLOTS, second_back, 0)
    for chunk in range(chunks):
        for one in line_move(chunk, chunk >= per_shard):
            one.wait()
    for which in range(2):
        for block in range(per_shard):
            total = got_line[0, block, which]
            for index in range(1, net.rows):
                total = total + got_line[index, block, which]
            part[which, block] = total


def middle(mesh, conv, conv_sums, x, gy, mask, params, point_two, wall):
    dp, rows = mesh
    pixels, channels = conv.shape
    hidden = 2 * LANES
    chunks = rows * (wall.shape[2] // hidden)
    lines = pixels // SLOTS

    def pair(*dims):
        return [pltpu.VMEM(dims, BF16)] * 2

    piece = channels * 2 // dp
    scratch = [
        pltpu.VMEM((4, 8, LANES), F32),
        [pltpu.VMEM((4, rows, 8, LANES), F32), pltpu.VMEM((4, 8, LANES), F32), pltpu.VMEM((4, dp, 8, LANES), F32)],
        pltpu.SemaphoreType.DMA((3, 2)),
        pltpu.VMEM((pixels, channels), F32),
        pltpu.VMEM((pixels, channels), F32),
        pltpu.VMEM((pixels, channels), F32),
        pair(pixels, channels),
        pair(pixels, channels),
        pair(channels, pixels),
        pair(pixels, channels),
        pair(channels, pixels),
        pair(channels, channels),
        pair(channels, hidden),
        pair(hidden, channels),
        pair(pixels, hidden),
        pair(pixels, hidden),
        pltpu.VMEM((2, channels, hidden), F32),
        pltpu.VMEM((2, hidden, channels), F32),
        pltpu.VMEM((2, 2, channels, hidden), F32),
        pltpu.VMEM((chunks, 2, channels, LANES), F32),
        pltpu.VMEM((chunks, 2, channels, LANES), F32),
        pltpu.VMEM((chunks, 2, channels, LANES), F32),
        pltpu.VMEM((rows, wall.shape[2] // hidden, 2, piece, LANES), F32),
    ]
    return exchange(
        "middle",
        2,
        mesh,
        middle_kernel,
        (conv, conv_sums, x, gy, mask, params, point_two, wall),
        [VMEM] * 7 + [HBM],
        [shape(pixels, channels)] * 2
        + [shape(8, LANES)] * 2
        + [shape(lines, SLOTS, channels), shape(channels, channels)]
        + [shape(2, wall.shape[2] // hidden, piece, LANES)],
        [VMEM] * 7,
        scratch,
        56,
        late=True,
    )


ZERO_ROW = 42
WINDOW_PAD = 48
LEFT_TAPS, RIGHT_TAPS = 24, 14
SIDES = ((0, LEFT_F, LEFT_TAPS), (2 * LEFT_F, RIGHT_F, RIGHT_TAPS))


def transform(window, to_freq, out, group):
    rows, _, width = window.shape
    for first in range(0, rows, group):
        part = window[first : first + group].reshape(group * SLOTS, width)
        out[first : first + group] = product_split(to_freq, part).reshape(group, FREQ, width)


def sum_table(table, rows, x_ref, k_ref, y_ref, flipped):
    width = x_ref.shape[-1]
    for side, (start, size, taps) in enumerate(SIDES):
        real, imag = pl.ds(start, size), pl.ds(start + size, size)

        def one_row(row, carry):
            yr, yi = jnp.zeros((size, width), F32), jnp.zeros((size, width), F32)
            for tap in range(taps):
                w = table[side * rows + row, tap]
                index = jnp.clip(row + SPAN - 1 - w if flipped else w - row, 0, SPAN)
                xr, xi = x_ref[w, real, :], x_ref[w, imag, :]
                kr, ki = k_ref[index, real, :], k_ref[index, imag, :]
                if flipped:
                    yr, yi = yr + (kr * xr - ki * xi), yi + (kr * xi + ki * xr)
                else:
                    yr, yi = yr + (kr * xr + ki * xi), yi + (kr * xi - ki * xr)
            y_ref[row, real, :] = yr
            y_ref[row, imag, :] = yi
            return carry

        lax.fori_loop(0, rows, one_row, 0)


TAP_GROUP = 9


def sum_taps(table, rows, d_ref, x_ref, g_ref):
    tile = (8, x_ref.shape[-1])
    for side, (start, size, _) in enumerate(SIDES):
        for first in range(start, start + size, 8):
            real, imag = pl.ds(first, 8), pl.ds(first + size, 8)

            def some_taps(group, carry):
                sums = [(jnp.zeros(tile, F32), jnp.zeros(tile, F32)) for _ in range(TAP_GROUP)]
                for row in range(rows):
                    dr, di = d_ref[REACH + row, real, :], d_ref[REACH + row, imag, :]
                    for k in range(TAP_GROUP):
                        w = table[side * SPAN + group * TAP_GROUP + k, row]
                        xr, xi = x_ref[w, real, :], x_ref[w, imag, :]
                        gr, gi = sums[k]
                        sums[k] = gr + (dr * xr + di * xi), gi + (dr * xi - di * xr)
                for k in range(TAP_GROUP):
                    g_ref[group * TAP_GROUP + k, real, :], g_ref[group * TAP_GROUP + k, imag, :] = sums[k]
                return carry

            lax.fori_loop(0, SPAN // TAP_GROUP, some_taps, 0)


def halo_moves(net, field, window, index):
    rows = field.shape[0]
    lanes = pl.ds(index * LANES, LANES)
    below, above = net.z < net.rows - 1, net.z > 0
    down = net.copy(
        field.at[pl.ds(rows - REACH, REACH), :, lanes], window.at[index, pl.ds(0, REACH)], net.line(1)
    )
    up = net.copy(
        field.at[pl.ds(0, REACH), :, lanes], window.at[index, pl.ds(REACH + rows, REACH)], net.line(net.rows - 1)
    )
    return [(down, below, above), (up, above, below)]


def start_halo(net, field, window):
    rows = field.shape[0]
    moves = [halo_moves(net, field, window, index) for index in range(window.shape[0])]
    for block in moves:
        for one, goes, _ in block:
            pl.when(goes)(one.start)
    empty = jnp.zeros((REACH,) + window.shape[2:], F32)
    for index in range(window.shape[0]):
        window[index, REACH : REACH + rows] = field[:, :, index * LANES : (index + 1) * LANES]
        window[index, 2 * REACH + rows :] = jnp.zeros(
            (window.shape[1] - 2 * REACH - rows,) + window.shape[2:], F32
        )

        @pl.when(net.z == 0)
        def _():
            window[index, :REACH] = empty

        @pl.when(net.z == net.rows - 1)
        def _():
            window[index, REACH + rows : 2 * REACH + rows] = empty

    def wait(index):
        for one, goes, comes in moves[index]:
            pl.when(comes)(one.wait_recv)
            pl.when(goes)(one.wait_send)

    return wait


def last_kernel(
    net,
    row_table,
    tap_table,
    dconv_in,
    xf,
    kf,
    mask_in,
    x_in,
    h_in,
    point_in,
    params,
    back_in,
    part_in,
    point_grad_in,
    to_freq,
    to_slots,
    to_taps,
    cells_out,
    total,
    one_out,
    two_out,
    up_out,
    down_out,
    cube_out,
    dconv,
    mask,
    xhat,
    slope,
    point_one,
    back_three,
    part,
    point_grad,
    load_sem,
    sums_own,
    sums_slots,
    own_sem,
    window,
    df,
    x_block,
    k_block,
    gf,
    yf,
    taps,
    taps_flat,
    cube,
    ut_pair,
    point_pair,
    dh_pair,
    du,
    one_grad,
    grad_one,
    grad_two,
    grad_up,
    down_t,
    two_scratch,
    one_scratch,
    taps_scratch,
):
    rows, _, channels = dconv.shape
    pixels = rows * SLOTS
    blocks = channels // LANES
    gain, inv, count, mean, bias = (params[row : row + 1, :] for row in range(5))
    loads = Loads(load_sem)
    came_dconv = loads.start(dconv_in, dconv)
    came_grad = loads.start(point_grad_in, point_grad)
    came_part = loads.start(part_in, part)
    came_x = loads.start(x_in, xhat)
    came_h = loads.start(h_in, slope)
    came_mask = loads.start(mask_in, mask)
    came_point = loads.start(point_in, point_one)

    def load_x(index):
        return pltpu.make_async_copy(
            xf.at[:, :, pl.ds(index * LANES, LANES)], x_block[index % 2].at[pl.ds(0, xf.shape[0])], own_sem.at[index % 2]
        )

    def load_k(index):
        return pltpu.make_async_copy(
            kf.at[:, :, pl.ds(index * LANES, LANES)], k_block[index % 2], own_sem.at[2 + index % 2]
        )

    load_k(0).start()
    load_x(0).start()
    came_back = loads.start(back_in, back_three)
    came_dconv.wait()
    net.ready()
    wait_halo = start_halo(net, dconv, window)
    came_grad.wait()
    came_part.wait()

    def keep_weights():
        point_one[...] = down_t[...].T
        loads.leave(point_one, down_out)
        loads.leave(grad_up, up_out)

    def keep_taps(half):
        lanes = pl.ds(half * 2 * LANES, 2 * LANES)
        for row in range(SPAN):
            cube[row, :, lanes] = taps_flat[half][row * SPAN : (row + 1) * SPAN, :]
        loads.leave(cube.at[:, :, lanes], cube_out.at[:, :, lanes])

    def then(job, after):
        yield from job
        after()

    background = [
        then(reduce_all_job(net, point_grad, *two_scratch, grad_two), lambda: loads.leave(grad_two, two_out)),
        then(gather_pieces_job(net, part, (grad_up, down_t)), keep_weights),
    ]

    def progress():
        background[:] = [job for job in background if next(job, StopIteration) is not StopIteration]

    progress()
    came_x.wait()
    came_h.wait()
    came_mask.wait()
    came_point.wait()

    def valid(where):
        return jnp.concatenate([mask[where, :]] * blocks, axis=1)

    def prepare(index, carry):
        where = pl.ds(aligned(index * LANES, LANES), LANES)
        hat = (xhat[where, :] - mean) * inv
        xhat[where, :] = hat
        m = valid(where)
        for side, half in enumerate(split_two(((hat * gain + bias) * m).T)):
            ut_pair[side][:, where] = half
        slope[where, :] = gelu_parts(slope[where, :])[1] * m
        return carry

    lax.fori_loop(0, pixels // LANES, prepare, 0)
    store_split(point_pair, Ellipsis, point_one[...])
    for slot in range(2):
        x_block[slot][ZERO_ROW:] = jnp.zeros((1,) + x_block[slot].shape[1:], F32)
    taps[:, SPAN * SPAN :, :] = jnp.zeros((taps.shape[0], taps.shape[1] - SPAN * SPAN, taps.shape[2]), F32)

    for index in range(blocks):
        load_k(index).wait()
        if index + 1 < blocks:
            load_k(index + 1).start()
        wait_halo(index)
        lanes = slice(index * LANES, (index + 1) * LANES)
        transform(window.at[index], to_freq, df.at[index], to_freq.shape[0] // FREQ)
        sum_table(row_table, rows, df.at[index], k_block[index % 2], yf, True)
        group = to_slots.shape[0] // SLOTS
        for first in range(0, rows, group):
            where = slice(first * SLOTS, (first + group) * SLOTS)
            dact = product_split(to_slots, yf[first : first + group].reshape(group * FREQ, LANES))
            dh_pair[0][where, lanes], dh_pair[1][where, lanes] = split_two(dact * slope[where, lanes])
    progress()
    one_grad[...] = dot_split(read_pair(ut_pair), read_pair(dh_pair))
    background.append(then(reduce_all_job(net, one_grad, *one_scratch, grad_one), lambda: loads.leave(grad_one, one_out)))
    progress()

    def last_sums(index, carry):
        where = pl.ds(aligned(index * TILE, TILE), TILE)
        dy = dot_split(read_pair(dh_pair, where), read_pair(point_pair), NT) * valid(where)
        du[where, :] = dy
        return carry[0] + column_sum(dy), carry[1] + column_sum(dy * xhat[where, :])

    zero = jnp.zeros((1, channels), F32)
    write_sums(sums_own, *lax.fori_loop(0, pixels // TILE, last_sums, (zero, zero)))
    background.append(all_sum_job(net, sums_own, total, *sums_slots))
    progress()
    for index in range(blocks):
        load_x(index).wait()
        if index + 1 < blocks:
            load_x(index + 1).start()
        sum_taps(tap_table, rows, df.at[index], x_block[index % 2], gf)
        group = to_taps.shape[0] // SPAN_PAD
        half, lanes = index // 2, slice(index % 2 * LANES, (index % 2 + 1) * LANES)
        for first in range(0, SPAN, group):
            out = product_split(to_taps, gf[first : first + group].reshape(group * FREQ, LANES))
            out = out.reshape(group, SPAN_PAD, LANES)
            for row in range(first, first + group):
                taps[half, row * SPAN : (row + 1) * SPAN, lanes] = out[row - first, :SPAN]
        if index % 2:
            job = reduce_all_job(net, taps.at[half], *taps_scratch[half], taps_flat[half])
            background.append(then(job, functools.partial(keep_taps, half)))
        progress()
    grad_bias, grad_gain = read_sums(total)
    came_back.wait()

    def last_back(index, carry):
        where = pl.ds(aligned(index * TILE, TILE), TILE)
        field = du[where, :] - grad_bias / count - xhat[where, :] * (grad_gain / count)
        back_three[where, :] += valid(where) * gain * inv * field
        return carry

    lax.fori_loop(0, pixels // TILE, last_back, 0)
    loads.leave(back_three, cells_out)
    while background:
        progress()
    loads.finish()


def gather_pieces_job(net, part, outs):
    core = net.bit(0)
    _, per_shard, size, _ = part.shape
    rows = outs[0].shape[0]
    halvings = [halving(net, order, rows) for order in (net.bits, net.bits[::-1])]

    def lanes(block):
        return pl.ds(aligned((2 * block + core) * LANES, LANES), LANES)

    own = []
    for which, out in enumerate(outs):
        base = halvings[which][1]
        for block in range(per_shard):
            own.append(net.own(part.at[which, block], out.at[pl.ds(aligned(base, 8), size), lanes(block)]))
            own[-1].start()
    for one in own:
        one.wait()
    for back_step in range(1, len(net.bits) + 1):
        moves = []
        for which, out in enumerate(outs):
            bit, base, span = halvings[which][0][-back_step]
            here = pl.ds(aligned(base + net.bit(bit) * (span // 2), 8), span // 2)
            for block in range(per_shard):
                piece = out.at[here, lanes(block)]
                moves.append(net.copy(piece, piece, net.across(bit)))
                moves[-1].start()
        yield
        for one in moves:
            one.wait()
    moves = []
    for out in outs:
        for block in range(per_shard):
            piece = out.at[:, lanes(block)]
            moves.append(net.copy(piece, piece, net.across(0)))
            moves[-1].start()
    yield
    for one in moves:
        one.wait()


def last(mesh, tables, dconv, xf, kf, mask, x, hidden, point_one, params, back_three, part, point_grad):
    dp, rows = mesh
    lines, _, channels = dconv.shape
    pixels = lines * SLOTS
    blocks = channels // LANES
    unit = 8 * dp * rows
    tap_rows = -(-SPAN * SPAN // unit) * unit
    constants = [
        jnp.asarray(split_constant(slots_to_freq(), 2)),
        jnp.asarray(split_constant(freq_to_slots(), 2)),
        jnp.asarray(split_constant(freq_to_taps(), 3)),
    ]

    def pair(*dims):
        return [pltpu.VMEM(dims, BF16)] * 2

    field = pltpu.VMEM((pixels, channels), F32)
    square = pltpu.VMEM((channels, channels), F32)
    scratch = [
        pltpu.VMEM(dconv.shape, F32),
        pltpu.VMEM(mask.shape, F32),
        field,
        field,
        square,
        field,
        pltpu.VMEM(part.shape, F32),
        square,
        pltpu.SemaphoreType.DMA((16,)),
        pltpu.VMEM((8, LANES), F32),
        sum_scratch(mesh, 8),
        pltpu.SemaphoreType.DMA((4,)),
        pltpu.VMEM((blocks, WINDOW_PAD, SLOTS, LANES), F32),
        pltpu.VMEM((blocks, WINDOW_PAD, FREQ, LANES), F32),
        [pltpu.VMEM((ZERO_ROW + 1, FREQ, LANES), F32)] * 2,
        [pltpu.VMEM((TAP_ROWS, FREQ, LANES), F32)] * 2,
        pltpu.VMEM((SPAN, FREQ, LANES), F32),
        pltpu.VMEM((lines, FREQ, LANES), F32),
        pltpu.VMEM((blocks // 2, tap_rows, 2 * LANES), F32),
        [pltpu.VMEM((tap_rows, 2 * LANES), F32)] * (blocks // 2),
        pltpu.VMEM((SPAN, SPAN, channels), F32),
        pair(channels, pixels),
        pair(channels, channels),
        pair(pixels, channels),
        field,
        square,
        square,
        square,
        square,
        square,
        all_scratch(mesh, channels, channels),
        all_scratch(mesh, channels, channels),
        [all_scratch(mesh, tap_rows, 2 * LANES)] * (blocks // 2),
    ]
    smem = pl.BlockSpec(memory_space=pltpu.SMEM)
    return exchange(
        "last",
        3,
        mesh,
        last_kernel,
        (*tables, dconv, xf, kf, mask, x, hidden, point_one, params, back_three, part, point_grad, *constants),
        [smem] * 2 + [HBM] * 7 + [VMEM] + [HBM] * 3 + [VMEM] * 3,
        [shape(pixels, channels), shape(8, LANES)] + [shape(channels, channels)] * 4 + [shape(SPAN, SPAN, channels)],
        [HBM, VMEM] + [HBM] * 5,
        scratch,
        60,
        late=True,
    )


def product(left, right):
    return jnp.dot(left, right, precision=HIGH, preferred_element_type=F32)


def product_t(left, right):
    return lax.dot_general(left, right, (((1,), (1,)), ((), ())), precision=HIGH, preferred_element_type=F32)


def contract(left, right):
    return lax.dot_general(left, right, (((0,), (0,)), ((), ())), precision=HIGH, preferred_element_type=F32)


def shards(
    dp,
    devices_rows,
    inputs,
    image_ids,
    first_norm_gain,
    first_norm_bias,
    point_one,
    kernel_big,
    kernel_small,
    second_norm_gain,
    second_norm_bias,
    point_two,
    feedforward_norm_gain,
    feedforward_norm_bias,
    w_up,
    w_down,
    out_grad,
):
    rows, canvases, columns, channels = inputs.shape
    assert canvases == 1 and kernel_big.shape[0] == SPAN
    pixels = rows * SLOTS
    ids = image_ids[:, 0]
    mesh = (dp, devices_rows)

    place = jnp.arange(columns, dtype=jnp.int32)[None, :]
    is_left = (ids >= 0) & (ids < LEFT_IDS)
    is_right = ids >= LEFT_IDS

    def side(member, width):
        name = jnp.max(jnp.where(member, ids, -1), axis=1)
        first = jnp.min(jnp.where(member, place, columns), axis=1)
        return name, jnp.minimum(first, columns - width)

    left_id, left_at = side(is_left, LEFT)
    right_id, right_at = side(is_right, RIGHT)
    slot_column = jnp.concatenate(
        [
            left_at[:, None] + jnp.arange(LEFT, dtype=jnp.int32)[None, :],
            right_at[:, None] + jnp.arange(RIGHT, dtype=jnp.int32)[None, :],
        ],
        axis=1,
    )
    slot_id = jnp.concatenate(
        [
            jnp.broadcast_to(left_id[:, None], (rows, LEFT)),
            jnp.broadcast_to(right_id[:, None], (rows, RIGHT)),
        ],
        axis=1,
    )
    hit = (slot_column[:, :, None] == place[:, None, :]) & (ids[:, None, :] == slot_id[:, :, None])
    hit = hit & (slot_id[:, :, None] >= 0)
    pick = hit.astype(F32)
    slot_mask = jnp.max(pick, axis=2)
    valid = (ids >= 0).astype(F32)

    def compact(field):
        out = lax.dot_general(
            pick, field[:, 0], (((2,), (1,)), ((0,), (0,))), precision=HIGHEST, preferred_element_type=F32
        )
        return out.reshape(pixels, channels)

    def expand(cells):
        return lax.dot_general(
            pick,
            cells.reshape(rows, SLOTS, channels),
            (((1,), (1,)), ((0,), (0,))),
            precision=HIGHEST,
            preferred_element_type=F32,
        )[:, None]

    def pack(first, second):
        return jnp.stack([first, second]).reshape(2 * channels // LANES, LANES)

    def sums(field):
        return jnp.sum(field, axis=0), jnp.sum(field * field, axis=0)

    names = jnp.stack([left_id, right_id], axis=1) + 1
    names_tile = jnp.pad(names.reshape(1, 2 * rows), ((0, 7), (0, LANES - 2 * rows)))
    x = compact(inputs)
    gy = compact(out_grad)
    total, all_names, wall = sums_names_weights(
        mesh,
        jnp.concatenate([pack(*sums(x)), pack(jnp.full((channels,), jnp.sum(valid)), jnp.zeros((channels,)))]),
        names_tile,
        w_up,
        w_down,
    )
    count = total[8, 0]
    total = total[:8].reshape(2, channels)
    all_names = jnp.pad(all_names[:, 0, : 2 * rows].reshape(devices_rows * rows, 2), ((REACH, REACH), (0, 0)))
    window_rows = rows + 2 * REACH
    window_names = lax.dynamic_slice_in_dim(all_names, lax.axis_index("rows") * rows, window_rows, 0)
    w_index = jnp.arange(window_rows, dtype=jnp.int32)[None, :]
    r_index = jnp.arange(rows, dtype=jnp.int32)[:, None]
    near = (w_index >= r_index) & (w_index <= r_index + 2 * REACH)
    bounds = []
    for which in range(2):
        same = near & (names[:, which][:, None] == window_names[:, which][None, :]) & (names[:, which][:, None] > 0)
        low = jnp.min(jnp.where(same, w_index, window_rows), axis=1)
        high = jnp.max(jnp.where(same, w_index + 1, 0), axis=1)
        bounds += [jnp.minimum(low, high), high]
    bounds = jnp.stack(bounds).astype(jnp.int32)
    low, high = bounds[0::2][:, :, None], bounds[1::2][:, :, None]
    listed = low + jnp.arange(LEFT_TAPS, dtype=jnp.int32)
    row_table = jnp.where(listed < high, listed, ZERO_ROW).reshape(2 * rows, LEFT_TAPS)
    listed = jnp.arange(rows, dtype=jnp.int32)[:, None] + jnp.arange(SPAN, dtype=jnp.int32)
    listed = jnp.where((listed >= low) & (listed < high), listed, ZERO_ROW)
    tables = (row_table, listed.transpose(0, 2, 1).reshape(2 * SPAN, rows))

    mask = slot_mask.reshape(pixels, 1)
    mask_wide = jnp.broadcast_to(slot_mask[:, :, None], (rows, SLOTS, CHUNK))

    def norm_scale(total):
        mean = total[0] / count
        return mean, lax.rsqrt(total[1] / count - mean * mean + EPSILON)

    mean_one, inv_one = norm_scale(total)
    xhat_one = (x - mean_one) * inv_one
    u1 = (xhat_one * first_norm_gain + first_norm_bias) * mask
    h1 = product(u1, point_one)
    act, act_slope = gelu_parts(h1)
    act = act.reshape(rows, SLOTS, channels)
    small_start = REACH - kernel_small.shape[0] // 2
    edge = (small_start, small_start)
    kernel = kernel_big + jnp.pad(kernel_small, (edge, edge, (0, 0)))
    taps = jnp.pad(kernel, ((0, TAP_ROWS - SPAN), (0, SPAN_PAD - SPAN), (0, 0)))
    act_window, wall = halo_weights(mesh, act, wall)
    conv, xf, kf, conv_sums = conv_forward(bounds, act_window, taps, mask_wide)
    conv = conv.reshape(pixels, channels)
    conv_sums = conv_sums[:2].reshape(8, LANES)
    vectors = [second_norm_gain, second_norm_bias, feedforward_norm_gain, feedforward_norm_bias]
    params = jnp.stack(vectors + [jnp.full((channels,), count)] + [jnp.zeros((channels,), F32)] * 3)
    mask_lanes = jnp.broadcast_to(mask, (pixels, LANES))
    delta, back_three, total_four, total_five, dconv, point_grad, part = middle(
        mesh, conv, conv_sums, x, gy, mask_lanes, params, point_two, wall
    )
    grad_bias_three, grad_gain_three = total_four.reshape(2, channels)
    grad_bias_two, grad_gain_two = total_five.reshape(2, channels)
    params = jnp.stack(
        [first_norm_gain, inv_one, jnp.full((channels,), count), mean_one, first_norm_bias]
        + [jnp.zeros((channels,), F32)] * 3
    )
    cells, total, grad_point_one, grad_point_two, grad_up, grad_down, grad_kernel = last(
        mesh, tables, dconv, xf, kf, mask_lanes, x, h1, point_one, params, back_three, part, point_grad
    )
    grad_bias_one, grad_gain_one = total.reshape(2, channels)
    output = inputs + expand(delta)
    grad_input = out_grad + expand(cells)
    small_end = small_start + kernel_small.shape[0]
    grad_small = grad_kernel[small_start:small_end, small_start:small_end]
    return (
        output,
        grad_input,
        grad_gain_one,
        grad_bias_one,
        grad_point_one,
        grad_kernel,
        grad_small,
        grad_gain_two,
        grad_bias_two,
        grad_point_two,
        grad_gain_three,
        grad_bias_three,
        grad_up,
        grad_down,
    )


def solution(mesh):
    field = P("rows", "dp", None, None)
    everywhere = P()
    up, down = P(None, "rows"), P("rows", None)
    return jax.shard_map(
        functools.partial(shards, mesh.shape["dp"], mesh.shape["rows"]),
        mesh=mesh,
        in_specs=(field, P("rows", "dp", None)) + (everywhere,) * 10 + (up, down, field),
        out_specs=(field, field) + (everywhere,) * 10 + (up, down),
        check_vma=False,
    )
```

```python
import functools

import jax
import jax.numpy as jnp
import numpy as np
from jax import lax
from jax.experimental import pallas as pl
from jax.experimental.pallas import tpu as pltpu
from jax.sharding import PartitionSpec as P

EPSILON = 1e-05
HIGHEST = lax.Precision.HIGHEST
HIGH = lax.Precision.HIGH
MESH = pl.DeviceIdType.MESH
F32 = jnp.float32
BF16 = jnp.bfloat16

LEFT, RIGHT = 24, 16
SLOTS = LEFT + RIGHT
LEFT_IDS = 3
LEFT_N, RIGHT_N = 37, 27
LEFT_F, RIGHT_F = 24, 16
FREQ = 2 * LEFT_F + 2 * RIGHT_F
REACH = 13
SPAN = 2 * REACH + 1
SPAN_PAD = 32
LANES = 128


def forward_transform(length, padded, positions, columns):
    count = length // 2 + 1
    out = np.zeros((2 * padded, columns))
    angle = 2 * np.pi * np.outer(np.arange(count), positions) / length
    out[:count, : len(positions)] = np.cos(angle)
    out[padded : padded + count, : len(positions)] = -np.sin(angle)
    return out


def backward_transform(length, padded, positions, rows):
    count = length // 2 + 1
    out = np.zeros((rows, 2 * padded))
    twice = np.where(np.arange(count) == 0, 1.0, 2.0)
    angle = 2 * np.pi * np.outer(positions, np.arange(count)) / length
    out[: len(positions), :count] = np.cos(angle) * twice / length
    out[: len(positions), padded : padded + count] = -np.sin(angle) * twice / length
    return out


def slots_to_freq():
    out = np.zeros((FREQ, SLOTS))
    out[: 2 * LEFT_F, :LEFT] = forward_transform(LEFT_N, LEFT_F, np.arange(LEFT), LEFT)
    out[2 * LEFT_F :, LEFT:] = forward_transform(RIGHT_N, RIGHT_F, np.arange(RIGHT), RIGHT)
    return out


def freq_to_slots():
    out = np.zeros((SLOTS, FREQ))
    out[:LEFT, : 2 * LEFT_F] = backward_transform(LEFT_N, LEFT_F, np.arange(LEFT), LEFT)
    out[LEFT:, 2 * LEFT_F :] = backward_transform(RIGHT_N, RIGHT_F, np.arange(RIGHT), RIGHT)
    return out


def taps_to_freq():
    taps = np.arange(SPAN) - REACH
    return np.concatenate(
        [
            forward_transform(LEFT_N, LEFT_F, taps, SPAN_PAD),
            forward_transform(RIGHT_N, RIGHT_F, taps, SPAN_PAD),
        ]
    )


def freq_to_taps():
    taps = np.arange(SPAN) - REACH
    return np.concatenate(
        [
            backward_transform(LEFT_N, LEFT_F, taps, SPAN_PAD),
            backward_transform(RIGHT_N, RIGHT_F, taps, SPAN_PAD),
        ],
        axis=1,
    )


def split_constant(matrix, group):
    whole = np.kron(np.eye(group), matrix).astype(np.float32)
    high = whole.astype(jnp.bfloat16)
    low = (whole - high.astype(np.float32)).astype(jnp.bfloat16)
    return np.concatenate([high, high, low], axis=1)


def split_stack(value):
    high = value.astype(BF16)
    low = (value - high.astype(F32)).astype(BF16)
    return jnp.concatenate([high, low, high], axis=0)


def product_split(constant_ref, value):
    return jnp.dot(constant_ref[...], split_stack(value), preferred_element_type=F32)


TAP_ROWS = 28


class Net:
    def __init__(self, dp, rows, send_sem, recv_sem):
        self.count, self.rows = dp, rows
        self.send_sem, self.recv_sem, self.used = send_sem, recv_sem, 0
        self.dp = lax.axis_index("dp")
        self.z = lax.axis_index("rows")
        self.bits = list(range(1, dp.bit_length() - 1))

    def bit(self, index):
        return lax.rem(self.dp // (1 << index), 2)

    def across(self, index):
        return (self.dp + (1 << index) * (1 - 2 * self.bit(index)), self.z)

    def line(self, step):
        return (self.dp, lax.rem(self.z + step, self.rows))

    def layer(self, step):
        return (lax.rem(self.dp + step, self.count), self.z)

    def greet(self):
        barrier = pltpu.get_barrier_semaphore()

        def greet_line(step, carry):
            pl.semaphore_signal(barrier, inc=1, device_id=self.line(step), device_id_type=MESH)
            return carry

        def greet_layer(step, carry):
            pl.semaphore_signal(barrier, inc=1, device_id=self.layer(step), device_id_type=MESH)
            return carry

        lax.fori_loop(1, self.rows, greet_line, 0)
        lax.fori_loop(1, self.count, greet_layer, 0)

    def ready(self):
        pl.semaphore_wait(pltpu.get_barrier_semaphore(), self.rows + self.count - 2)

    def copy(self, src, dst, device):
        made = pltpu.make_async_remote_copy(
            src_ref=src,
            dst_ref=dst,
            send_sem=self.send_sem.at[self.used],
            recv_sem=self.recv_sem.at[self.used],
            device_id=device,
            device_id_type=MESH,
        )
        self.used += 1
        return made

    def reserve(self, number):
        self.used += number
        return self.used - number

    def copy_at(self, index, src, dst, device):
        return pltpu.make_async_remote_copy(
            src_ref=src,
            dst_ref=dst,
            send_sem=self.send_sem.at[index],
            recv_sem=self.recv_sem.at[index],
            device_id=device,
            device_id_type=MESH,
        )

    def own(self, src, dst):
        made = pltpu.make_async_copy(src, dst, self.recv_sem.at[self.used])
        self.used += 1
        return made


def all_sum_job(net, value, out, line_slots, part, layer_slots):
    own = net.own(value, line_slots.at[net.z])
    own.start()
    sent = [net.copy(value, line_slots.at[net.z], net.line(s)) for s in range(1, net.rows)]
    for one in sent:
        one.start()
    yield
    own.wait()
    for one in sent:
        one.wait()
    total = line_slots[0]
    for index in range(1, net.rows):
        total = total + line_slots[index]
    part[...] = total
    own = net.own(part, layer_slots.at[net.dp])
    own.start()
    sent = [net.copy(part, layer_slots.at[net.dp], net.layer(s)) for s in range(1, net.count)]
    for one in sent:
        one.start()
    yield
    own.wait()
    for one in sent:
        one.wait()
    total = layer_slots[0]
    for index in range(1, net.count):
        total = total + layer_slots[index]
    out[...] = total


def aligned(value, unit):
    return pl.multiple_of(value, unit)


def halving(net, order, rows):
    base, steps = 0, []
    for bit in order:
        steps.append((bit, base, rows))
        rows //= 2
        base = base + net.bit(bit) * rows
    return steps, base, rows


def add_rows(dst, src, count, step):
    def one(i, carry):
        at = aligned(i * step, step)
        to, of = dst(at), src(at)
        to[...] = to[...] + of[...]
        return carry

    lax.fori_loop(0, count // step, one, 0)


def run(*jobs):
    jobs = list(jobs)
    while jobs:
        jobs = [job for job in jobs if next(job, StopIteration) is not StopIteration]


def sides(net, rows):
    core = net.bit(0)
    return [
        (pl.ds(aligned((2 * core + side) * LANES, LANES), LANES), *halving(net, order, rows))
        for side, order in enumerate((net.bits, net.bits[::-1]))
    ]


def weights_line_job(net, up, down, wall):
    own = [net.own(up, wall.at[net.z, 0]), net.own(down, wall.at[net.z, 1])]
    last = net.rows - 1
    for step in range(1, net.rows):
        moves = []
        for lanes, _, base, rows in sides(net, up.shape[0]):
            mine = pl.ds(aligned(base, 8), rows)
            for way in (1, -1):
                shard = net.z - way * (step - 1)
                going = (net.z >= step - 1) & (net.z < last) if way > 0 else (net.z <= last - (step - 1)) & (net.z > 0)
                coming = net.z >= step if way > 0 else net.z <= last - step
                shard = lax.rem(shard + net.rows, net.rows)
                for which, ref in enumerate((up, down)):
                    piece = wall.at[shard, which, mine, lanes]
                    one = net.copy(ref.at[mine, lanes] if step == 1 else piece, piece, net.line(way % net.rows))
                    pl.when(going)(one.start)
                    moves.append((one, going, coming))
        if step == 1:
            for one in own:
                one.start()
        yield
        for one, going, coming in moves:
            pl.when(coming)(one.wait_recv)
            pl.when(going)(one.wait_send)
    for one in own:
        one.wait()


def weights_layer_job(net, wall):
    parts = sides(net, wall.shape[2])
    for back in range(1, len(net.bits) + 1):
        moves = []
        for lanes, steps, _, _ in parts:
            bit, base, rows = steps[-back]
            mine = pl.ds(aligned(base + net.bit(bit) * (rows // 2), 8), rows // 2)
            for step in range(1, net.rows):
                piece = wall.at[lax.rem(net.z + step, net.rows), :, mine, lanes]
                moves.append(net.copy(piece, piece, net.across(bit)))
        for one in moves:
            one.start()
        yield
        for one in moves:
            one.wait()


def weights_pair_job(net, wall):
    half = wall.shape[3] // 2
    lanes = pl.ds(aligned(net.bit(0) * half, LANES), half)
    moves = []
    for step in range(1, net.rows):
        piece = wall.at[lax.rem(net.z + step, net.rows), :, :, lanes]
        moves.append(net.copy(piece, piece, net.across(0)))
    for one in moves:
        one.start()
    yield
    for one in moves:
        one.wait()


def halo_job(net, field, window, zeros):
    rows = field.shape[0]
    own = net.own(field, window.at[pl.ds(REACH, rows)])
    own.start()
    has_above, has_below = net.z > 0, net.z < net.rows - 1
    down = net.copy(field.at[pl.ds(rows - REACH, REACH)], window.at[pl.ds(0, REACH)], net.line(1))
    up = net.copy(field.at[pl.ds(0, REACH)], window.at[pl.ds(REACH + rows, REACH)], net.line(net.rows - 1))
    pl.when(has_below)(down.start)
    pl.when(has_above)(up.start)
    zeros[...] = jnp.zeros(zeros.shape, F32)
    top = net.own(zeros, window.at[pl.ds(0, REACH)])
    bottom = net.own(zeros, window.at[pl.ds(REACH + rows, REACH)])
    pl.when(jnp.logical_not(has_above))(top.start)
    pl.when(jnp.logical_not(has_below))(bottom.start)
    yield
    own.wait()
    pl.when(jnp.logical_not(has_above))(top.wait)
    pl.when(jnp.logical_not(has_below))(bottom.wait)
    pl.when(has_above)(down.wait_recv)
    pl.when(has_below)(down.wait_send)
    pl.when(has_below)(up.wait_recv)
    pl.when(has_above)(up.wait_send)


def shares(net, rows, width):
    core, out = net.bit(0), []
    by_rows = width == 2 * LANES
    for side, order in enumerate((net.bits, net.bits[::-1])):
        start = side * (rows // 2) if by_rows else 0
        steps, base, size = halving(net, order, rows // 2 if by_rows else rows)
        steps = [(bit, start + first, count) for bit, first, count in steps]
        block = 0 if by_rows else side
        outer = pl.ds(aligned((core if by_rows else 2 * core + side) * LANES, LANES), LANES)
        out.append((pl.ds(block * LANES, LANES), outer, steps, start + base, size))
    return out


def reduce_all_job(net, source, acc, got_pair, got, got_line, out):
    rows, width = source.shape
    half = width // 2
    core = net.bit(0)
    own = net.own(source.at[:, pl.ds(aligned(core * half, LANES), half)], acc)
    sent = net.copy(source.at[:, pl.ds(aligned((1 - core) * half, LANES), half)], got_pair, net.across(0))
    own.start()
    sent.start()
    yield
    own.wait()
    sent.wait()
    add_rows(lambda at: acc.at[pl.ds(at, 64)], lambda at: got_pair.at[pl.ds(at, 64)], rows, 64)
    parts = shares(net, rows, width)
    for index in range(len(net.bits)):
        moves = []
        for side, (inner, _, steps, _, _) in enumerate(parts):
            bit, base, size = steps[index]
            size //= 2
            give = base + (1 - net.bit(bit)) * size
            keep = base + net.bit(bit) * size
            place = got.at[side, pl.ds(rows - 2 * size, size)]
            one = net.copy(acc.at[pl.ds(aligned(give, 8), size), inner], place, net.across(bit))
            one.start()
            moves.append((one, keep, size, inner, side))
        yield
        for one, keep, size, inner, side in moves:
            one.wait()
            unit = 64 if size % 64 == 0 else 8
            add_rows(
                lambda at: acc.at[pl.ds(aligned(keep + at, 8), unit), inner],
                lambda at: got.at[side, pl.ds(aligned(rows - 2 * size + at, 8), unit)],
                size,
                unit,
            )
    moves, own = [], []
    for side, (inner, _, _, base, size) in enumerate(parts):
        size //= net.rows
        own.append(net.own(acc.at[pl.ds(aligned(base + net.z * size, 8), size), inner], got_line.at[side, net.z]))
        for step in range(1, net.rows):
            other = lax.rem(net.z + step, net.rows)
            piece = acc.at[pl.ds(aligned(base + other * size, 8), size), inner]
            moves.append(net.copy(piece, got_line.at[side, net.z], net.line(step)))
    for one in own + moves:
        one.start()
    yield
    for one in own + moves:
        one.wait()
    moves = []
    for side, (_, outer, _, base, size) in enumerate(parts):
        size //= net.rows
        total = got_line[side, 0]
        for index in range(1, net.rows):
            total = total + got_line[side, index]
        piece = out.at[pl.ds(aligned(base + net.z * size, 8), size), outer]
        out[pl.ds(aligned(base + net.z * size, 8), size), outer] = total
        for step in range(1, net.rows):
            moves.append(net.copy(piece, piece, net.line(step)))
            moves[-1].start()
    yield
    for one in moves:
        one.wait()
    for back in range(1, len(net.bits) + 1):
        moves = []
        for _, outer, steps, _, _ in parts:
            bit, base, size = steps[-back]
            piece = out.at[pl.ds(aligned(base + net.bit(bit) * (size // 2), 8), size // 2), outer]
            moves.append(net.copy(piece, piece, net.across(bit)))
            moves[-1].start()
        yield
        for one in moves:
            one.wait()
    piece = out.at[:, pl.ds(aligned(core * half, LANES), half)]
    one = net.copy(piece, piece, net.across(0))
    one.start()
    yield
    one.wait()


VMEM = pl.BlockSpec(memory_space=pltpu.VMEM)
HBM = pl.BlockSpec(memory_space=pltpu.HBM)
COPIES = 448


def shape(*dims):
    return jax.ShapeDtypeStruct(dims, F32)


def exchange(name, number, mesh, body, args, in_specs, outs, out_specs, scratch, limit, aliases=None, late=False):
    dp, rows = mesh

    def kernel(*refs):
        *refs, send_sem, recv_sem = refs
        net = Net(dp, rows, send_sem, recv_sem)
        net.greet()
        if not late:
            net.ready()
        body(net, *refs)
        assert net.used <= COPIES

    return pl.pallas_call(
        kernel,
        out_shape=outs,
        in_specs=in_specs,
        out_specs=out_specs,
        scratch_shapes=scratch + [pltpu.SemaphoreType.DMA((COPIES,))] * 2,
        input_output_aliases=aliases or {},
        compiler_params=pltpu.CompilerParams(
            collective_id=number, has_side_effects=True, vmem_limit_bytes=limit << 20
        ),
        name=name,
    )(*args)


def sum_scratch(mesh, height):
    dp, rows = mesh
    return [pltpu.VMEM((rows, height, LANES), F32), pltpu.VMEM((height, LANES), F32), pltpu.VMEM((dp, height, LANES), F32)]


def all_scratch(mesh, rows, width):
    size = (rows // 2 if width == 2 * LANES else rows) * 2 // mesh[0] // mesh[1]
    return [
        pltpu.VMEM((rows, width // 2), F32),
        pltpu.VMEM((rows, width // 2), F32),
        pltpu.VMEM((2, rows, LANES), F32),
        pltpu.VMEM((2, mesh[1], size, LANES), F32),
    ]


class Loads:
    def __init__(self, sems):
        self.sems, self.used, self.leaving = sems, 0, []

    def start(self, src, dst):
        one = pltpu.make_async_copy(src, dst, self.sems.at[self.used])
        self.used += 1
        one.start()
        return one

    def leave(self, src, dst):
        self.leaving.append(self.start(src, dst))

    def finish(self):
        for one in self.leaving:
            one.wait()


def gelu_parts(x):
    scale, cubic = 0.7978845608028654, 0.044715
    square = x * x
    t = jnp.tanh(scale * (x + cubic * (x * square)))
    half = 0.5 * (1.0 + t)
    return (x * half, half + 0.5 * x * (1.0 - t * t) * (scale * (1.0 + 3.0 * cubic * square)))


NN = (((1,), (0,)), ((), ()))
NT = (((1,), (1,)), ((), ()))
TILE = 320


def split_two(value):
    high = value.astype(BF16)
    return high, (value - high.astype(F32)).astype(BF16)


def store_split(refs, where, value):
    refs[0][where], refs[1][where] = split_two(value)


def dot_split(left, right, dims=NN):
    def one(a, b):
        return lax.dot_general(a, b, dims, preferred_element_type=F32)

    return one(left[0], right[0]) + (one(left[0], right[1]) + one(left[1], right[0]))


def read_pair(refs, where=Ellipsis):
    return refs[0][where], refs[1][where]


def write_sums(value, first, second):
    for row in range(4):
        lanes = slice(row * LANES, (row + 1) * LANES)
        value[row : row + 1, :] = first[:, lanes]
        value[4 + row : 5 + row, :] = second[:, lanes]


def read_sums(total):
    return tuple(
        jnp.concatenate([total[4 * k + row : 4 * k + row + 1, :] for row in range(4)], axis=1) for k in range(2)
    )


def column_sum(value):
    return jnp.sum(value, axis=0, keepdims=True)


def norm_terms(total, count):
    first, second = read_sums(total)
    mean = first / count
    return mean, lax.rsqrt(second / count - mean * mean + EPSILON)


def finish(job):
    for _ in job:
        pass


def rem(value, unit):
    return value % unit if isinstance(value, int) else lax.rem(value, unit)


def middle_kernel(
    net,
    conv_in,
    conv_sums,
    x_in,
    gy_in,
    mask_in,
    params,
    total_one,
    point_in,
    wall_in,
    delta_out,
    back_out,
    total_four,
    total_five,
    dconv_out,
    point_out,
    part,
    wall,
    x,
    gy,
    mask,
    point_two,
    delta,
    back,
    dconv,
    point_grad,
    load_sem,
    sums_own,
    sums_slots,
    own_sem,
    mixed,
    xhat,
    slope_two,
    act_pair,
    u_pair,
    ut_pair,
    g_pair,
    gt_pair,
    point_pair,
    up_pair,
    down_pair,
    hid_pair,
    dpre_pair,
    w_up,
    w_down,
    made,
    acc,
    got_pair,
    got_layer,
    got_line,
):
    pixels, channels = x.shape
    tiles = pixels // TILE
    hidden = w_up.shape[2]
    per_shard = wall.shape[2] // hidden
    chunks = net.rows * per_shard
    core = net.bit(0)
    gain_two, bias_two, gain_three, bias_three = (params[row : row + 1, :] for row in range(4))
    count = read_count(total_one)
    loads = Loads(load_sem)
    came_point = loads.start(point_in, point_two)
    came_gy = loads.start(gy_in, gy)
    came = [loads.start(src, dst) for src, dst in ((conv_in, xhat), (x_in, x), (mask_in, mask))]

    def each_tile(body):
        def one(index, carry):
            return body(pl.ds(aligned(index * TILE, TILE), TILE), carry)

        zero = jnp.zeros((1, channels), F32)
        return lax.fori_loop(0, tiles, one, (zero, zero))

    def valid(rows):
        return jnp.concatenate([mask[rows, :]] * (channels // LANES), axis=1)

    def total_job(which, out):
        return all_sum_job(net, sums_own.at[which], out, *(slots.at[which] for slots in sums_slots))

    def shard_of(chunk):
        return lax.rem(net.z + chunk // per_shard, net.rows)

    def load(chunk):
        slot, shard, part = rem(chunk, 2), shard_of(chunk), rem(chunk, per_shard)
        span = pl.ds(aligned(part * hidden, hidden), hidden)
        return (
            pltpu.make_async_copy(wall.at[shard, 0, :, span], w_up.at[slot], own_sem.at[0, slot]),
            pltpu.make_async_copy(wall.at[shard, 1, span, :], w_down.at[slot], own_sem.at[1, slot]),
        )

    sums_own[0] = conv_sums[...]
    net.ready()
    job = total_job(0, sums_slots[1].at[0])
    next(job)

    def weights_job():
        yield from weights_layer_job(net, wall)
        yield from weights_pair_job(net, wall)

    weights = weights_job()
    next(weights)
    for one in load(0):
        one.start()
    came_point.wait()
    store_split(point_pair, Ellipsis, point_two[...])
    came_gy.wait()
    store_split(g_pair, Ellipsis, gy[...])
    next(job)
    store_split(gt_pair, Ellipsis, gy[...].T)
    finish(job)
    for one in came:
        one.wait()
    mean, inv_two = norm_terms(sums_slots[1].at[0], count)

    def second_norm(rows, carry):
        m = valid(rows)
        hat = (xhat[rows, :] - mean) * inv_two
        act, slope = gelu_parts((hat * gain_two + bias_two) * m)
        xhat[rows, :] = hat
        slope_two[rows, :] = slope * m
        store_split(act_pair, rows, act)
        field = x[rows, :] + dot_split(read_pair(act_pair, rows), read_pair(point_pair))
        mixed[rows, :] = field
        return carry[0] + column_sum(field), carry[1] + column_sum(field * field)

    write_sums(sums_own.at[1], *each_tile(second_norm))
    job = total_job(1, sums_slots[1].at[1])
    next(job)
    next(weights)
    next(job)
    finish(job)
    mean_three, inv_three = norm_terms(sums_slots[1].at[1], count)

    def third_norm(rows, carry):
        hat = (mixed[rows, :] - mean_three) * inv_three
        store_split(u_pair, rows, (hat * gain_three + bias_three) * valid(rows))
        delta[rows, :] = mixed[rows, :] - x[rows, :]
        back[rows, :] = jnp.zeros((TILE, channels), F32)
        return carry

    each_tile(third_norm)
    for side in range(2):
        ut_pair[side][...] = u_pair[side][...].T

    mine = pl.ds(aligned(core * LANES, LANES), LANES)
    other = pl.ds(aligned((1 - core) * LANES, LANES), LANES)
    halvings = [halving(net, order, channels) for order in (net.bits, net.bits[::-1])]
    stages = len(net.bits)
    pair_base = net.reserve(chunks)
    layer_base = net.reserve(2 * stages * chunks)
    line_base = net.reserve(2 * chunks)

    def pair_move(chunk):
        slot = rem(chunk, 2)
        return (
            net.copy_at(pair_base + chunk, made.at[slot, :, :, other], got_pair.at[chunk], net.across(0)),
            pltpu.make_async_copy(made.at[slot, :, :, mine], acc.at[chunk], own_sem.at[2, slot]),
        )

    def layer_move(stage, chunk):
        moves = []
        for side, (steps, _, _) in enumerate(halvings):
            bit, base, size = steps[stage]
            size //= 2
            give, keep = base + (1 - net.bit(bit)) * size, base + net.bit(bit) * size
            place = pl.ds(channels - 2 * size, size)
            moves.append(
                (
                    net.copy_at(
                        layer_base + (2 * stage + side) * chunks + chunk,
                        acc.at[chunk, side, pl.ds(aligned(give, 8), size), :],
                        got_layer.at[chunk, side, place, :],
                        net.across(bit),
                    ),
                    keep,
                    size,
                    side,
                )
            )
        return moves

    def line_move(chunk, remote):
        moves = []
        shard, part = shard_of(chunk), rem(chunk, per_shard)
        for side, (_, base, size) in enumerate(halvings):
            piece = acc.at[chunk, side, pl.ds(aligned(base, 8), size), :]
            place = got_line.at[net.z, part, side]
            if remote:
                moves.append(net.copy_at(line_base + 2 * chunk + side, piece, place, (net.dp, shard)))
            else:
                moves.append(pltpu.make_async_copy(piece, place, net.recv_sem.at[line_base + 2 * chunk + side]))
        return moves

    def when(test, body):
        if isinstance(test, bool):
            if test:
                body()
        else:
            pl.when(test)(body)

    def within(chunk):
        if isinstance(chunk, int):
            return 0 <= chunk < chunks
        return (chunk >= 0) & (chunk < chunks)

    def progress(step):
        def after_pair():
            chunk = step - 1
            sent, own = pair_move(chunk)
            own.wait()
            sent.wait()
            for side in range(2):
                add_rows(
                    lambda at: acc.at[chunk, side, pl.ds(at, 64), :],
                    lambda at: got_pair.at[chunk, side, pl.ds(at, 64), :],
                    channels,
                    64,
                )
            for one, *_ in layer_move(0, chunk):
                one.start()

        def after_layer(stage):
            chunk = step - 2 - stage
            for one, keep, size, side in layer_move(stage, chunk):
                one.wait()
                unit = min(size, 64)
                add_rows(
                    lambda at: acc.at[chunk, side, pl.ds(aligned(keep + at, 8), unit), :],
                    lambda at: got_layer.at[chunk, side, pl.ds(aligned(channels - 2 * size + at, 8), unit), :],
                    size,
                    unit,
                )
            if stage + 1 < stages:
                for one, *_ in layer_move(stage + 1, chunk):
                    one.start()
            else:

                def go(remote):
                    def start():
                        for one in line_move(chunk, remote):
                            one.start()

                    return start

                when(chunk >= per_shard, go(True))
                when(chunk < per_shard, go(False))

        when(within(step - 1), after_pair)
        for stage in range(stages):
            when(within(step - 2 - stage), functools.partial(after_layer, stage))

    def feed_forward(chunk, carry):
        progress(chunk)
        slot = rem(chunk, 2)
        for one in load(chunk):
            one.wait()

        @pl.when((chunk + 1 < chunks) & (chunk + 1 != per_shard))
        def _():
            for one in load(chunk + 1):
                one.start()

        store_split(up_pair, Ellipsis, w_up[slot])
        store_split(down_pair, Ellipsis, w_down[slot])

        def first_half(rows, carry):
            hid, slope = gelu_parts(dot_split(read_pair(u_pair, rows), read_pair(up_pair)))
            store_split(hid_pair, rows, hid)
            store_split(
                dpre_pair, rows, dot_split(read_pair(g_pair, rows), read_pair(down_pair), NT) * slope
            )
            return carry

        each_tile(first_half)
        made[slot, 0] = dot_split(read_pair(ut_pair), read_pair(dpre_pair))
        made[slot, 1] = dot_split(read_pair(gt_pair), read_pair(hid_pair))
        for one in pair_move(chunk):
            one.start()

        def second_half(rows, carry):
            delta[rows, :] += dot_split(read_pair(hid_pair, rows), read_pair(down_pair))
            back[rows, :] += dot_split(read_pair(dpre_pair, rows), read_pair(up_pair), NT)
            return carry

        each_tile(second_half)
        return carry

    lax.fori_loop(0, per_shard - 1, feed_forward, 0)
    for _ in range(stages - 1):
        next(weights)
    lax.fori_loop(per_shard - 1, per_shard, feed_forward, 0)
    finish(weights)
    for one in load(per_shard):
        one.start()
    lax.fori_loop(per_shard, chunks, feed_forward, 0)

    loads.leave(delta, delta_out)

    def third_sums(rows, carry):
        dy = back[rows, :] * valid(rows)
        back[rows, :] = dy
        hat = (mixed[rows, :] - mean_three) * inv_three
        return carry[0] + column_sum(dy), carry[1] + column_sum(dy * hat)

    write_sums(sums_own.at[2], *each_tile(third_sums))
    job = total_job(2, total_four)
    next(job)
    progress(chunks)
    next(job)
    progress(chunks + 1)
    finish(job)
    for step in range(chunks + 2, chunks + 1 + stages):
        progress(step)
    grad_bias, grad_gain = read_sums(total_four)

    def third_back(rows, carry):
        m = valid(rows)
        hat = (mixed[rows, :] - mean_three) * inv_three
        field = m * gain_three * inv_three * (back[rows, :] - grad_bias / count - hat * (grad_gain / count))
        back[rows, :] = field
        dmixed = gy[rows, :] + field
        store_split(g_pair, rows, dmixed)
        du = dot_split(read_pair(g_pair, rows), read_pair(point_pair), NT) * slope_two[rows, :]
        mixed[rows, :] = du
        return carry[0] + column_sum(du), carry[1] + column_sum(du * xhat[rows, :])

    write_sums(sums_own.at[3], *each_tile(third_back))
    loads.leave(back, back_out)
    job = total_job(3, total_five)
    next(job)
    for side in range(2):
        ut_pair[side][...] = act_pair[side][...].T
    next(job)
    point_grad[...] = dot_split(read_pair(ut_pair), read_pair(g_pair))
    loads.leave(point_grad, point_out)
    finish(job)
    grad_bias_two, grad_gain_two = read_sums(total_five)

    def second_back(row, carry):
        rows = pl.ds(aligned(row * SLOTS, 8), SLOTS)
        field = mixed[rows, :] - grad_bias_two / count - xhat[rows, :] * (grad_gain_two / count)
        dconv[row] = valid(rows) * gain_two * inv_two * field
        return carry

    lax.fori_loop(0, pixels // SLOTS, second_back, 0)
    loads.leave(dconv, dconv_out)
    for chunk in range(chunks):
        for one in line_move(chunk, chunk >= per_shard):
            one.wait()
    for which in range(2):
        for block in range(per_shard):
            total = got_line[0, block, which]
            for index in range(1, net.rows):
                total = total + got_line[index, block, which]
            part[which, block] = total
    loads.finish()


def middle(mesh, conv, conv_sums, x, gy, mask, params, total_one, point_two, wall):
    dp, rows = mesh
    pixels, channels = conv.shape
    hidden = 2 * LANES
    chunks = rows * (wall.shape[2] // hidden)
    lines = pixels // SLOTS

    def pair(*dims):
        return [pltpu.VMEM(dims, BF16)] * 2

    piece = channels * 2 // dp
    field = pltpu.VMEM((pixels, channels), F32)
    square = pltpu.VMEM((channels, channels), F32)
    scratch = [
        field,
        field,
        pltpu.VMEM(mask.shape, F32),
        square,
        field,
        field,
        pltpu.VMEM((lines, SLOTS, channels), F32),
        square,
        pltpu.SemaphoreType.DMA((16,)),
        pltpu.VMEM((4, 8, LANES), F32),
        [pltpu.VMEM((4, rows, 8, LANES), F32), pltpu.VMEM((4, 8, LANES), F32), pltpu.VMEM((4, dp, 8, LANES), F32)],
        pltpu.SemaphoreType.DMA((3, 2)),
        pltpu.VMEM((pixels, channels), F32),
        pltpu.VMEM((pixels, channels), F32),
        pltpu.VMEM((pixels, channels), F32),
        pair(pixels, channels),
        pair(pixels, channels),
        pair(channels, pixels),
        pair(pixels, channels),
        pair(channels, pixels),
        pair(channels, channels),
        pair(channels, hidden),
        pair(hidden, channels),
        pair(pixels, hidden),
        pair(pixels, hidden),
        pltpu.VMEM((2, channels, hidden), F32),
        pltpu.VMEM((2, hidden, channels), F32),
        pltpu.VMEM((2, 2, channels, hidden), F32),
        pltpu.VMEM((chunks, 2, channels, LANES), F32),
        pltpu.VMEM((chunks, 2, channels, LANES), F32),
        pltpu.VMEM((chunks, 2, channels, LANES), F32),
        pltpu.VMEM((rows, wall.shape[2] // hidden, 2, piece, LANES), F32),
    ]
    return exchange(
        "middle",
        2,
        mesh,
        middle_kernel,
        (conv, conv_sums, x, gy, mask, params, total_one, point_two, wall),
        [HBM, VMEM] + [HBM] * 3 + [VMEM] * 2 + [HBM] * 2,
        [shape(pixels, channels)] * 2
        + [shape(8, LANES)] * 2
        + [shape(lines, SLOTS, channels), shape(channels, channels)]
        + [shape(2, wall.shape[2] // hidden, piece, LANES), shape(*wall.shape)],
        [HBM] * 2 + [VMEM] * 2 + [HBM] * 2 + [VMEM, HBM],
        scratch,
        56,
        {8: 7},
        late=True,
    )


ZERO_ROW = 42
WINDOW_PAD = 48
LEFT_TAPS, RIGHT_TAPS = 24, 14
SIDES = ((0, LEFT_F, LEFT_TAPS), (2 * LEFT_F, RIGHT_F, RIGHT_TAPS))


def transform(window, to_freq, out, group):
    rows, _, width = window.shape
    for first in range(0, rows, group):
        part = window[first : first + group].reshape(group * SLOTS, width)
        out[first : first + group] = product_split(to_freq, part).reshape(group, FREQ, width)


def sum_table(table, rows, x_ref, k_ref, y_ref, flipped):
    width = x_ref.shape[-1]
    for side, (start, size, taps) in enumerate(SIDES):
        real, imag = pl.ds(start, size), pl.ds(start + size, size)

        def one_row(row, carry):
            yr, yi = jnp.zeros((size, width), F32), jnp.zeros((size, width), F32)
            for tap in range(taps):
                w = table[side * rows + row, tap]
                index = jnp.clip(row + SPAN - 1 - w if flipped else w - row, 0, SPAN)
                xr, xi = x_ref[w, real, :], x_ref[w, imag, :]
                kr, ki = k_ref[index, real, :], k_ref[index, imag, :]
                if flipped:
                    yr, yi = yr + (kr * xr - ki * xi), yi + (kr * xi + ki * xr)
                else:
                    yr, yi = yr + (kr * xr + ki * xi), yi + (kr * xi - ki * xr)
            y_ref[row, real, :] = yr
            y_ref[row, imag, :] = yi
            return carry

        lax.fori_loop(0, rows, one_row, 0)


TAP_GROUP = 9


def sum_taps(table, rows, d_ref, x_ref, g_ref):
    tile = (8, x_ref.shape[-1])
    for side, (start, size, _) in enumerate(SIDES):
        for first in range(start, start + size, 8):
            real, imag = pl.ds(first, 8), pl.ds(first + size, 8)

            def some_taps(group, carry):
                sums = [(jnp.zeros(tile, F32), jnp.zeros(tile, F32)) for _ in range(TAP_GROUP)]
                for row in range(rows):
                    dr, di = d_ref[REACH + row, real, :], d_ref[REACH + row, imag, :]
                    for k in range(TAP_GROUP):
                        w = table[side * rows + row, group * TAP_GROUP + k]
                        xr, xi = x_ref[w, real, :], x_ref[w, imag, :]
                        gr, gi = sums[k]
                        sums[k] = gr + (dr * xr + di * xi), gi + (dr * xi - di * xr)
                for k in range(TAP_GROUP):
                    g_ref[group * TAP_GROUP + k, real, :], g_ref[group * TAP_GROUP + k, imag, :] = sums[k]
                return carry

            lax.fori_loop(0, SPAN // TAP_GROUP, some_taps, 0)


def halo_moves(net, field, window, index):
    rows = field.shape[0]
    lanes = pl.ds(index * LANES, LANES)
    below, above = net.z < net.rows - 1, net.z > 0
    down = net.copy(
        field.at[pl.ds(rows - REACH, REACH), :, lanes], window.at[index, pl.ds(0, REACH)], net.line(1)
    )
    up = net.copy(
        field.at[pl.ds(0, REACH), :, lanes], window.at[index, pl.ds(REACH + rows, REACH)], net.line(net.rows - 1)
    )
    return [(down, below, above), (up, above, below)]


def start_halo(net, field, window, index):
    rows = field.shape[0]
    moves = halo_moves(net, field, window, index)
    for one, goes, _ in moves:
        pl.when(goes)(one.start)
    empty = jnp.zeros((REACH,) + window.shape[2:], F32)
    window[index, REACH : REACH + rows] = field[:, :, index * LANES : (index + 1) * LANES]
    window[index, 2 * REACH + rows :] = jnp.zeros((window.shape[1] - 2 * REACH - rows,) + window.shape[2:], F32)

    @pl.when(net.z == 0)
    def _():
        window[index, :REACH] = empty

    @pl.when(net.z == net.rows - 1)
    def _():
        window[index, REACH + rows : 2 * REACH + rows] = empty

    def wait():
        for one, goes, comes in moves:
            pl.when(comes)(one.wait_recv)
            pl.when(goes)(one.wait_send)

    return wait


def last_kernel(
    net,
    row_table,
    tap_table,
    dconv_in,
    xf,
    kf,
    mask_in,
    x_in,
    h_in,
    point_in,
    params,
    total_one,
    back_in,
    part_in,
    point_grad_in,
    to_freq,
    to_slots,
    to_taps,
    cells_out,
    total,
    one_out,
    two_out,
    up_out,
    down_out,
    cube_out,
    dconv,
    mask,
    xhat,
    slope,
    point_one,
    back_three,
    part,
    point_grad,
    load_sem,
    sums_own,
    sums_slots,
    own_sem,
    window,
    df,
    x_block,
    k_block,
    gf,
    yf,
    taps,
    taps_flat,
    cube,
    ut_pair,
    point_pair,
    dh_pair,
    du,
    one_grad,
    grad_one,
    grad_two,
    grad_up,
    down_t,
    two_scratch,
    one_scratch,
    taps_scratch,
):
    rows, _, channels = dconv.shape
    pixels = rows * SLOTS
    blocks = channels // LANES
    gain, bias = params[0:1, :], params[1:2, :]
    count = read_count(total_one)
    mean, inv = norm_terms(total_one, count)
    loads = Loads(load_sem)
    came_dconv = loads.start(dconv_in, dconv)
    came_grad = loads.start(point_grad_in, point_grad)
    came_part = loads.start(part_in, part)
    came_x = loads.start(x_in, xhat)
    came_h = loads.start(h_in, slope)
    came_mask = loads.start(mask_in, mask)
    came_point = loads.start(point_in, point_one)

    def load_x(index):
        return pltpu.make_async_copy(xf.at[index], x_block[index % 2], own_sem.at[index % 2])

    def load_k(index):
        return pltpu.make_async_copy(kf.at[index], k_block[index % 2], own_sem.at[2 + index % 2])

    load_k(0).start()
    load_x(0).start()
    came_back = loads.start(back_in, back_three)
    came_dconv.wait()
    net.ready()
    waits = [start_halo(net, dconv, window, index) for index in range(blocks)]
    came_grad.wait()
    came_part.wait()

    def keep_weights():
        point_one[...] = down_t[...].T
        loads.leave(point_one, down_out)
        loads.leave(grad_up, up_out)

    def keep_taps(half):
        lanes = pl.ds(half * 2 * LANES, 2 * LANES)
        for row in range(SPAN):
            cube[row, :, lanes] = taps_flat[half][row * SPAN : (row + 1) * SPAN, :]
        loads.leave(cube.at[:, :, lanes], cube_out.at[:, :, lanes])

    def then(job, after):
        yield from job
        after()

    background = [
        then(reduce_all_job(net, point_grad, *two_scratch, grad_two), lambda: loads.leave(grad_two, two_out)),
        then(gather_pieces_job(net, part, (grad_up, down_t)), keep_weights),
    ]

    def progress():
        background[:] = [job for job in background if next(job, StopIteration) is not StopIteration]

    progress()
    came_x.wait()
    came_h.wait()
    came_mask.wait()
    came_point.wait()

    def valid(where):
        return jnp.concatenate([mask[where, :]] * blocks, axis=1)

    def prepare(index, carry):
        where = pl.ds(aligned(index * LANES, LANES), LANES)
        hat = (xhat[where, :] - mean) * inv
        xhat[where, :] = hat
        m = valid(where)
        for side, half in enumerate(split_two(((hat * gain + bias) * m).T)):
            ut_pair[side][:, where] = half
        slope[where, :] = gelu_parts(slope[where, :])[1] * m
        return carry

    lax.fori_loop(0, pixels // LANES, prepare, 0)
    store_split(point_pair, Ellipsis, point_one[...])
    taps[:, SPAN * SPAN :, :] = jnp.zeros((taps.shape[0], taps.shape[1] - SPAN * SPAN, taps.shape[2]), F32)

    def block_back(index):
        load_k(index).wait()
        if index + 1 < blocks:
            load_k(index + 1).start()
        waits[index]()
        lanes = slice(index * LANES, (index + 1) * LANES)
        transform(window.at[index], to_freq, df.at[index], to_freq.shape[0] // FREQ)
        sum_table(row_table, rows, df.at[index], k_block[index % 2], yf, True)
        group = to_slots.shape[0] // SLOTS
        for first in range(0, rows, group):
            where = slice(first * SLOTS, (first + group) * SLOTS)
            dact = product_split(to_slots, yf[first : first + group].reshape(group * FREQ, LANES))
            dh_pair[0][where, lanes], dh_pair[1][where, lanes] = split_two(dact * slope[where, lanes])

    def block_taps(index):
        load_x(index).wait()
        if index + 1 < blocks:
            load_x(index + 1).start()
        sum_taps(tap_table, rows, df.at[index], x_block[index % 2], gf)
        group = to_taps.shape[0] // SPAN_PAD
        half, lanes = index // 2, slice(index % 2 * LANES, (index % 2 + 1) * LANES)
        for first in range(0, SPAN, group):
            out = product_split(to_taps, gf[first : first + group].reshape(group * FREQ, LANES))
            out = out.reshape(group, SPAN_PAD, LANES)
            for row in range(first, first + group):
                taps[half, row * SPAN : (row + 1) * SPAN, lanes] = out[row - first, :SPAN]
        if index % 2:
            job = reduce_all_job(net, taps.at[half], *taps_scratch[half], taps_flat[half])
            background.append(then(job, functools.partial(keep_taps, half)))

    early = blocks // 2
    for index in range(blocks):
        block_back(index)
        if 1 <= index <= early:
            block_taps(index - 1)
        progress()
    one_grad[...] = dot_split(read_pair(ut_pair), read_pair(dh_pair))
    job = reduce_all_job(net, one_grad, *one_scratch, grad_one)
    background.append(then(job, lambda: loads.leave(grad_one, one_out)))
    progress()

    def last_sums(index, carry):
        where = pl.ds(aligned(index * TILE, TILE), TILE)
        dy = dot_split(read_pair(dh_pair, where), read_pair(point_pair), NT) * valid(where)
        du[where, :] = dy
        return carry[0] + column_sum(dy), carry[1] + column_sum(dy * xhat[where, :])

    zero = jnp.zeros((1, channels), F32)
    write_sums(sums_own, *lax.fori_loop(0, pixels // TILE, last_sums, (zero, zero)))
    sums = all_sum_job(net, sums_own, total, *sums_slots)
    next(sums)
    for index in range(early, blocks):
        block_taps(index)
        progress()
        next(sums, None)
    finish(sums)
    grad_bias, grad_gain = read_sums(total)
    came_back.wait()

    def last_back(index, carry):
        where = pl.ds(aligned(index * TILE, TILE), TILE)
        field = du[where, :] - grad_bias / count - xhat[where, :] * (grad_gain / count)
        back_three[where, :] += valid(where) * gain * inv * field
        return carry

    lax.fori_loop(0, pixels // TILE, last_back, 0)
    loads.leave(back_three, cells_out)
    while background:
        progress()
    loads.finish()


def gather_pieces_job(net, part, outs):
    core = net.bit(0)
    _, per_shard, size, _ = part.shape
    rows = outs[0].shape[0]
    halvings = [halving(net, order, rows) for order in (net.bits, net.bits[::-1])]

    def lanes(block):
        return pl.ds(aligned((2 * block + core) * LANES, LANES), LANES)

    own = []
    for which, out in enumerate(outs):
        base = halvings[which][1]
        for block in range(per_shard):
            own.append(net.own(part.at[which, block], out.at[pl.ds(aligned(base, 8), size), lanes(block)]))
            own[-1].start()
    for one in own:
        one.wait()
    for back_step in range(1, len(net.bits) + 1):
        moves = []
        for which, out in enumerate(outs):
            bit, base, span = halvings[which][0][-back_step]
            here = pl.ds(aligned(base + net.bit(bit) * (span // 2), 8), span // 2)
            for block in range(per_shard):
                piece = out.at[here, lanes(block)]
                moves.append(net.copy(piece, piece, net.across(bit)))
                moves[-1].start()
        yield
        for one in moves:
            one.wait()
    moves = []
    for out in outs:
        for block in range(per_shard):
            piece = out.at[:, lanes(block)]
            moves.append(net.copy(piece, piece, net.across(0)))
            moves[-1].start()
    yield
    for one in moves:
        one.wait()


def last(mesh, tables, dconv, xf, kf, mask, x, hidden, point_one, params, total_one, back_three, part, point_grad):
    dp, rows = mesh
    lines, _, channels = dconv.shape
    pixels = lines * SLOTS
    blocks = channels // LANES
    unit = 8 * dp * rows
    tap_rows = -(-SPAN * SPAN // unit) * unit
    constants = [
        jnp.asarray(split_constant(slots_to_freq(), 2)),
        jnp.asarray(split_constant(freq_to_slots(), 2)),
        jnp.asarray(split_constant(freq_to_taps(), 3)),
    ]

    def pair(*dims):
        return [pltpu.VMEM(dims, BF16)] * 2

    field = pltpu.VMEM((pixels, channels), F32)
    square = pltpu.VMEM((channels, channels), F32)
    scratch = [
        pltpu.VMEM(dconv.shape, F32),
        pltpu.VMEM(mask.shape, F32),
        field,
        field,
        square,
        field,
        pltpu.VMEM(part.shape, F32),
        square,
        pltpu.SemaphoreType.DMA((16,)),
        pltpu.VMEM((8, LANES), F32),
        sum_scratch(mesh, 8),
        pltpu.SemaphoreType.DMA((4,)),
        pltpu.VMEM((blocks, WINDOW_PAD, SLOTS, LANES), F32),
        pltpu.VMEM((blocks, WINDOW_PAD, FREQ, LANES), F32),
        [pltpu.VMEM((ZERO_ROW + 1, FREQ, LANES), F32)] * 2,
        [pltpu.VMEM((TAP_ROWS, FREQ, LANES), F32)] * 2,
        pltpu.VMEM((SPAN, FREQ, LANES), F32),
        pltpu.VMEM((lines, FREQ, LANES), F32),
        pltpu.VMEM((blocks // 2, tap_rows, 2 * LANES), F32),
        [pltpu.VMEM((tap_rows, 2 * LANES), F32)] * (blocks // 2),
        pltpu.VMEM((SPAN, SPAN, channels), F32),
        pair(channels, pixels),
        pair(channels, channels),
        pair(pixels, channels),
        field,
        square,
        square,
        square,
        square,
        square,
        all_scratch(mesh, channels, channels),
        all_scratch(mesh, channels, channels),
        [all_scratch(mesh, tap_rows, 2 * LANES)] * (blocks // 2),
    ]
    smem = pl.BlockSpec(memory_space=pltpu.SMEM)
    return exchange(
        "last",
        3,
        mesh,
        last_kernel,
        (*tables, dconv, xf, kf, mask, x, hidden, point_one, params, total_one, back_three, part, point_grad, *constants),
        [smem] * 2 + [HBM] * 7 + [VMEM] * 2 + [HBM] * 3 + [VMEM] * 3,
        [shape(pixels, channels), shape(8, LANES)] + [shape(channels, channels)] * 4 + [shape(SPAN, SPAN, channels)],
        [HBM, VMEM] + [HBM] * 5,
        scratch,
        60,
        late=True,
    )


def first_kernel(
    net,
    value,
    names,
    x_in,
    up_in,
    down_in,
    point_in,
    taps_in,
    mask_in,
    params,
    to_freq,
    taps_freq,
    to_slots,
    hidden_out,
    wall,
    xf_out,
    kf_out,
    conv_out,
    conv_sums,
    total,
    row_table,
    tap_table,
    x,
    up,
    down,
    point_one,
    taps,
    mask,
    load_sem,
    sums_slots,
    got_names,
    name_rows,
    u_pair,
    point_pair,
    hidden,
    act,
    window,
    xf,
    kf,
    yf,
    conv,
):
    rows, _, channels = act.shape
    pixels = rows * SLOTS
    blocks = channels // LANES
    gain, bias = params[0:1, :], params[1:2, :]
    loads = Loads(load_sem)
    came_up = loads.start(up_in, up)
    came_down = loads.start(down_in, down)
    came_x = loads.start(x_in, x)
    came_point = loads.start(point_in, point_one)
    came_mask = loads.start(mask_in, mask)
    came_taps = loads.start(taps_in, taps)
    net.ready()
    sums = all_sum_job(net, value, total, *sums_slots)
    next(sums)
    below, above = net.z < net.rows - 1, net.z > 0
    name_moves = [
        (net.copy(names.at[1], got_names.at[0], net.line(1)), below, above),
        (net.copy(names.at[2], got_names.at[1], net.line(net.rows - 1)), above, below),
    ]
    for one, goes, _ in name_moves:
        pl.when(goes)(one.start)

    @pl.when(net.z == 0)
    def _():
        got_names[0] = jnp.zeros(got_names.shape[1:], jnp.int32)

    @pl.when(net.z == net.rows - 1)
    def _():
        got_names[1] = jnp.zeros(got_names.shape[1:], jnp.int32)

    came_up.wait()
    came_down.wait()

    background = [weights_line_job(net, up, down, wall)]

    def progress():
        background[:] = [job for job in background if next(job, StopIteration) is not StopIteration]

    progress()
    next(sums)
    came_point.wait()
    store_split(point_pair, Ellipsis, point_one[...])
    came_x.wait()
    came_mask.wait()
    finish(sums)
    progress()
    mean, inv = norm_terms(total, read_count(total))

    def first_norm(index, carry):
        where = pl.ds(aligned(index * LANES, LANES), LANES)
        m = jnp.concatenate([mask[where, :]] * blocks, axis=1)
        store_split(u_pair, where, ((x[where, :] - mean) * inv * gain + bias) * m)
        return carry

    lax.fori_loop(0, pixels // LANES, first_norm, 0)
    waits = []
    for half in range(blocks // 2):
        lanes = slice(half * 2 * LANES, (half + 1) * 2 * LANES)
        for tile in range(pixels // TILE):
            where = slice(tile * TILE, (tile + 1) * TILE)
            pre = dot_split(
                (u_pair[0][where, :], u_pair[1][where, :]), (point_pair[0][:, lanes], point_pair[1][:, lanes])
            )
            hidden[where, lanes] = pre
            act[where.start // SLOTS : where.stop // SLOTS, :, lanes] = gelu_parts(pre)[0].reshape(
                TILE // SLOTS, SLOTS, 2 * LANES
            )
        waits += [start_halo(net, act, window, index) for index in (2 * half, 2 * half + 1)]
    loads.leave(hidden, hidden_out)
    came_taps.wait()
    group = taps_freq.shape[0] // FREQ
    for index in range(blocks):
        for first in range(0, taps.shape[0], group):
            part = taps[first : first + group, :, index * LANES : (index + 1) * LANES]
            freq = product_split(taps_freq, part.reshape(group * SPAN_PAD, LANES))
            kf[index][first : first + group] = freq.reshape(group, FREQ, LANES)
        loads.leave(kf[index], kf_out.at[index])
    for one, goes, comes in name_moves:
        pl.when(comes)(one.wait_recv)
        pl.when(goes)(one.wait_send)
    moved = [loads.start(src, name_rows.at[k]) for k, src in enumerate((names.at[0], got_names.at[0], got_names.at[1]))]
    for one in moved:
        one.wait()
    list_rows(rows, name_rows, row_table, tap_table)
    sums = [jnp.zeros((1, LANES), F32)] * 2 * blocks
    for index in range(blocks):
        lanes = slice(index * LANES, (index + 1) * LANES)
        waits[index]()
        transform(window.at[index], to_freq, xf[index], to_freq.shape[0] // FREQ)
        loads.leave(xf[index].at[pl.ds(0, ZERO_ROW + 1)], xf_out.at[index])
        sum_table(row_table, rows, xf[index], kf[index], yf, False)
        group = to_slots.shape[0] // SLOTS
        for first in range(0, rows, group):
            where = slice(first * SLOTS, (first + group) * SLOTS)
            cells = product_split(to_slots, yf[first : first + group].reshape(group * FREQ, LANES)) * mask[where, :]
            conv[where, lanes] = cells
            sums[2 * index] = sums[2 * index] + column_sum(cells)
            sums[2 * index + 1] = sums[2 * index + 1] + column_sum(cells * cells)
        if index == 0:
            progress()
    loads.leave(conv, conv_out)
    for index in range(blocks):
        conv_sums[index : index + 1, :] = sums[2 * index]
        conv_sums[4 + index : 5 + index, :] = sums[2 * index + 1]
    while background:
        progress()
    loads.finish()


def list_rows(rows, names, row_table, tap_table):
    for side in range(2):

        def name(w):
            return names[0, side, w] + names[1, side, w] + names[2, side, w]

        def one_row(row, carry):
            at = row + REACH
            own = name(at)

            def count(first):
                same = jnp.int32(0)
                for k in range(REACH):
                    same = same + jnp.where(name(first + k) == own, 1, 0)
                return same

            low = at - count(row)
            high = jnp.where(own > 0, at + 1 + count(at + 1), low)
            for tap in range(LEFT_TAPS):
                row_table[side * rows + row, tap] = jnp.where(low + tap < high, low + tap, ZERO_ROW)
            for tap in range(SPAN):
                w = row + tap
                tap_table[side * rows + row, tap] = jnp.where((w >= low) & (w < high), w, ZERO_ROW)
            return carry

        lax.fori_loop(0, rows, one_row, 0)


def read_count(total):
    return jnp.concatenate([total[8 + row : 9 + row, :] for row in range(4)], axis=1)


def first(mesh, value, names, x, up, down, point_one, taps, mask, params):
    dp, devices = mesh
    pixels, channels = x.shape
    lines = pixels // SLOTS
    blocks = channels // LANES
    constants = [
        jnp.asarray(split_constant(slots_to_freq(), 2)),
        jnp.asarray(split_constant(taps_to_freq(), 4)),
        jnp.asarray(split_constant(freq_to_slots(), 2)),
    ]

    def pair(*dims):
        return [pltpu.VMEM(dims, BF16)] * 2

    field = pltpu.VMEM((pixels, channels), F32)
    scratch = [
        field,
        pltpu.VMEM(up.shape, F32),
        pltpu.VMEM(down.shape, F32),
        pltpu.VMEM(point_one.shape, F32),
        pltpu.VMEM(taps.shape, F32),
        pltpu.VMEM(mask.shape, F32),
        pltpu.SemaphoreType.DMA((24,)),
        sum_scratch(mesh, value.shape[0]),
        pltpu.VMEM((2, 8, LANES), jnp.int32),
        pltpu.SMEM((3, 8, LANES), jnp.int32),
        pair(pixels, channels),
        pair(channels, channels),
        field,
        pltpu.VMEM((lines, SLOTS, channels), F32),
        pltpu.VMEM((blocks, WINDOW_PAD, SLOTS, LANES), F32),
        [pltpu.VMEM((WINDOW_PAD, FREQ, LANES), F32)] * blocks,
        [pltpu.VMEM((TAP_ROWS, FREQ, LANES), F32)] * blocks,
        pltpu.VMEM((lines, FREQ, LANES), F32),
        field,
    ]
    smem = pl.BlockSpec(memory_space=pltpu.SMEM)
    table = jax.ShapeDtypeStruct((2 * lines, LANES), jnp.int32)
    return exchange(
        "first",
        0,
        mesh,
        first_kernel,
        (value, names, x, up, down, point_one, taps, mask, params, *constants),
        [VMEM, VMEM] + [HBM] * 6 + [VMEM] * 4,
        [
            shape(pixels, channels),
            shape(devices, 2, *up.shape),
            shape(blocks, ZERO_ROW + 1, FREQ, LANES),
            shape(blocks, TAP_ROWS, FREQ, LANES),
            shape(pixels, channels),
            shape(8, LANES),
            shape(*value.shape),
            table,
            table,
        ],
        [HBM] * 5 + [VMEM] * 2 + [smem] * 2,
        scratch,
        48,
        late=True,
    )


def shards(
    dp,
    devices_rows,
    inputs,
    image_ids,
    first_norm_gain,
    first_norm_bias,
    point_one,
    kernel_big,
    kernel_small,
    second_norm_gain,
    second_norm_bias,
    point_two,
    feedforward_norm_gain,
    feedforward_norm_bias,
    w_up,
    w_down,
    out_grad,
):
    rows, canvases, columns, channels = inputs.shape
    assert canvases == 1 and kernel_big.shape[0] == SPAN
    pixels = rows * SLOTS
    ids = image_ids[:, 0]
    mesh = (dp, devices_rows)

    place = jnp.arange(columns, dtype=jnp.int32)[None, :]
    is_left = (ids >= 0) & (ids < LEFT_IDS)
    is_right = ids >= LEFT_IDS

    def side(member, width):
        name = jnp.max(jnp.where(member, ids, -1), axis=1)
        first = jnp.min(jnp.where(member, place, columns), axis=1)
        return name, jnp.minimum(first, columns - width)

    left_id, left_at = side(is_left, LEFT)
    right_id, right_at = side(is_right, RIGHT)
    slot_column = jnp.concatenate(
        [
            left_at[:, None] + jnp.arange(LEFT, dtype=jnp.int32)[None, :],
            right_at[:, None] + jnp.arange(RIGHT, dtype=jnp.int32)[None, :],
        ],
        axis=1,
    )
    slot_id = jnp.concatenate(
        [
            jnp.broadcast_to(left_id[:, None], (rows, LEFT)),
            jnp.broadcast_to(right_id[:, None], (rows, RIGHT)),
        ],
        axis=1,
    )
    hit = (slot_column[:, :, None] == place[:, None, :]) & (ids[:, None, :] == slot_id[:, :, None])
    hit = hit & (slot_id[:, :, None] >= 0)
    pick = hit.astype(F32)
    slot_mask = jnp.max(pick, axis=2)
    valid = (ids >= 0).astype(F32)

    def compact(field):
        out = lax.dot_general(
            pick, field[:, 0], (((2,), (1,)), ((0,), (0,))), precision=HIGHEST, preferred_element_type=F32
        )
        return out.reshape(pixels, channels)

    def expand(cells):
        return lax.dot_general(
            pick,
            cells.reshape(rows, SLOTS, channels),
            (((1,), (1,)), ((0,), (0,))),
            precision=HIGHEST,
            preferred_element_type=F32,
        )[:, None]

    def pack(first, second):
        return jnp.stack([first, second]).reshape(2 * channels // LANES, LANES)

    def sums(field):
        return jnp.sum(field, axis=0), jnp.sum(field * field, axis=0)

    names = jnp.stack([left_id, right_id]) + 1

    def name_tile(first, last, lane):
        return jnp.pad(names[:, first:last], ((0, 6), (lane, LANES - lane - (last - first))))

    names = jnp.stack(
        [
            name_tile(0, rows, REACH),
            name_tile(rows - REACH, rows, 0),
            name_tile(0, REACH, REACH + rows),
        ]
    )
    x = compact(inputs)
    gy = compact(out_grad)
    mask_lanes = jnp.broadcast_to(slot_mask.reshape(pixels, 1), (pixels, LANES))
    small_start = REACH - kernel_small.shape[0] // 2
    edge = (small_start, small_start)
    kernel = kernel_big + jnp.pad(kernel_small, (edge, edge, (0, 0)))
    taps = jnp.pad(kernel, ((0, TAP_ROWS - SPAN), (0, SPAN_PAD - SPAN), (0, 0)))
    vectors = [
        first_norm_gain,
        first_norm_bias,
        second_norm_gain,
        second_norm_bias,
        feedforward_norm_gain,
        feedforward_norm_bias,
    ]
    params = jnp.pad(jnp.stack(vectors), ((0, 10), (0, 0)))
    hidden, wall, xf, kf, conv, conv_sums, total_one, *tables = first(
        mesh,
        jnp.concatenate([pack(*sums(x)), pack(jnp.full((channels,), jnp.sum(valid)), jnp.zeros((channels,)))]),
        names,
        x,
        w_up,
        w_down,
        point_one,
        taps,
        mask_lanes,
        params[0:8],
    )
    delta, back_three, total_four, total_five, dconv, point_grad, part, _ = middle(
        mesh, conv, conv_sums, x, gy, mask_lanes, params[2:10], total_one, point_two, wall
    )
    grad_bias_three, grad_gain_three = total_four.reshape(2, channels)
    grad_bias_two, grad_gain_two = total_five.reshape(2, channels)
    cells, total, grad_point_one, grad_point_two, grad_up, grad_down, grad_kernel = last(
        mesh,
        tables,
        dconv,
        xf,
        kf,
        mask_lanes,
        x,
        hidden,
        point_one,
        params[0:8],
        total_one,
        back_three,
        part,
        point_grad,
    )
    grad_bias_one, grad_gain_one = total.reshape(2, channels)
    output = inputs + expand(delta)
    grad_input = out_grad + expand(cells)
    small_end = small_start + kernel_small.shape[0]
    grad_small = grad_kernel[small_start:small_end, small_start:small_end]
    return (
        output,
        grad_input,
        grad_gain_one,
        grad_bias_one,
        grad_point_one,
        grad_kernel,
        grad_small,
        grad_gain_two,
        grad_bias_two,
        grad_point_two,
        grad_gain_three,
        grad_bias_three,
        grad_up,
        grad_down,
    )


def solution(mesh):
    field = P("rows", "dp", None, None)
    everywhere = P()
    up, down = P(None, "rows"), P("rows", None)
    return jax.shard_map(
        functools.partial(shards, mesh.shape["dp"], mesh.shape["rows"]),
        mesh=mesh,
        in_specs=(field, P("rows", "dp", None)) + (everywhere,) * 10 + (up, down, field),
        out_specs=(field, field) + (everywhere,) * 10 + (up, down),
        check_vma=False,
    )
```

```python
import functools

import jax
import jax.numpy as jnp
import numpy as np
from jax import lax
from jax.experimental import pallas as pl
from jax.experimental.pallas import tpu as pltpu
from jax.sharding import PartitionSpec as P

EPSILON = 1e-05
HIGHEST = lax.Precision.HIGHEST
HIGH = lax.Precision.HIGH
MESH = pl.DeviceIdType.MESH
F32 = jnp.float32
BF16 = jnp.bfloat16

LEFT, RIGHT = 24, 16
SLOTS = LEFT + RIGHT
LEFT_IDS = 3
LEFT_N, RIGHT_N = 37, 27
LEFT_F, RIGHT_F = 24, 16
FREQ = 2 * LEFT_F + 2 * RIGHT_F
REACH = 13
SPAN = 2 * REACH + 1
SPAN_PAD = 32
LANES = 128


def forward_transform(length, padded, positions, columns):
    count = length // 2 + 1
    out = np.zeros((2 * padded, columns))
    angle = 2 * np.pi * np.outer(np.arange(count), positions) / length
    out[:count, : len(positions)] = np.cos(angle)
    out[padded : padded + count, : len(positions)] = -np.sin(angle)
    return out


def backward_transform(length, padded, positions, rows):
    count = length // 2 + 1
    out = np.zeros((rows, 2 * padded))
    twice = np.where(np.arange(count) == 0, 1.0, 2.0)
    angle = 2 * np.pi * np.outer(positions, np.arange(count)) / length
    out[: len(positions), :count] = np.cos(angle) * twice / length
    out[: len(positions), padded : padded + count] = -np.sin(angle) * twice / length
    return out


def slots_to_freq():
    out = np.zeros((FREQ, SLOTS))
    out[: 2 * LEFT_F, :LEFT] = forward_transform(LEFT_N, LEFT_F, np.arange(LEFT), LEFT)
    out[2 * LEFT_F :, LEFT:] = forward_transform(RIGHT_N, RIGHT_F, np.arange(RIGHT), RIGHT)
    return out


def freq_to_slots():
    out = np.zeros((SLOTS, FREQ))
    out[:LEFT, : 2 * LEFT_F] = backward_transform(LEFT_N, LEFT_F, np.arange(LEFT), LEFT)
    out[LEFT:, 2 * LEFT_F :] = backward_transform(RIGHT_N, RIGHT_F, np.arange(RIGHT), RIGHT)
    return out


def taps_to_freq():
    taps = np.arange(SPAN) - REACH
    return np.concatenate(
        [
            forward_transform(LEFT_N, LEFT_F, taps, SPAN_PAD),
            forward_transform(RIGHT_N, RIGHT_F, taps, SPAN_PAD),
        ]
    )


def freq_to_taps():
    taps = np.arange(SPAN) - REACH
    return np.concatenate(
        [
            backward_transform(LEFT_N, LEFT_F, taps, SPAN_PAD),
            backward_transform(RIGHT_N, RIGHT_F, taps, SPAN_PAD),
        ],
        axis=1,
    )


def split_constant(matrix, group):
    whole = np.kron(np.eye(group), matrix).astype(np.float32)
    high = whole.astype(jnp.bfloat16)
    low = (whole - high.astype(np.float32)).astype(jnp.bfloat16)
    return np.concatenate([high, high, low], axis=1)


def split_stack(value):
    high = value.astype(BF16)
    low = (value - high.astype(F32)).astype(BF16)
    return jnp.concatenate([high, low, high], axis=0)


def product_split(constant_ref, value):
    return jnp.dot(constant_ref[...], split_stack(value), preferred_element_type=F32)


TAP_ROWS = 28


class Net:
    def __init__(self, dp, rows, send_sem, recv_sem):
        self.count, self.rows = dp, rows
        self.send_sem, self.recv_sem, self.used = send_sem, recv_sem, 0
        self.dp = lax.axis_index("dp")
        self.z = lax.axis_index("rows")
        self.bits = list(range(1, dp.bit_length() - 1))

    def bit(self, index):
        return lax.rem(self.dp // (1 << index), 2)

    def across(self, index):
        return (self.dp + (1 << index) * (1 - 2 * self.bit(index)), self.z)

    def line(self, step):
        return (self.dp, lax.rem(self.z + step, self.rows))

    def layer(self, step):
        return (lax.rem(self.dp + step, self.count), self.z)

    def greet(self):
        barrier = pltpu.get_barrier_semaphore()

        def greet_line(step, carry):
            pl.semaphore_signal(barrier, inc=1, device_id=self.line(step), device_id_type=MESH)
            return carry

        def greet_layer(step, carry):
            pl.semaphore_signal(barrier, inc=1, device_id=self.layer(step), device_id_type=MESH)
            return carry

        lax.fori_loop(1, self.rows, greet_line, 0)
        lax.fori_loop(1, self.count, greet_layer, 0)

    def ready(self):
        pl.semaphore_wait(pltpu.get_barrier_semaphore(), self.rows + self.count - 2)

    def copy(self, src, dst, device):
        made = pltpu.make_async_remote_copy(
            src_ref=src,
            dst_ref=dst,
            send_sem=self.send_sem.at[self.used],
            recv_sem=self.recv_sem.at[self.used],
            device_id=device,
            device_id_type=MESH,
        )
        self.used += 1
        return made

    def reserve(self, number):
        self.used += number
        return self.used - number

    def copy_at(self, index, src, dst, device):
        return pltpu.make_async_remote_copy(
            src_ref=src,
            dst_ref=dst,
            send_sem=self.send_sem.at[index],
            recv_sem=self.recv_sem.at[index],
            device_id=device,
            device_id_type=MESH,
        )

    def own(self, src, dst):
        made = pltpu.make_async_copy(src, dst, self.recv_sem.at[self.used])
        self.used += 1
        return made


def all_sum_job(net, value, out, line_slots, part, layer_slots):
    own = net.own(value, line_slots.at[net.z])
    own.start()
    sent = [net.copy(value, line_slots.at[net.z], net.line(s)) for s in range(1, net.rows)]
    for one in sent:
        one.start()
    yield
    own.wait()
    for one in sent:
        one.wait()
    total = line_slots[0]
    for index in range(1, net.rows):
        total = total + line_slots[index]
    part[...] = total
    own = net.own(part, layer_slots.at[net.dp])
    own.start()
    sent = [net.copy(part, layer_slots.at[net.dp], net.layer(s)) for s in range(1, net.count)]
    for one in sent:
        one.start()
    yield
    own.wait()
    for one in sent:
        one.wait()
    total = layer_slots[0]
    for index in range(1, net.count):
        total = total + layer_slots[index]
    out[...] = total


def aligned(value, unit):
    return pl.multiple_of(value, unit)


def halving(net, order, rows):
    base, steps = 0, []
    for bit in order:
        steps.append((bit, base, rows))
        rows //= 2
        base = base + net.bit(bit) * rows
    return steps, base, rows


def add_rows(dst, src, count, step):
    def one(i, carry):
        at = aligned(i * step, step)
        to, of = dst(at), src(at)
        to[...] = to[...] + of[...]
        return carry

    lax.fori_loop(0, count // step, one, 0)


def run(*jobs):
    jobs = list(jobs)
    while jobs:
        jobs = [job for job in jobs if next(job, StopIteration) is not StopIteration]


def sides(net, rows):
    core = net.bit(0)
    return [
        (pl.ds(aligned((2 * core + side) * LANES, LANES), LANES), *halving(net, order, rows))
        for side, order in enumerate((net.bits, net.bits[::-1]))
    ]


def weights_line_job(net, up, down, wall):
    own = [net.own(up, wall.at[net.z, 0]), net.own(down, wall.at[net.z, 1])]
    last = net.rows - 1
    for step in range(1, net.rows):
        moves = []
        for lanes, _, base, rows in sides(net, up.shape[0]):
            mine = pl.ds(aligned(base, 8), rows)
            for way in (1, -1):
                shard = net.z - way * (step - 1)
                going = (net.z >= step - 1) & (net.z < last) if way > 0 else (net.z <= last - (step - 1)) & (net.z > 0)
                coming = net.z >= step if way > 0 else net.z <= last - step
                shard = lax.rem(shard + net.rows, net.rows)
                for which, ref in enumerate((up, down)):
                    piece = wall.at[shard, which, mine, lanes]
                    one = net.copy(ref.at[mine, lanes] if step == 1 else piece, piece, net.line(way % net.rows))
                    pl.when(going)(one.start)
                    moves.append((one, going, coming))
        if step == 1:
            for one in own:
                one.start()
        yield
        for one, going, coming in moves:
            pl.when(coming)(one.wait_recv)
            pl.when(going)(one.wait_send)
    for one in own:
        one.wait()


def weights_layer_job(net, wall, distances):
    parts = sides(net, wall.shape[2])
    shards = [net.z + way * distance for distance in distances for way in (1, -1)]
    shards = [(lax.rem(shard + net.rows, net.rows), (shard >= 0) & (shard < net.rows)) for shard in shards]
    for back in range(1, len(net.bits) + 1):
        moves = []
        for lanes, steps, _, _ in parts:
            bit, base, rows = steps[-back]
            mine = pl.ds(aligned(base + net.bit(bit) * (rows // 2), 8), rows // 2)
            for shard, there in shards:
                piece = wall.at[shard, :, mine, lanes]
                moves.append((net.copy(piece, piece, net.across(bit)), there))
        for one, there in moves:
            pl.when(there)(one.start)
        yield
        for one, there in moves:
            pl.when(there)(one.wait)


def weights_pair_job(net, wall):
    half = wall.shape[3] // 2
    lanes = pl.ds(aligned(net.bit(0) * half, LANES), half)
    moves = []
    for step in range(1, net.rows):
        piece = wall.at[lax.rem(net.z + step, net.rows), :, :, lanes]
        moves.append(net.copy(piece, piece, net.across(0)))
    for one in moves:
        one.start()
    yield
    for one in moves:
        one.wait()


def halo_job(net, field, window, zeros):
    rows = field.shape[0]
    own = net.own(field, window.at[pl.ds(REACH, rows)])
    own.start()
    has_above, has_below = net.z > 0, net.z < net.rows - 1
    down = net.copy(field.at[pl.ds(rows - REACH, REACH)], window.at[pl.ds(0, REACH)], net.line(1))
    up = net.copy(field.at[pl.ds(0, REACH)], window.at[pl.ds(REACH + rows, REACH)], net.line(net.rows - 1))
    pl.when(has_below)(down.start)
    pl.when(has_above)(up.start)
    zeros[...] = jnp.zeros(zeros.shape, F32)
    top = net.own(zeros, window.at[pl.ds(0, REACH)])
    bottom = net.own(zeros, window.at[pl.ds(REACH + rows, REACH)])
    pl.when(jnp.logical_not(has_above))(top.start)
    pl.when(jnp.logical_not(has_below))(bottom.start)
    yield
    own.wait()
    pl.when(jnp.logical_not(has_above))(top.wait)
    pl.when(jnp.logical_not(has_below))(bottom.wait)
    pl.when(has_above)(down.wait_recv)
    pl.when(has_below)(down.wait_send)
    pl.when(has_below)(up.wait_recv)
    pl.when(has_above)(up.wait_send)


def shares(net, rows, width):
    core, out = net.bit(0), []
    by_rows = width == 2 * LANES
    for side, order in enumerate((net.bits, net.bits[::-1])):
        start = side * (rows // 2) if by_rows else 0
        steps, base, size = halving(net, order, rows // 2 if by_rows else rows)
        steps = [(bit, start + first, count) for bit, first, count in steps]
        block = 0 if by_rows else side
        outer = pl.ds(aligned((core if by_rows else 2 * core + side) * LANES, LANES), LANES)
        out.append((pl.ds(block * LANES, LANES), outer, steps, start + base, size))
    return out


def reduce_all_job(net, source, acc, got_pair, got, got_line, out):
    rows, width = source.shape
    half = width // 2
    core = net.bit(0)
    own = net.own(source.at[:, pl.ds(aligned(core * half, LANES), half)], acc)
    sent = net.copy(source.at[:, pl.ds(aligned((1 - core) * half, LANES), half)], got_pair, net.across(0))
    own.start()
    sent.start()
    yield
    own.wait()
    sent.wait()
    add_rows(lambda at: acc.at[pl.ds(at, 64)], lambda at: got_pair.at[pl.ds(at, 64)], rows, 64)
    parts = shares(net, rows, width)
    for index in range(len(net.bits)):
        moves = []
        for side, (inner, _, steps, _, _) in enumerate(parts):
            bit, base, size = steps[index]
            size //= 2
            give = base + (1 - net.bit(bit)) * size
            keep = base + net.bit(bit) * size
            place = got.at[side, pl.ds(rows - 2 * size, size)]
            one = net.copy(acc.at[pl.ds(aligned(give, 8), size), inner], place, net.across(bit))
            one.start()
            moves.append((one, keep, size, inner, side))
        yield
        for one, keep, size, inner, side in moves:
            one.wait()
            unit = 64 if size % 64 == 0 else 8
            add_rows(
                lambda at: acc.at[pl.ds(aligned(keep + at, 8), unit), inner],
                lambda at: got.at[side, pl.ds(aligned(rows - 2 * size + at, 8), unit)],
                size,
                unit,
            )
    moves, own = [], []
    for side, (inner, _, _, base, size) in enumerate(parts):
        size //= net.rows
        own.append(net.own(acc.at[pl.ds(aligned(base + net.z * size, 8), size), inner], got_line.at[side, net.z]))
        for step in range(1, net.rows):
            other = lax.rem(net.z + step, net.rows)
            piece = acc.at[pl.ds(aligned(base + other * size, 8), size), inner]
            moves.append(net.copy(piece, got_line.at[side, net.z], net.line(step)))
    for one in own + moves:
        one.start()
    yield
    for one in own + moves:
        one.wait()
    moves = []
    for side, (_, outer, _, base, size) in enumerate(parts):
        size //= net.rows
        total = got_line[side, 0]
        for index in range(1, net.rows):
            total = total + got_line[side, index]
        piece = out.at[pl.ds(aligned(base + net.z * size, 8), size), outer]
        out[pl.ds(aligned(base + net.z * size, 8), size), outer] = total
        for step in range(1, net.rows):
            moves.append(net.copy(piece, piece, net.line(step)))
            moves[-1].start()
    yield
    for one in moves:
        one.wait()
    for back in range(1, len(net.bits) + 1):
        moves = []
        for _, outer, steps, _, _ in parts:
            bit, base, size = steps[-back]
            piece = out.at[pl.ds(aligned(base + net.bit(bit) * (size // 2), 8), size // 2), outer]
            moves.append(net.copy(piece, piece, net.across(bit)))
            moves[-1].start()
        yield
        for one in moves:
            one.wait()
    piece = out.at[:, pl.ds(aligned(core * half, LANES), half)]
    one = net.copy(piece, piece, net.across(0))
    one.start()
    yield
    one.wait()


VMEM = pl.BlockSpec(memory_space=pltpu.VMEM)
HBM = pl.BlockSpec(memory_space=pltpu.HBM)
COPIES = 448


def shape(*dims):
    return jax.ShapeDtypeStruct(dims, F32)


def exchange(name, number, mesh, body, args, in_specs, outs, out_specs, scratch, limit, aliases=None, late=False):
    dp, rows = mesh

    def kernel(*refs):
        *refs, send_sem, recv_sem = refs
        net = Net(dp, rows, send_sem, recv_sem)
        net.greet()
        if not late:
            net.ready()
        body(net, *refs)
        assert net.used <= COPIES

    return pl.pallas_call(
        kernel,
        out_shape=outs,
        in_specs=in_specs,
        out_specs=out_specs,
        scratch_shapes=scratch + [pltpu.SemaphoreType.DMA((COPIES,))] * 2,
        input_output_aliases=aliases or {},
        compiler_params=pltpu.CompilerParams(
            collective_id=number, has_side_effects=True, vmem_limit_bytes=limit << 20
        ),
        name=name,
    )(*args)


def sum_scratch(mesh, height):
    dp, rows = mesh
    return [pltpu.VMEM((rows, height, LANES), F32), pltpu.VMEM((height, LANES), F32), pltpu.VMEM((dp, height, LANES), F32)]


def all_scratch(mesh, rows, width):
    size = (rows // 2 if width == 2 * LANES else rows) * 2 // mesh[0] // mesh[1]
    return [
        pltpu.VMEM((rows, width // 2), F32),
        pltpu.VMEM((rows, width // 2), F32),
        pltpu.VMEM((2, rows, LANES), F32),
        pltpu.VMEM((2, mesh[1], size, LANES), F32),
    ]


class Loads:
    def __init__(self, sems):
        self.sems, self.used, self.leaving = sems, 0, []

    def start(self, src, dst):
        one = pltpu.make_async_copy(src, dst, self.sems.at[self.used])
        self.used += 1
        one.start()
        return one

    def leave(self, src, dst):
        self.leaving.append(self.start(src, dst))

    def finish(self):
        for one in self.leaving:
            one.wait()


def gelu_parts(x):
    scale, cubic = 0.7978845608028654, 0.044715
    square = x * x
    t = jnp.tanh(scale * (x + cubic * (x * square)))
    half = 0.5 * (1.0 + t)
    return (x * half, half + 0.5 * x * (1.0 - t * t) * (scale * (1.0 + 3.0 * cubic * square)))


NN = (((1,), (0,)), ((), ()))
NT = (((1,), (1,)), ((), ()))
TILE = 320


def split_two(value):
    high = value.astype(BF16)
    return high, (value - high.astype(F32)).astype(BF16)


def store_split(refs, where, value):
    refs[0][where], refs[1][where] = split_two(value)


def dot_split(left, right, dims=NN):
    def one(a, b):
        return lax.dot_general(a, b, dims, preferred_element_type=F32)

    return one(left[0], right[0]) + (one(left[0], right[1]) + one(left[1], right[0]))


def read_pair(refs, where=Ellipsis):
    return refs[0][where], refs[1][where]


def write_sums(value, first, second):
    for row in range(4):
        lanes = slice(row * LANES, (row + 1) * LANES)
        value[row : row + 1, :] = first[:, lanes]
        value[4 + row : 5 + row, :] = second[:, lanes]


def read_sums(total):
    return tuple(
        jnp.concatenate([total[4 * k + row : 4 * k + row + 1, :] for row in range(4)], axis=1) for k in range(2)
    )


def column_sum(value):
    return jnp.sum(value, axis=0, keepdims=True)


def norm_terms(total, count):
    first, second = read_sums(total)
    mean = first / count
    return mean, lax.rsqrt(second / count - mean * mean + EPSILON)


def finish(job):
    for _ in job:
        pass


def rem(value, unit):
    return value % unit if isinstance(value, int) else lax.rem(value, unit)


def middle_kernel(
    net,
    conv_in,
    conv_sums,
    x_in,
    gy_in,
    mask_in,
    params,
    total_one,
    point_in,
    wall_in,
    delta_out,
    back_out,
    total_four,
    total_five,
    dconv_out,
    point_out,
    part,
    wall,
    x,
    gy,
    mask,
    point_two,
    delta,
    back,
    dconv,
    point_grad,
    load_sem,
    sums_own,
    sums_slots,
    own_sem,
    mixed,
    xhat,
    slope_two,
    act_pair,
    u_pair,
    ut_pair,
    g_pair,
    gt_pair,
    point_pair,
    up_pair,
    down_pair,
    hid_pair,
    dpre_pair,
    w_up,
    w_down,
    made,
    acc,
    got_pair,
    got_layer,
    got_line,
):
    pixels, channels = x.shape
    tiles = pixels // TILE
    hidden = w_up.shape[2]
    per_shard = wall.shape[2] // hidden
    chunks = net.rows * per_shard
    core = net.bit(0)
    gain_two, bias_two, gain_three, bias_three = (params[row : row + 1, :] for row in range(2, 6))
    count = read_count(total_one)
    loads = Loads(load_sem)
    came_point = loads.start(point_in, point_two)
    came_gy = loads.start(gy_in, gy)
    came = [loads.start(src, dst) for src, dst in ((conv_in, xhat), (x_in, x), (mask_in, mask))]

    def each_tile(body):
        def one(index, carry):
            return body(pl.ds(aligned(index * TILE, TILE), TILE), carry)

        zero = jnp.zeros((1, channels), F32)
        return lax.fori_loop(0, tiles, one, (zero, zero))

    def valid(rows):
        return jnp.concatenate([mask[rows, :]] * (channels // LANES), axis=1)

    def total_job(which, out):
        return all_sum_job(net, sums_own.at[which], out, *(slots.at[which] for slots in sums_slots))

    def shard_of(chunk):
        return lax.rem(net.z + chunk // per_shard, net.rows)

    def load(chunk):
        slot, shard, part = rem(chunk, 2), shard_of(chunk), rem(chunk, per_shard)
        span = pl.ds(aligned(part * hidden, hidden), hidden)
        return (
            pltpu.make_async_copy(wall.at[shard, 0, :, span], w_up.at[slot], own_sem.at[0, slot]),
            pltpu.make_async_copy(wall.at[shard, 1, span, :], w_down.at[slot], own_sem.at[1, slot]),
        )

    sums_own[0] = conv_sums[...]
    net.ready()
    job = total_job(0, sums_slots[1].at[0])
    next(job)

    def weights_job():
        yield from weights_layer_job(net, wall, range(2, net.rows))
        yield from weights_pair_job(net, wall)

    weights = weights_job()
    next(weights)
    for one in load(0):
        one.start()
    came_point.wait()
    store_split(point_pair, Ellipsis, point_two[...])
    came_gy.wait()
    store_split(g_pair, Ellipsis, gy[...])
    next(job)
    store_split(gt_pair, Ellipsis, gy[...].T)
    finish(job)
    for one in came:
        one.wait()
    mean, inv_two = norm_terms(sums_slots[1].at[0], count)

    def second_norm(rows, carry):
        m = valid(rows)
        hat = (xhat[rows, :] - mean) * inv_two
        act, slope = gelu_parts((hat * gain_two + bias_two) * m)
        xhat[rows, :] = hat
        slope_two[rows, :] = slope * m
        store_split(act_pair, rows, act)
        field = x[rows, :] + dot_split(read_pair(act_pair, rows), read_pair(point_pair))
        mixed[rows, :] = field
        return carry[0] + column_sum(field), carry[1] + column_sum(field * field)

    write_sums(sums_own.at[1], *each_tile(second_norm))
    job = total_job(1, sums_slots[1].at[1])
    next(job)
    next(weights)
    next(job)
    finish(job)
    mean_three, inv_three = norm_terms(sums_slots[1].at[1], count)

    def third_norm(rows, carry):
        hat = (mixed[rows, :] - mean_three) * inv_three
        store_split(u_pair, rows, (hat * gain_three + bias_three) * valid(rows))
        delta[rows, :] = mixed[rows, :] - x[rows, :]
        back[rows, :] = jnp.zeros((TILE, channels), F32)
        return carry

    each_tile(third_norm)
    for side in range(2):
        ut_pair[side][...] = u_pair[side][...].T

    mine = pl.ds(aligned(core * LANES, LANES), LANES)
    other = pl.ds(aligned((1 - core) * LANES, LANES), LANES)
    halvings = [halving(net, order, channels) for order in (net.bits, net.bits[::-1])]
    stages = len(net.bits)
    pair_base = net.reserve(chunks)
    layer_base = net.reserve(2 * stages * chunks)
    line_base = net.reserve(2 * chunks)

    def pair_move(chunk):
        slot = rem(chunk, 2)
        return (
            net.copy_at(pair_base + chunk, made.at[slot, :, :, other], got_pair.at[chunk], net.across(0)),
            pltpu.make_async_copy(made.at[slot, :, :, mine], acc.at[chunk], own_sem.at[2, slot]),
        )

    def layer_move(stage, chunk):
        moves = []
        for side, (steps, _, _) in enumerate(halvings):
            bit, base, size = steps[stage]
            size //= 2
            give, keep = base + (1 - net.bit(bit)) * size, base + net.bit(bit) * size
            place = pl.ds(channels - 2 * size, size)
            moves.append(
                (
                    net.copy_at(
                        layer_base + (2 * stage + side) * chunks + chunk,
                        acc.at[chunk, side, pl.ds(aligned(give, 8), size), :],
                        got_layer.at[chunk, side, place, :],
                        net.across(bit),
                    ),
                    keep,
                    size,
                    side,
                )
            )
        return moves

    def line_move(chunk, remote):
        moves = []
        shard, part = shard_of(chunk), rem(chunk, per_shard)
        for side, (_, base, size) in enumerate(halvings):
            piece = acc.at[chunk, side, pl.ds(aligned(base, 8), size), :]
            place = got_line.at[net.z, part, side]
            if remote:
                moves.append(net.copy_at(line_base + 2 * chunk + side, piece, place, (net.dp, shard)))
            else:
                moves.append(pltpu.make_async_copy(piece, place, net.recv_sem.at[line_base + 2 * chunk + side]))
        return moves

    def when(test, body):
        if isinstance(test, bool):
            if test:
                body()
        else:
            pl.when(test)(body)

    def within(chunk):
        if isinstance(chunk, int):
            return 0 <= chunk < chunks
        return (chunk >= 0) & (chunk < chunks)

    def progress(step):
        def after_pair():
            chunk = step - 1
            sent, own = pair_move(chunk)
            own.wait()
            sent.wait()
            for side in range(2):
                add_rows(
                    lambda at: acc.at[chunk, side, pl.ds(at, 64), :],
                    lambda at: got_pair.at[chunk, side, pl.ds(at, 64), :],
                    channels,
                    64,
                )
            for one, *_ in layer_move(0, chunk):
                one.start()

        def after_layer(stage):
            chunk = step - 2 - stage
            for one, keep, size, side in layer_move(stage, chunk):
                one.wait()
                unit = min(size, 64)
                add_rows(
                    lambda at: acc.at[chunk, side, pl.ds(aligned(keep + at, 8), unit), :],
                    lambda at: got_layer.at[chunk, side, pl.ds(aligned(channels - 2 * size + at, 8), unit), :],
                    size,
                    unit,
                )
            if stage + 1 < stages:
                for one, *_ in layer_move(stage + 1, chunk):
                    one.start()
            else:

                def go(remote):
                    def start():
                        for one in line_move(chunk, remote):
                            one.start()

                    return start

                when(chunk >= per_shard, go(True))
                when(chunk < per_shard, go(False))

        when(within(step - 1), after_pair)
        for stage in range(stages):
            when(within(step - 2 - stage), functools.partial(after_layer, stage))

    def feed_forward(chunk, carry):
        progress(chunk)
        slot = rem(chunk, 2)
        for one in load(chunk):
            one.wait()

        @pl.when((chunk + 1 < chunks) & (chunk + 1 != per_shard))
        def _():
            for one in load(chunk + 1):
                one.start()

        store_split(up_pair, Ellipsis, w_up[slot])
        store_split(down_pair, Ellipsis, w_down[slot])

        def first_half(rows):
            hid, slope = gelu_parts(dot_split(read_pair(u_pair, rows), read_pair(up_pair)))
            store_split(hid_pair, rows, hid)
            store_split(
                dpre_pair, rows, dot_split(read_pair(g_pair, rows), read_pair(down_pair), NT) * slope
            )

        first_half(pl.ds(0, pixels))
        made[slot, 0] = dot_split(read_pair(ut_pair), read_pair(dpre_pair))
        made[slot, 1] = dot_split(read_pair(gt_pair), read_pair(hid_pair))
        for one in pair_move(chunk):
            one.start()

        def second_half(rows):
            delta[rows, :] += dot_split(read_pair(hid_pair, rows), read_pair(down_pair))
            back[rows, :] += dot_split(read_pair(dpre_pair, rows), read_pair(up_pair), NT)

        second_half(pl.ds(0, pixels))
        return carry

    lax.fori_loop(0, per_shard - 1, feed_forward, 0)
    for _ in range(stages - 1):
        next(weights)
    lax.fori_loop(per_shard - 1, per_shard, feed_forward, 0)
    finish(weights)
    for one in load(per_shard):
        one.start()
    lax.fori_loop(per_shard, chunks, feed_forward, 0)

    loads.leave(delta, delta_out)

    def third_sums(rows, carry):
        dy = back[rows, :] * valid(rows)
        back[rows, :] = dy
        hat = (mixed[rows, :] - mean_three) * inv_three
        return carry[0] + column_sum(dy), carry[1] + column_sum(dy * hat)

    write_sums(sums_own.at[2], *each_tile(third_sums))
    job = total_job(2, total_four)
    next(job)
    progress(chunks)
    next(job)
    progress(chunks + 1)
    finish(job)
    for step in range(chunks + 2, chunks + 1 + stages):
        progress(step)
    grad_bias, grad_gain = read_sums(total_four)

    def third_back(rows, carry):
        m = valid(rows)
        hat = (mixed[rows, :] - mean_three) * inv_three
        field = m * gain_three * inv_three * (back[rows, :] - grad_bias / count - hat * (grad_gain / count))
        back[rows, :] = field
        dmixed = gy[rows, :] + field
        store_split(g_pair, rows, dmixed)
        du = dot_split(read_pair(g_pair, rows), read_pair(point_pair), NT) * slope_two[rows, :]
        mixed[rows, :] = du
        return carry[0] + column_sum(du), carry[1] + column_sum(du * xhat[rows, :])

    write_sums(sums_own.at[3], *each_tile(third_back))
    loads.leave(back, back_out)
    job = total_job(3, total_five)
    next(job)
    for side in range(2):
        ut_pair[side][...] = act_pair[side][...].T
    next(job)
    point_grad[...] = dot_split(read_pair(ut_pair), read_pair(g_pair))
    loads.leave(point_grad, point_out)
    finish(job)
    grad_bias_two, grad_gain_two = read_sums(total_five)

    def second_back(row, carry):
        rows = pl.ds(aligned(row * SLOTS, 8), SLOTS)
        field = mixed[rows, :] - grad_bias_two / count - xhat[rows, :] * (grad_gain_two / count)
        dconv[row] = valid(rows) * gain_two * inv_two * field
        return carry

    lax.fori_loop(0, pixels // SLOTS, second_back, 0)
    loads.leave(dconv, dconv_out)
    for chunk in range(chunks):
        for one in line_move(chunk, chunk >= per_shard):
            one.wait()
    for which in range(2):
        for block in range(per_shard):
            total = got_line[0, block, which]
            for index in range(1, net.rows):
                total = total + got_line[index, block, which]
            part[which, block] = total
    loads.finish()


def middle(mesh, conv, conv_sums, x, gy, mask, params, total_one, point_two, wall):
    dp, rows = mesh
    pixels, channels = conv.shape
    hidden = 2 * LANES
    chunks = rows * (wall.shape[2] // hidden)
    lines = pixels // SLOTS

    def pair(*dims):
        return [pltpu.VMEM(dims, BF16)] * 2

    piece = channels * 2 // dp
    field = pltpu.VMEM((pixels, channels), F32)
    square = pltpu.VMEM((channels, channels), F32)
    scratch = [
        field,
        field,
        pltpu.VMEM(mask.shape, F32),
        square,
        field,
        field,
        pltpu.VMEM((lines, SLOTS, channels), F32),
        square,
        pltpu.SemaphoreType.DMA((16,)),
        pltpu.VMEM((4, 8, LANES), F32),
        [pltpu.VMEM((4, rows, 8, LANES), F32), pltpu.VMEM((4, 8, LANES), F32), pltpu.VMEM((4, dp, 8, LANES), F32)],
        pltpu.SemaphoreType.DMA((3, 2)),
        pltpu.VMEM((pixels, channels), F32),
        pltpu.VMEM((pixels, channels), F32),
        pltpu.VMEM((pixels, channels), F32),
        pair(pixels, channels),
        pair(pixels, channels),
        pair(channels, pixels),
        pair(pixels, channels),
        pair(channels, pixels),
        pair(channels, channels),
        pair(channels, hidden),
        pair(hidden, channels),
        pair(pixels, hidden),
        pair(pixels, hidden),
        pltpu.VMEM((2, channels, hidden), F32),
        pltpu.VMEM((2, hidden, channels), F32),
        pltpu.VMEM((2, 2, channels, hidden), F32),
        pltpu.VMEM((chunks, 2, channels, LANES), F32),
        pltpu.VMEM((chunks, 2, channels, LANES), F32),
        pltpu.VMEM((chunks, 2, channels, LANES), F32),
        pltpu.VMEM((rows, wall.shape[2] // hidden, 2, piece, LANES), F32),
    ]
    return exchange(
        "middle",
        2,
        mesh,
        middle_kernel,
        (conv, conv_sums, x, gy, mask, params, total_one, point_two, wall),
        [HBM, VMEM] + [HBM] * 3 + [VMEM] * 2 + [HBM] * 2,
        [shape(pixels, channels)] * 2
        + [shape(8, LANES)] * 2
        + [shape(lines, SLOTS, channels), shape(channels, channels)]
        + [shape(2, wall.shape[2] // hidden, piece, LANES), shape(*wall.shape)],
        [HBM] * 2 + [VMEM] * 2 + [HBM] * 2 + [VMEM, HBM],
        scratch,
        56,
        {8: 7},
        late=True,
    )


ZERO_ROW = 42
WINDOW_PAD = 48
LEFT_TAPS, RIGHT_TAPS = 24, 14
SIDES = ((0, LEFT_F, LEFT_TAPS), (2 * LEFT_F, RIGHT_F, RIGHT_TAPS))


def transform(window, to_freq, out, group):
    rows, _, width = window.shape
    for first in range(0, rows, group):
        part = window[first : first + group].reshape(group * SLOTS, width)
        out[first : first + group] = product_split(to_freq, part).reshape(group, FREQ, width)


def sum_table(table, rows, x_ref, k_ref, y_ref, flipped):
    width = x_ref.shape[-1]
    for side, (start, size, taps) in enumerate(SIDES):
        real, imag = pl.ds(start, size), pl.ds(start + size, size)

        def one_row(row, carry):
            yr, yi = jnp.zeros((size, width), F32), jnp.zeros((size, width), F32)
            for tap in range(taps):
                w = table[side * rows + row, tap]
                index = jnp.clip(row + SPAN - 1 - w if flipped else w - row, 0, SPAN)
                xr, xi = x_ref[w, real, :], x_ref[w, imag, :]
                kr, ki = k_ref[index, real, :], k_ref[index, imag, :]
                if flipped:
                    yr, yi = yr + (kr * xr - ki * xi), yi + (kr * xi + ki * xr)
                else:
                    yr, yi = yr + (kr * xr + ki * xi), yi + (kr * xi - ki * xr)
            y_ref[row, real, :] = yr
            y_ref[row, imag, :] = yi
            return carry

        lax.fori_loop(0, rows, one_row, 0)


TAP_GROUP = 9


def sum_taps(table, rows, d_ref, x_ref, g_ref):
    tile = (8, x_ref.shape[-1])
    for side, (start, size, _) in enumerate(SIDES):
        for first in range(start, start + size, 8):
            real, imag = pl.ds(first, 8), pl.ds(first + size, 8)

            def some_taps(group, carry):
                sums = [(jnp.zeros(tile, F32), jnp.zeros(tile, F32)) for _ in range(TAP_GROUP)]
                for row in range(rows):
                    dr, di = d_ref[REACH + row, real, :], d_ref[REACH + row, imag, :]
                    for k in range(TAP_GROUP):
                        w = table[side * rows + row, group * TAP_GROUP + k]
                        xr, xi = x_ref[w, real, :], x_ref[w, imag, :]
                        gr, gi = sums[k]
                        sums[k] = gr + (dr * xr + di * xi), gi + (dr * xi - di * xr)
                for k in range(TAP_GROUP):
                    g_ref[group * TAP_GROUP + k, real, :], g_ref[group * TAP_GROUP + k, imag, :] = sums[k]
                return carry

            lax.fori_loop(0, SPAN // TAP_GROUP, some_taps, 0)


def halo_moves(net, field, window, index):
    rows = field.shape[0]
    lanes = pl.ds(index * LANES, LANES)
    below, above = net.z < net.rows - 1, net.z > 0
    down = net.copy(
        field.at[pl.ds(rows - REACH, REACH), :, lanes], window.at[index, pl.ds(0, REACH)], net.line(1)
    )
    up = net.copy(
        field.at[pl.ds(0, REACH), :, lanes], window.at[index, pl.ds(REACH + rows, REACH)], net.line(net.rows - 1)
    )
    return [(down, below, above), (up, above, below)]


def start_halo(net, field, window, index):
    rows = field.shape[0]
    moves = halo_moves(net, field, window, index)
    for one, goes, _ in moves:
        pl.when(goes)(one.start)
    empty = jnp.zeros((REACH,) + window.shape[2:], F32)
    window[index, REACH : REACH + rows] = field[:, :, index * LANES : (index + 1) * LANES]
    window[index, 2 * REACH + rows :] = jnp.zeros((window.shape[1] - 2 * REACH - rows,) + window.shape[2:], F32)

    @pl.when(net.z == 0)
    def _():
        window[index, :REACH] = empty

    @pl.when(net.z == net.rows - 1)
    def _():
        window[index, REACH + rows : 2 * REACH + rows] = empty

    def wait():
        for one, goes, comes in moves:
            pl.when(comes)(one.wait_recv)
            pl.when(goes)(one.wait_send)

    return wait


def last_kernel(
    net,
    row_table,
    tap_table,
    dconv_in,
    xf,
    kf,
    mask_in,
    x_in,
    h_in,
    point_in,
    params,
    total_one,
    back_in,
    part_in,
    point_grad_in,
    to_freq,
    to_slots,
    to_taps,
    cells_out,
    total,
    one_out,
    two_out,
    up_out,
    down_out,
    cube_out,
    dconv,
    mask,
    xhat,
    slope,
    point_one,
    back_three,
    part,
    point_grad,
    load_sem,
    sums_own,
    sums_slots,
    own_sem,
    window,
    df,
    x_block,
    k_block,
    gf,
    yf,
    taps,
    taps_flat,
    cube,
    ut_pair,
    point_pair,
    dh_pair,
    du,
    one_grad,
    grad_one,
    grad_two,
    grad_up,
    down_t,
    two_scratch,
    one_scratch,
    taps_scratch,
):
    rows, _, channels = dconv.shape
    pixels = rows * SLOTS
    blocks = channels // LANES
    gain, bias = params[0:1, :], params[1:2, :]
    count = read_count(total_one)
    mean, inv = norm_terms(total_one, count)
    loads = Loads(load_sem)
    came_dconv = loads.start(dconv_in, dconv)
    came_grad = loads.start(point_grad_in, point_grad)
    came_part = loads.start(part_in, part)
    came_x = loads.start(x_in, xhat)
    came_h = loads.start(h_in, slope)
    came_mask = loads.start(mask_in, mask)
    came_point = loads.start(point_in, point_one)

    def load_x(index):
        return pltpu.make_async_copy(xf.at[index], x_block[index % 2], own_sem.at[index % 2])

    def load_k(index):
        return pltpu.make_async_copy(kf.at[index], k_block[index % 2], own_sem.at[2 + index % 2])

    load_k(0).start()
    load_x(0).start()
    came_back = loads.start(back_in, back_three)
    came_dconv.wait()
    net.ready()
    waits = [start_halo(net, dconv, window, index) for index in range(blocks)]
    came_grad.wait()
    came_part.wait()

    def keep_weights():
        point_one[...] = down_t[...].T
        loads.leave(point_one, down_out)
        loads.leave(grad_up, up_out)

    def keep_taps(half):
        lanes = pl.ds(half * 2 * LANES, 2 * LANES)
        for row in range(SPAN):
            cube[row, :, lanes] = taps_flat[half][row * SPAN : (row + 1) * SPAN, :]
        loads.leave(cube.at[:, :, lanes], cube_out.at[:, :, lanes])

    def then(job, after):
        yield from job
        after()

    background = [
        then(reduce_all_job(net, point_grad, *two_scratch, grad_two), lambda: loads.leave(grad_two, two_out)),
        then(gather_pieces_job(net, part, (grad_up, down_t)), keep_weights),
    ]

    def progress():
        background[:] = [job for job in background if next(job, StopIteration) is not StopIteration]

    progress()
    came_x.wait()
    came_h.wait()
    came_mask.wait()
    came_point.wait()

    def valid(where):
        return jnp.concatenate([mask[where, :]] * blocks, axis=1)

    def prepare(index, carry):
        where = pl.ds(aligned(index * LANES, LANES), LANES)
        hat = (xhat[where, :] - mean) * inv
        xhat[where, :] = hat
        m = valid(where)
        for side, half in enumerate(split_two(((hat * gain + bias) * m).T)):
            ut_pair[side][:, where] = half
        slope[where, :] = gelu_parts(slope[where, :])[1] * m
        return carry

    lax.fori_loop(0, pixels // LANES, prepare, 0)
    store_split(point_pair, Ellipsis, point_one[...])
    taps[:, SPAN * SPAN :, :] = jnp.zeros((taps.shape[0], taps.shape[1] - SPAN * SPAN, taps.shape[2]), F32)

    def block_back(index):
        load_k(index).wait()
        if index + 1 < blocks:
            load_k(index + 1).start()
        lanes = slice(index * LANES, (index + 1) * LANES)
        sum_table(row_table, rows, df.at[index], k_block[index % 2], yf, True)
        group = to_slots.shape[0] // SLOTS
        for first in range(0, rows, group):
            where = slice(first * SLOTS, (first + group) * SLOTS)
            dact = product_split(to_slots, yf[first : first + group].reshape(group * FREQ, LANES))
            dh_pair[0][where, lanes], dh_pair[1][where, lanes] = split_two(dact * slope[where, lanes])

    def block_taps(index):
        load_x(index).wait()
        if index + 1 < blocks:
            load_x(index + 1).start()
        waits[index]()
        transform(window.at[index], to_freq, df.at[index], to_freq.shape[0] // FREQ)
        sum_taps(tap_table, rows, df.at[index], x_block[index % 2], gf)
        group = to_taps.shape[0] // SPAN_PAD
        half, lanes = index // 2, slice(index % 2 * LANES, (index % 2 + 1) * LANES)
        for first in range(0, SPAN, group):
            out = product_split(to_taps, gf[first : first + group].reshape(group * FREQ, LANES))
            out = out.reshape(group, SPAN_PAD, LANES)
            for row in range(first, first + group):
                taps[half, row * SPAN : (row + 1) * SPAN, lanes] = out[row - first, :SPAN]
        if index % 2:
            job = reduce_all_job(net, taps.at[half], *taps_scratch[half], taps_flat[half])
            background.append(then(job, functools.partial(keep_taps, half)))

    def point_part(part):
        width = channels // len(one_grad)
        lanes = slice(part * width, (part + 1) * width)
        one_grad[part][...] = dot_split(read_pair(ut_pair), (dh_pair[0][:, lanes], dh_pair[1][:, lanes]))
        job = reduce_all_job(net, one_grad[part], *one_scratch[part], grad_one[part])
        background.append(then(job, lambda: loads.leave(grad_one[part], one_out.at[:, pl.ds(part * width, width)])))

    early = blocks // 2
    for index in range(blocks):
        block_taps(index)
        if 1 <= index <= early:
            block_back(index - 1)
        if index == early and len(one_grad) == 2:
            point_part(0)
        progress()
    for index in range(early, blocks):
        block_back(index)
        progress()
    point_part(len(one_grad) - 1)
    progress()

    def last_sums(index, carry):
        where = pl.ds(aligned(index * TILE, TILE), TILE)
        dy = dot_split(read_pair(dh_pair, where), read_pair(point_pair), NT) * valid(where)
        du[where, :] = dy
        return carry[0] + column_sum(dy), carry[1] + column_sum(dy * xhat[where, :])

    zero = jnp.zeros((1, channels), F32)
    write_sums(sums_own, *lax.fori_loop(0, pixels // TILE, last_sums, (zero, zero)))
    sums = all_sum_job(net, sums_own, total, *sums_slots)
    next(sums)
    next(sums)
    progress()
    finish(sums)
    grad_bias, grad_gain = read_sums(total)
    came_back.wait()

    def last_back(index, carry):
        where = pl.ds(aligned(index * TILE, TILE), TILE)
        field = du[where, :] - grad_bias / count - xhat[where, :] * (grad_gain / count)
        back_three[where, :] += valid(where) * gain * inv * field
        return carry

    lax.fori_loop(0, pixels // TILE, last_back, 0)
    loads.leave(back_three, cells_out)
    while background:
        progress()
    loads.finish()


def gather_pieces_job(net, part, outs):
    core = net.bit(0)
    _, per_shard, size, _ = part.shape
    rows = outs[0].shape[0]
    halvings = [halving(net, order, rows) for order in (net.bits, net.bits[::-1])]

    def lanes(block):
        return pl.ds(aligned((2 * block + core) * LANES, LANES), LANES)

    own = []
    for which, out in enumerate(outs):
        base = halvings[which][1]
        for block in range(per_shard):
            own.append(net.own(part.at[which, block], out.at[pl.ds(aligned(base, 8), size), lanes(block)]))
            own[-1].start()
    for one in own:
        one.wait()
    for back_step in range(1, len(net.bits) + 1):
        moves = []
        for which, out in enumerate(outs):
            bit, base, span = halvings[which][0][-back_step]
            here = pl.ds(aligned(base + net.bit(bit) * (span // 2), 8), span // 2)
            for block in range(per_shard):
                piece = out.at[here, lanes(block)]
                moves.append(net.copy(piece, piece, net.across(bit)))
                moves[-1].start()
        yield
        for one in moves:
            one.wait()
    moves = []
    for out in outs:
        for block in range(per_shard):
            piece = out.at[:, lanes(block)]
            moves.append(net.copy(piece, piece, net.across(0)))
            moves[-1].start()
    yield
    for one in moves:
        one.wait()


def last(mesh, tables, dconv, xf, kf, mask, x, hidden, point_one, params, total_one, back_three, part, point_grad):
    dp, rows = mesh
    lines, _, channels = dconv.shape
    pixels = lines * SLOTS
    blocks = channels // LANES
    unit = 8 * dp * rows
    tap_rows = -(-SPAN * SPAN // unit) * unit
    constants = [
        jnp.asarray(split_constant(slots_to_freq(), 2)),
        jnp.asarray(split_constant(freq_to_slots(), 2)),
        jnp.asarray(split_constant(freq_to_taps(), 3)),
    ]

    def pair(*dims):
        return [pltpu.VMEM(dims, BF16)] * 2

    halves = 2 if channels // (dp * rows) % 8 == 0 else 1
    one_part = [pltpu.VMEM((channels, channels // halves), F32)] * halves
    field = pltpu.VMEM((pixels, channels), F32)
    square = pltpu.VMEM((channels, channels), F32)
    scratch = [
        pltpu.VMEM(dconv.shape, F32),
        pltpu.VMEM(mask.shape, F32),
        field,
        field,
        square,
        field,
        pltpu.VMEM(part.shape, F32),
        square,
        pltpu.SemaphoreType.DMA((16,)),
        pltpu.VMEM((8, LANES), F32),
        sum_scratch(mesh, 8),
        pltpu.SemaphoreType.DMA((4,)),
        pltpu.VMEM((blocks, WINDOW_PAD, SLOTS, LANES), F32),
        pltpu.VMEM((blocks, WINDOW_PAD, FREQ, LANES), F32),
        [pltpu.VMEM((ZERO_ROW + 1, FREQ, LANES), F32)] * 2,
        [pltpu.VMEM((TAP_ROWS, FREQ, LANES), F32)] * 2,
        pltpu.VMEM((SPAN, FREQ, LANES), F32),
        pltpu.VMEM((lines, FREQ, LANES), F32),
        pltpu.VMEM((blocks // 2, tap_rows, 2 * LANES), F32),
        [pltpu.VMEM((tap_rows, 2 * LANES), F32)] * (blocks // 2),
        pltpu.VMEM((SPAN, SPAN, channels), F32),
        pair(channels, pixels),
        pair(channels, channels),
        pair(pixels, channels),
        field,
        one_part,
        one_part,
        square,
        square,
        square,
        all_scratch(mesh, channels, channels),
        [all_scratch(mesh, channels, channels // halves)] * halves,
        [all_scratch(mesh, tap_rows, 2 * LANES)] * (blocks // 2),
    ]
    smem = pl.BlockSpec(memory_space=pltpu.SMEM)
    return exchange(
        "last",
        3,
        mesh,
        last_kernel,
        (*tables, dconv, xf, kf, mask, x, hidden, point_one, params, total_one, back_three, part, point_grad, *constants),
        [smem] * 2 + [HBM] * 7 + [VMEM] * 2 + [HBM] * 3 + [VMEM] * 3,
        [shape(pixels, channels), shape(8, LANES)] + [shape(channels, channels)] * 4 + [shape(SPAN, SPAN, channels)],
        [HBM, VMEM] + [HBM] * 5,
        scratch,
        60,
        late=True,
    )


def first_kernel(
    net,
    value,
    names,
    x_in,
    up_in,
    down_in,
    point_in,
    big_in,
    small,
    mask_in,
    params,
    to_freq,
    taps_freq,
    to_slots,
    hidden_out,
    wall,
    xf_out,
    kf_out,
    conv_out,
    conv_sums,
    total,
    row_table,
    tap_table,
    x,
    up,
    down,
    point_one,
    big,
    taps,
    mask,
    load_sem,
    sums_slots,
    got_names,
    name_rows,
    u_pair,
    point_pair,
    hidden,
    act,
    window,
    xf,
    kf,
    yf,
    conv,
):
    rows, _, channels = act.shape
    pixels = rows * SLOTS
    blocks = channels // LANES
    gain, bias = params[0:1, :], params[1:2, :]
    loads = Loads(load_sem)
    came_up = loads.start(up_in, up)
    came_down = loads.start(down_in, down)
    came_x = loads.start(x_in, x)
    came_point = loads.start(point_in, point_one)
    came_mask = loads.start(mask_in, mask)
    came_taps = loads.start(big_in, big)
    net.ready()
    sums = all_sum_job(net, value, total, *sums_slots)
    next(sums)
    below, above = net.z < net.rows - 1, net.z > 0
    name_moves = [
        (net.copy(names.at[1], got_names.at[0], net.line(1)), below, above),
        (net.copy(names.at[2], got_names.at[1], net.line(net.rows - 1)), above, below),
    ]
    for one, goes, _ in name_moves:
        pl.when(goes)(one.start)

    @pl.when(net.z == 0)
    def _():
        got_names[0] = jnp.zeros(got_names.shape[1:], jnp.int32)

    @pl.when(net.z == net.rows - 1)
    def _():
        got_names[1] = jnp.zeros(got_names.shape[1:], jnp.int32)

    came_up.wait()
    came_down.wait()

    background = [weights_line_job(net, up, down, wall)]

    def progress():
        background[:] = [job for job in background if next(job, StopIteration) is not StopIteration]

    progress()
    next(sums)
    came_point.wait()
    store_split(point_pair, Ellipsis, point_one[...])
    came_x.wait()
    came_mask.wait()
    finish(sums)
    progress()
    near = weights_layer_job(net, wall, (1,))
    next(near)
    mean, inv = norm_terms(total, read_count(total))

    def first_norm(index, carry):
        where = pl.ds(aligned(index * LANES, LANES), LANES)
        m = jnp.concatenate([mask[where, :]] * blocks, axis=1)
        store_split(u_pair, where, ((x[where, :] - mean) * inv * gain + bias) * m)
        return carry

    lax.fori_loop(0, pixels // LANES, first_norm, 0)
    waits = []
    for half in range(blocks // 2):
        lanes = slice(half * 2 * LANES, (half + 1) * 2 * LANES)
        for tile in range(pixels // TILE):
            where = slice(tile * TILE, (tile + 1) * TILE)
            pre = dot_split(
                (u_pair[0][where, :], u_pair[1][where, :]), (point_pair[0][:, lanes], point_pair[1][:, lanes])
            )
            hidden[where, lanes] = pre
            act[where.start // SLOTS : where.stop // SLOTS, :, lanes] = gelu_parts(pre)[0].reshape(
                TILE // SLOTS, SLOTS, 2 * LANES
            )
        waits += [start_halo(net, act, window, index) for index in (2 * half, 2 * half + 1)]
    loads.leave(hidden, hidden_out)
    came_taps.wait()
    taps[...] = jnp.zeros(taps.shape, F32)
    taps[:SPAN, :SPAN, :] = big[...]
    small_span = small.shape[0]
    middle_taps = slice(REACH - small_span // 2, REACH + small_span // 2 + 1)
    taps[middle_taps, middle_taps, :] = big[middle_taps, middle_taps, :] + small[...]
    group = taps_freq.shape[0] // FREQ
    for index in range(blocks):
        for first in range(0, taps.shape[0], group):
            part = taps[first : first + group, :, index * LANES : (index + 1) * LANES]
            freq = product_split(taps_freq, part.reshape(group * SPAN_PAD, LANES))
            kf[index][first : first + group] = freq.reshape(group, FREQ, LANES)
        loads.leave(kf[index], kf_out.at[index])
    for one, goes, comes in name_moves:
        pl.when(comes)(one.wait_recv)
        pl.when(goes)(one.wait_send)
    moved = [loads.start(src, name_rows.at[k]) for k, src in enumerate((names.at[0], got_names.at[0], got_names.at[1]))]
    for one in moved:
        one.wait()
    list_rows(rows, name_rows, row_table, tap_table)
    next(near, None)
    sums = [jnp.zeros((1, LANES), F32)] * 2 * blocks
    for index in range(blocks):
        lanes = slice(index * LANES, (index + 1) * LANES)
        waits[index]()
        transform(window.at[index], to_freq, xf[index], to_freq.shape[0] // FREQ)
        loads.leave(xf[index].at[pl.ds(0, ZERO_ROW + 1)], xf_out.at[index])
        sum_table(row_table, rows, xf[index], kf[index], yf, False)
        group = to_slots.shape[0] // SLOTS
        for first in range(0, rows, group):
            where = slice(first * SLOTS, (first + group) * SLOTS)
            cells = product_split(to_slots, yf[first : first + group].reshape(group * FREQ, LANES)) * mask[where, :]
            conv[where, lanes] = cells
            sums[2 * index] = sums[2 * index] + column_sum(cells)
            sums[2 * index + 1] = sums[2 * index + 1] + column_sum(cells * cells)
        if index == 0:
            progress()
    loads.leave(conv, conv_out)
    for index in range(blocks):
        conv_sums[index : index + 1, :] = sums[2 * index]
        conv_sums[4 + index : 5 + index, :] = sums[2 * index + 1]
    finish(near)
    while background:
        progress()
    loads.finish()


def list_rows(rows, names, row_table, tap_table):
    for side in range(2):

        def name(w):
            return names[0, side, w] + names[1, side, w] + names[2, side, w]

        def one_row(row, carry):
            at = row + REACH
            own = name(at)

            def count(first):
                same = jnp.int32(0)
                for k in range(REACH):
                    same = same + jnp.where(name(first + k) == own, 1, 0)
                return same

            low = at - count(row)
            high = jnp.where(own > 0, at + 1 + count(at + 1), low)
            for tap in range(LEFT_TAPS):
                row_table[side * rows + row, tap] = jnp.where(low + tap < high, low + tap, ZERO_ROW)
            for tap in range(SPAN):
                w = row + tap
                tap_table[side * rows + row, tap] = jnp.where((w >= low) & (w < high), w, ZERO_ROW)
            return carry

        lax.fori_loop(0, rows, one_row, 0)


def read_count(total):
    return jnp.concatenate([total[8 + row : 9 + row, :] for row in range(4)], axis=1)


def first(mesh, value, names, x, up, down, point_one, big, small, mask, params):
    dp, devices = mesh
    pixels, channels = x.shape
    lines = pixels // SLOTS
    blocks = channels // LANES
    constants = [
        jnp.asarray(split_constant(slots_to_freq(), 2)),
        jnp.asarray(split_constant(taps_to_freq(), 4)),
        jnp.asarray(split_constant(freq_to_slots(), 2)),
    ]

    def pair(*dims):
        return [pltpu.VMEM(dims, BF16)] * 2

    field = pltpu.VMEM((pixels, channels), F32)
    scratch = [
        field,
        pltpu.VMEM(up.shape, F32),
        pltpu.VMEM(down.shape, F32),
        pltpu.VMEM(point_one.shape, F32),
        pltpu.VMEM(big.shape, F32),
        pltpu.VMEM((TAP_ROWS, SPAN_PAD, channels), F32),
        pltpu.VMEM(mask.shape, F32),
        pltpu.SemaphoreType.DMA((24,)),
        sum_scratch(mesh, value.shape[0]),
        pltpu.VMEM((2, 8, LANES), jnp.int32),
        pltpu.SMEM((3, 8, LANES), jnp.int32),
        pair(pixels, channels),
        pair(channels, channels),
        field,
        pltpu.VMEM((lines, SLOTS, channels), F32),
        pltpu.VMEM((blocks, WINDOW_PAD, SLOTS, LANES), F32),
        [pltpu.VMEM((WINDOW_PAD, FREQ, LANES), F32)] * blocks,
        [pltpu.VMEM((TAP_ROWS, FREQ, LANES), F32)] * blocks,
        pltpu.VMEM((lines, FREQ, LANES), F32),
        field,
    ]
    smem = pl.BlockSpec(memory_space=pltpu.SMEM)
    table = jax.ShapeDtypeStruct((2 * lines, LANES), jnp.int32)
    return exchange(
        "first",
        0,
        mesh,
        first_kernel,
        (value, names, x, up, down, point_one, big, small, mask, params, *constants),
        [VMEM, VMEM] + [HBM] * 5 + [VMEM, HBM] + [VMEM] * 4,
        [
            shape(pixels, channels),
            shape(devices, 2, *up.shape),
            shape(blocks, ZERO_ROW + 1, FREQ, LANES),
            shape(blocks, TAP_ROWS, FREQ, LANES),
            shape(pixels, channels),
            shape(8, LANES),
            shape(*value.shape),
            table,
            table,
        ],
        [HBM] * 5 + [VMEM] * 2 + [smem] * 2,
        scratch,
        48,
        late=True,
    )


def begin_kernel(place, id_lanes, inputs, grads, x, gy, mask, value):
    rows = x.shape[0] // SLOTS
    columns = id_lanes.shape[0] // rows
    blocks = x.shape[1] // LANES

    def one_row(row, sums):
        sums = list(sums)
        for side, (start, width) in enumerate(((0, LEFT), (LEFT, RIGHT))):
            name, at = place[2 * side, row], place[2 * side + 1, row]
            pixel = row * columns + at
            slots = pl.ds(row * SLOTS + start, width)
            own = jnp.where(name < 0, -9, name).astype(F32)
            m = jnp.where(id_lanes[pl.ds(pixel, width), :] == own, 1.0, 0.0)
            mask[slots, :] = m
            sums[-1] = sums[-1] + column_sum(m)
            for block in range(blocks):
                lanes = slice(block * LANES, (block + 1) * LANES)
                cells = pl.ds(pixel * blocks + block, width, stride=blocks)
                v = inputs[cells, :] * m
                x[slots, lanes] = v
                gy[slots, lanes] = grads[cells, :] * m
                sums[block] = sums[block] + column_sum(v)
                sums[blocks + block] = sums[blocks + block] + column_sum(v * v)
        return tuple(sums)

    sums = lax.fori_loop(0, rows, one_row, (jnp.zeros((1, LANES), F32),) * (2 * blocks + 1))
    for row in range(2 * blocks):
        value[row : row + 1, :] = sums[row]
    for row in range(blocks):
        value[2 * blocks + row : 2 * blocks + row + 1, :] = sums[-1]
    value[3 * blocks :, :] = jnp.zeros((value.shape[0] - 3 * blocks, LANES), F32)


def begin(place, id_lanes, inputs, grads, rows, channels):
    return pl.pallas_call(
        begin_kernel,
        out_shape=[
            shape(rows * SLOTS, channels),
            shape(rows * SLOTS, channels),
            shape(rows * SLOTS, LANES),
            shape(16, LANES),
        ],
        in_specs=[pl.BlockSpec(memory_space=pltpu.SMEM)] + [VMEM] * 3,
        out_specs=[VMEM] * 4,
        compiler_params=pltpu.CompilerParams(vmem_limit_bytes=16 << 20),
        name="begin",
    )(place, id_lanes, inputs, grads)


def finish_kernel(place, inputs, grads, delta, cells, output, grad_input):
    rows = delta.shape[0] // SLOTS
    blocks = delta.shape[1] // LANES
    columns = inputs.shape[0] // rows // blocks
    output[...] = inputs[...]
    grad_input[...] = grads[...]

    def one_row(row, carry):
        for side, (start, width) in enumerate(((0, LEFT), (LEFT, RIGHT))):
            pixel = row * columns + place[2 * side + 1, row]
            slots = pl.ds(row * SLOTS + start, width)
            for block in range(blocks):
                lanes = slice(block * LANES, (block + 1) * LANES)
                where = pl.ds(pixel * blocks + block, width, stride=blocks)
                output[where, :] = output[where, :] + delta[slots, lanes]
                grad_input[where, :] = grad_input[where, :] + cells[slots, lanes]
        return carry

    lax.fori_loop(0, rows, one_row, 0)


def place_results(place, inputs, grads, delta, cells):
    return pl.pallas_call(
        finish_kernel,
        out_shape=[shape(*inputs.shape)] * 2,
        in_specs=[pl.BlockSpec(memory_space=pltpu.SMEM)] + [VMEM] * 4,
        out_specs=[VMEM] * 2,
        compiler_params=pltpu.CompilerParams(vmem_limit_bytes=16 << 20),
        name="finish",
    )(place, inputs, grads, delta, cells)


def shards(
    dp,
    devices_rows,
    inputs,
    image_ids,
    first_norm_gain,
    first_norm_bias,
    point_one,
    kernel_big,
    kernel_small,
    second_norm_gain,
    second_norm_bias,
    point_two,
    feedforward_norm_gain,
    feedforward_norm_bias,
    w_up,
    w_down,
    out_grad,
):
    rows, canvases, columns, channels = inputs.shape
    assert canvases == 1 and kernel_big.shape[0] == SPAN
    pixels = rows * SLOTS
    ids = image_ids[:, 0]
    mesh = (dp, devices_rows)

    place = jnp.arange(columns, dtype=jnp.int32)[None, :]
    is_left = (ids >= 0) & (ids < LEFT_IDS)
    is_right = ids >= LEFT_IDS

    def side(member, width):
        name = jnp.max(jnp.where(member, ids, -1), axis=1)
        first = jnp.min(jnp.where(member, place, columns), axis=1)
        return name, jnp.minimum(first, columns - width)

    left_id, left_at = side(is_left, LEFT)
    right_id, right_at = side(is_right, RIGHT)
    spot = jnp.stack([left_id, left_at, right_id, right_at])
    lines = (rows * columns * channels // LANES, LANES)
    id_lanes = jnp.broadcast_to(ids.reshape(rows * columns, 1).astype(F32), (rows * columns, LANES))
    x, gy, mask_lanes, value = begin(spot, id_lanes, inputs.reshape(lines), out_grad.reshape(lines), rows, channels)
    names = jnp.stack([left_id, right_id]) + 1

    def name_tile(first, last, lane):
        return jnp.pad(names[:, first:last], ((0, 6), (lane, LANES - lane - (last - first))))

    names = jnp.stack(
        [
            name_tile(0, rows, REACH),
            name_tile(rows - REACH, rows, 0),
            name_tile(0, REACH, REACH + rows),
        ]
    )
    small_start = REACH - kernel_small.shape[0] // 2
    vectors = [
        first_norm_gain,
        first_norm_bias,
        second_norm_gain,
        second_norm_bias,
        feedforward_norm_gain,
        feedforward_norm_bias,
    ]
    params = jnp.stack(vectors + [jnp.zeros((channels,), F32)] * 2)
    hidden, wall, xf, kf, conv, conv_sums, total_one, *tables = first(
        mesh,
        value,
        names,
        x,
        w_up,
        w_down,
        point_one,
        kernel_big,
        kernel_small,
        mask_lanes,
        params,
    )
    delta, back_three, total_four, total_five, dconv, point_grad, part, _ = middle(
        mesh, conv, conv_sums, x, gy, mask_lanes, params, total_one, point_two, wall
    )
    grad_bias_three, grad_gain_three = total_four.reshape(2, channels)
    grad_bias_two, grad_gain_two = total_five.reshape(2, channels)
    cells, total, grad_point_one, grad_point_two, grad_up, grad_down, grad_kernel = last(
        mesh,
        tables,
        dconv,
        xf,
        kf,
        mask_lanes,
        x,
        hidden,
        point_one,
        params,
        total_one,
        back_three,
        part,
        point_grad,
    )
    grad_bias_one, grad_gain_one = total.reshape(2, channels)
    output, grad_input = place_results(spot, inputs.reshape(lines), out_grad.reshape(lines), delta, cells)
    small_end = small_start + kernel_small.shape[0]
    grad_small = grad_kernel[small_start:small_end, small_start:small_end]
    return (
        output.reshape(inputs.shape),
        grad_input.reshape(inputs.shape),
        grad_gain_one,
        grad_bias_one,
        grad_point_one,
        grad_kernel,
        grad_small,
        grad_gain_two,
        grad_bias_two,
        grad_point_two,
        grad_gain_three,
        grad_bias_three,
        grad_up,
        grad_down,
    )


def solution(mesh):
    field = P("rows", "dp", None, None)
    everywhere = P()
    up, down = P(None, "rows"), P("rows", None)
    return jax.shard_map(
        functools.partial(shards, mesh.shape["dp"], mesh.shape["rows"]),
        mesh=mesh,
        in_specs=(field, P("rows", "dp", None)) + (everywhere,) * 10 + (up, down, field),
        out_specs=(field, field) + (everywhere,) * 10 + (up, down),
        check_vma=False,
    )
```

```python
import functools

import jax
import jax.numpy as jnp
import numpy as np
from jax import lax
from jax.experimental import pallas as pl
from jax.experimental.pallas import tpu as pltpu
from jax.sharding import PartitionSpec as P

EPSILON = 1e-05
HIGHEST = lax.Precision.HIGHEST
HIGH = lax.Precision.HIGH
MESH = pl.DeviceIdType.MESH
F32 = jnp.float32
BF16 = jnp.bfloat16

LEFT, RIGHT = 24, 16
SLOTS = LEFT + RIGHT
LEFT_IDS = 3
LEFT_N, RIGHT_N = 37, 27
LEFT_F, RIGHT_F = 24, 16
FREQ = 2 * LEFT_F + 2 * RIGHT_F
REACH = 13
SPAN = 2 * REACH + 1
SPAN_PAD = 32
LANES = 128


def forward_transform(length, padded, positions, columns):
    count = length // 2 + 1
    out = np.zeros((2 * padded, columns))
    angle = 2 * np.pi * np.outer(np.arange(count), positions) / length
    out[:count, : len(positions)] = np.cos(angle)
    out[padded : padded + count, : len(positions)] = -np.sin(angle)
    return out


def backward_transform(length, padded, positions, rows):
    count = length // 2 + 1
    out = np.zeros((rows, 2 * padded))
    twice = np.where(np.arange(count) == 0, 1.0, 2.0)
    angle = 2 * np.pi * np.outer(positions, np.arange(count)) / length
    out[: len(positions), :count] = np.cos(angle) * twice / length
    out[: len(positions), padded : padded + count] = -np.sin(angle) * twice / length
    return out


def slots_to_freq():
    out = np.zeros((FREQ, SLOTS))
    out[: 2 * LEFT_F, :LEFT] = forward_transform(LEFT_N, LEFT_F, np.arange(LEFT), LEFT)
    out[2 * LEFT_F :, LEFT:] = forward_transform(RIGHT_N, RIGHT_F, np.arange(RIGHT), RIGHT)
    return out


def freq_to_slots():
    out = np.zeros((SLOTS, FREQ))
    out[:LEFT, : 2 * LEFT_F] = backward_transform(LEFT_N, LEFT_F, np.arange(LEFT), LEFT)
    out[LEFT:, 2 * LEFT_F :] = backward_transform(RIGHT_N, RIGHT_F, np.arange(RIGHT), RIGHT)
    return out


def taps_to_freq():
    taps = np.arange(SPAN) - REACH
    return np.concatenate(
        [
            forward_transform(LEFT_N, LEFT_F, taps, SPAN_PAD),
            forward_transform(RIGHT_N, RIGHT_F, taps, SPAN_PAD),
        ]
    )


def freq_to_taps():
    taps = np.arange(SPAN) - REACH
    return np.concatenate(
        [
            backward_transform(LEFT_N, LEFT_F, taps, SPAN_PAD),
            backward_transform(RIGHT_N, RIGHT_F, taps, SPAN_PAD),
        ],
        axis=1,
    )


def split_constant(matrix, group):
    whole = np.kron(np.eye(group), matrix).astype(np.float32)
    high = whole.astype(jnp.bfloat16)
    low = (whole - high.astype(np.float32)).astype(jnp.bfloat16)
    return np.concatenate([high, high, low], axis=1)


def split_stack(value):
    high = value.astype(BF16)
    low = (value - high.astype(F32)).astype(BF16)
    return jnp.concatenate([high, low, high], axis=0)


def product_split(constant_ref, value):
    return jnp.dot(constant_ref[...], split_stack(value), preferred_element_type=F32)


TAP_ROWS = 28


class Net:
    def __init__(self, dp, rows, send_sem, recv_sem):
        self.count, self.rows = dp, rows
        self.send_sem, self.recv_sem, self.used = send_sem, recv_sem, 0
        self.dp = lax.axis_index("dp")
        self.z = lax.axis_index("rows")
        self.bits = list(range(1, dp.bit_length() - 1))

    def bit(self, index):
        return lax.rem(self.dp // (1 << index), 2)

    def across(self, index):
        return (self.dp + (1 << index) * (1 - 2 * self.bit(index)), self.z)

    def line(self, step):
        return (self.dp, lax.rem(self.z + step, self.rows))

    def layer(self, step):
        return (lax.rem(self.dp + step, self.count), self.z)

    def greet(self):
        barrier = pltpu.get_barrier_semaphore()

        def greet_line(step, carry):
            pl.semaphore_signal(barrier, inc=1, device_id=self.line(step), device_id_type=MESH)
            return carry

        def greet_layer(step, carry):
            pl.semaphore_signal(barrier, inc=1, device_id=self.layer(step), device_id_type=MESH)
            return carry

        lax.fori_loop(1, self.rows, greet_line, 0)
        lax.fori_loop(1, self.count, greet_layer, 0)

    def ready(self):
        pl.semaphore_wait(pltpu.get_barrier_semaphore(), self.rows + self.count - 2)

    def copy(self, src, dst, device):
        made = pltpu.make_async_remote_copy(
            src_ref=src,
            dst_ref=dst,
            send_sem=self.send_sem.at[self.used],
            recv_sem=self.recv_sem.at[self.used],
            device_id=device,
            device_id_type=MESH,
        )
        self.used += 1
        return made

    def reserve(self, number):
        self.used += number
        return self.used - number

    def copy_at(self, index, src, dst, device):
        return pltpu.make_async_remote_copy(
            src_ref=src,
            dst_ref=dst,
            send_sem=self.send_sem.at[index],
            recv_sem=self.recv_sem.at[index],
            device_id=device,
            device_id_type=MESH,
        )

    def own(self, src, dst):
        made = pltpu.make_async_copy(src, dst, self.recv_sem.at[self.used])
        self.used += 1
        return made


def all_sum_job(net, value, out, line_slots, part, layer_slots):
    own = net.own(value, line_slots.at[net.z])
    own.start()
    sent = [net.copy(value, line_slots.at[net.z], net.line(s)) for s in range(1, net.rows)]
    for one in sent:
        one.start()
    yield
    own.wait()
    for one in sent:
        one.wait()
    total = line_slots[0]
    for index in range(1, net.rows):
        total = total + line_slots[index]
    part[...] = total
    own = net.own(part, layer_slots.at[net.dp])
    own.start()
    sent = [net.copy(part, layer_slots.at[net.dp], net.layer(s)) for s in range(1, net.count)]
    for one in sent:
        one.start()
    yield
    own.wait()
    for one in sent:
        one.wait()
    total = layer_slots[0]
    for index in range(1, net.count):
        total = total + layer_slots[index]
    out[...] = total


def aligned(value, unit):
    return pl.multiple_of(value, unit)


def halving(net, order, rows):
    base, steps = 0, []
    for bit in order:
        steps.append((bit, base, rows))
        rows //= 2
        base = base + net.bit(bit) * rows
    return steps, base, rows


def add_rows(dst, src, count, step):
    def one(i, carry):
        at = aligned(i * step, step)
        to, of = dst(at), src(at)
        to[...] = to[...] + of[...]
        return carry

    lax.fori_loop(0, count // step, one, 0)


def run(*jobs):
    jobs = list(jobs)
    while jobs:
        jobs = [job for job in jobs if next(job, StopIteration) is not StopIteration]


def sides(net, rows):
    core = net.bit(0)
    return [
        (pl.ds(aligned((2 * core + side) * LANES, LANES), LANES), *halving(net, order, rows))
        for side, order in enumerate((net.bits, net.bits[::-1]))
    ]


def weights_line_job(net, up, down, wall, distances):
    own = [net.own(up, wall.at[net.z, 0]), net.own(down, wall.at[net.z, 1])] if 1 in distances else []
    last = net.rows - 1
    for step in distances:
        moves = []
        for lanes, _, base, rows in sides(net, wall.shape[2]):
            mine = pl.ds(aligned(base, 8), rows)
            for way in (1, -1):
                shard = net.z - way * (step - 1)
                going = (net.z >= step - 1) & (net.z < last) if way > 0 else (net.z <= last - (step - 1)) & (net.z > 0)
                coming = net.z >= step if way > 0 else net.z <= last - step
                shard = lax.rem(shard + net.rows, net.rows)
                for which in range(2):
                    piece = wall.at[shard, which, mine, lanes]
                    source = (up, down)[which].at[mine, lanes] if step == 1 else piece
                    one = net.copy(source, piece, net.line(way % net.rows))
                    pl.when(going)(one.start)
                    moves.append((one, going, coming))
        if step == 1:
            for one in own:
                one.start()
        yield
        for one, going, coming in moves:
            pl.when(coming)(one.wait_recv)
            pl.when(going)(one.wait_send)
    for one in own:
        one.wait()


def weights_layer_job(net, wall, distances):
    parts = sides(net, wall.shape[2])
    shards = [net.z + way * distance for distance in distances for way in (1, -1)]
    shards = [(lax.rem(shard + net.rows, net.rows), (shard >= 0) & (shard < net.rows)) for shard in shards]
    for back in range(1, len(net.bits) + 1):
        moves = []
        for lanes, steps, _, _ in parts:
            bit, base, rows = steps[-back]
            mine = pl.ds(aligned(base + net.bit(bit) * (rows // 2), 8), rows // 2)
            for shard, there in shards:
                piece = wall.at[shard, :, mine, lanes]
                moves.append((net.copy(piece, piece, net.across(bit)), there))
        for one, there in moves:
            pl.when(there)(one.start)
        yield
        for one, there in moves:
            pl.when(there)(one.wait)


def weights_pair_job(net, wall):
    half = wall.shape[3] // 2
    lanes = pl.ds(aligned(net.bit(0) * half, LANES), half)
    moves = []
    for step in range(1, net.rows):
        piece = wall.at[lax.rem(net.z + step, net.rows), :, :, lanes]
        moves.append(net.copy(piece, piece, net.across(0)))
    for one in moves:
        one.start()
    yield
    for one in moves:
        one.wait()


def halo_job(net, field, window, zeros):
    rows = field.shape[0]
    own = net.own(field, window.at[pl.ds(REACH, rows)])
    own.start()
    has_above, has_below = net.z > 0, net.z < net.rows - 1
    down = net.copy(field.at[pl.ds(rows - REACH, REACH)], window.at[pl.ds(0, REACH)], net.line(1))
    up = net.copy(field.at[pl.ds(0, REACH)], window.at[pl.ds(REACH + rows, REACH)], net.line(net.rows - 1))
    pl.when(has_below)(down.start)
    pl.when(has_above)(up.start)
    zeros[...] = jnp.zeros(zeros.shape, F32)
    top = net.own(zeros, window.at[pl.ds(0, REACH)])
    bottom = net.own(zeros, window.at[pl.ds(REACH + rows, REACH)])
    pl.when(jnp.logical_not(has_above))(top.start)
    pl.when(jnp.logical_not(has_below))(bottom.start)
    yield
    own.wait()
    pl.when(jnp.logical_not(has_above))(top.wait)
    pl.when(jnp.logical_not(has_below))(bottom.wait)
    pl.when(has_above)(down.wait_recv)
    pl.when(has_below)(down.wait_send)
    pl.when(has_below)(up.wait_recv)
    pl.when(has_above)(up.wait_send)


def shares(net, rows, width):
    core, out = net.bit(0), []
    by_rows = width == 2 * LANES
    for side, order in enumerate((net.bits, net.bits[::-1])):
        start = side * (rows // 2) if by_rows else 0
        steps, base, size = halving(net, order, rows // 2 if by_rows else rows)
        steps = [(bit, start + first, count) for bit, first, count in steps]
        block = 0 if by_rows else side
        outer = pl.ds(aligned((core if by_rows else 2 * core + side) * LANES, LANES), LANES)
        out.append((pl.ds(block * LANES, LANES), outer, steps, start + base, size))
    return out


def reduce_all_job(net, source, acc, got_pair, got, got_line, out):
    rows, width = source.shape
    half = width // 2
    core = net.bit(0)
    own = net.own(source.at[:, pl.ds(aligned(core * half, LANES), half)], acc)
    sent = net.copy(source.at[:, pl.ds(aligned((1 - core) * half, LANES), half)], got_pair, net.across(0))
    own.start()
    sent.start()
    yield
    own.wait()
    sent.wait()
    add_rows(lambda at: acc.at[pl.ds(at, 64)], lambda at: got_pair.at[pl.ds(at, 64)], rows, 64)
    parts = shares(net, rows, width)
    for index in range(len(net.bits)):
        moves = []
        for side, (inner, _, steps, _, _) in enumerate(parts):
            bit, base, size = steps[index]
            size //= 2
            give = base + (1 - net.bit(bit)) * size
            keep = base + net.bit(bit) * size
            place = got.at[side, pl.ds(rows - 2 * size, size)]
            one = net.copy(acc.at[pl.ds(aligned(give, 8), size), inner], place, net.across(bit))
            one.start()
            moves.append((one, keep, size, inner, side))
        yield
        for one, keep, size, inner, side in moves:
            one.wait()
            unit = 64 if size % 64 == 0 else 8
            add_rows(
                lambda at: acc.at[pl.ds(aligned(keep + at, 8), unit), inner],
                lambda at: got.at[side, pl.ds(aligned(rows - 2 * size + at, 8), unit)],
                size,
                unit,
            )
    moves, own = [], []
    for side, (inner, _, _, base, size) in enumerate(parts):
        size //= net.rows
        own.append(net.own(acc.at[pl.ds(aligned(base + net.z * size, 8), size), inner], got_line.at[side, net.z]))
        for step in range(1, net.rows):
            other = lax.rem(net.z + step, net.rows)
            piece = acc.at[pl.ds(aligned(base + other * size, 8), size), inner]
            moves.append(net.copy(piece, got_line.at[side, net.z], net.line(step)))
    for one in own + moves:
        one.start()
    yield
    for one in own + moves:
        one.wait()
    moves = []
    for side, (_, outer, _, base, size) in enumerate(parts):
        size //= net.rows
        total = got_line[side, 0]
        for index in range(1, net.rows):
            total = total + got_line[side, index]
        piece = out.at[pl.ds(aligned(base + net.z * size, 8), size), outer]
        out[pl.ds(aligned(base + net.z * size, 8), size), outer] = total
        for step in range(1, net.rows):
            moves.append(net.copy(piece, piece, net.line(step)))
            moves[-1].start()
    yield
    for one in moves:
        one.wait()
    for back in range(1, len(net.bits) + 1):
        moves = []
        for _, outer, steps, _, _ in parts:
            bit, base, size = steps[-back]
            piece = out.at[pl.ds(aligned(base + net.bit(bit) * (size // 2), 8), size // 2), outer]
            moves.append(net.copy(piece, piece, net.across(bit)))
            moves[-1].start()
        yield
        for one in moves:
            one.wait()
    piece = out.at[:, pl.ds(aligned(core * half, LANES), half)]
    one = net.copy(piece, piece, net.across(0))
    one.start()
    yield
    one.wait()


VMEM = pl.BlockSpec(memory_space=pltpu.VMEM)
HBM = pl.BlockSpec(memory_space=pltpu.HBM)
COPIES = 448


def shape(*dims):
    return jax.ShapeDtypeStruct(dims, F32)


def exchange(name, number, mesh, body, args, in_specs, outs, out_specs, scratch, limit, aliases=None, late=False):
    dp, rows = mesh

    def kernel(*refs):
        *refs, send_sem, recv_sem = refs
        net = Net(dp, rows, send_sem, recv_sem)
        net.greet()
        if not late:
            net.ready()
        body(net, *refs)
        assert net.used <= COPIES

    return pl.pallas_call(
        kernel,
        out_shape=outs,
        in_specs=in_specs,
        out_specs=out_specs,
        scratch_shapes=scratch + [pltpu.SemaphoreType.DMA((COPIES,))] * 2,
        input_output_aliases=aliases or {},
        compiler_params=pltpu.CompilerParams(
            collective_id=number, has_side_effects=True, vmem_limit_bytes=limit << 20
        ),
        name=name,
    )(*args)


def sum_scratch(mesh, height):
    dp, rows = mesh
    return [pltpu.VMEM((rows, height, LANES), F32), pltpu.VMEM((height, LANES), F32), pltpu.VMEM((dp, height, LANES), F32)]


def all_scratch(mesh, rows, width):
    size = (rows // 2 if width == 2 * LANES else rows) * 2 // mesh[0] // mesh[1]
    return [
        pltpu.VMEM((rows, width // 2), F32),
        pltpu.VMEM((rows, width // 2), F32),
        pltpu.VMEM((2, rows, LANES), F32),
        pltpu.VMEM((2, mesh[1], size, LANES), F32),
    ]


class Loads:
    def __init__(self, sems):
        self.sems, self.used, self.leaving = sems, 0, []

    def start(self, src, dst):
        one = pltpu.make_async_copy(src, dst, self.sems.at[self.used])
        self.used += 1
        one.start()
        return one

    def leave(self, src, dst):
        self.leaving.append(self.start(src, dst))

    def finish(self):
        for one in self.leaving:
            one.wait()


def gelu_parts(x):
    scale, cubic = 0.7978845608028654, 0.044715
    square = x * x
    t = jnp.tanh(scale * (x + cubic * (x * square)))
    half = 0.5 * (1.0 + t)
    return (x * half, half + 0.5 * x * (1.0 - t * t) * (scale * (1.0 + 3.0 * cubic * square)))


NN = (((1,), (0,)), ((), ()))
NT = (((1,), (1,)), ((), ()))
TILE = 320


def split_two(value):
    high = value.astype(BF16)
    return high, (value - high.astype(F32)).astype(BF16)


def store_split(refs, where, value):
    refs[0][where], refs[1][where] = split_two(value)


def dot_split(left, right, dims=NN):
    def one(a, b):
        return lax.dot_general(a, b, dims, preferred_element_type=F32)

    return one(left[0], right[0]) + (one(left[0], right[1]) + one(left[1], right[0]))


def read_pair(refs, where=Ellipsis):
    return refs[0][where], refs[1][where]


def write_sums(value, first, second):
    for row in range(4):
        lanes = slice(row * LANES, (row + 1) * LANES)
        value[row : row + 1, :] = first[:, lanes]
        value[4 + row : 5 + row, :] = second[:, lanes]


def read_sums(total):
    return tuple(
        jnp.concatenate([total[4 * k + row : 4 * k + row + 1, :] for row in range(4)], axis=1) for k in range(2)
    )


def column_sum(value):
    return jnp.sum(value, axis=0, keepdims=True)


def norm_terms(total, count):
    first, second = read_sums(total)
    mean = first / count
    return mean, lax.rsqrt(second / count - mean * mean + EPSILON)


def finish(job):
    for _ in job:
        pass


def rem(value, unit):
    return value % unit if isinstance(value, int) else lax.rem(value, unit)


def middle_kernel(
    net,
    conv_in,
    conv_sums,
    x_in,
    gy_in,
    mask_in,
    params,
    total_one,
    point_in,
    wall_in,
    delta_out,
    back_out,
    total_four,
    total_five,
    dconv_out,
    point_out,
    part,
    wall,
    x,
    gy,
    mask,
    point_two,
    delta,
    back,
    dconv,
    point_grad,
    load_sem,
    sums_own,
    sums_slots,
    own_sem,
    mixed,
    xhat,
    slope_two,
    act_pair,
    u_pair,
    ut_pair,
    g_pair,
    gt_pair,
    point_pair,
    up_pair,
    down_pair,
    hid_pair,
    dpre_pair,
    w_up,
    w_down,
    made,
    acc,
    got_pair,
    got_layer,
    got_line,
):
    pixels, channels = x.shape
    tiles = pixels // TILE
    hidden = w_up.shape[2]
    per_shard = wall.shape[2] // hidden
    chunks = net.rows * per_shard
    core = net.bit(0)
    gain_two, bias_two, gain_three, bias_three = (params[row : row + 1, :] for row in range(2, 6))
    count = read_count(total_one)
    loads = Loads(load_sem)
    came_point = loads.start(point_in, point_two)
    came_gy = loads.start(gy_in, gy)
    came = [loads.start(src, dst) for src, dst in ((conv_in, xhat), (x_in, x), (mask_in, mask))]

    def each_tile(body):
        def one(index, carry):
            return body(pl.ds(aligned(index * TILE, TILE), TILE), carry)

        zero = jnp.zeros((1, channels), F32)
        return lax.fori_loop(0, tiles, one, (zero, zero))

    def valid(rows):
        return jnp.concatenate([mask[rows, :]] * (channels // LANES), axis=1)

    def total_job(which, out):
        return all_sum_job(net, sums_own.at[which], out, *(slots.at[which] for slots in sums_slots))

    def shard_of(chunk):
        return lax.rem(net.z + chunk // per_shard, net.rows)

    def load(chunk):
        slot, shard, part = rem(chunk, 2), shard_of(chunk), rem(chunk, per_shard)
        span = pl.ds(aligned(part * hidden, hidden), hidden)
        return (
            pltpu.make_async_copy(wall.at[shard, 0, :, span], w_up.at[slot], own_sem.at[0, slot]),
            pltpu.make_async_copy(wall.at[shard, 1, span, :], w_down.at[slot], own_sem.at[1, slot]),
        )

    sums_own[0] = conv_sums[...]
    net.ready()
    job = total_job(0, sums_slots[1].at[0])
    next(job)

    far_line = weights_line_job(net, None, None, wall, (net.rows - 1,))
    next(far_line)
    near = weights_layer_job(net, wall, range(2, net.rows - 1))
    next(near, None)
    for one in load(0):
        one.start()
    came_point.wait()
    store_split(point_pair, Ellipsis, point_two[...])
    came_gy.wait()
    store_split(g_pair, Ellipsis, gy[...])
    next(job)
    store_split(gt_pair, Ellipsis, gy[...].T)
    finish(job)
    next(near, None)
    for one in came:
        one.wait()
    mean, inv_two = norm_terms(sums_slots[1].at[0], count)

    def second_norm(rows, carry):
        m = valid(rows)
        hat = (xhat[rows, :] - mean) * inv_two
        act, slope = gelu_parts((hat * gain_two + bias_two) * m)
        xhat[rows, :] = hat
        slope_two[rows, :] = slope * m
        store_split(act_pair, rows, act)
        field = x[rows, :] + dot_split(read_pair(act_pair, rows), read_pair(point_pair))
        mixed[rows, :] = field
        return carry[0] + column_sum(field), carry[1] + column_sum(field * field)

    write_sums(sums_own.at[1], *each_tile(second_norm))
    job = total_job(1, sums_slots[1].at[1])
    next(job)
    finish(far_line)
    far = weights_layer_job(net, wall, (net.rows - 1,))
    next(far)
    next(job)
    finish(job)
    finish(near)
    next(far)
    mean_three, inv_three = norm_terms(sums_slots[1].at[1], count)

    def third_norm(rows, carry):
        hat = (mixed[rows, :] - mean_three) * inv_three
        store_split(u_pair, rows, (hat * gain_three + bias_three) * valid(rows))
        delta[rows, :] = mixed[rows, :] - x[rows, :]
        back[rows, :] = jnp.zeros((TILE, channels), F32)
        return carry

    each_tile(third_norm)
    for side in range(2):
        ut_pair[side][...] = u_pair[side][...].T

    mine = pl.ds(aligned(core * LANES, LANES), LANES)
    other = pl.ds(aligned((1 - core) * LANES, LANES), LANES)
    halvings = [halving(net, order, channels) for order in (net.bits, net.bits[::-1])]
    stages = len(net.bits)
    pair_base = net.reserve(chunks)
    layer_base = net.reserve(2 * stages * chunks)
    line_base = net.reserve(2 * chunks)

    def pair_move(chunk):
        slot = rem(chunk, 2)
        return (
            net.copy_at(pair_base + chunk, made.at[slot, :, :, other], got_pair.at[chunk], net.across(0)),
            pltpu.make_async_copy(made.at[slot, :, :, mine], acc.at[chunk], own_sem.at[2, slot]),
        )

    def layer_move(stage, chunk):
        moves = []
        for side, (steps, _, _) in enumerate(halvings):
            bit, base, size = steps[stage]
            size //= 2
            give, keep = base + (1 - net.bit(bit)) * size, base + net.bit(bit) * size
            place = pl.ds(channels - 2 * size, size)
            moves.append(
                (
                    net.copy_at(
                        layer_base + (2 * stage + side) * chunks + chunk,
                        acc.at[chunk, side, pl.ds(aligned(give, 8), size), :],
                        got_layer.at[chunk, side, place, :],
                        net.across(bit),
                    ),
                    keep,
                    size,
                    side,
                )
            )
        return moves

    def line_move(chunk, remote):
        moves = []
        shard, part = shard_of(chunk), rem(chunk, per_shard)
        for side, (_, base, size) in enumerate(halvings):
            piece = acc.at[chunk, side, pl.ds(aligned(base, 8), size), :]
            place = got_line.at[net.z, part, side]
            if remote:
                moves.append(net.copy_at(line_base + 2 * chunk + side, piece, place, (net.dp, shard)))
            else:
                moves.append(pltpu.make_async_copy(piece, place, net.recv_sem.at[line_base + 2 * chunk + side]))
        return moves

    def when(test, body):
        if isinstance(test, bool):
            if test:
                body()
        else:
            pl.when(test)(body)

    def within(chunk):
        if isinstance(chunk, int):
            return 0 <= chunk < chunks
        return (chunk >= 0) & (chunk < chunks)

    def progress(step):
        def after_pair():
            chunk = step - 1
            sent, own = pair_move(chunk)
            own.wait()
            sent.wait()
            for side in range(2):
                add_rows(
                    lambda at: acc.at[chunk, side, pl.ds(at, 64), :],
                    lambda at: got_pair.at[chunk, side, pl.ds(at, 64), :],
                    channels,
                    64,
                )
            for one, *_ in layer_move(0, chunk):
                one.start()

        def after_layer(stage):
            chunk = step - 2 - stage
            for one, keep, size, side in layer_move(stage, chunk):
                one.wait()
                unit = min(size, 64)
                add_rows(
                    lambda at: acc.at[chunk, side, pl.ds(aligned(keep + at, 8), unit), :],
                    lambda at: got_layer.at[chunk, side, pl.ds(aligned(channels - 2 * size + at, 8), unit), :],
                    size,
                    unit,
                )
            if stage + 1 < stages:
                for one, *_ in layer_move(stage + 1, chunk):
                    one.start()
            else:

                def go(remote):
                    def start():
                        for one in line_move(chunk, remote):
                            one.start()

                    return start

                when(chunk >= per_shard, go(True))
                when(chunk < per_shard, go(False))

        when(within(step - 1), after_pair)
        for stage in range(stages):
            when(within(step - 2 - stage), functools.partial(after_layer, stage))

    def feed_forward(chunk, carry):
        progress(chunk)
        slot = rem(chunk, 2)
        for one in load(chunk):
            one.wait()

        @pl.when((chunk + 1 < chunks) & (chunk + 1 != per_shard))
        def _():
            for one in load(chunk + 1):
                one.start()

        store_split(up_pair, Ellipsis, w_up[slot])
        store_split(down_pair, Ellipsis, w_down[slot])

        def first_half(rows):
            hid, slope = gelu_parts(dot_split(read_pair(u_pair, rows), read_pair(up_pair)))
            store_split(hid_pair, rows, hid)
            store_split(
                dpre_pair, rows, dot_split(read_pair(g_pair, rows), read_pair(down_pair), NT) * slope
            )

        first_half(pl.ds(0, pixels))
        made[slot, 0] = dot_split(read_pair(ut_pair), read_pair(dpre_pair))
        made[slot, 1] = dot_split(read_pair(gt_pair), read_pair(hid_pair))
        for one in pair_move(chunk):
            one.start()

        def second_half(rows):
            delta[rows, :] += dot_split(read_pair(hid_pair, rows), read_pair(down_pair))
            back[rows, :] += dot_split(read_pair(dpre_pair, rows), read_pair(up_pair), NT)

        second_half(pl.ds(0, pixels))
        return carry

    lax.fori_loop(0, per_shard - 1, feed_forward, 0)
    finish(far)
    pairs = weights_pair_job(net, wall)
    next(pairs)
    lax.fori_loop(per_shard - 1, per_shard, feed_forward, 0)
    finish(pairs)
    for one in load(per_shard):
        one.start()
    lax.fori_loop(per_shard, chunks, feed_forward, 0)

    loads.leave(delta, delta_out)

    def third_sums(rows, carry):
        dy = back[rows, :] * valid(rows)
        back[rows, :] = dy
        hat = (mixed[rows, :] - mean_three) * inv_three
        return carry[0] + column_sum(dy), carry[1] + column_sum(dy * hat)

    write_sums(sums_own.at[2], *each_tile(third_sums))
    job = total_job(2, total_four)
    next(job)
    progress(chunks)
    next(job)
    finish(job)
    progress(chunks + 1)
    grad_bias, grad_gain = read_sums(total_four)

    def third_back(rows, carry):
        m = valid(rows)
        hat = (mixed[rows, :] - mean_three) * inv_three
        field = m * gain_three * inv_three * (back[rows, :] - grad_bias / count - hat * (grad_gain / count))
        back[rows, :] = field
        dmixed = gy[rows, :] + field
        store_split(g_pair, rows, dmixed)
        du = dot_split(read_pair(g_pair, rows), read_pair(point_pair), NT) * slope_two[rows, :]
        mixed[rows, :] = du
        return carry[0] + column_sum(du), carry[1] + column_sum(du * xhat[rows, :])

    write_sums(sums_own.at[3], *each_tile(third_back))
    loads.leave(back, back_out)
    job = total_job(3, total_five)
    next(job)
    for step in range(chunks + 2, chunks + 1 + stages):
        progress(step)
    for side in range(2):
        ut_pair[side][...] = act_pair[side][...].T
    next(job)
    point_grad[...] = dot_split(read_pair(ut_pair), read_pair(g_pair))
    loads.leave(point_grad, point_out)
    finish(job)
    grad_bias_two, grad_gain_two = read_sums(total_five)

    def second_back(row, carry):
        rows = pl.ds(aligned(row * SLOTS, 8), SLOTS)
        field = mixed[rows, :] - grad_bias_two / count - xhat[rows, :] * (grad_gain_two / count)
        dconv[row] = valid(rows) * gain_two * inv_two * field
        return carry

    lax.fori_loop(0, pixels // SLOTS, second_back, 0)
    loads.leave(dconv, dconv_out)
    for chunk in range(chunks):
        for one in line_move(chunk, chunk >= per_shard):
            one.wait()
    for which in range(2):
        for block in range(per_shard):
            total = got_line[0, block, which]
            for index in range(1, net.rows):
                total = total + got_line[index, block, which]
            part[which, block] = total
    loads.finish()


def middle(mesh, conv, conv_sums, x, gy, mask, params, total_one, point_two, wall):
    dp, rows = mesh
    pixels, channels = conv.shape
    hidden = 2 * LANES
    chunks = rows * (wall.shape[2] // hidden)
    lines = pixels // SLOTS

    def pair(*dims):
        return [pltpu.VMEM(dims, BF16)] * 2

    piece = channels * 2 // dp
    field = pltpu.VMEM((pixels, channels), F32)
    square = pltpu.VMEM((channels, channels), F32)
    scratch = [
        field,
        field,
        pltpu.VMEM(mask.shape, F32),
        square,
        field,
        field,
        pltpu.VMEM((lines, SLOTS, channels), F32),
        square,
        pltpu.SemaphoreType.DMA((16,)),
        pltpu.VMEM((4, 8, LANES), F32),
        [pltpu.VMEM((4, rows, 8, LANES), F32), pltpu.VMEM((4, 8, LANES), F32), pltpu.VMEM((4, dp, 8, LANES), F32)],
        pltpu.SemaphoreType.DMA((3, 2)),
        pltpu.VMEM((pixels, channels), F32),
        pltpu.VMEM((pixels, channels), F32),
        pltpu.VMEM((pixels, channels), F32),
        pair(pixels, channels),
        pair(pixels, channels),
        pair(channels, pixels),
        pair(pixels, channels),
        pair(channels, pixels),
        pair(channels, channels),
        pair(channels, hidden),
        pair(hidden, channels),
        pair(pixels, hidden),
        pair(pixels, hidden),
        pltpu.VMEM((2, channels, hidden), F32),
        pltpu.VMEM((2, hidden, channels), F32),
        pltpu.VMEM((2, 2, channels, hidden), F32),
        pltpu.VMEM((chunks, 2, channels, LANES), F32),
        pltpu.VMEM((chunks, 2, channels, LANES), F32),
        pltpu.VMEM((chunks, 2, channels, LANES), F32),
        pltpu.VMEM((rows, wall.shape[2] // hidden, 2, piece, LANES), F32),
    ]
    return exchange(
        "middle",
        2,
        mesh,
        middle_kernel,
        (conv, conv_sums, x, gy, mask, params, total_one, point_two, wall),
        [HBM, VMEM] + [HBM] * 3 + [VMEM] * 2 + [HBM] * 2,
        [shape(pixels, channels)] * 2
        + [shape(8, LANES)] * 2
        + [shape(lines, SLOTS, channels), shape(channels, channels)]
        + [shape(2, wall.shape[2] // hidden, piece, LANES), shape(*wall.shape)],
        [HBM] * 2 + [VMEM] * 2 + [HBM] * 2 + [VMEM, HBM],
        scratch,
        56,
        {8: 7},
        late=True,
    )


ZERO_ROW = 42
WINDOW_PAD = 48
LEFT_TAPS, RIGHT_TAPS = 24, 14
SIDES = ((0, LEFT_F, LEFT_TAPS), (2 * LEFT_F, RIGHT_F, RIGHT_TAPS))


def transform(window, to_freq, out, group):
    rows, _, width = window.shape
    for first in range(0, rows, group):
        part = window[first : first + group].reshape(group * SLOTS, width)
        out[first : first + group] = product_split(to_freq, part).reshape(group, FREQ, width)


def sum_table(table, rows, x_ref, k_ref, y_ref, flipped):
    width = x_ref.shape[-1]
    for side, (start, size, taps) in enumerate(SIDES):
        real, imag = pl.ds(start, size), pl.ds(start + size, size)

        def one_row(row, carry):
            yr, yi = jnp.zeros((size, width), F32), jnp.zeros((size, width), F32)
            for tap in range(taps):
                w = table[side * rows + row, tap]
                index = jnp.clip(row + SPAN - 1 - w if flipped else w - row, 0, SPAN)
                xr, xi = x_ref[w, real, :], x_ref[w, imag, :]
                kr, ki = k_ref[index, real, :], k_ref[index, imag, :]
                if flipped:
                    yr, yi = yr + (kr * xr - ki * xi), yi + (kr * xi + ki * xr)
                else:
                    yr, yi = yr + (kr * xr + ki * xi), yi + (kr * xi - ki * xr)
            y_ref[row, real, :] = yr
            y_ref[row, imag, :] = yi
            return carry

        lax.fori_loop(0, rows, one_row, 0)


TAP_GROUP = 9


def sum_taps(table, rows, d_ref, x_ref, g_ref):
    tile = (8, x_ref.shape[-1])
    for side, (start, size, _) in enumerate(SIDES):
        for first in range(start, start + size, 8):
            real, imag = pl.ds(first, 8), pl.ds(first + size, 8)

            def some_taps(group, carry):
                sums = [(jnp.zeros(tile, F32), jnp.zeros(tile, F32)) for _ in range(TAP_GROUP)]
                for row in range(rows):
                    dr, di = d_ref[REACH + row, real, :], d_ref[REACH + row, imag, :]
                    for k in range(TAP_GROUP):
                        w = table[side * SPAN + group * TAP_GROUP + k, row]
                        xr, xi = x_ref[w, real, :], x_ref[w, imag, :]
                        gr, gi = sums[k]
                        sums[k] = gr + (dr * xr + di * xi), gi + (dr * xi - di * xr)
                for k in range(TAP_GROUP):
                    g_ref[group * TAP_GROUP + k, real, :], g_ref[group * TAP_GROUP + k, imag, :] = sums[k]
                return carry

            lax.fori_loop(0, SPAN // TAP_GROUP, some_taps, 0)


def halo_moves(net, field, window, index):
    rows = field.shape[0]
    lanes = pl.ds(index * LANES, LANES)
    below, above = net.z < net.rows - 1, net.z > 0
    down = net.copy(
        field.at[pl.ds(rows - REACH, REACH), :, lanes], window.at[index, pl.ds(0, REACH)], net.line(1)
    )
    up = net.copy(
        field.at[pl.ds(0, REACH), :, lanes], window.at[index, pl.ds(REACH + rows, REACH)], net.line(net.rows - 1)
    )
    return [(down, below, above), (up, above, below)]


def start_halo(net, field, window, index):
    rows = field.shape[0]
    moves = halo_moves(net, field, window, index)
    for one, goes, _ in moves:
        pl.when(goes)(one.start)
    empty = jnp.zeros((REACH,) + window.shape[2:], F32)
    window[index, REACH : REACH + rows] = field[:, :, index * LANES : (index + 1) * LANES]
    window[index, 2 * REACH + rows :] = jnp.zeros((window.shape[1] - 2 * REACH - rows,) + window.shape[2:], F32)

    @pl.when(net.z == 0)
    def _():
        window[index, :REACH] = empty

    @pl.when(net.z == net.rows - 1)
    def _():
        window[index, REACH + rows : 2 * REACH + rows] = empty

    def wait():
        for one, goes, comes in moves:
            pl.when(comes)(one.wait_recv)
            pl.when(goes)(one.wait_send)

    return wait


def last_kernel(
    net,
    row_table,
    tap_table,
    dconv_in,
    xf,
    kf,
    mask_in,
    x_in,
    h_in,
    point_in,
    params,
    total_one,
    back_in,
    part_in,
    point_grad_in,
    to_freq,
    to_slots,
    to_taps,
    cells_out,
    total,
    one_out,
    two_out,
    up_out,
    down_out,
    cube_out,
    dconv,
    mask,
    xhat,
    slope,
    point_one,
    back_three,
    part,
    point_grad,
    load_sem,
    sums_own,
    sums_slots,
    own_sem,
    window,
    df,
    x_block,
    k_block,
    gf,
    yf,
    taps,
    taps_flat,
    cube,
    ut_pair,
    point_pair,
    dh_pair,
    du,
    one_grad,
    grad_one,
    grad_two,
    grad_up,
    down_t,
    two_scratch,
    one_scratch,
    taps_scratch,
):
    rows, _, channels = dconv.shape
    pixels = rows * SLOTS
    blocks = channels // LANES
    gain, bias = params[0:1, :], params[1:2, :]
    count = read_count(total_one)
    mean, inv = norm_terms(total_one, count)
    loads = Loads(load_sem)
    came_dconv = loads.start(dconv_in, dconv)
    came_grad = loads.start(point_grad_in, point_grad)
    came_part = loads.start(part_in, part)
    came_x = loads.start(x_in, xhat)
    came_h = loads.start(h_in, slope)
    came_mask = loads.start(mask_in, mask)
    came_point = loads.start(point_in, point_one)

    def load_x(index):
        return pltpu.make_async_copy(xf.at[index], x_block[index % 2], own_sem.at[index % 2])

    def load_k(index):
        return pltpu.make_async_copy(kf.at[index], k_block[index % 2], own_sem.at[2 + index % 2])

    load_k(0).start()
    load_x(0).start()
    came_back = loads.start(back_in, back_three)
    came_dconv.wait()
    net.ready()
    waits = [start_halo(net, dconv, window, index) for index in range(blocks)]
    came_grad.wait()
    came_part.wait()

    def keep_weights():
        point_one[...] = down_t[...].T
        loads.leave(point_one, down_out)
        loads.leave(grad_up, up_out)

    def keep_taps(half):
        lanes = pl.ds(half * 2 * LANES, 2 * LANES)
        for row in range(SPAN):
            cube[row, :, lanes] = taps_flat[half][row * SPAN : (row + 1) * SPAN, :]
        loads.leave(cube.at[:, :, lanes], cube_out.at[:, :, lanes])

    def then(job, after):
        yield from job
        after()

    background = [
        then(reduce_all_job(net, point_grad, *two_scratch, grad_two), lambda: loads.leave(grad_two, two_out)),
        then(gather_pieces_job(net, part, (grad_up, down_t)), keep_weights),
    ]

    def progress():
        background[:] = [job for job in background if next(job, StopIteration) is not StopIteration]

    progress()
    came_x.wait()
    came_h.wait()
    came_mask.wait()
    came_point.wait()

    def valid(where):
        return jnp.concatenate([mask[where, :]] * blocks, axis=1)

    def prepare(index, carry):
        where = pl.ds(aligned(index * LANES, LANES), LANES)
        hat = (xhat[where, :] - mean) * inv
        xhat[where, :] = hat
        m = valid(where)
        for side, half in enumerate(split_two(((hat * gain + bias) * m).T)):
            ut_pair[side][:, where] = half
        slope[where, :] = gelu_parts(slope[where, :])[1] * m
        return carry

    lax.fori_loop(0, pixels // LANES, prepare, 0)
    store_split(point_pair, Ellipsis, point_one[...])
    taps[:, SPAN * SPAN :, :] = jnp.zeros((taps.shape[0], taps.shape[1] - SPAN * SPAN, taps.shape[2]), F32)

    def block_back(index):
        load_k(index).wait()
        if index + 1 < blocks:
            load_k(index + 1).start()
        lanes = slice(index * LANES, (index + 1) * LANES)
        sum_table(row_table, rows, df.at[index], k_block[index % 2], yf, True)
        group = to_slots.shape[0] // SLOTS
        for first in range(0, rows, group):
            where = slice(first * SLOTS, (first + group) * SLOTS)
            dact = product_split(to_slots, yf[first : first + group].reshape(group * FREQ, LANES))
            dh_pair[0][where, lanes], dh_pair[1][where, lanes] = split_two(dact * slope[where, lanes])

    def block_taps(index):
        load_x(index).wait()
        if index + 1 < blocks:
            load_x(index + 1).start()
        waits[index]()
        transform(window.at[index], to_freq, df.at[index], to_freq.shape[0] // FREQ)
        sum_taps(tap_table, rows, df.at[index], x_block[index % 2], gf)
        group = to_taps.shape[0] // SPAN_PAD
        half, lanes = index // 2, slice(index % 2 * LANES, (index % 2 + 1) * LANES)
        for first in range(0, SPAN, group):
            out = product_split(to_taps, gf[first : first + group].reshape(group * FREQ, LANES))
            out = out.reshape(group, SPAN_PAD, LANES)
            for row in range(first, first + group):
                taps[half, row * SPAN : (row + 1) * SPAN, lanes] = out[row - first, :SPAN]
        if index % 2:
            job = reduce_all_job(net, taps.at[half], *taps_scratch[half], taps_flat[half])
            background.append(then(job, functools.partial(keep_taps, half)))

    def point_part(part):
        width = channels // len(one_grad)
        lanes = slice(part * width, (part + 1) * width)
        one_grad[part][...] = dot_split(read_pair(ut_pair), (dh_pair[0][:, lanes], dh_pair[1][:, lanes]))
        job = reduce_all_job(net, one_grad[part], *one_scratch[part], grad_one[part])
        background.append(then(job, lambda: loads.leave(grad_one[part], one_out.at[:, pl.ds(part * width, width)])))

    early = blocks // 2
    for index in range(blocks):
        block_taps(index)
        if 1 <= index <= early:
            block_back(index - 1)
        if index == early and len(one_grad) == 2:
            point_part(0)
        progress()
    for index in range(early, blocks):
        block_back(index)
        progress()
    point_part(len(one_grad) - 1)
    progress()

    def last_sums(index, carry):
        where = pl.ds(aligned(index * TILE, TILE), TILE)
        dy = dot_split(read_pair(dh_pair, where), read_pair(point_pair), NT) * valid(where)
        du[where, :] = dy
        return carry[0] + column_sum(dy), carry[1] + column_sum(dy * xhat[where, :])

    zero = jnp.zeros((1, channels), F32)
    write_sums(sums_own, *lax.fori_loop(0, pixels // TILE, last_sums, (zero, zero)))
    sums = all_sum_job(net, sums_own, total, *sums_slots)
    next(sums)
    next(sums)
    progress()
    finish(sums)
    grad_bias, grad_gain = read_sums(total)
    came_back.wait()

    def last_back(index, carry):
        where = pl.ds(aligned(index * TILE, TILE), TILE)
        field = du[where, :] - grad_bias / count - xhat[where, :] * (grad_gain / count)
        back_three[where, :] += valid(where) * gain * inv * field
        return carry

    lax.fori_loop(0, pixels // TILE, last_back, 0)
    loads.leave(back_three, cells_out)
    while background:
        progress()
    loads.finish()


def gather_pieces_job(net, part, outs):
    core = net.bit(0)
    _, per_shard, size, _ = part.shape
    rows = outs[0].shape[0]
    halvings = [halving(net, order, rows) for order in (net.bits, net.bits[::-1])]

    def lanes(block):
        return pl.ds(aligned((2 * block + core) * LANES, LANES), LANES)

    own = []
    for which, out in enumerate(outs):
        base = halvings[which][1]
        for block in range(per_shard):
            own.append(net.own(part.at[which, block], out.at[pl.ds(aligned(base, 8), size), lanes(block)]))
            own[-1].start()
    for one in own:
        one.wait()
    for back_step in range(1, len(net.bits) + 1):
        moves = []
        for which, out in enumerate(outs):
            bit, base, span = halvings[which][0][-back_step]
            here = pl.ds(aligned(base + net.bit(bit) * (span // 2), 8), span // 2)
            for block in range(per_shard):
                piece = out.at[here, lanes(block)]
                moves.append(net.copy(piece, piece, net.across(bit)))
                moves[-1].start()
        yield
        for one in moves:
            one.wait()
    moves = []
    for out in outs:
        for block in range(per_shard):
            piece = out.at[:, lanes(block)]
            moves.append(net.copy(piece, piece, net.across(0)))
            moves[-1].start()
    yield
    for one in moves:
        one.wait()


def last(mesh, tables, dconv, xf, kf, mask, x, hidden, point_one, params, total_one, back_three, part, point_grad):
    dp, rows = mesh
    lines, _, channels = dconv.shape
    pixels = lines * SLOTS
    blocks = channels // LANES
    unit = 8 * dp * rows
    tap_rows = -(-SPAN * SPAN // unit) * unit
    constants = [
        jnp.asarray(split_constant(slots_to_freq(), 2)),
        jnp.asarray(split_constant(freq_to_slots(), 2)),
        jnp.asarray(split_constant(freq_to_taps(), 3)),
    ]

    def pair(*dims):
        return [pltpu.VMEM(dims, BF16)] * 2

    halves = 2 if channels // (dp * rows) % 8 == 0 else 1
    one_part = [pltpu.VMEM((channels, channels // halves), F32)] * halves
    field = pltpu.VMEM((pixels, channels), F32)
    square = pltpu.VMEM((channels, channels), F32)
    scratch = [
        pltpu.VMEM(dconv.shape, F32),
        pltpu.VMEM(mask.shape, F32),
        field,
        field,
        square,
        field,
        pltpu.VMEM(part.shape, F32),
        square,
        pltpu.SemaphoreType.DMA((16,)),
        pltpu.VMEM((8, LANES), F32),
        sum_scratch(mesh, 8),
        pltpu.SemaphoreType.DMA((4,)),
        pltpu.VMEM((blocks, WINDOW_PAD, SLOTS, LANES), F32),
        pltpu.VMEM((blocks, WINDOW_PAD, FREQ, LANES), F32),
        [pltpu.VMEM((ZERO_ROW + 1, FREQ, LANES), F32)] * 2,
        [pltpu.VMEM((TAP_ROWS, FREQ, LANES), F32)] * 2,
        pltpu.VMEM((SPAN, FREQ, LANES), F32),
        pltpu.VMEM((lines, FREQ, LANES), F32),
        pltpu.VMEM((blocks // 2, tap_rows, 2 * LANES), F32),
        [pltpu.VMEM((tap_rows, 2 * LANES), F32)] * (blocks // 2),
        pltpu.VMEM((SPAN, SPAN, channels), F32),
        pair(channels, pixels),
        pair(channels, channels),
        pair(pixels, channels),
        field,
        one_part,
        one_part,
        square,
        square,
        square,
        all_scratch(mesh, channels, channels),
        [all_scratch(mesh, channels, channels // halves)] * halves,
        [all_scratch(mesh, tap_rows, 2 * LANES)] * (blocks // 2),
    ]
    smem = pl.BlockSpec(memory_space=pltpu.SMEM)
    return exchange(
        "last",
        3,
        mesh,
        last_kernel,
        (*tables, dconv, xf, kf, mask, x, hidden, point_one, params, total_one, back_three, part, point_grad, *constants),
        [smem] * 2 + [HBM] * 7 + [VMEM] * 2 + [HBM] * 3 + [VMEM] * 3,
        [shape(pixels, channels), shape(8, LANES)] + [shape(channels, channels)] * 4 + [shape(SPAN, SPAN, channels)],
        [HBM, VMEM] + [HBM] * 5,
        scratch,
        60,
        late=True,
    )


def first_kernel(
    net,
    value,
    names,
    x_in,
    up_in,
    down_in,
    point_in,
    big_in,
    small,
    mask_in,
    params,
    to_freq,
    taps_freq,
    to_slots,
    hidden_out,
    wall,
    xf_out,
    kf_out,
    conv_out,
    conv_sums,
    total,
    row_table,
    tap_table,
    x,
    up,
    down,
    point_one,
    big,
    taps,
    mask,
    load_sem,
    sums_slots,
    got_names,
    name_rows,
    u_pair,
    point_pair,
    hidden,
    act,
    window,
    xf,
    kf,
    yf,
    conv,
):
    rows, _, channels = act.shape
    pixels = rows * SLOTS
    blocks = channels // LANES
    gain, bias = params[0:1, :], params[1:2, :]
    loads = Loads(load_sem)
    came_up = loads.start(up_in, up)
    came_down = loads.start(down_in, down)
    came_x = loads.start(x_in, x)
    came_point = loads.start(point_in, point_one)
    came_mask = loads.start(mask_in, mask)
    came_taps = loads.start(big_in, big)
    net.ready()
    sums = all_sum_job(net, value, total, *sums_slots)
    next(sums)
    below, above = net.z < net.rows - 1, net.z > 0
    name_moves = [
        (net.copy(names.at[1], got_names.at[0], net.line(1)), below, above),
        (net.copy(names.at[2], got_names.at[1], net.line(net.rows - 1)), above, below),
    ]
    for one, goes, _ in name_moves:
        pl.when(goes)(one.start)

    @pl.when(net.z == 0)
    def _():
        got_names[0] = jnp.zeros(got_names.shape[1:], jnp.int32)

    @pl.when(net.z == net.rows - 1)
    def _():
        got_names[1] = jnp.zeros(got_names.shape[1:], jnp.int32)

    came_up.wait()
    came_down.wait()

    background = [weights_line_job(net, up, down, wall, range(1, net.rows - 1))]

    def progress():
        background[:] = [job for job in background if next(job, StopIteration) is not StopIteration]

    progress()
    next(sums)
    came_point.wait()
    store_split(point_pair, Ellipsis, point_one[...])
    came_x.wait()
    came_mask.wait()
    finish(sums)
    mean, inv = norm_terms(total, read_count(total))

    def first_norm(index, carry):
        where = pl.ds(aligned(index * LANES, LANES), LANES)
        m = jnp.concatenate([mask[where, :]] * blocks, axis=1)
        store_split(u_pair, where, ((x[where, :] - mean) * inv * gain + bias) * m)
        return carry

    lax.fori_loop(0, pixels // LANES, first_norm, 0)
    waits = []
    for half in range(blocks // 2):
        lanes = slice(half * 2 * LANES, (half + 1) * 2 * LANES)
        for tile in range(pixels // TILE):
            where = slice(tile * TILE, (tile + 1) * TILE)
            pre = dot_split(
                (u_pair[0][where, :], u_pair[1][where, :]), (point_pair[0][:, lanes], point_pair[1][:, lanes])
            )
            hidden[where, lanes] = pre
            act[where.start // SLOTS : where.stop // SLOTS, :, lanes] = gelu_parts(pre)[0].reshape(
                TILE // SLOTS, SLOTS, 2 * LANES
            )
        waits += [start_halo(net, act, window, index) for index in (2 * half, 2 * half + 1)]
    progress()
    near = weights_layer_job(net, wall, (1,))
    next(near)
    loads.leave(hidden, hidden_out)
    came_taps.wait()
    taps[...] = jnp.zeros(taps.shape, F32)
    taps[:SPAN, :SPAN, :] = big[...]
    small_span = small.shape[0]
    middle_taps = slice(REACH - small_span // 2, REACH + small_span // 2 + 1)
    taps[middle_taps, middle_taps, :] = big[middle_taps, middle_taps, :] + small[...]
    group = taps_freq.shape[0] // FREQ
    for index in range(blocks):
        for first in range(0, taps.shape[0], group):
            part = taps[first : first + group, :, index * LANES : (index + 1) * LANES]
            freq = product_split(taps_freq, part.reshape(group * SPAN_PAD, LANES))
            kf[index][first : first + group] = freq.reshape(group, FREQ, LANES)
        loads.leave(kf[index], kf_out.at[index])
    for one, goes, comes in name_moves:
        pl.when(comes)(one.wait_recv)
        pl.when(goes)(one.wait_send)
    moved = [loads.start(src, name_rows.at[k]) for k, src in enumerate((names.at[0], got_names.at[0], got_names.at[1]))]
    for one in moved:
        one.wait()
    list_rows(rows, name_rows, row_table, tap_table)
    next(near, None)
    sums = [jnp.zeros((1, LANES), F32)] * 2 * blocks
    for index in range(blocks):
        lanes = slice(index * LANES, (index + 1) * LANES)
        waits[index]()
        transform(window.at[index], to_freq, xf[index], to_freq.shape[0] // FREQ)
        loads.leave(xf[index].at[pl.ds(0, ZERO_ROW + 1)], xf_out.at[index])
        sum_table(row_table, rows, xf[index], kf[index], yf, False)
        group = to_slots.shape[0] // SLOTS
        for first in range(0, rows, group):
            where = slice(first * SLOTS, (first + group) * SLOTS)
            cells = product_split(to_slots, yf[first : first + group].reshape(group * FREQ, LANES)) * mask[where, :]
            conv[where, lanes] = cells
            sums[2 * index] = sums[2 * index] + column_sum(cells)
            sums[2 * index + 1] = sums[2 * index + 1] + column_sum(cells * cells)
    loads.leave(conv, conv_out)
    for index in range(blocks):
        conv_sums[index : index + 1, :] = sums[2 * index]
        conv_sums[4 + index : 5 + index, :] = sums[2 * index + 1]
    finish(near)
    while background:
        progress()
    loads.finish()


def list_rows(rows, names, row_table, tap_table):
    for side in range(2):

        def name(w):
            return names[0, side, w] + names[1, side, w] + names[2, side, w]

        def one_row(row, carry):
            at = row + REACH
            own = name(at)

            def count(first):
                same = jnp.int32(0)
                for k in range(REACH):
                    same = same + jnp.where(name(first + k) == own, 1, 0)
                return same

            low = at - count(row)
            high = jnp.where(own > 0, at + 1 + count(at + 1), low)
            for tap in range(LEFT_TAPS):
                row_table[side * rows + row, tap] = jnp.where(low + tap < high, low + tap, ZERO_ROW)
            for tap in range(SPAN):
                w = row + tap
                tap_table[side * SPAN + tap, row] = jnp.where((w >= low) & (w < high), w, ZERO_ROW)
            return carry

        lax.fori_loop(0, rows, one_row, 0)


def read_count(total):
    return jnp.concatenate([total[8 + row : 9 + row, :] for row in range(4)], axis=1)


def first(mesh, value, names, x, up, down, point_one, big, small, mask, params):
    dp, devices = mesh
    pixels, channels = x.shape
    lines = pixels // SLOTS
    blocks = channels // LANES
    constants = [
        jnp.asarray(split_constant(slots_to_freq(), 2)),
        jnp.asarray(split_constant(taps_to_freq(), 4)),
        jnp.asarray(split_constant(freq_to_slots(), 2)),
    ]

    def pair(*dims):
        return [pltpu.VMEM(dims, BF16)] * 2

    field = pltpu.VMEM((pixels, channels), F32)
    scratch = [
        field,
        pltpu.VMEM(up.shape, F32),
        pltpu.VMEM(down.shape, F32),
        pltpu.VMEM(point_one.shape, F32),
        pltpu.VMEM(big.shape, F32),
        pltpu.VMEM((TAP_ROWS, SPAN_PAD, channels), F32),
        pltpu.VMEM(mask.shape, F32),
        pltpu.SemaphoreType.DMA((24,)),
        sum_scratch(mesh, value.shape[0]),
        pltpu.VMEM((2, 8, LANES), jnp.int32),
        pltpu.SMEM((3, 8, LANES), jnp.int32),
        pair(pixels, channels),
        pair(channels, channels),
        field,
        pltpu.VMEM((lines, SLOTS, channels), F32),
        pltpu.VMEM((blocks, WINDOW_PAD, SLOTS, LANES), F32),
        [pltpu.VMEM((WINDOW_PAD, FREQ, LANES), F32)] * blocks,
        [pltpu.VMEM((TAP_ROWS, FREQ, LANES), F32)] * blocks,
        pltpu.VMEM((lines, FREQ, LANES), F32),
        field,
    ]
    smem = pl.BlockSpec(memory_space=pltpu.SMEM)
    return exchange(
        "first",
        0,
        mesh,
        first_kernel,
        (value, names, x, up, down, point_one, big, small, mask, params, *constants),
        [VMEM, VMEM] + [HBM] * 5 + [VMEM, HBM] + [VMEM] * 4,
        [
            shape(pixels, channels),
            shape(devices, 2, *up.shape),
            shape(blocks, ZERO_ROW + 1, FREQ, LANES),
            shape(blocks, TAP_ROWS, FREQ, LANES),
            shape(pixels, channels),
            shape(8, LANES),
            shape(*value.shape),
            jax.ShapeDtypeStruct((2 * lines, LANES), jnp.int32),
            jax.ShapeDtypeStruct((2 * SPAN, LANES), jnp.int32),
        ],
        [HBM] * 5 + [VMEM] * 2 + [smem] * 2,
        scratch,
        60,
        late=True,
    )


def begin_kernel(place, id_lanes, inputs, grads, x, gy, mask, value):
    rows = x.shape[0] // SLOTS
    columns = id_lanes.shape[0] // rows
    blocks = x.shape[1] // LANES

    def one_row(row, sums):
        sums = list(sums)
        for side, (start, width) in enumerate(((0, LEFT), (LEFT, RIGHT))):
            name, at = place[2 * side, row], place[2 * side + 1, row]
            pixel = row * columns + at
            slots = pl.ds(row * SLOTS + start, width)
            own = jnp.where(name < 0, -9, name).astype(F32)
            m = jnp.where(id_lanes[pl.ds(pixel, width), :] == own, 1.0, 0.0)
            mask[slots, :] = m
            sums[-1] = sums[-1] + column_sum(m)
            for block in range(blocks):
                lanes = slice(block * LANES, (block + 1) * LANES)
                cells = pl.ds(pixel * blocks + block, width, stride=blocks)
                v = inputs[cells, :] * m
                x[slots, lanes] = v
                gy[slots, lanes] = grads[cells, :] * m
                sums[block] = sums[block] + column_sum(v)
                sums[blocks + block] = sums[blocks + block] + column_sum(v * v)
        return tuple(sums)

    sums = lax.fori_loop(0, rows, one_row, (jnp.zeros((1, LANES), F32),) * (2 * blocks + 1))
    for row in range(2 * blocks):
        value[row : row + 1, :] = sums[row]
    for row in range(blocks):
        value[2 * blocks + row : 2 * blocks + row + 1, :] = sums[-1]
    value[3 * blocks :, :] = jnp.zeros((value.shape[0] - 3 * blocks, LANES), F32)


def begin(place, id_lanes, inputs, grads, rows, channels):
    return pl.pallas_call(
        begin_kernel,
        out_shape=[
            shape(rows * SLOTS, channels),
            shape(rows * SLOTS, channels),
            shape(rows * SLOTS, LANES),
            shape(16, LANES),
        ],
        in_specs=[pl.BlockSpec(memory_space=pltpu.SMEM)] + [VMEM] * 3,
        out_specs=[VMEM] * 4,
        compiler_params=pltpu.CompilerParams(vmem_limit_bytes=16 << 20),
        name="begin",
    )(place, id_lanes, inputs, grads)


def finish_kernel(place, inputs, grads, delta, cells, output, grad_input):
    rows = delta.shape[0] // SLOTS
    blocks = delta.shape[1] // LANES
    columns = inputs.shape[0] // rows // blocks
    output[...] = inputs[...]
    grad_input[...] = grads[...]

    def one_row(row, carry):
        for side, (start, width) in enumerate(((0, LEFT), (LEFT, RIGHT))):
            pixel = row * columns + place[2 * side + 1, row]
            slots = pl.ds(row * SLOTS + start, width)
            for block in range(blocks):
                lanes = slice(block * LANES, (block + 1) * LANES)
                where = pl.ds(pixel * blocks + block, width, stride=blocks)
                output[where, :] = output[where, :] + delta[slots, lanes]
                grad_input[where, :] = grad_input[where, :] + cells[slots, lanes]
        return carry

    lax.fori_loop(0, rows, one_row, 0)


def place_results(place, inputs, grads, delta, cells):
    return pl.pallas_call(
        finish_kernel,
        out_shape=[shape(*inputs.shape)] * 2,
        in_specs=[pl.BlockSpec(memory_space=pltpu.SMEM)] + [VMEM] * 4,
        out_specs=[VMEM] * 2,
        compiler_params=pltpu.CompilerParams(vmem_limit_bytes=60 << 20),
        name="finish",
    )(place, inputs, grads, delta, cells)


def shards(
    dp,
    devices_rows,
    inputs,
    image_ids,
    first_norm_gain,
    first_norm_bias,
    point_one,
    kernel_big,
    kernel_small,
    second_norm_gain,
    second_norm_bias,
    point_two,
    feedforward_norm_gain,
    feedforward_norm_bias,
    w_up,
    w_down,
    out_grad,
):
    rows, canvases, columns, channels = inputs.shape
    assert canvases == 1 and kernel_big.shape[0] == SPAN
    pixels = rows * SLOTS
    ids = image_ids[:, 0]
    mesh = (dp, devices_rows)

    place = jnp.arange(columns, dtype=jnp.int32)[None, :]
    is_left = (ids >= 0) & (ids < LEFT_IDS)
    is_right = ids >= LEFT_IDS

    def side(member, width):
        name = jnp.max(jnp.where(member, ids, -1), axis=1)
        first = jnp.min(jnp.where(member, place, columns), axis=1)
        return name, jnp.minimum(first, columns - width)

    left_id, left_at = side(is_left, LEFT)
    right_id, right_at = side(is_right, RIGHT)
    spot = jnp.stack([left_id, left_at, right_id, right_at])
    lines = (rows * columns * channels // LANES, LANES)
    id_lanes = jnp.broadcast_to(ids.reshape(rows * columns, 1).astype(F32), (rows * columns, LANES))
    x, gy, mask_lanes, value = begin(spot, id_lanes, inputs.reshape(lines), out_grad.reshape(lines), rows, channels)
    names = jnp.stack([left_id, right_id]) + 1

    def name_tile(first, last, lane):
        return jnp.pad(names[:, first:last], ((0, 6), (lane, LANES - lane - (last - first))))

    names = jnp.stack(
        [
            name_tile(0, rows, REACH),
            name_tile(rows - REACH, rows, 0),
            name_tile(0, REACH, REACH + rows),
        ]
    )
    small_start = REACH - kernel_small.shape[0] // 2
    vectors = [
        first_norm_gain,
        first_norm_bias,
        second_norm_gain,
        second_norm_bias,
        feedforward_norm_gain,
        feedforward_norm_bias,
    ]
    params = jnp.stack(vectors + [jnp.zeros((channels,), F32)] * 2)
    hidden, wall, xf, kf, conv, conv_sums, total_one, *tables = first(
        mesh,
        value,
        names,
        x,
        w_up,
        w_down,
        point_one,
        kernel_big,
        kernel_small,
        mask_lanes,
        params,
    )
    delta, back_three, total_four, total_five, dconv, point_grad, part, _ = middle(
        mesh, conv, conv_sums, x, gy, mask_lanes, params, total_one, point_two, wall
    )
    grad_bias_three, grad_gain_three = total_four.reshape(2, channels)
    grad_bias_two, grad_gain_two = total_five.reshape(2, channels)
    cells, total, grad_point_one, grad_point_two, grad_up, grad_down, grad_kernel = last(
        mesh,
        tables,
        dconv,
        xf,
        kf,
        mask_lanes,
        x,
        hidden,
        point_one,
        params,
        total_one,
        back_three,
        part,
        point_grad,
    )
    grad_bias_one, grad_gain_one = total.reshape(2, channels)
    output, grad_input = place_results(spot, inputs.reshape(lines), out_grad.reshape(lines), delta, cells)
    small_end = small_start + kernel_small.shape[0]
    grad_small = grad_kernel[small_start:small_end, small_start:small_end]
    return (
        output.reshape(inputs.shape),
        grad_input.reshape(inputs.shape),
        grad_gain_one,
        grad_bias_one,
        grad_point_one,
        grad_kernel,
        grad_small,
        grad_gain_two,
        grad_bias_two,
        grad_point_two,
        grad_gain_three,
        grad_bias_three,
        grad_up,
        grad_down,
    )


def solution(mesh):
    field = P("rows", "dp", None, None)
    everywhere = P()
    up, down = P(None, "rows"), P("rows", None)
    return jax.shard_map(
        functools.partial(shards, mesh.shape["dp"], mesh.shape["rows"]),
        mesh=mesh,
        in_specs=(field, P("rows", "dp", None)) + (everywhere,) * 10 + (up, down, field),
        out_specs=(field, field) + (everywhere,) * 10 + (up, down),
        check_vma=False,
    )
```

```python
import functools

import jax
import jax.numpy as jnp
import numpy as np
from jax import lax
from jax.experimental import pallas as pl
from jax.experimental.pallas import tpu as pltpu
from jax.sharding import PartitionSpec as P

EPSILON = 1e-05
HIGHEST = lax.Precision.HIGHEST
HIGH = lax.Precision.HIGH
MESH = pl.DeviceIdType.MESH
F32 = jnp.float32
BF16 = jnp.bfloat16

LEFT, RIGHT = 24, 16
SLOTS = LEFT + RIGHT
LEFT_IDS = 3
LEFT_N, RIGHT_N = 37, 27
LEFT_F, RIGHT_F = 24, 16
FREQ = 2 * LEFT_F + 2 * RIGHT_F
REACH = 13
SPAN = 2 * REACH + 1
SPAN_PAD = 32
LANES = 128


def forward_transform(length, padded, positions, columns):
    count = length // 2 + 1
    out = np.zeros((2 * padded, columns))
    angle = 2 * np.pi * np.outer(np.arange(count), positions) / length
    out[:count, : len(positions)] = np.cos(angle)
    out[padded : padded + count, : len(positions)] = -np.sin(angle)
    return out


def backward_transform(length, padded, positions, rows):
    count = length // 2 + 1
    out = np.zeros((rows, 2 * padded))
    twice = np.where(np.arange(count) == 0, 1.0, 2.0)
    angle = 2 * np.pi * np.outer(positions, np.arange(count)) / length
    out[: len(positions), :count] = np.cos(angle) * twice / length
    out[: len(positions), padded : padded + count] = -np.sin(angle) * twice / length
    return out


def slots_to_freq():
    out = np.zeros((FREQ, SLOTS))
    out[: 2 * LEFT_F, :LEFT] = forward_transform(LEFT_N, LEFT_F, np.arange(LEFT), LEFT)
    out[2 * LEFT_F :, LEFT:] = forward_transform(RIGHT_N, RIGHT_F, np.arange(RIGHT), RIGHT)
    return out


def freq_to_slots():
    out = np.zeros((SLOTS, FREQ))
    out[:LEFT, : 2 * LEFT_F] = backward_transform(LEFT_N, LEFT_F, np.arange(LEFT), LEFT)
    out[LEFT:, 2 * LEFT_F :] = backward_transform(RIGHT_N, RIGHT_F, np.arange(RIGHT), RIGHT)
    return out


def taps_to_freq():
    taps = np.arange(SPAN) - REACH
    return np.concatenate(
        [
            forward_transform(LEFT_N, LEFT_F, taps, SPAN_PAD),
            forward_transform(RIGHT_N, RIGHT_F, taps, SPAN_PAD),
        ]
    )


def freq_to_taps():
    taps = np.arange(SPAN) - REACH
    return np.concatenate(
        [
            backward_transform(LEFT_N, LEFT_F, taps, SPAN_PAD),
            backward_transform(RIGHT_N, RIGHT_F, taps, SPAN_PAD),
        ],
        axis=1,
    )


def split_constant(matrix, group):
    whole = np.kron(np.eye(group), matrix).astype(np.float32)
    high = whole.astype(jnp.bfloat16)
    low = (whole - high.astype(np.float32)).astype(jnp.bfloat16)
    return np.concatenate([high, high, low], axis=1)


def split_stack(value):
    high = value.astype(BF16)
    low = (value - high.astype(F32)).astype(BF16)
    return jnp.concatenate([high, low, high], axis=0)


def product_split(constant_ref, value):
    return jnp.dot(constant_ref[...], split_stack(value), preferred_element_type=F32)


TAP_ROWS = 28


class Net:
    def __init__(self, dp, rows, send_sem, recv_sem):
        self.count, self.rows = dp, rows
        self.send_sem, self.recv_sem, self.used = send_sem, recv_sem, 0
        self.dp = lax.axis_index("dp")
        self.z = lax.axis_index("rows")
        self.bits = list(range(1, dp.bit_length() - 1))

    def bit(self, index):
        return lax.rem(self.dp // (1 << index), 2)

    def across(self, index):
        return (self.dp + (1 << index) * (1 - 2 * self.bit(index)), self.z)

    def line(self, step):
        return (self.dp, lax.rem(self.z + step, self.rows))

    def layer(self, step):
        return (lax.rem(self.dp + step, self.count), self.z)

    def greet(self):
        barrier = pltpu.get_barrier_semaphore()

        def greet_line(step, carry):
            pl.semaphore_signal(barrier, inc=1, device_id=self.line(step), device_id_type=MESH)
            return carry

        def greet_layer(step, carry):
            pl.semaphore_signal(barrier, inc=1, device_id=self.layer(step), device_id_type=MESH)
            return carry

        lax.fori_loop(1, self.rows, greet_line, 0)
        lax.fori_loop(1, self.count, greet_layer, 0)

    def ready(self):
        pl.semaphore_wait(pltpu.get_barrier_semaphore(), self.rows + self.count - 2)

    def copy(self, src, dst, device):
        made = pltpu.make_async_remote_copy(
            src_ref=src,
            dst_ref=dst,
            send_sem=self.send_sem.at[self.used],
            recv_sem=self.recv_sem.at[self.used],
            device_id=device,
            device_id_type=MESH,
        )
        self.used += 1
        return made

    def reserve(self, number):
        self.used += number
        return self.used - number

    def copy_at(self, index, src, dst, device):
        return pltpu.make_async_remote_copy(
            src_ref=src,
            dst_ref=dst,
            send_sem=self.send_sem.at[index],
            recv_sem=self.recv_sem.at[index],
            device_id=device,
            device_id_type=MESH,
        )

    def own(self, src, dst):
        made = pltpu.make_async_copy(src, dst, self.recv_sem.at[self.used])
        self.used += 1
        return made


def all_sum_job(net, value, out, line_slots, part, layer_slots):
    own = net.own(value, line_slots.at[net.z])
    own.start()
    sent = [net.copy(value, line_slots.at[net.z], net.line(s)) for s in range(1, net.rows)]
    for one in sent:
        one.start()
    yield
    own.wait()
    for one in sent:
        one.wait()
    total = line_slots[0]
    for index in range(1, net.rows):
        total = total + line_slots[index]
    part[...] = total
    own = net.own(part, layer_slots.at[net.dp])
    own.start()
    sent = [net.copy(part, layer_slots.at[net.dp], net.layer(s)) for s in range(1, net.count)]
    for one in sent:
        one.start()
    yield
    own.wait()
    for one in sent:
        one.wait()
    total = layer_slots[0]
    for index in range(1, net.count):
        total = total + layer_slots[index]
    out[...] = total


def aligned(value, unit):
    return pl.multiple_of(value, unit)


def halving(net, order, rows):
    base, steps = 0, []
    for bit in order:
        steps.append((bit, base, rows))
        rows //= 2
        base = base + net.bit(bit) * rows
    return steps, base, rows


def add_rows(dst, src, count, step):
    def one(i, carry):
        at = aligned(i * step, step)
        to, of = dst(at), src(at)
        to[...] = to[...] + of[...]
        return carry

    lax.fori_loop(0, count // step, one, 0)


def run(*jobs):
    jobs = list(jobs)
    while jobs:
        jobs = [job for job in jobs if next(job, StopIteration) is not StopIteration]


def sides(net, rows):
    core = net.bit(0)
    return [
        (pl.ds(aligned((2 * core + side) * LANES, LANES), LANES), *halving(net, order, rows))
        for side, order in enumerate((net.bits, net.bits[::-1]))
    ]


def weights_line_job(net, up, down, wall, distances):
    own = [net.own(up, wall.at[net.z, 0]), net.own(down, wall.at[net.z, 1])] if 1 in distances else []
    last = net.rows - 1
    for step in distances:
        moves = []
        for lanes, _, base, rows in sides(net, wall.shape[2]):
            mine = pl.ds(aligned(base, 8), rows)
            for way in (1, -1):
                shard = net.z - way * (step - 1)
                going = (net.z >= step - 1) & (net.z < last) if way > 0 else (net.z <= last - (step - 1)) & (net.z > 0)
                coming = net.z >= step if way > 0 else net.z <= last - step
                shard = lax.rem(shard + net.rows, net.rows)
                for which in range(2):
                    piece = wall.at[shard, which, mine, lanes]
                    source = (up, down)[which].at[mine, lanes] if step == 1 else piece
                    one = net.copy(source, piece, net.line(way % net.rows))
                    pl.when(going)(one.start)
                    moves.append((one, going, coming))
        if step == 1:
            for one in own:
                one.start()
        yield
        for one, going, coming in moves:
            pl.when(coming)(one.wait_recv)
            pl.when(going)(one.wait_send)
    for one in own:
        one.wait()


def weights_layer_job(net, wall, distances):
    parts = sides(net, wall.shape[2])
    shards = [net.z + way * distance for distance in distances for way in (1, -1)]
    shards = [(lax.rem(shard + net.rows, net.rows), (shard >= 0) & (shard < net.rows)) for shard in shards]
    for back in range(1, len(net.bits) + 1):
        moves = []
        for lanes, steps, _, _ in parts:
            bit, base, rows = steps[-back]
            mine = pl.ds(aligned(base + net.bit(bit) * (rows // 2), 8), rows // 2)
            for shard, there in shards:
                piece = wall.at[shard, :, mine, lanes]
                moves.append((net.copy(piece, piece, net.across(bit)), there))
        for one, there in moves:
            pl.when(there)(one.start)
        yield
        for one, there in moves:
            pl.when(there)(one.wait)


def weights_pair_job(net, wall):
    half = wall.shape[3] // 2
    lanes = pl.ds(aligned(net.bit(0) * half, LANES), half)
    moves = []
    for step in range(1, net.rows):
        piece = wall.at[lax.rem(net.z + step, net.rows), :, :, lanes]
        moves.append(net.copy(piece, piece, net.across(0)))
    for one in moves:
        one.start()
    yield
    for one in moves:
        one.wait()


def halo_job(net, field, window, zeros):
    rows = field.shape[0]
    own = net.own(field, window.at[pl.ds(REACH, rows)])
    own.start()
    has_above, has_below = net.z > 0, net.z < net.rows - 1
    down = net.copy(field.at[pl.ds(rows - REACH, REACH)], window.at[pl.ds(0, REACH)], net.line(1))
    up = net.copy(field.at[pl.ds(0, REACH)], window.at[pl.ds(REACH + rows, REACH)], net.line(net.rows - 1))
    pl.when(has_below)(down.start)
    pl.when(has_above)(up.start)
    zeros[...] = jnp.zeros(zeros.shape, F32)
    top = net.own(zeros, window.at[pl.ds(0, REACH)])
    bottom = net.own(zeros, window.at[pl.ds(REACH + rows, REACH)])
    pl.when(jnp.logical_not(has_above))(top.start)
    pl.when(jnp.logical_not(has_below))(bottom.start)
    yield
    own.wait()
    pl.when(jnp.logical_not(has_above))(top.wait)
    pl.when(jnp.logical_not(has_below))(bottom.wait)
    pl.when(has_above)(down.wait_recv)
    pl.when(has_below)(down.wait_send)
    pl.when(has_below)(up.wait_recv)
    pl.when(has_above)(up.wait_send)


def shares(net, rows, width):
    core, out = net.bit(0), []
    by_rows = width == 2 * LANES
    for side, order in enumerate((net.bits, net.bits[::-1])):
        start = side * (rows // 2) if by_rows else 0
        steps, base, size = halving(net, order, rows // 2 if by_rows else rows)
        steps = [(bit, start + first, count) for bit, first, count in steps]
        block = 0 if by_rows else side
        outer = pl.ds(aligned((core if by_rows else 2 * core + side) * LANES, LANES), LANES)
        out.append((pl.ds(block * LANES, LANES), outer, steps, start + base, size))
    return out


def reduce_all_job(net, source, acc, got_pair, got, got_line, out):
    rows, width = source.shape
    half = width // 2
    core = net.bit(0)
    own = net.own(source.at[:, pl.ds(aligned(core * half, LANES), half)], acc)
    sent = net.copy(source.at[:, pl.ds(aligned((1 - core) * half, LANES), half)], got_pair, net.across(0))
    own.start()
    sent.start()
    yield
    own.wait()
    sent.wait()
    add_rows(lambda at: acc.at[pl.ds(at, 64)], lambda at: got_pair.at[pl.ds(at, 64)], rows, 64)
    parts = shares(net, rows, width)
    for index in range(len(net.bits)):
        moves = []
        for side, (inner, _, steps, _, _) in enumerate(parts):
            bit, base, size = steps[index]
            size //= 2
            give = base + (1 - net.bit(bit)) * size
            keep = base + net.bit(bit) * size
            place = got.at[side, pl.ds(rows - 2 * size, size)]
            one = net.copy(acc.at[pl.ds(aligned(give, 8), size), inner], place, net.across(bit))
            one.start()
            moves.append((one, keep, size, inner, side))
        yield
        for one, keep, size, inner, side in moves:
            one.wait()
            unit = 64 if size % 64 == 0 else 8
            add_rows(
                lambda at: acc.at[pl.ds(aligned(keep + at, 8), unit), inner],
                lambda at: got.at[side, pl.ds(aligned(rows - 2 * size + at, 8), unit)],
                size,
                unit,
            )
    moves, own = [], []
    for side, (inner, _, _, base, size) in enumerate(parts):
        size //= net.rows
        own.append(net.own(acc.at[pl.ds(aligned(base + net.z * size, 8), size), inner], got_line.at[side, net.z]))
        for step in range(1, net.rows):
            other = lax.rem(net.z + step, net.rows)
            piece = acc.at[pl.ds(aligned(base + other * size, 8), size), inner]
            moves.append(net.copy(piece, got_line.at[side, net.z], net.line(step)))
    for one in own + moves:
        one.start()
    yield
    for one in own + moves:
        one.wait()
    moves = []
    for side, (_, outer, _, base, size) in enumerate(parts):
        size //= net.rows
        total = got_line[side, 0]
        for index in range(1, net.rows):
            total = total + got_line[side, index]
        piece = out.at[pl.ds(aligned(base + net.z * size, 8), size), outer]
        out[pl.ds(aligned(base + net.z * size, 8), size), outer] = total
        for step in range(1, net.rows):
            moves.append(net.copy(piece, piece, net.line(step)))
            moves[-1].start()
    yield
    for one in moves:
        one.wait()
    for back in range(1, len(net.bits) + 1):
        moves = []
        for _, outer, steps, _, _ in parts:
            bit, base, size = steps[-back]
            piece = out.at[pl.ds(aligned(base + net.bit(bit) * (size // 2), 8), size // 2), outer]
            moves.append(net.copy(piece, piece, net.across(bit)))
            moves[-1].start()
        yield
        for one in moves:
            one.wait()
    piece = out.at[:, pl.ds(aligned(core * half, LANES), half)]
    one = net.copy(piece, piece, net.across(0))
    one.start()
    yield
    one.wait()


VMEM = pl.BlockSpec(memory_space=pltpu.VMEM)
HBM = pl.BlockSpec(memory_space=pltpu.HBM)
COPIES = 448


def shape(*dims):
    return jax.ShapeDtypeStruct(dims, F32)


def exchange(name, number, mesh, body, args, in_specs, outs, out_specs, scratch, limit, aliases=None, late=False):
    dp, rows = mesh

    def kernel(*refs):
        *refs, send_sem, recv_sem = refs
        net = Net(dp, rows, send_sem, recv_sem)
        net.greet()
        if not late:
            net.ready()
        body(net, *refs)
        assert net.used <= COPIES

    return pl.pallas_call(
        kernel,
        out_shape=outs,
        in_specs=in_specs,
        out_specs=out_specs,
        scratch_shapes=scratch + [pltpu.SemaphoreType.DMA((COPIES,))] * 2,
        input_output_aliases=aliases or {},
        compiler_params=pltpu.CompilerParams(
            collective_id=number, has_side_effects=True, vmem_limit_bytes=limit << 20
        ),
        name=name,
    )(*args)


def sum_scratch(mesh, height):
    dp, rows = mesh
    return [pltpu.VMEM((rows, height, LANES), F32), pltpu.VMEM((height, LANES), F32), pltpu.VMEM((dp, height, LANES), F32)]


def all_scratch(mesh, rows, width):
    size = (rows // 2 if width == 2 * LANES else rows) * 2 // mesh[0] // mesh[1]
    return [
        pltpu.VMEM((rows, width // 2), F32),
        pltpu.VMEM((rows, width // 2), F32),
        pltpu.VMEM((2, rows, LANES), F32),
        pltpu.VMEM((2, mesh[1], size, LANES), F32),
    ]


class Loads:
    def __init__(self, sems):
        self.sems, self.used, self.leaving = sems, 0, []

    def start(self, src, dst):
        one = pltpu.make_async_copy(src, dst, self.sems.at[self.used])
        self.used += 1
        one.start()
        return one

    def leave(self, src, dst):
        self.leaving.append(self.start(src, dst))

    def finish(self):
        for one in self.leaving:
            one.wait()


def gelu_parts(x):
    scale, cubic = 0.7978845608028654, 0.044715
    square = x * x
    t = jnp.tanh(scale * (x + cubic * (x * square)))
    half = 0.5 * (1.0 + t)
    return (x * half, half + 0.5 * x * (1.0 - t * t) * (scale * (1.0 + 3.0 * cubic * square)))


NN = (((1,), (0,)), ((), ()))
NT = (((1,), (1,)), ((), ()))
TILE = 320


def split_two(value):
    high = value.astype(BF16)
    return high, (value - high.astype(F32)).astype(BF16)


def store_split(refs, where, value):
    refs[0][where], refs[1][where] = split_two(value)


def dot_split(left, right, dims=NN):
    def one(a, b):
        return lax.dot_general(a, b, dims, preferred_element_type=F32)

    return one(left[0], right[0]) + (one(left[0], right[1]) + one(left[1], right[0]))


def read_pair(refs, where=Ellipsis):
    return refs[0][where], refs[1][where]


def write_sums(value, first, second):
    for row in range(4):
        lanes = slice(row * LANES, (row + 1) * LANES)
        value[row : row + 1, :] = first[:, lanes]
        value[4 + row : 5 + row, :] = second[:, lanes]


def read_sums(total):
    return tuple(
        jnp.concatenate([total[4 * k + row : 4 * k + row + 1, :] for row in range(4)], axis=1) for k in range(2)
    )


def column_sum(value):
    return jnp.sum(value, axis=0, keepdims=True)


def norm_terms(total, count):
    first, second = read_sums(total)
    mean = first / count
    return mean, lax.rsqrt(second / count - mean * mean + EPSILON)


def finish(job):
    for _ in job:
        pass


def rem(value, unit):
    return value % unit if isinstance(value, int) else lax.rem(value, unit)


def middle_kernel(
    net,
    conv_in,
    conv_sums,
    x_in,
    gy_in,
    mask_in,
    params,
    total_one,
    point_in,
    wall_in,
    delta_out,
    back_out,
    total_four,
    total_five,
    dconv_out,
    point_out,
    part,
    wall,
    x,
    gy,
    mask,
    point_two,
    delta,
    back,
    dconv,
    point_grad,
    load_sem,
    sums_own,
    sums_slots,
    own_sem,
    mixed,
    xhat,
    slope_two,
    act_pair,
    u_pair,
    ut_pair,
    g_pair,
    gt_pair,
    point_pair,
    up_pair,
    down_pair,
    hid_pair,
    dpre_pair,
    w_up,
    w_down,
    made,
    acc,
    got_pair,
    got_layer,
    got_line,
):
    pixels, channels = x.shape
    tiles = pixels // TILE
    hidden = w_up.shape[2]
    per_shard = wall.shape[2] // hidden
    chunks = net.rows * per_shard
    core = net.bit(0)
    gain_two, bias_two, gain_three, bias_three = (params[row : row + 1, :] for row in range(2, 6))
    count = read_count(total_one)
    loads = Loads(load_sem)
    came_point = loads.start(point_in, point_two)
    came_gy = loads.start(gy_in, gy)
    came = [loads.start(src, dst) for src, dst in ((conv_in, xhat), (x_in, x), (mask_in, mask))]

    def each_tile(body):
        def one(index, carry):
            return body(pl.ds(aligned(index * TILE, TILE), TILE), carry)

        zero = jnp.zeros((1, channels), F32)
        return lax.fori_loop(0, tiles, one, (zero, zero))

    def valid(rows):
        return jnp.concatenate([mask[rows, :]] * (channels // LANES), axis=1)

    def total_job(which, out):
        return all_sum_job(net, sums_own.at[which], out, *(slots.at[which] for slots in sums_slots))

    def shard_of(chunk):
        return lax.rem(net.z + chunk // per_shard, net.rows)

    def load(chunk):
        slot, shard, part = rem(chunk, 2), shard_of(chunk), rem(chunk, per_shard)
        span = pl.ds(aligned(part * hidden, hidden), hidden)
        return (
            pltpu.make_async_copy(wall.at[shard, 0, :, span], w_up.at[slot], own_sem.at[0, slot]),
            pltpu.make_async_copy(wall.at[shard, 1, span, :], w_down.at[slot], own_sem.at[1, slot]),
        )

    sums_own[0] = conv_sums[...]
    net.ready()
    job = total_job(0, sums_slots[1].at[0])
    next(job)

    far_line = weights_line_job(net, None, None, wall, (net.rows - 1,))
    next(far_line)
    near = weights_layer_job(net, wall, range(2, net.rows - 1))
    next(near, None)
    for one in load(0):
        one.start()
    came_point.wait()
    store_split(point_pair, Ellipsis, point_two[...])
    came_gy.wait()
    store_split(g_pair, Ellipsis, gy[...])
    next(job)
    store_split(gt_pair, Ellipsis, gy[...].T)
    finish(job)
    next(near, None)
    for one in came:
        one.wait()
    mean, inv_two = norm_terms(sums_slots[1].at[0], count)

    def second_norm(rows, carry):
        m = valid(rows)
        hat = (xhat[rows, :] - mean) * inv_two
        act, slope = gelu_parts((hat * gain_two + bias_two) * m)
        xhat[rows, :] = hat
        slope_two[rows, :] = slope * m
        store_split(act_pair, rows, act)
        field = x[rows, :] + dot_split(read_pair(act_pair, rows), read_pair(point_pair))
        mixed[rows, :] = field
        return carry[0] + column_sum(field), carry[1] + column_sum(field * field)

    write_sums(sums_own.at[1], *each_tile(second_norm))
    job = total_job(1, sums_slots[1].at[1])
    next(job)
    finish(far_line)
    far = weights_layer_job(net, wall, (net.rows - 1,))
    next(far)
    next(job)
    finish(job)
    finish(near)
    next(far)
    mean_three, inv_three = norm_terms(sums_slots[1].at[1], count)

    def third_norm(rows, carry):
        hat = (mixed[rows, :] - mean_three) * inv_three
        store_split(u_pair, rows, (hat * gain_three + bias_three) * valid(rows))
        delta[rows, :] = mixed[rows, :] - x[rows, :]
        back[rows, :] = jnp.zeros((TILE, channels), F32)
        return carry

    each_tile(third_norm)
    for side in range(2):
        ut_pair[side][...] = u_pair[side][...].T

    mine = pl.ds(aligned(core * LANES, LANES), LANES)
    other = pl.ds(aligned((1 - core) * LANES, LANES), LANES)
    halvings = [halving(net, order, channels) for order in (net.bits, net.bits[::-1])]
    stages = len(net.bits)
    pair_base = net.reserve(chunks)
    layer_base = net.reserve(2 * stages * chunks)
    line_base = net.reserve(2 * chunks)

    def pair_move(chunk):
        slot = rem(chunk, 2)
        return (
            net.copy_at(pair_base + chunk, made.at[slot, :, :, other], got_pair.at[chunk], net.across(0)),
            pltpu.make_async_copy(made.at[slot, :, :, mine], acc.at[chunk], own_sem.at[2, slot]),
        )

    def layer_move(stage, chunk):
        moves = []
        for side, (steps, _, _) in enumerate(halvings):
            bit, base, size = steps[stage]
            size //= 2
            give, keep = base + (1 - net.bit(bit)) * size, base + net.bit(bit) * size
            place = pl.ds(channels - 2 * size, size)
            moves.append(
                (
                    net.copy_at(
                        layer_base + (2 * stage + side) * chunks + chunk,
                        acc.at[chunk, side, pl.ds(aligned(give, 8), size), :],
                        got_layer.at[chunk, side, place, :],
                        net.across(bit),
                    ),
                    keep,
                    size,
                    side,
                )
            )
        return moves

    def line_move(chunk, remote):
        moves = []
        shard, part = shard_of(chunk), rem(chunk, per_shard)
        for side, (_, base, size) in enumerate(halvings):
            piece = acc.at[chunk, side, pl.ds(aligned(base, 8), size), :]
            place = got_line.at[net.z, part, side]
            if remote:
                moves.append(net.copy_at(line_base + 2 * chunk + side, piece, place, (net.dp, shard)))
            else:
                moves.append(pltpu.make_async_copy(piece, place, net.recv_sem.at[line_base + 2 * chunk + side]))
        return moves

    def when(test, body):
        if isinstance(test, bool):
            if test:
                body()
        else:
            pl.when(test)(body)

    def within(chunk):
        if isinstance(chunk, int):
            return 0 <= chunk < chunks
        return (chunk >= 0) & (chunk < chunks)

    def progress(step):
        def after_pair():
            chunk = step - 1
            sent, own = pair_move(chunk)
            own.wait()
            sent.wait()
            for side in range(2):
                add_rows(
                    lambda at: acc.at[chunk, side, pl.ds(at, 64), :],
                    lambda at: got_pair.at[chunk, side, pl.ds(at, 64), :],
                    channels,
                    64,
                )
            for one, *_ in layer_move(0, chunk):
                one.start()

        def after_layer(stage):
            chunk = step - 2 - stage
            for one, keep, size, side in layer_move(stage, chunk):
                one.wait()
                unit = min(size, 64)
                add_rows(
                    lambda at: acc.at[chunk, side, pl.ds(aligned(keep + at, 8), unit), :],
                    lambda at: got_layer.at[chunk, side, pl.ds(aligned(channels - 2 * size + at, 8), unit), :],
                    size,
                    unit,
                )
            if stage + 1 < stages:
                for one, *_ in layer_move(stage + 1, chunk):
                    one.start()
            else:

                def go(remote):
                    def start():
                        for one in line_move(chunk, remote):
                            one.start()

                    return start

                when(chunk >= per_shard, go(True))
                when(chunk < per_shard, go(False))

        when(within(step - 1), after_pair)
        for stage in range(stages):
            when(within(step - 2 - stage), functools.partial(after_layer, stage))

    def feed_forward(chunk, carry):
        progress(chunk)
        slot = rem(chunk, 2)
        for one in load(chunk):
            one.wait()

        @pl.when((chunk + 1 < chunks) & (chunk + 1 != per_shard))
        def _():
            for one in load(chunk + 1):
                one.start()

        store_split(up_pair, Ellipsis, w_up[slot])
        store_split(down_pair, Ellipsis, w_down[slot])

        def first_half(rows):
            hid, slope = gelu_parts(dot_split(read_pair(u_pair, rows), read_pair(up_pair)))
            store_split(hid_pair, rows, hid)
            store_split(
                dpre_pair, rows, dot_split(read_pair(g_pair, rows), read_pair(down_pair), NT) * slope
            )

        first_half(pl.ds(0, pixels))
        made[slot, 0] = dot_split(read_pair(ut_pair), read_pair(dpre_pair))
        made[slot, 1] = dot_split(read_pair(gt_pair), read_pair(hid_pair))
        for one in pair_move(chunk):
            one.start()

        def second_half(rows):
            delta[rows, :] += dot_split(read_pair(hid_pair, rows), read_pair(down_pair))
            back[rows, :] += dot_split(read_pair(dpre_pair, rows), read_pair(up_pair), NT)

        second_half(pl.ds(0, pixels))
        return carry

    lax.fori_loop(0, per_shard - 1, feed_forward, 0)
    finish(far)
    pairs = weights_pair_job(net, wall)
    next(pairs)
    lax.fori_loop(per_shard - 1, per_shard, feed_forward, 0)
    finish(pairs)
    for one in load(per_shard):
        one.start()
    lax.fori_loop(per_shard, chunks, feed_forward, 0)

    loads.leave(delta, delta_out)

    def third_sums(rows, carry):
        dy = back[rows, :] * valid(rows)
        back[rows, :] = dy
        hat = (mixed[rows, :] - mean_three) * inv_three
        return carry[0] + column_sum(dy), carry[1] + column_sum(dy * hat)

    write_sums(sums_own.at[2], *each_tile(third_sums))
    job = total_job(2, total_four)
    next(job)
    progress(chunks)
    next(job)
    finish(job)
    progress(chunks + 1)
    grad_bias, grad_gain = read_sums(total_four)

    def third_back(rows, carry):
        m = valid(rows)
        hat = (mixed[rows, :] - mean_three) * inv_three
        field = m * gain_three * inv_three * (back[rows, :] - grad_bias / count - hat * (grad_gain / count))
        back[rows, :] = field
        dmixed = gy[rows, :] + field
        store_split(g_pair, rows, dmixed)
        du = dot_split(read_pair(g_pair, rows), read_pair(point_pair), NT) * slope_two[rows, :]
        mixed[rows, :] = du
        return carry[0] + column_sum(du), carry[1] + column_sum(du * xhat[rows, :])

    write_sums(sums_own.at[3], *each_tile(third_back))
    loads.leave(back, back_out)
    job = total_job(3, total_five)
    next(job)
    for step in range(chunks + 2, chunks + 1 + stages):
        progress(step)
    for side in range(2):
        ut_pair[side][...] = act_pair[side][...].T
    next(job)
    point_grad[...] = dot_split(read_pair(ut_pair), read_pair(g_pair))
    loads.leave(point_grad, point_out)
    finish(job)
    grad_bias_two, grad_gain_two = read_sums(total_five)

    def second_back(row, carry):
        rows = pl.ds(aligned(row * SLOTS, 8), SLOTS)
        field = mixed[rows, :] - grad_bias_two / count - xhat[rows, :] * (grad_gain_two / count)
        dconv[row] = valid(rows) * gain_two * inv_two * field
        return carry

    lax.fori_loop(0, pixels // SLOTS, second_back, 0)
    loads.leave(dconv, dconv_out)
    for chunk in range(chunks):
        for one in line_move(chunk, chunk >= per_shard):
            one.wait()
    for which in range(2):
        for block in range(per_shard):
            total = got_line[0, block, which]
            for index in range(1, net.rows):
                total = total + got_line[index, block, which]
            part[which, block] = total
    loads.finish()


def middle(mesh, conv, conv_sums, x, gy, mask, params, total_one, point_two, wall):
    dp, rows = mesh
    pixels, channels = conv.shape
    hidden = 2 * LANES
    chunks = rows * (wall.shape[2] // hidden)
    lines = pixels // SLOTS

    def pair(*dims):
        return [pltpu.VMEM(dims, BF16)] * 2

    piece = channels * 2 // dp
    field = pltpu.VMEM((pixels, channels), F32)
    square = pltpu.VMEM((channels, channels), F32)
    scratch = [
        field,
        field,
        pltpu.VMEM(mask.shape, F32),
        square,
        field,
        field,
        pltpu.VMEM((lines, SLOTS, channels), F32),
        square,
        pltpu.SemaphoreType.DMA((16,)),
        pltpu.VMEM((4, 8, LANES), F32),
        [pltpu.VMEM((4, rows, 8, LANES), F32), pltpu.VMEM((4, 8, LANES), F32), pltpu.VMEM((4, dp, 8, LANES), F32)],
        pltpu.SemaphoreType.DMA((3, 2)),
        pltpu.VMEM((pixels, channels), F32),
        pltpu.VMEM((pixels, channels), F32),
        pltpu.VMEM((pixels, channels), F32),
        pair(pixels, channels),
        pair(pixels, channels),
        pair(channels, pixels),
        pair(pixels, channels),
        pair(channels, pixels),
        pair(channels, channels),
        pair(channels, hidden),
        pair(hidden, channels),
        pair(pixels, hidden),
        pair(pixels, hidden),
        pltpu.VMEM((2, channels, hidden), F32),
        pltpu.VMEM((2, hidden, channels), F32),
        pltpu.VMEM((2, 2, channels, hidden), F32),
        pltpu.VMEM((chunks, 2, channels, LANES), F32),
        pltpu.VMEM((chunks, 2, channels, LANES), F32),
        pltpu.VMEM((chunks, 2, channels, LANES), F32),
        pltpu.VMEM((rows, wall.shape[2] // hidden, 2, piece, LANES), F32),
    ]
    return exchange(
        "middle",
        2,
        mesh,
        middle_kernel,
        (conv, conv_sums, x, gy, mask, params, total_one, point_two, wall),
        [HBM, VMEM] + [HBM] * 3 + [VMEM] * 2 + [HBM] * 2,
        [shape(pixels, channels)] * 2
        + [shape(8, LANES)] * 2
        + [shape(lines, SLOTS, channels), shape(channels, channels)]
        + [shape(2, wall.shape[2] // hidden, piece, LANES), shape(*wall.shape)],
        [HBM] * 2 + [VMEM] * 2 + [HBM] * 2 + [VMEM, HBM],
        scratch,
        56,
        {8: 7},
        late=True,
    )


ZERO_ROW = 42
WINDOW_PAD = 48
LEFT_TAPS, RIGHT_TAPS = 24, 14
SIDES = ((0, LEFT_F, LEFT_TAPS), (2 * LEFT_F, RIGHT_F, RIGHT_TAPS))


def transform(window, to_freq, out, group):
    rows, _, width = window.shape
    for first in range(0, rows, group):
        part = window[first : first + group].reshape(group * SLOTS, width)
        out[first : first + group] = product_split(to_freq, part).reshape(group, FREQ, width)


def sum_table(table, rows, x_ref, k_ref, y_ref, flipped):
    width = x_ref.shape[-1]
    for side, (start, size, taps) in enumerate(SIDES):
        real, imag = pl.ds(start, size), pl.ds(start + size, size)

        def one_row(row, carry):
            yr, yi = jnp.zeros((size, width), F32), jnp.zeros((size, width), F32)
            for tap in range(taps):
                w = table[side * rows + row, tap]
                index = jnp.clip(row + SPAN - 1 - w if flipped else w - row, 0, SPAN)
                xr, xi = x_ref[w, real, :], x_ref[w, imag, :]
                kr, ki = k_ref[index, real, :], k_ref[index, imag, :]
                if flipped:
                    yr, yi = yr + (kr * xr - ki * xi), yi + (kr * xi + ki * xr)
                else:
                    yr, yi = yr + (kr * xr + ki * xi), yi + (kr * xi - ki * xr)
            y_ref[row, real, :] = yr
            y_ref[row, imag, :] = yi
            return carry

        lax.fori_loop(0, rows, one_row, 0)


TAP_GROUP = 9


def sum_taps(table, rows, d_ref, x_ref, g_ref):
    tile = (8, x_ref.shape[-1])
    for side, (start, size, _) in enumerate(SIDES):
        for first in range(start, start + size, 8):
            real, imag = pl.ds(first, 8), pl.ds(first + size, 8)

            def some_taps(group, carry):
                sums = [(jnp.zeros(tile, F32), jnp.zeros(tile, F32)) for _ in range(TAP_GROUP)]
                for row in range(rows):
                    dr, di = d_ref[REACH + row, real, :], d_ref[REACH + row, imag, :]
                    for k in range(TAP_GROUP):
                        w = table[side * SPAN + group * TAP_GROUP + k, row]
                        xr, xi = x_ref[w, real, :], x_ref[w, imag, :]
                        gr, gi = sums[k]
                        sums[k] = gr + (dr * xr + di * xi), gi + (dr * xi - di * xr)
                for k in range(TAP_GROUP):
                    g_ref[group * TAP_GROUP + k, real, :], g_ref[group * TAP_GROUP + k, imag, :] = sums[k]
                return carry

            lax.fori_loop(0, SPAN // TAP_GROUP, some_taps, 0)


def halo_moves(net, field, window, index):
    rows = field.shape[0]
    lanes = pl.ds(index * LANES, LANES)
    below, above = net.z < net.rows - 1, net.z > 0
    down = net.copy(
        field.at[pl.ds(rows - REACH, REACH), :, lanes], window.at[index, pl.ds(0, REACH)], net.line(1)
    )
    up = net.copy(
        field.at[pl.ds(0, REACH), :, lanes], window.at[index, pl.ds(REACH + rows, REACH)], net.line(net.rows - 1)
    )
    return [(down, below, above), (up, above, below)]


def start_halo(net, field, window, index):
    rows = field.shape[0]
    moves = halo_moves(net, field, window, index)
    for one, goes, _ in moves:
        pl.when(goes)(one.start)
    empty = jnp.zeros((REACH,) + window.shape[2:], F32)
    window[index, REACH : REACH + rows] = field[:, :, index * LANES : (index + 1) * LANES]
    window[index, 2 * REACH + rows :] = jnp.zeros((window.shape[1] - 2 * REACH - rows,) + window.shape[2:], F32)

    @pl.when(net.z == 0)
    def _():
        window[index, :REACH] = empty

    @pl.when(net.z == net.rows - 1)
    def _():
        window[index, REACH + rows : 2 * REACH + rows] = empty

    def wait():
        for one, goes, comes in moves:
            pl.when(comes)(one.wait_recv)
            pl.when(goes)(one.wait_send)

    return wait


def last_kernel(
    net,
    row_table,
    tap_table,
    dconv_in,
    xf,
    kf,
    mask_in,
    x_in,
    h_in,
    point_in,
    params,
    total_one,
    back_in,
    part_in,
    point_grad_in,
    to_freq,
    to_slots,
    to_taps,
    cells_out,
    total,
    one_out,
    two_out,
    up_out,
    down_out,
    cube_out,
    dconv,
    mask,
    xhat,
    slope,
    point_one,
    back_three,
    part,
    point_grad,
    load_sem,
    sums_own,
    sums_slots,
    own_sem,
    window,
    df,
    x_block,
    k_block,
    gf,
    yf,
    taps,
    taps_flat,
    cube,
    ut_pair,
    point_pair,
    dh_pair,
    du,
    one_grad,
    grad_one,
    grad_two,
    grad_up,
    down_t,
    two_scratch,
    one_scratch,
    taps_scratch,
):
    rows, _, channels = dconv.shape
    pixels = rows * SLOTS
    blocks = channels // LANES
    gain, bias = params[0:1, :], params[1:2, :]
    count = read_count(total_one)
    mean, inv = norm_terms(total_one, count)
    loads = Loads(load_sem)
    came_dconv = loads.start(dconv_in, dconv)
    came_grad = loads.start(point_grad_in, point_grad)
    came_part = loads.start(part_in, part)
    came_x = loads.start(x_in, xhat)
    came_h = loads.start(h_in, slope)
    came_mask = loads.start(mask_in, mask)
    came_point = loads.start(point_in, point_one)

    def load_x(index):
        return pltpu.make_async_copy(xf.at[index], x_block[index % 2], own_sem.at[index % 2])

    def load_k(index):
        return pltpu.make_async_copy(kf.at[index], k_block[index % 2], own_sem.at[2 + index % 2])

    load_k(0).start()
    load_x(0).start()
    came_back = loads.start(back_in, back_three)
    came_dconv.wait()
    net.ready()
    waits = [start_halo(net, dconv, window, index) for index in range(blocks)]
    came_grad.wait()
    came_part.wait()

    def keep_weights():
        point_one[...] = down_t[...].T
        loads.leave(point_one, down_out)
        loads.leave(grad_up, up_out)

    def keep_taps(half):
        lanes = pl.ds(half * 2 * LANES, 2 * LANES)
        for row in range(SPAN):
            cube[row, :, lanes] = taps_flat[half][row * SPAN : (row + 1) * SPAN, :]
        loads.leave(cube.at[:, :, lanes], cube_out.at[:, :, lanes])

    def then(job, after):
        yield from job
        after()

    background = [
        then(reduce_all_job(net, point_grad, *two_scratch, grad_two), lambda: loads.leave(grad_two, two_out)),
        then(gather_pieces_job(net, part, (grad_up, down_t)), keep_weights),
    ]

    def progress():
        background[:] = [job for job in background if next(job, StopIteration) is not StopIteration]

    progress()
    came_x.wait()
    came_h.wait()
    came_mask.wait()
    came_point.wait()

    def valid(where):
        return jnp.concatenate([mask[where, :]] * blocks, axis=1)

    def prepare(index, carry):
        where = pl.ds(aligned(index * LANES, LANES), LANES)
        hat = (xhat[where, :] - mean) * inv
        xhat[where, :] = hat
        m = valid(where)
        for side, half in enumerate(split_two(((hat * gain + bias) * m).T)):
            ut_pair[side][:, where] = half
        slope[where, :] = gelu_parts(slope[where, :])[1] * m
        return carry

    lax.fori_loop(0, pixels // LANES, prepare, 0)
    store_split(point_pair, Ellipsis, point_one[...])
    taps[:, SPAN * SPAN :, :] = jnp.zeros((taps.shape[0], taps.shape[1] - SPAN * SPAN, taps.shape[2]), F32)

    def block_back(index):
        load_k(index).wait()
        if index + 1 < blocks:
            load_k(index + 1).start()
        lanes = slice(index * LANES, (index + 1) * LANES)
        sum_table(row_table, rows, df.at[index], k_block[index % 2], yf, True)
        group = to_slots.shape[0] // SLOTS
        for first in range(0, rows, group):
            where = slice(first * SLOTS, (first + group) * SLOTS)
            dact = product_split(to_slots, yf[first : first + group].reshape(group * FREQ, LANES))
            dh_pair[0][where, lanes], dh_pair[1][where, lanes] = split_two(dact * slope[where, lanes])

    def block_taps(index):
        load_x(index).wait()
        if index + 1 < blocks:
            load_x(index + 1).start()
        waits[index]()
        transform(window.at[index], to_freq, df.at[index], to_freq.shape[0] // FREQ)
        sum_taps(tap_table, rows, df.at[index], x_block[index % 2], gf)
        group = to_taps.shape[0] // SPAN_PAD
        half, lanes = index // 2, slice(index % 2 * LANES, (index % 2 + 1) * LANES)
        for first in range(0, SPAN, group):
            out = product_split(to_taps, gf[first : first + group].reshape(group * FREQ, LANES))
            out = out.reshape(group, SPAN_PAD, LANES)
            for row in range(first, first + group):
                taps[half, row * SPAN : (row + 1) * SPAN, lanes] = out[row - first, :SPAN]
        if index % 2:
            job = reduce_all_job(net, taps.at[half], *taps_scratch[half], taps_flat[half])
            background.append(then(job, functools.partial(keep_taps, half)))

    def point_part(part):
        width = channels // len(one_grad)
        lanes = slice(part * width, (part + 1) * width)
        one_grad[part][...] = dot_split(read_pair(ut_pair), (dh_pair[0][:, lanes], dh_pair[1][:, lanes]))
        job = reduce_all_job(net, one_grad[part], *one_scratch[part], grad_one[part])
        background.append(then(job, lambda: loads.leave(grad_one[part], one_out.at[:, pl.ds(part * width, width)])))

    early = blocks // 2
    for index in range(blocks):
        block_taps(index)
        if 1 <= index <= early:
            block_back(index - 1)
        if index == early and len(one_grad) == 2:
            point_part(0)
        progress()
    for index in range(early, blocks):
        block_back(index)
        progress()
    point_part(len(one_grad) - 1)
    progress()

    def last_sums(index, carry):
        where = pl.ds(aligned(index * TILE, TILE), TILE)
        dy = dot_split(read_pair(dh_pair, where), read_pair(point_pair), NT) * valid(where)
        du[where, :] = dy
        return carry[0] + column_sum(dy), carry[1] + column_sum(dy * xhat[where, :])

    zero = jnp.zeros((1, channels), F32)
    write_sums(sums_own, *lax.fori_loop(0, pixels // TILE, last_sums, (zero, zero)))
    sums = all_sum_job(net, sums_own, total, *sums_slots)
    next(sums)
    next(sums)
    progress()
    finish(sums)
    grad_bias, grad_gain = read_sums(total)
    came_back.wait()

    def last_back(index, carry):
        where = pl.ds(aligned(index * TILE, TILE), TILE)
        field = du[where, :] - grad_bias / count - xhat[where, :] * (grad_gain / count)
        back_three[where, :] += valid(where) * gain * inv * field
        return carry

    lax.fori_loop(0, pixels // TILE, last_back, 0)
    loads.leave(back_three, cells_out)
    while background:
        progress()
    loads.finish()


def gather_pieces_job(net, part, outs):
    core = net.bit(0)
    _, per_shard, size, _ = part.shape
    rows = outs[0].shape[0]
    halvings = [halving(net, order, rows) for order in (net.bits, net.bits[::-1])]

    def lanes(block):
        return pl.ds(aligned((2 * block + core) * LANES, LANES), LANES)

    own = []
    for which, out in enumerate(outs):
        base = halvings[which][1]
        for block in range(per_shard):
            own.append(net.own(part.at[which, block], out.at[pl.ds(aligned(base, 8), size), lanes(block)]))
            own[-1].start()
    for one in own:
        one.wait()
    for back_step in range(1, len(net.bits) + 1):
        moves = []
        for which, out in enumerate(outs):
            bit, base, span = halvings[which][0][-back_step]
            here = pl.ds(aligned(base + net.bit(bit) * (span // 2), 8), span // 2)
            for block in range(per_shard):
                piece = out.at[here, lanes(block)]
                moves.append(net.copy(piece, piece, net.across(bit)))
                moves[-1].start()
        yield
        for one in moves:
            one.wait()
    moves = []
    for out in outs:
        for block in range(per_shard):
            piece = out.at[:, lanes(block)]
            moves.append(net.copy(piece, piece, net.across(0)))
            moves[-1].start()
    yield
    for one in moves:
        one.wait()


def last(mesh, tables, dconv, xf, kf, mask, x, hidden, point_one, params, total_one, back_three, part, point_grad):
    dp, rows = mesh
    lines, _, channels = dconv.shape
    pixels = lines * SLOTS
    blocks = channels // LANES
    unit = 8 * dp * rows
    tap_rows = -(-SPAN * SPAN // unit) * unit
    constants = [
        jnp.asarray(split_constant(slots_to_freq(), 2)),
        jnp.asarray(split_constant(freq_to_slots(), 2)),
        jnp.asarray(split_constant(freq_to_taps(), 3)),
    ]

    def pair(*dims):
        return [pltpu.VMEM(dims, BF16)] * 2

    halves = 2 if channels // (dp * rows) % 8 == 0 else 1
    one_part = [pltpu.VMEM((channels, channels // halves), F32)] * halves
    field = pltpu.VMEM((pixels, channels), F32)
    square = pltpu.VMEM((channels, channels), F32)
    scratch = [
        pltpu.VMEM(dconv.shape, F32),
        pltpu.VMEM(mask.shape, F32),
        field,
        field,
        square,
        field,
        pltpu.VMEM(part.shape, F32),
        square,
        pltpu.SemaphoreType.DMA((16,)),
        pltpu.VMEM((8, LANES), F32),
        sum_scratch(mesh, 8),
        pltpu.SemaphoreType.DMA((4,)),
        pltpu.VMEM((blocks, WINDOW_PAD, SLOTS, LANES), F32),
        pltpu.VMEM((blocks, WINDOW_PAD, FREQ, LANES), F32),
        [pltpu.VMEM((ZERO_ROW + 1, FREQ, LANES), F32)] * 2,
        [pltpu.VMEM((TAP_ROWS, FREQ, LANES), F32)] * 2,
        pltpu.VMEM((SPAN, FREQ, LANES), F32),
        pltpu.VMEM((lines, FREQ, LANES), F32),
        pltpu.VMEM((blocks // 2, tap_rows, 2 * LANES), F32),
        [pltpu.VMEM((tap_rows, 2 * LANES), F32)] * (blocks // 2),
        pltpu.VMEM((SPAN, SPAN, channels), F32),
        pair(channels, pixels),
        pair(channels, channels),
        pair(pixels, channels),
        field,
        one_part,
        one_part,
        square,
        square,
        square,
        all_scratch(mesh, channels, channels),
        [all_scratch(mesh, channels, channels // halves)] * halves,
        [all_scratch(mesh, tap_rows, 2 * LANES)] * (blocks // 2),
    ]
    smem = pl.BlockSpec(memory_space=pltpu.SMEM)
    return exchange(
        "last",
        3,
        mesh,
        last_kernel,
        (*tables, dconv, xf, kf, mask, x, hidden, point_one, params, total_one, back_three, part, point_grad, *constants),
        [smem] * 2 + [HBM] * 7 + [VMEM] * 2 + [HBM] * 3 + [VMEM] * 3,
        [shape(pixels, channels), shape(8, LANES)] + [shape(channels, channels)] * 4 + [shape(SPAN, SPAN, channels)],
        [HBM, VMEM] + [HBM] * 5,
        scratch,
        60,
        late=True,
    )


def first_kernel(
    net,
    value,
    names,
    x_in,
    up_in,
    down_in,
    point_in,
    big_in,
    small,
    mask_in,
    params,
    to_freq,
    taps_freq,
    to_slots,
    hidden_out,
    wall,
    xf_out,
    kf_out,
    conv_out,
    conv_sums,
    total,
    row_table,
    tap_table,
    x,
    up,
    down,
    point_one,
    big,
    taps,
    mask,
    load_sem,
    sums_slots,
    got_names,
    name_rows,
    u_pair,
    point_pair,
    hidden,
    act,
    window,
    xf,
    kf,
    yf,
    conv,
):
    rows, _, channels = act.shape
    pixels = rows * SLOTS
    blocks = channels // LANES
    gain, bias = params[0:1, :], params[1:2, :]
    loads = Loads(load_sem)
    came_up = loads.start(up_in, up)
    came_down = loads.start(down_in, down)
    came_x = loads.start(x_in, x)
    came_point = loads.start(point_in, point_one)
    came_mask = loads.start(mask_in, mask)
    came_taps = loads.start(big_in, big)
    net.ready()
    sums = all_sum_job(net, value, total, *sums_slots)
    next(sums)
    below, above = net.z < net.rows - 1, net.z > 0
    name_moves = [
        (net.copy(names.at[1], got_names.at[0], net.line(1)), below, above),
        (net.copy(names.at[2], got_names.at[1], net.line(net.rows - 1)), above, below),
    ]
    for one, goes, _ in name_moves:
        pl.when(goes)(one.start)

    @pl.when(net.z == 0)
    def _():
        got_names[0] = jnp.zeros(got_names.shape[1:], jnp.int32)

    @pl.when(net.z == net.rows - 1)
    def _():
        got_names[1] = jnp.zeros(got_names.shape[1:], jnp.int32)

    came_up.wait()
    came_down.wait()

    background = [weights_line_job(net, up, down, wall, range(1, net.rows - 1))]

    def progress():
        background[:] = [job for job in background if next(job, StopIteration) is not StopIteration]

    progress()
    next(sums)
    came_point.wait()
    store_split(point_pair, Ellipsis, point_one[...])
    came_x.wait()
    came_mask.wait()
    finish(sums)
    mean, inv = norm_terms(total, read_count(total))

    def first_norm(index, carry):
        where = pl.ds(aligned(index * LANES, LANES), LANES)
        m = jnp.concatenate([mask[where, :]] * blocks, axis=1)
        store_split(u_pair, where, ((x[where, :] - mean) * inv * gain + bias) * m)
        return carry

    lax.fori_loop(0, pixels // LANES, first_norm, 0)
    waits = []
    for half in range(blocks // 2):
        lanes = slice(half * 2 * LANES, (half + 1) * 2 * LANES)
        for tile in range(pixels // TILE):
            where = slice(tile * TILE, (tile + 1) * TILE)
            pre = dot_split(
                (u_pair[0][where, :], u_pair[1][where, :]), (point_pair[0][:, lanes], point_pair[1][:, lanes])
            )
            hidden[where, lanes] = pre
            act[where.start // SLOTS : where.stop // SLOTS, :, lanes] = gelu_parts(pre)[0].reshape(
                TILE // SLOTS, SLOTS, 2 * LANES
            )
        waits += [start_halo(net, act, window, index) for index in (2 * half, 2 * half + 1)]
    progress()
    near = weights_layer_job(net, wall, (1,))
    next(near)
    loads.leave(hidden, hidden_out)
    came_taps.wait()
    taps[...] = jnp.zeros(taps.shape, F32)
    taps[:SPAN, :SPAN, :] = big[...]
    small_span = small.shape[0]
    middle_taps = slice(REACH - small_span // 2, REACH + small_span // 2 + 1)
    taps[middle_taps, middle_taps, :] = big[middle_taps, middle_taps, :] + small[...]
    group = taps_freq.shape[0] // FREQ
    for index in range(blocks):
        for first in range(0, taps.shape[0], group):
            part = taps[first : first + group, :, index * LANES : (index + 1) * LANES]
            freq = product_split(taps_freq, part.reshape(group * SPAN_PAD, LANES))
            kf[index][first : first + group] = freq.reshape(group, FREQ, LANES)
        loads.leave(kf[index], kf_out.at[index])
    for one, goes, comes in name_moves:
        pl.when(comes)(one.wait_recv)
        pl.when(goes)(one.wait_send)
    moved = [loads.start(src, name_rows.at[k]) for k, src in enumerate((names.at[0], got_names.at[0], got_names.at[1]))]
    for one in moved:
        one.wait()
    list_rows(rows, name_rows, row_table, tap_table)
    next(near, None)
    sums = [jnp.zeros((1, LANES), F32)] * 2 * blocks
    for index in range(blocks):
        lanes = slice(index * LANES, (index + 1) * LANES)
        waits[index]()
        transform(window.at[index], to_freq, xf[index], to_freq.shape[0] // FREQ)
        loads.leave(xf[index].at[pl.ds(0, ZERO_ROW + 1)], xf_out.at[index])
        sum_table(row_table, rows, xf[index], kf[index], yf, False)
        group = to_slots.shape[0] // SLOTS
        for first in range(0, rows, group):
            where = slice(first * SLOTS, (first + group) * SLOTS)
            cells = product_split(to_slots, yf[first : first + group].reshape(group * FREQ, LANES)) * mask[where, :]
            conv[where, lanes] = cells
            sums[2 * index] = sums[2 * index] + column_sum(cells)
            sums[2 * index + 1] = sums[2 * index + 1] + column_sum(cells * cells)
    loads.leave(conv, conv_out)
    for index in range(blocks):
        conv_sums[index : index + 1, :] = sums[2 * index]
        conv_sums[4 + index : 5 + index, :] = sums[2 * index + 1]
    finish(near)
    while background:
        progress()
    loads.finish()


def list_rows(rows, names, row_table, tap_table):
    for side in range(2):

        def name(w):
            return names[0, side, w] + names[1, side, w] + names[2, side, w]

        def one_row(row, carry):
            at = row + REACH
            own = name(at)

            def count(first):
                same = jnp.int32(0)
                for k in range(REACH):
                    same = same + jnp.where(name(first + k) == own, 1, 0)
                return same

            low = at - count(row)
            high = jnp.where(own > 0, at + 1 + count(at + 1), low)
            for tap in range(LEFT_TAPS):
                row_table[side * rows + row, tap] = jnp.where(low + tap < high, low + tap, ZERO_ROW)
            for tap in range(SPAN):
                w = row + tap
                tap_table[side * SPAN + tap, row] = jnp.where((w >= low) & (w < high), w, ZERO_ROW)
            return carry

        lax.fori_loop(0, rows, one_row, 0)


def read_count(total):
    return jnp.concatenate([total[8 + row : 9 + row, :] for row in range(4)], axis=1)


def first(mesh, value, names, x, up, down, point_one, big, small, mask, params):
    dp, devices = mesh
    pixels, channels = x.shape
    lines = pixels // SLOTS
    blocks = channels // LANES
    constants = [
        jnp.asarray(split_constant(slots_to_freq(), 2)),
        jnp.asarray(split_constant(taps_to_freq(), 4)),
        jnp.asarray(split_constant(freq_to_slots(), 2)),
    ]

    def pair(*dims):
        return [pltpu.VMEM(dims, BF16)] * 2

    field = pltpu.VMEM((pixels, channels), F32)
    scratch = [
        field,
        pltpu.VMEM(up.shape, F32),
        pltpu.VMEM(down.shape, F32),
        pltpu.VMEM(point_one.shape, F32),
        pltpu.VMEM(big.shape, F32),
        pltpu.VMEM((TAP_ROWS, SPAN_PAD, channels), F32),
        pltpu.VMEM(mask.shape, F32),
        pltpu.SemaphoreType.DMA((24,)),
        sum_scratch(mesh, value.shape[0]),
        pltpu.VMEM((2, 8, LANES), jnp.int32),
        pltpu.SMEM((3, 8, LANES), jnp.int32),
        pair(pixels, channels),
        pair(channels, channels),
        field,
        pltpu.VMEM((lines, SLOTS, channels), F32),
        pltpu.VMEM((blocks, WINDOW_PAD, SLOTS, LANES), F32),
        [pltpu.VMEM((WINDOW_PAD, FREQ, LANES), F32)] * blocks,
        [pltpu.VMEM((TAP_ROWS, FREQ, LANES), F32)] * blocks,
        pltpu.VMEM((lines, FREQ, LANES), F32),
        field,
    ]
    smem = pl.BlockSpec(memory_space=pltpu.SMEM)
    return exchange(
        "first",
        0,
        mesh,
        first_kernel,
        (value, names, x, up, down, point_one, big, small, mask, params, *constants),
        [VMEM, VMEM] + [HBM] * 5 + [VMEM, HBM] + [VMEM] * 4,
        [
            shape(pixels, channels),
            shape(devices, 2, *up.shape),
            shape(blocks, ZERO_ROW + 1, FREQ, LANES),
            shape(blocks, TAP_ROWS, FREQ, LANES),
            shape(pixels, channels),
            shape(8, LANES),
            shape(*value.shape),
            jax.ShapeDtypeStruct((2 * lines, LANES), jnp.int32),
            jax.ShapeDtypeStruct((2 * SPAN, LANES), jnp.int32),
        ],
        [HBM] * 5 + [VMEM] * 2 + [smem] * 2,
        scratch,
        60,
        late=True,
    )


def begin_kernel(place, id_lanes, inputs, grads, x, gy, mask, value):
    rows = x.shape[0] // SLOTS
    columns = id_lanes.shape[0] // rows
    blocks = x.shape[1] // LANES

    def one_row(row, sums):
        sums = list(sums)
        for side, (start, width) in enumerate(((0, LEFT), (LEFT, RIGHT))):
            name, at = place[2 * side, row], place[2 * side + 1, row]
            pixel = row * columns + at
            slots = pl.ds(row * SLOTS + start, width)
            own = jnp.where(name < 0, -9, name).astype(F32)
            m = jnp.where(id_lanes[pl.ds(pixel, width), :] == own, 1.0, 0.0)
            mask[slots, :] = m
            sums[-1] = sums[-1] + column_sum(m)
            for block in range(blocks):
                lanes = slice(block * LANES, (block + 1) * LANES)
                cells = pl.ds(pixel * blocks + block, width, stride=blocks)
                v = inputs[cells, :] * m
                x[slots, lanes] = v
                gy[slots, lanes] = grads[cells, :] * m
                sums[block] = sums[block] + column_sum(v)
                sums[blocks + block] = sums[blocks + block] + column_sum(v * v)
        return tuple(sums)

    sums = lax.fori_loop(0, rows, one_row, (jnp.zeros((1, LANES), F32),) * (2 * blocks + 1))
    for row in range(2 * blocks):
        value[row : row + 1, :] = sums[row]
    for row in range(blocks):
        value[2 * blocks + row : 2 * blocks + row + 1, :] = sums[-1]
    value[3 * blocks :, :] = jnp.zeros((value.shape[0] - 3 * blocks, LANES), F32)


def begin(place, id_lanes, inputs, grads, rows, channels):
    return pl.pallas_call(
        begin_kernel,
        out_shape=[
            shape(rows * SLOTS, channels),
            shape(rows * SLOTS, channels),
            shape(rows * SLOTS, LANES),
            shape(16, LANES),
        ],
        in_specs=[pl.BlockSpec(memory_space=pltpu.SMEM)] + [VMEM] * 3,
        out_specs=[VMEM] * 4,
        compiler_params=pltpu.CompilerParams(vmem_limit_bytes=16 << 20),
        name="begin",
    )(place, id_lanes, inputs, grads)


def finish_kernel(
    place,
    inputs,
    grads,
    delta_in,
    cells_in,
    one_in,
    two_in,
    up_in,
    down_in,
    cube_in,
    total_three,
    total_two,
    total_one,
    output,
    grad_input,
    one_out,
    two_out,
    up_out,
    down_out,
    cube_out,
    small,
    *rest,
):
    vectors, (field, field_back, delta, cells, squares, cube, sems) = rest[:6], rest[6:]
    rows = delta.shape[0] // SLOTS
    blocks = delta.shape[1] // LANES
    columns = field.shape[0] // rows // blocks
    loads = Loads(sems)
    came = [[loads.start(inputs, field), loads.start(delta_in, delta)], [loads.start(grads, field_back), loads.start(cells_in, cells)]]
    through = [
        (loads.start(src, middle), middle, out)
        for src, middle, out in zip(
            (one_in, two_in, up_in, down_in, cube_in), (*squares, cube), (one_out, two_out, up_out, down_out, cube_out)
        )
    ]
    for copies, whole, part, out in zip(came, (field, field_back), (delta, cells), (output, grad_input)):
        for one in copies:
            one.wait()

        def one_row(row, carry):
            for side, (start, width) in enumerate(((0, LEFT), (LEFT, RIGHT))):
                pixel = row * columns + place[2 * side + 1, row]
                slots = pl.ds(row * SLOTS + start, width)
                for block in range(blocks):
                    where = pl.ds(pixel * blocks + block, width, stride=blocks)
                    whole[where, :] = whole[where, :] + part[slots, block * LANES : (block + 1) * LANES]
            return carry

        lax.fori_loop(0, rows, one_row, 0)
        loads.leave(whole, out)
    for one, middle, out in through:
        one.wait()
        loads.leave(middle, out)
    first = REACH - small.shape[0] // 2
    last = first + small.shape[0]
    small[...] = cube[first:last, first:last, :]
    for which, total in enumerate((total_one, total_two, total_three)):
        for out, value in zip(vectors[2 * which : 2 * which + 2], read_sums(total)):
            out[...] = value
    loads.finish()


def place_results(place, inputs, grads, delta, cells, squares, cube, totals, small_span):
    channels = delta.shape[1]
    square = pltpu.VMEM((channels, channels), F32)
    return pl.pallas_call(
        finish_kernel,
        out_shape=[shape(*inputs.shape)] * 2
        + [shape(channels, channels)] * 4
        + [shape(*cube.shape), shape(small_span, small_span, channels)]
        + [shape(1, channels)] * 6,
        in_specs=[pl.BlockSpec(memory_space=pltpu.SMEM)] + [HBM] * 9 + [VMEM] * 3,
        out_specs=[HBM] * 7 + [VMEM] * 7,
        scratch_shapes=[
            pltpu.VMEM(inputs.shape, F32),
            pltpu.VMEM(inputs.shape, F32),
            pltpu.VMEM(delta.shape, F32),
            pltpu.VMEM(delta.shape, F32),
            [square] * 4,
            pltpu.VMEM(cube.shape, F32),
            pltpu.SemaphoreType.DMA((16,)),
        ],
        compiler_params=pltpu.CompilerParams(vmem_limit_bytes=60 << 20),
        name="finish",
    )(place, inputs, grads, delta, cells, *squares, cube, *totals)


def shards(
    dp,
    devices_rows,
    inputs,
    image_ids,
    first_norm_gain,
    first_norm_bias,
    point_one,
    kernel_big,
    kernel_small,
    second_norm_gain,
    second_norm_bias,
    point_two,
    feedforward_norm_gain,
    feedforward_norm_bias,
    w_up,
    w_down,
    out_grad,
):
    rows, canvases, columns, channels = inputs.shape
    assert canvases == 1 and kernel_big.shape[0] == SPAN
    pixels = rows * SLOTS
    ids = image_ids[:, 0]
    mesh = (dp, devices_rows)

    place = jnp.arange(columns, dtype=jnp.int32)[None, :]
    is_left = (ids >= 0) & (ids < LEFT_IDS)
    is_right = ids >= LEFT_IDS

    def side(member, width):
        name = jnp.max(jnp.where(member, ids, -1), axis=1)
        first = jnp.min(jnp.where(member, place, columns), axis=1)
        return name, jnp.minimum(first, columns - width)

    left_id, left_at = side(is_left, LEFT)
    right_id, right_at = side(is_right, RIGHT)
    spot = jnp.stack([left_id, left_at, right_id, right_at])
    lines = (rows * columns * channels // LANES, LANES)
    id_lanes = jnp.broadcast_to(ids.reshape(rows * columns, 1).astype(F32), (rows * columns, LANES))
    x, gy, mask_lanes, value = begin(spot, id_lanes, inputs.reshape(lines), out_grad.reshape(lines), rows, channels)
    names = jnp.stack([left_id, right_id]) + 1

    def name_tile(first, last, lane):
        return jnp.pad(names[:, first:last], ((0, 6), (lane, LANES - lane - (last - first))))

    names = jnp.stack(
        [
            name_tile(0, rows, REACH),
            name_tile(rows - REACH, rows, 0),
            name_tile(0, REACH, REACH + rows),
        ]
    )
    vectors = [
        first_norm_gain,
        first_norm_bias,
        second_norm_gain,
        second_norm_bias,
        feedforward_norm_gain,
        feedforward_norm_bias,
    ]
    params = jnp.stack(vectors + [jnp.zeros((channels,), F32)] * 2)
    hidden, wall, xf, kf, conv, conv_sums, total_one, *tables = first(
        mesh,
        value,
        names,
        x,
        w_up,
        w_down,
        point_one,
        kernel_big,
        kernel_small,
        mask_lanes,
        params,
    )
    delta, back_three, total_four, total_five, dconv, point_grad, part, _ = middle(
        mesh, conv, conv_sums, x, gy, mask_lanes, params, total_one, point_two, wall
    )
    cells, total, grad_point_one, grad_point_two, grad_up, grad_down, grad_kernel = last(
        mesh,
        tables,
        dconv,
        xf,
        kf,
        mask_lanes,
        x,
        hidden,
        point_one,
        params,
        total_one,
        back_three,
        part,
        point_grad,
    )
    squares = (grad_point_one, grad_point_two, grad_up, grad_down)
    output, grad_input, grad_point_one, grad_point_two, grad_up, grad_down, grad_kernel, grad_small, *vectors = place_results(
        spot,
        inputs.reshape(lines),
        out_grad.reshape(lines),
        delta,
        cells,
        squares,
        grad_kernel,
        (total_four, total_five, total),
        kernel_small.shape[0],
    )
    vectors = [vector.reshape(channels) for vector in vectors]
    grad_bias_one, grad_gain_one, grad_bias_two, grad_gain_two, grad_bias_three, grad_gain_three = vectors
    return (
        output.reshape(inputs.shape),
        grad_input.reshape(inputs.shape),
        grad_gain_one,
        grad_bias_one,
        grad_point_one,
        grad_kernel,
        grad_small,
        grad_gain_two,
        grad_bias_two,
        grad_point_two,
        grad_gain_three,
        grad_bias_three,
        grad_up,
        grad_down,
    )


def solution(mesh):
    field = P("rows", "dp", None, None)
    everywhere = P()
    up, down = P(None, "rows"), P("rows", None)
    return jax.shard_map(
        functools.partial(shards, mesh.shape["dp"], mesh.shape["rows"]),
        mesh=mesh,
        in_specs=(field, P("rows", "dp", None)) + (everywhere,) * 10 + (up, down, field),
        out_specs=(field, field) + (everywhere,) * 10 + (up, down),
        check_vma=False,
    )
```

```python
import functools

import jax
import jax.numpy as jnp
import numpy as np
from jax import lax
from jax.experimental import pallas as pl
from jax.experimental.pallas import tpu as pltpu
from jax.sharding import PartitionSpec as P

EPSILON = 1e-05
HIGHEST = lax.Precision.HIGHEST
HIGH = lax.Precision.HIGH
MESH = pl.DeviceIdType.MESH
F32 = jnp.float32
BF16 = jnp.bfloat16

LEFT, RIGHT = 24, 16
SLOTS = LEFT + RIGHT
LEFT_IDS = 3
LEFT_N, RIGHT_N = 37, 27
LEFT_F, RIGHT_F = 24, 16
FREQ = 2 * LEFT_F + 2 * RIGHT_F
REACH = 13
SPAN = 2 * REACH + 1
SPAN_PAD = 32
LANES = 128


def forward_transform(length, padded, positions, columns):
    count = length // 2 + 1
    out = np.zeros((2 * padded, columns))
    angle = 2 * np.pi * np.outer(np.arange(count), positions) / length
    out[:count, : len(positions)] = np.cos(angle)
    out[padded : padded + count, : len(positions)] = -np.sin(angle)
    return out


def backward_transform(length, padded, positions, rows):
    count = length // 2 + 1
    out = np.zeros((rows, 2 * padded))
    twice = np.where(np.arange(count) == 0, 1.0, 2.0)
    angle = 2 * np.pi * np.outer(positions, np.arange(count)) / length
    out[: len(positions), :count] = np.cos(angle) * twice / length
    out[: len(positions), padded : padded + count] = -np.sin(angle) * twice / length
    return out


def slots_to_freq():
    out = np.zeros((FREQ, SLOTS))
    out[: 2 * LEFT_F, :LEFT] = forward_transform(LEFT_N, LEFT_F, np.arange(LEFT), LEFT)
    out[2 * LEFT_F :, LEFT:] = forward_transform(RIGHT_N, RIGHT_F, np.arange(RIGHT), RIGHT)
    return out


def freq_to_slots():
    out = np.zeros((SLOTS, FREQ))
    out[:LEFT, : 2 * LEFT_F] = backward_transform(LEFT_N, LEFT_F, np.arange(LEFT), LEFT)
    out[LEFT:, 2 * LEFT_F :] = backward_transform(RIGHT_N, RIGHT_F, np.arange(RIGHT), RIGHT)
    return out


def taps_to_freq():
    taps = np.arange(SPAN) - REACH
    return np.concatenate(
        [
            forward_transform(LEFT_N, LEFT_F, taps, SPAN_PAD),
            forward_transform(RIGHT_N, RIGHT_F, taps, SPAN_PAD),
        ]
    )


def freq_to_taps():
    taps = np.arange(SPAN) - REACH
    return np.concatenate(
        [
            backward_transform(LEFT_N, LEFT_F, taps, SPAN_PAD),
            backward_transform(RIGHT_N, RIGHT_F, taps, SPAN_PAD),
        ],
        axis=1,
    )


def split_constant(matrix, group):
    whole = np.kron(np.eye(group), matrix).astype(np.float32)
    high = whole.astype(jnp.bfloat16)
    low = (whole - high.astype(np.float32)).astype(jnp.bfloat16)
    return np.concatenate([high, high, low], axis=1)


def split_stack(value):
    high = value.astype(BF16)
    low = (value - high.astype(F32)).astype(BF16)
    return jnp.concatenate([high, low, high], axis=0)


def product_split(constant_ref, value):
    return jnp.dot(constant_ref[...], split_stack(value), preferred_element_type=F32)


TAP_ROWS = 28


class Net:
    def __init__(self, dp, rows, send_sem, recv_sem):
        self.count, self.rows = dp, rows
        self.send_sem, self.recv_sem, self.used = send_sem, recv_sem, 0
        self.dp = lax.axis_index("dp")
        self.z = lax.axis_index("rows")
        self.bits = list(range(1, dp.bit_length() - 1))

    def bit(self, index):
        return lax.rem(self.dp // (1 << index), 2)

    def across(self, index):
        return (self.dp + (1 << index) * (1 - 2 * self.bit(index)), self.z)

    def line(self, step):
        return (self.dp, lax.rem(self.z + step, self.rows))

    def layer(self, step):
        return (lax.rem(self.dp + step, self.count), self.z)

    def greet(self):
        barrier = pltpu.get_barrier_semaphore()

        def greet_line(step, carry):
            pl.semaphore_signal(barrier, inc=1, device_id=self.line(step), device_id_type=MESH)
            return carry

        def greet_layer(step, carry):
            pl.semaphore_signal(barrier, inc=1, device_id=self.layer(step), device_id_type=MESH)
            return carry

        lax.fori_loop(1, self.rows, greet_line, 0)
        lax.fori_loop(1, self.count, greet_layer, 0)

    def ready(self):
        pl.semaphore_wait(pltpu.get_barrier_semaphore(), self.rows + self.count - 2)

    def copy(self, src, dst, device):
        made = pltpu.make_async_remote_copy(
            src_ref=src,
            dst_ref=dst,
            send_sem=self.send_sem.at[self.used],
            recv_sem=self.recv_sem.at[self.used],
            device_id=device,
            device_id_type=MESH,
        )
        self.used += 1
        return made

    def reserve(self, number):
        self.used += number
        return self.used - number

    def copy_at(self, index, src, dst, device):
        return pltpu.make_async_remote_copy(
            src_ref=src,
            dst_ref=dst,
            send_sem=self.send_sem.at[index],
            recv_sem=self.recv_sem.at[index],
            device_id=device,
            device_id_type=MESH,
        )

    def own(self, src, dst):
        made = pltpu.make_async_copy(src, dst, self.recv_sem.at[self.used])
        self.used += 1
        return made


def all_sum_job(net, value, out, line_slots, part, layer_slots):
    own = net.own(value, line_slots.at[net.z])
    own.start()
    sent = [net.copy(value, line_slots.at[net.z], net.line(s)) for s in range(1, net.rows)]
    for one in sent:
        one.start()
    yield
    own.wait()
    for one in sent:
        one.wait()
    total = line_slots[0]
    for index in range(1, net.rows):
        total = total + line_slots[index]
    part[...] = total
    own = net.own(part, layer_slots.at[net.dp])
    own.start()
    sent = [net.copy(part, layer_slots.at[net.dp], net.layer(s)) for s in range(1, net.count)]
    for one in sent:
        one.start()
    yield
    own.wait()
    for one in sent:
        one.wait()
    total = layer_slots[0]
    for index in range(1, net.count):
        total = total + layer_slots[index]
    out[...] = total


def aligned(value, unit):
    return pl.multiple_of(value, unit)


def halving(net, order, rows):
    base, steps = 0, []
    for bit in order:
        steps.append((bit, base, rows))
        rows //= 2
        base = base + net.bit(bit) * rows
    return steps, base, rows


def add_rows(dst, src, count, step):
    def one(i, carry):
        at = aligned(i * step, step)
        to, of = dst(at), src(at)
        to[...] = to[...] + of[...]
        return carry

    lax.fori_loop(0, count // step, one, 0)


def run(*jobs):
    jobs = list(jobs)
    while jobs:
        jobs = [job for job in jobs if next(job, StopIteration) is not StopIteration]


def sides(net, rows):
    core = net.bit(0)
    return [
        (pl.ds(aligned((2 * core + side) * LANES, LANES), LANES), *halving(net, order, rows))
        for side, order in enumerate((net.bits, net.bits[::-1]))
    ]


def weights_line_job(net, up, down, wall, distances):
    own = [net.own(up, wall.at[net.z, 0]), net.own(down, wall.at[net.z, 1])] if 1 in distances else []
    last = net.rows - 1
    for step in distances:
        moves = []
        for lanes, _, base, rows in sides(net, wall.shape[2]):
            mine = pl.ds(aligned(base, 8), rows)
            for way in (1, -1):
                shard = net.z - way * (step - 1)
                going = (net.z >= step - 1) & (net.z < last) if way > 0 else (net.z <= last - (step - 1)) & (net.z > 0)
                coming = net.z >= step if way > 0 else net.z <= last - step
                shard = lax.rem(shard + net.rows, net.rows)
                for which in range(2):
                    piece = wall.at[shard, which, mine, lanes]
                    source = (up, down)[which].at[mine, lanes] if step == 1 else piece
                    one = net.copy(source, piece, net.line(way % net.rows))
                    pl.when(going)(one.start)
                    moves.append((one, going, coming))
        if step == 1:
            for one in own:
                one.start()
        yield
        for one, going, coming in moves:
            pl.when(coming)(one.wait_recv)
            pl.when(going)(one.wait_send)
    for one in own:
        one.wait()


def weights_layer_job(net, wall, distances):
    parts = sides(net, wall.shape[2])
    shards = [net.z + way * distance for distance in distances for way in (1, -1)]
    shards = [(lax.rem(shard + net.rows, net.rows), (shard >= 0) & (shard < net.rows)) for shard in shards]
    for back in range(1, len(net.bits) + 1):
        moves = []
        for lanes, steps, _, _ in parts:
            bit, base, rows = steps[-back]
            mine = pl.ds(aligned(base + net.bit(bit) * (rows // 2), 8), rows // 2)
            for shard, there in shards:
                piece = wall.at[shard, :, mine, lanes]
                moves.append((net.copy(piece, piece, net.across(bit)), there))
        for one, there in moves:
            pl.when(there)(one.start)
        yield
        for one, there in moves:
            pl.when(there)(one.wait)


def weights_pair_job(net, wall):
    half = wall.shape[3] // 2
    lanes = pl.ds(aligned(net.bit(0) * half, LANES), half)
    moves = []
    for step in range(1, net.rows):
        piece = wall.at[lax.rem(net.z + step, net.rows), :, :, lanes]
        moves.append(net.copy(piece, piece, net.across(0)))
    for one in moves:
        one.start()
    yield
    for one in moves:
        one.wait()


def halo_job(net, field, window, zeros):
    rows = field.shape[0]
    own = net.own(field, window.at[pl.ds(REACH, rows)])
    own.start()
    has_above, has_below = net.z > 0, net.z < net.rows - 1
    down = net.copy(field.at[pl.ds(rows - REACH, REACH)], window.at[pl.ds(0, REACH)], net.line(1))
    up = net.copy(field.at[pl.ds(0, REACH)], window.at[pl.ds(REACH + rows, REACH)], net.line(net.rows - 1))
    pl.when(has_below)(down.start)
    pl.when(has_above)(up.start)
    zeros[...] = jnp.zeros(zeros.shape, F32)
    top = net.own(zeros, window.at[pl.ds(0, REACH)])
    bottom = net.own(zeros, window.at[pl.ds(REACH + rows, REACH)])
    pl.when(jnp.logical_not(has_above))(top.start)
    pl.when(jnp.logical_not(has_below))(bottom.start)
    yield
    own.wait()
    pl.when(jnp.logical_not(has_above))(top.wait)
    pl.when(jnp.logical_not(has_below))(bottom.wait)
    pl.when(has_above)(down.wait_recv)
    pl.when(has_below)(down.wait_send)
    pl.when(has_below)(up.wait_recv)
    pl.when(has_above)(up.wait_send)


def shares(net, rows, width):
    core, out = net.bit(0), []
    by_rows = width == 2 * LANES
    for side, order in enumerate((net.bits, net.bits[::-1])):
        start = side * (rows // 2) if by_rows else 0
        steps, base, size = halving(net, order, rows // 2 if by_rows else rows)
        steps = [(bit, start + first, count) for bit, first, count in steps]
        block = 0 if by_rows else side
        outer = pl.ds(aligned((core if by_rows else 2 * core + side) * LANES, LANES), LANES)
        out.append((pl.ds(block * LANES, LANES), outer, steps, start + base, size))
    return out


def corners(net, steps):
    (first, base, size), (second, _, _) = steps
    one, two = net.bit(first), net.bit(second)
    found = []
    for turn_one, turn_two in ((1, 0), (0, 1), (1, 1)):
        step_one, step_two = turn_one * (1 - 2 * one), turn_two * (1 - 2 * two)
        place = base + (one + step_one) * (size // 2) + (two + step_two) * (size // 4)
        found.append((place, (net.dp + (1 << first) * step_one + (1 << second) * step_two, net.z)))
    return found


def reduce_all_job(net, source, acc, got_pair, got, got_line, out):
    rows, width = source.shape
    half = width // 2
    core = net.bit(0)
    own = net.own(source.at[:, pl.ds(aligned(core * half, LANES), half)], acc)
    sent = net.copy(source.at[:, pl.ds(aligned((1 - core) * half, LANES), half)], got_pair, net.across(0))
    own.start()
    sent.start()
    yield
    own.wait()
    sent.wait()
    add_rows(lambda at: acc.at[pl.ds(at, 64)], lambda at: got_pair.at[pl.ds(at, 64)], rows, 64)
    parts = shares(net, rows, width)
    direct = len(net.bits) == 2
    if direct:
        moves = []
        for side, (inner, _, steps, _, size) in enumerate(parts):
            for slot, (base, device) in enumerate(corners(net, steps)):
                place = got.at[side, pl.ds(slot * size, size)]
                moves.append(net.copy(acc.at[pl.ds(aligned(base, 8), size), inner], place, device))
                moves[-1].start()
        yield
        for one in moves:
            one.wait()
        for side, (inner, _, _, base, size) in enumerate(parts):
            for slot in range(3):
                add_rows(
                    lambda at: acc.at[pl.ds(aligned(base + at, 8), 8), inner],
                    lambda at: got.at[side, pl.ds(aligned(slot * size + at, 8), 8)],
                    size,
                    8,
                )
    for index in range(0 if direct else len(net.bits)):
        moves = []
        for side, (inner, _, steps, _, _) in enumerate(parts):
            bit, base, size = steps[index]
            size //= 2
            give = base + (1 - net.bit(bit)) * size
            keep = base + net.bit(bit) * size
            place = got.at[side, pl.ds(rows - 2 * size, size)]
            one = net.copy(acc.at[pl.ds(aligned(give, 8), size), inner], place, net.across(bit))
            one.start()
            moves.append((one, keep, size, inner, side))
        yield
        for one, keep, size, inner, side in moves:
            one.wait()
            unit = 64 if size % 64 == 0 else 8
            add_rows(
                lambda at: acc.at[pl.ds(aligned(keep + at, 8), unit), inner],
                lambda at: got.at[side, pl.ds(aligned(rows - 2 * size + at, 8), unit)],
                size,
                unit,
            )
    moves, own = [], []
    for side, (inner, _, _, base, size) in enumerate(parts):
        size //= net.rows
        own.append(net.own(acc.at[pl.ds(aligned(base + net.z * size, 8), size), inner], got_line.at[side, net.z]))
        for step in range(1, net.rows):
            other = lax.rem(net.z + step, net.rows)
            piece = acc.at[pl.ds(aligned(base + other * size, 8), size), inner]
            moves.append(net.copy(piece, got_line.at[side, net.z], net.line(step)))
    for one in own + moves:
        one.start()
    yield
    for one in own + moves:
        one.wait()
    moves = []
    for side, (_, outer, _, base, size) in enumerate(parts):
        size //= net.rows
        total = got_line[side, 0]
        for index in range(1, net.rows):
            total = total + got_line[side, index]
        piece = out.at[pl.ds(aligned(base + net.z * size, 8), size), outer]
        out[pl.ds(aligned(base + net.z * size, 8), size), outer] = total
        for step in range(1, net.rows):
            moves.append(net.copy(piece, piece, net.line(step)))
            moves[-1].start()
    yield
    for one in moves:
        one.wait()
    if direct:
        moves = []
        for _, outer, steps, base, size in parts:
            piece = out.at[pl.ds(aligned(base, 8), size), outer]
            for _, device in corners(net, steps):
                moves.append(net.copy(piece, piece, device))
                moves[-1].start()
        yield
        for one in moves:
            one.wait()
    for back in range(1, 1 if direct else len(net.bits) + 1):
        moves = []
        for _, outer, steps, _, _ in parts:
            bit, base, size = steps[-back]
            piece = out.at[pl.ds(aligned(base + net.bit(bit) * (size // 2), 8), size // 2), outer]
            moves.append(net.copy(piece, piece, net.across(bit)))
            moves[-1].start()
        yield
        for one in moves:
            one.wait()
    piece = out.at[:, pl.ds(aligned(core * half, LANES), half)]
    one = net.copy(piece, piece, net.across(0))
    one.start()
    yield
    one.wait()


VMEM = pl.BlockSpec(memory_space=pltpu.VMEM)
HBM = pl.BlockSpec(memory_space=pltpu.HBM)
COPIES = 448


def shape(*dims):
    return jax.ShapeDtypeStruct(dims, F32)


def exchange(name, number, mesh, body, args, in_specs, outs, out_specs, scratch, limit, aliases=None, late=False):
    dp, rows = mesh

    def kernel(*refs):
        *refs, send_sem, recv_sem = refs
        net = Net(dp, rows, send_sem, recv_sem)
        net.greet()
        if not late:
            net.ready()
        body(net, *refs)
        assert net.used <= COPIES

    return pl.pallas_call(
        kernel,
        out_shape=outs,
        in_specs=in_specs,
        out_specs=out_specs,
        scratch_shapes=scratch + [pltpu.SemaphoreType.DMA((COPIES,))] * 2,
        input_output_aliases=aliases or {},
        compiler_params=pltpu.CompilerParams(
            collective_id=number, has_side_effects=True, vmem_limit_bytes=limit << 20
        ),
        name=name,
    )(*args)


def sum_scratch(mesh, height):
    dp, rows = mesh
    return [pltpu.VMEM((rows, height, LANES), F32), pltpu.VMEM((height, LANES), F32), pltpu.VMEM((dp, height, LANES), F32)]


def all_scratch(mesh, rows, width):
    size = (rows // 2 if width == 2 * LANES else rows) * 2 // mesh[0] // mesh[1]
    return [
        pltpu.VMEM((rows, width // 2), F32),
        pltpu.VMEM((rows, width // 2), F32),
        pltpu.VMEM((2, rows, LANES), F32),
        pltpu.VMEM((2, mesh[1], size, LANES), F32),
    ]


class Loads:
    def __init__(self, sems):
        self.sems, self.used, self.leaving = sems, 0, []

    def start(self, src, dst):
        one = pltpu.make_async_copy(src, dst, self.sems.at[self.used])
        self.used += 1
        one.start()
        return one

    def leave(self, src, dst):
        self.leaving.append(self.start(src, dst))

    def finish(self):
        for one in self.leaving:
            one.wait()


def gelu_parts(x):
    scale, cubic = 0.7978845608028654, 0.044715
    square = x * x
    t = jnp.tanh(scale * (x + cubic * (x * square)))
    half = 0.5 * (1.0 + t)
    return (x * half, half + 0.5 * x * (1.0 - t * t) * (scale * (1.0 + 3.0 * cubic * square)))


NN = (((1,), (0,)), ((), ()))
NT = (((1,), (1,)), ((), ()))
TILE = 320


def split_two(value):
    high = value.astype(BF16)
    return high, (value - high.astype(F32)).astype(BF16)


def store_split(refs, where, value):
    refs[0][where], refs[1][where] = split_two(value)


def dot_split(left, right, dims=NN):
    def one(a, b):
        return lax.dot_general(a, b, dims, preferred_element_type=F32)

    return one(left[0], right[0]) + (one(left[0], right[1]) + one(left[1], right[0]))


def read_pair(refs, where=Ellipsis):
    return refs[0][where], refs[1][where]


def write_sums(value, first, second):
    for row in range(4):
        lanes = slice(row * LANES, (row + 1) * LANES)
        value[row : row + 1, :] = first[:, lanes]
        value[4 + row : 5 + row, :] = second[:, lanes]


def read_sums(total):
    return tuple(
        jnp.concatenate([total[4 * k + row : 4 * k + row + 1, :] for row in range(4)], axis=1) for k in range(2)
    )


def column_sum(value):
    return jnp.sum(value, axis=0, keepdims=True)


def norm_terms(total, count):
    first, second = read_sums(total)
    mean = first / count
    return mean, lax.rsqrt(second / count - mean * mean + EPSILON)


def finish(job):
    for _ in job:
        pass


def rem(value, unit):
    return value % unit if isinstance(value, int) else lax.rem(value, unit)


def middle_kernel(
    net,
    conv_in,
    conv_sums,
    x_in,
    gy_in,
    mask_in,
    params,
    total_one,
    point_in,
    wall_in,
    delta_out,
    back_out,
    total_four,
    total_five,
    dconv_out,
    point_out,
    part,
    wall,
    x,
    gy,
    mask,
    point_two,
    delta,
    back,
    dconv,
    point_grad,
    load_sem,
    sums_own,
    sums_slots,
    own_sem,
    mixed,
    xhat,
    slope_two,
    act_pair,
    u_pair,
    ut_pair,
    g_pair,
    gt_pair,
    point_pair,
    up_pair,
    down_pair,
    hid_pair,
    dpre_pair,
    w_up,
    w_down,
    made,
    acc,
    got_pair,
    got_layer,
    got_line,
):
    pixels, channels = x.shape
    tiles = pixels // TILE
    hidden = w_up.shape[2]
    per_shard = wall.shape[2] // hidden
    chunks = net.rows * per_shard
    core = net.bit(0)
    gain_two, bias_two, gain_three, bias_three = (params[row : row + 1, :] for row in range(2, 6))
    count = read_count(total_one)
    loads = Loads(load_sem)
    came_point = loads.start(point_in, point_two)
    came_gy = loads.start(gy_in, gy)
    came = [loads.start(src, dst) for src, dst in ((conv_in, xhat), (x_in, x), (mask_in, mask))]

    def each_tile(body):
        def one(index, carry):
            return body(pl.ds(aligned(index * TILE, TILE), TILE), carry)

        zero = jnp.zeros((1, channels), F32)
        return lax.fori_loop(0, tiles, one, (zero, zero))

    def valid(rows):
        return jnp.concatenate([mask[rows, :]] * (channels // LANES), axis=1)

    def total_job(which, out):
        return all_sum_job(net, sums_own.at[which], out, *(slots.at[which] for slots in sums_slots))

    def shard_of(chunk):
        return lax.rem(net.z + chunk // per_shard, net.rows)

    def load(chunk):
        slot, shard, part = rem(chunk, 2), shard_of(chunk), rem(chunk, per_shard)
        span = pl.ds(aligned(part * hidden, hidden), hidden)
        return (
            pltpu.make_async_copy(wall.at[shard, 0, :, span], w_up.at[slot], own_sem.at[0, slot]),
            pltpu.make_async_copy(wall.at[shard, 1, span, :], w_down.at[slot], own_sem.at[1, slot]),
        )

    sums_own[0] = conv_sums[...]
    net.ready()
    job = total_job(0, sums_slots[1].at[0])
    next(job)

    far_line = weights_line_job(net, None, None, wall, (net.rows - 1,))
    next(far_line)
    near = weights_layer_job(net, wall, range(2, net.rows - 1))
    next(near, None)
    for one in load(0):
        one.start()
    came_point.wait()
    store_split(point_pair, Ellipsis, point_two[...])
    came_gy.wait()
    store_split(g_pair, Ellipsis, gy[...])
    next(job)
    store_split(gt_pair, Ellipsis, gy[...].T)
    finish(job)
    next(near, None)
    for one in came:
        one.wait()
    mean, inv_two = norm_terms(sums_slots[1].at[0], count)

    def second_norm(rows, carry):
        m = valid(rows)
        hat = (xhat[rows, :] - mean) * inv_two
        act, slope = gelu_parts((hat * gain_two + bias_two) * m)
        xhat[rows, :] = hat
        slope_two[rows, :] = slope * m
        store_split(act_pair, rows, act)
        field = x[rows, :] + dot_split(read_pair(act_pair, rows), read_pair(point_pair))
        mixed[rows, :] = field
        return carry[0] + column_sum(field), carry[1] + column_sum(field * field)

    write_sums(sums_own.at[1], *each_tile(second_norm))
    job = total_job(1, sums_slots[1].at[1])
    next(job)
    finish(far_line)
    far = weights_layer_job(net, wall, (net.rows - 1,))
    next(far)
    next(job)
    finish(job)
    finish(near)
    next(far)
    mean_three, inv_three = norm_terms(sums_slots[1].at[1], count)

    def third_norm(rows, carry):
        hat = (mixed[rows, :] - mean_three) * inv_three
        store_split(u_pair, rows, (hat * gain_three + bias_three) * valid(rows))
        delta[rows, :] = mixed[rows, :] - x[rows, :]
        back[rows, :] = jnp.zeros((TILE, channels), F32)
        return carry

    each_tile(third_norm)
    for side in range(2):
        ut_pair[side][...] = u_pair[side][...].T

    mine = pl.ds(aligned(core * LANES, LANES), LANES)
    other = pl.ds(aligned((1 - core) * LANES, LANES), LANES)
    halvings = [halving(net, order, channels) for order in (net.bits, net.bits[::-1])]
    stages = len(net.bits)
    pair_base = net.reserve(chunks)
    layer_base = net.reserve(2 * stages * chunks)
    line_base = net.reserve(2 * chunks)

    def pair_move(chunk):
        slot = rem(chunk, 2)
        return (
            net.copy_at(pair_base + chunk, made.at[slot, :, :, other], got_pair.at[chunk], net.across(0)),
            pltpu.make_async_copy(made.at[slot, :, :, mine], acc.at[chunk], own_sem.at[2, slot]),
        )

    def layer_move(stage, chunk):
        moves = []
        for side, (steps, _, _) in enumerate(halvings):
            bit, base, size = steps[stage]
            size //= 2
            give, keep = base + (1 - net.bit(bit)) * size, base + net.bit(bit) * size
            place = pl.ds(channels - 2 * size, size)
            moves.append(
                (
                    net.copy_at(
                        layer_base + (2 * stage + side) * chunks + chunk,
                        acc.at[chunk, side, pl.ds(aligned(give, 8), size), :],
                        got_layer.at[chunk, side, place, :],
                        net.across(bit),
                    ),
                    keep,
                    size,
                    side,
                )
            )
        return moves

    def line_move(chunk, remote):
        moves = []
        shard, part = shard_of(chunk), rem(chunk, per_shard)
        for side, (_, base, size) in enumerate(halvings):
            piece = acc.at[chunk, side, pl.ds(aligned(base, 8), size), :]
            place = got_line.at[net.z, part, side]
            if remote:
                moves.append(net.copy_at(line_base + 2 * chunk + side, piece, place, (net.dp, shard)))
            else:
                moves.append(pltpu.make_async_copy(piece, place, net.recv_sem.at[line_base + 2 * chunk + side]))
        return moves

    def when(test, body):
        if isinstance(test, bool):
            if test:
                body()
        else:
            pl.when(test)(body)

    def within(chunk):
        if isinstance(chunk, int):
            return 0 <= chunk < chunks
        return (chunk >= 0) & (chunk < chunks)

    def progress(step):
        def after_pair():
            chunk = step - 1
            sent, own = pair_move(chunk)
            own.wait()
            sent.wait()
            for side in range(2):
                add_rows(
                    lambda at: acc.at[chunk, side, pl.ds(at, 64), :],
                    lambda at: got_pair.at[chunk, side, pl.ds(at, 64), :],
                    channels,
                    64,
                )
            for one, *_ in layer_move(0, chunk):
                one.start()

        def after_layer(stage):
            chunk = step - 2 - stage
            for one, keep, size, side in layer_move(stage, chunk):
                one.wait()
                unit = min(size, 64)
                add_rows(
                    lambda at: acc.at[chunk, side, pl.ds(aligned(keep + at, 8), unit), :],
                    lambda at: got_layer.at[chunk, side, pl.ds(aligned(channels - 2 * size + at, 8), unit), :],
                    size,
                    unit,
                )
            if stage + 1 < stages:
                for one, *_ in layer_move(stage + 1, chunk):
                    one.start()
            else:

                def go(remote):
                    def start():
                        for one in line_move(chunk, remote):
                            one.start()

                    return start

                when(chunk >= per_shard, go(True))
                when(chunk < per_shard, go(False))

        when(within(step - 1), after_pair)
        for stage in range(stages):
            when(within(step - 2 - stage), functools.partial(after_layer, stage))

    def feed_forward(chunk, carry):
        progress(chunk)
        slot = rem(chunk, 2)
        for one in load(chunk):
            one.wait()

        @pl.when((chunk + 1 < chunks) & (chunk + 1 != per_shard))
        def _():
            for one in load(chunk + 1):
                one.start()

        store_split(up_pair, Ellipsis, w_up[slot])
        store_split(down_pair, Ellipsis, w_down[slot])

        def first_half(rows):
            hid, slope = gelu_parts(dot_split(read_pair(u_pair, rows), read_pair(up_pair)))
            store_split(hid_pair, rows, hid)
            store_split(
                dpre_pair, rows, dot_split(read_pair(g_pair, rows), read_pair(down_pair), NT) * slope
            )

        first_half(pl.ds(0, pixels))
        made[slot, 0] = dot_split(read_pair(ut_pair), read_pair(dpre_pair))
        made[slot, 1] = dot_split(read_pair(gt_pair), read_pair(hid_pair))
        for one in pair_move(chunk):
            one.start()

        def second_half(rows):
            delta[rows, :] += dot_split(read_pair(hid_pair, rows), read_pair(down_pair))
            back[rows, :] += dot_split(read_pair(dpre_pair, rows), read_pair(up_pair), NT)

        second_half(pl.ds(0, pixels))
        return carry

    lax.fori_loop(0, per_shard - 1, feed_forward, 0)
    finish(far)
    pairs = weights_pair_job(net, wall)
    next(pairs)
    lax.fori_loop(per_shard - 1, per_shard, feed_forward, 0)
    finish(pairs)
    for one in load(per_shard):
        one.start()
    lax.fori_loop(per_shard, chunks, feed_forward, 0)

    loads.leave(delta, delta_out)

    def third_sums(rows, carry):
        dy = back[rows, :] * valid(rows)
        back[rows, :] = dy
        hat = (mixed[rows, :] - mean_three) * inv_three
        return carry[0] + column_sum(dy), carry[1] + column_sum(dy * hat)

    write_sums(sums_own.at[2], *each_tile(third_sums))
    job = total_job(2, total_four)
    next(job)
    progress(chunks)
    next(job)
    finish(job)
    progress(chunks + 1)
    grad_bias, grad_gain = read_sums(total_four)

    def third_back(rows, carry):
        m = valid(rows)
        hat = (mixed[rows, :] - mean_three) * inv_three
        field = m * gain_three * inv_three * (back[rows, :] - grad_bias / count - hat * (grad_gain / count))
        back[rows, :] = field
        dmixed = gy[rows, :] + field
        store_split(g_pair, rows, dmixed)
        du = dot_split(read_pair(g_pair, rows), read_pair(point_pair), NT) * slope_two[rows, :]
        mixed[rows, :] = du
        return carry[0] + column_sum(du), carry[1] + column_sum(du * xhat[rows, :])

    write_sums(sums_own.at[3], *each_tile(third_back))
    loads.leave(back, back_out)
    job = total_job(3, total_five)
    next(job)
    for step in range(chunks + 2, chunks + 1 + stages):
        progress(step)
    for side in range(2):
        ut_pair[side][...] = act_pair[side][...].T
    next(job)
    point_grad[...] = dot_split(read_pair(ut_pair), read_pair(g_pair))
    loads.leave(point_grad, point_out)
    finish(job)
    grad_bias_two, grad_gain_two = read_sums(total_five)

    def second_back(row, carry):
        rows = pl.ds(aligned(row * SLOTS, 8), SLOTS)
        field = mixed[rows, :] - grad_bias_two / count - xhat[rows, :] * (grad_gain_two / count)
        dconv[row] = valid(rows) * gain_two * inv_two * field
        return carry

    lax.fori_loop(0, pixels // SLOTS, second_back, 0)
    loads.leave(dconv, dconv_out)
    for chunk in range(chunks):
        for one in line_move(chunk, chunk >= per_shard):
            one.wait()
    for which in range(2):
        for block in range(per_shard):
            total = got_line[0, block, which]
            for index in range(1, net.rows):
                total = total + got_line[index, block, which]
            part[which, block] = total
    loads.finish()


def middle(mesh, conv, conv_sums, x, gy, mask, params, total_one, point_two, wall):
    dp, rows = mesh
    pixels, channels = conv.shape
    hidden = 2 * LANES
    chunks = rows * (wall.shape[2] // hidden)
    lines = pixels // SLOTS

    def pair(*dims):
        return [pltpu.VMEM(dims, BF16)] * 2

    piece = channels * 2 // dp
    field = pltpu.VMEM((pixels, channels), F32)
    square = pltpu.VMEM((channels, channels), F32)
    scratch = [
        field,
        field,
        pltpu.VMEM(mask.shape, F32),
        square,
        field,
        field,
        pltpu.VMEM((lines, SLOTS, channels), F32),
        square,
        pltpu.SemaphoreType.DMA((16,)),
        pltpu.VMEM((4, 8, LANES), F32),
        [pltpu.VMEM((4, rows, 8, LANES), F32), pltpu.VMEM((4, 8, LANES), F32), pltpu.VMEM((4, dp, 8, LANES), F32)],
        pltpu.SemaphoreType.DMA((3, 2)),
        pltpu.VMEM((pixels, channels), F32),
        pltpu.VMEM((pixels, channels), F32),
        pltpu.VMEM((pixels, channels), F32),
        pair(pixels, channels),
        pair(pixels, channels),
        pair(channels, pixels),
        pair(pixels, channels),
        pair(channels, pixels),
        pair(channels, channels),
        pair(channels, hidden),
        pair(hidden, channels),
        pair(pixels, hidden),
        pair(pixels, hidden),
        pltpu.VMEM((2, channels, hidden), F32),
        pltpu.VMEM((2, hidden, channels), F32),
        pltpu.VMEM((2, 2, channels, hidden), F32),
        pltpu.VMEM((chunks, 2, channels, LANES), F32),
        pltpu.VMEM((chunks, 2, channels, LANES), F32),
        pltpu.VMEM((chunks, 2, channels, LANES), F32),
        pltpu.VMEM((rows, wall.shape[2] // hidden, 2, piece, LANES), F32),
    ]
    return exchange(
        "middle",
        2,
        mesh,
        middle_kernel,
        (conv, conv_sums, x, gy, mask, params, total_one, point_two, wall),
        [HBM, VMEM] + [HBM] * 3 + [VMEM] * 2 + [HBM] * 2,
        [shape(pixels, channels)] * 2
        + [shape(8, LANES)] * 2
        + [shape(lines, SLOTS, channels), shape(channels, channels)]
        + [shape(2, wall.shape[2] // hidden, piece, LANES), shape(*wall.shape)],
        [HBM] * 2 + [VMEM] * 2 + [HBM] * 2 + [VMEM, HBM],
        scratch,
        56,
        {8: 7},
        late=True,
    )


ZERO_ROW = 42
WINDOW_PAD = 48
LEFT_TAPS, RIGHT_TAPS = 24, 14
SIDES = ((0, LEFT_F, LEFT_TAPS), (2 * LEFT_F, RIGHT_F, RIGHT_TAPS))


def transform(window, to_freq, out, group):
    rows, _, width = window.shape
    for first in range(0, rows, group):
        part = window[first : first + group].reshape(group * SLOTS, width)
        out[first : first + group] = product_split(to_freq, part).reshape(group, FREQ, width)


def sum_table(table, rows, x_ref, k_ref, y_ref, flipped):
    width = x_ref.shape[-1]
    for side, (start, size, taps) in enumerate(SIDES):
        real, imag = pl.ds(start, size), pl.ds(start + size, size)

        def one_row(row, carry):
            yr, yi = jnp.zeros((size, width), F32), jnp.zeros((size, width), F32)
            for tap in range(taps):
                w = table[side * rows + row, tap]
                index = jnp.clip(row + SPAN - 1 - w if flipped else w - row, 0, SPAN)
                xr, xi = x_ref[w, real, :], x_ref[w, imag, :]
                kr, ki = k_ref[index, real, :], k_ref[index, imag, :]
                if flipped:
                    yr, yi = yr + (kr * xr - ki * xi), yi + (kr * xi + ki * xr)
                else:
                    yr, yi = yr + (kr * xr + ki * xi), yi + (kr * xi - ki * xr)
            y_ref[row, real, :] = yr
            y_ref[row, imag, :] = yi
            return carry

        lax.fori_loop(0, rows, one_row, 0)


TAP_GROUP = 9


def sum_taps(table, rows, d_ref, x_ref, g_ref):
    tile = (8, x_ref.shape[-1])
    for side, (start, size, _) in enumerate(SIDES):
        for first in range(start, start + size, 8):
            real, imag = pl.ds(first, 8), pl.ds(first + size, 8)

            def some_taps(group, carry):
                sums = [(jnp.zeros(tile, F32), jnp.zeros(tile, F32)) for _ in range(TAP_GROUP)]
                for row in range(rows):
                    dr, di = d_ref[REACH + row, real, :], d_ref[REACH + row, imag, :]
                    for k in range(TAP_GROUP):
                        w = table[side * SPAN + group * TAP_GROUP + k, row]
                        xr, xi = x_ref[w, real, :], x_ref[w, imag, :]
                        gr, gi = sums[k]
                        sums[k] = gr + (dr * xr + di * xi), gi + (dr * xi - di * xr)
                for k in range(TAP_GROUP):
                    g_ref[group * TAP_GROUP + k, real, :], g_ref[group * TAP_GROUP + k, imag, :] = sums[k]
                return carry

            lax.fori_loop(0, SPAN // TAP_GROUP, some_taps, 0)


def halo_moves(net, field, window, index):
    rows = field.shape[0]
    lanes = pl.ds(index * LANES, LANES)
    below, above = net.z < net.rows - 1, net.z > 0
    down = net.copy(
        field.at[pl.ds(rows - REACH, REACH), :, lanes], window.at[index, pl.ds(0, REACH)], net.line(1)
    )
    up = net.copy(
        field.at[pl.ds(0, REACH), :, lanes], window.at[index, pl.ds(REACH + rows, REACH)], net.line(net.rows - 1)
    )
    return [(down, below, above), (up, above, below)]


def start_halo(net, field, window, index):
    rows = field.shape[0]
    moves = halo_moves(net, field, window, index)
    for one, goes, _ in moves:
        pl.when(goes)(one.start)
    empty = jnp.zeros((REACH,) + window.shape[2:], F32)
    window[index, REACH : REACH + rows] = field[:, :, index * LANES : (index + 1) * LANES]
    window[index, 2 * REACH + rows :] = jnp.zeros((window.shape[1] - 2 * REACH - rows,) + window.shape[2:], F32)

    @pl.when(net.z == 0)
    def _():
        window[index, :REACH] = empty

    @pl.when(net.z == net.rows - 1)
    def _():
        window[index, REACH + rows : 2 * REACH + rows] = empty

    def wait():
        for one, goes, comes in moves:
            pl.when(comes)(one.wait_recv)
            pl.when(goes)(one.wait_send)

    return wait


def last_kernel(
    net,
    row_table,
    tap_table,
    dconv_in,
    xf,
    kf,
    mask_in,
    x_in,
    h_in,
    point_in,
    params,
    total_one,
    back_in,
    part_in,
    point_grad_in,
    to_freq,
    to_slots,
    to_taps,
    cells_out,
    total,
    one_out,
    two_out,
    up_out,
    down_out,
    cube_out,
    dconv,
    mask,
    xhat,
    slope,
    point_one,
    back_three,
    part,
    point_grad,
    load_sem,
    sums_own,
    sums_slots,
    own_sem,
    window,
    df,
    x_block,
    k_block,
    gf,
    yf,
    taps,
    taps_flat,
    cube,
    ut_pair,
    point_pair,
    dh_pair,
    du,
    one_grad,
    grad_one,
    grad_two,
    grad_up,
    down_t,
    two_scratch,
    one_scratch,
    taps_scratch,
):
    rows, _, channels = dconv.shape
    pixels = rows * SLOTS
    blocks = channels // LANES
    gain, bias = params[0:1, :], params[1:2, :]
    count = read_count(total_one)
    mean, inv = norm_terms(total_one, count)
    loads = Loads(load_sem)
    came_dconv = loads.start(dconv_in, dconv)
    came_grad = loads.start(point_grad_in, point_grad)
    came_part = loads.start(part_in, part)
    came_x = loads.start(x_in, xhat)
    came_h = loads.start(h_in, slope)
    came_mask = loads.start(mask_in, mask)
    came_point = loads.start(point_in, point_one)

    def load_x(index):
        return pltpu.make_async_copy(xf.at[index], x_block[index % 2], own_sem.at[index % 2])

    def load_k(index):
        return pltpu.make_async_copy(kf.at[index], k_block[index % 2], own_sem.at[2 + index % 2])

    load_k(0).start()
    load_x(0).start()
    came_back = loads.start(back_in, back_three)
    came_dconv.wait()
    net.ready()
    waits = [start_halo(net, dconv, window, index) for index in range(blocks)]
    came_grad.wait()
    came_part.wait()

    def keep_weights():
        point_one[...] = down_t[...].T
        loads.leave(point_one, down_out)
        loads.leave(grad_up, up_out)

    def keep_taps(half):
        lanes = pl.ds(half * 2 * LANES, 2 * LANES)
        for row in range(SPAN):
            cube[row, :, lanes] = taps_flat[half][row * SPAN : (row + 1) * SPAN, :]
        loads.leave(cube.at[:, :, lanes], cube_out.at[:, :, lanes])

    def then(job, after):
        yield from job
        after()

    background = [
        then(reduce_all_job(net, point_grad, *two_scratch, grad_two), lambda: loads.leave(grad_two, two_out)),
        then(gather_pieces_job(net, part, (grad_up, down_t)), keep_weights),
    ]

    def progress():
        background[:] = [job for job in background if next(job, StopIteration) is not StopIteration]

    progress()
    came_x.wait()
    came_h.wait()
    came_mask.wait()
    came_point.wait()

    def valid(where):
        return jnp.concatenate([mask[where, :]] * blocks, axis=1)

    def prepare(index, carry):
        where = pl.ds(aligned(index * LANES, LANES), LANES)
        hat = (xhat[where, :] - mean) * inv
        xhat[where, :] = hat
        m = valid(where)
        for side, half in enumerate(split_two(((hat * gain + bias) * m).T)):
            ut_pair[side][:, where] = half
        slope[where, :] = gelu_parts(slope[where, :])[1] * m
        return carry

    lax.fori_loop(0, pixels // LANES, prepare, 0)
    store_split(point_pair, Ellipsis, point_one[...])
    taps[:, SPAN * SPAN :, :] = jnp.zeros((taps.shape[0], taps.shape[1] - SPAN * SPAN, taps.shape[2]), F32)

    def block_back(index):
        load_k(index).wait()
        if index + 1 < blocks:
            load_k(index + 1).start()
        lanes = slice(index * LANES, (index + 1) * LANES)
        sum_table(row_table, rows, df.at[index], k_block[index % 2], yf, True)
        group = to_slots.shape[0] // SLOTS
        for first in range(0, rows, group):
            where = slice(first * SLOTS, (first + group) * SLOTS)
            dact = product_split(to_slots, yf[first : first + group].reshape(group * FREQ, LANES))
            dh_pair[0][where, lanes], dh_pair[1][where, lanes] = split_two(dact * slope[where, lanes])

    def block_taps(index):
        load_x(index).wait()
        if index + 1 < blocks:
            load_x(index + 1).start()
        waits[index]()
        transform(window.at[index], to_freq, df.at[index], to_freq.shape[0] // FREQ)
        sum_taps(tap_table, rows, df.at[index], x_block[index % 2], gf)
        group = to_taps.shape[0] // SPAN_PAD
        half, lanes = index // 2, slice(index % 2 * LANES, (index % 2 + 1) * LANES)
        for first in range(0, SPAN, group):
            out = product_split(to_taps, gf[first : first + group].reshape(group * FREQ, LANES))
            out = out.reshape(group, SPAN_PAD, LANES)
            for row in range(first, first + group):
                taps[half, row * SPAN : (row + 1) * SPAN, lanes] = out[row - first, :SPAN]
        if index % 2:
            job = reduce_all_job(net, taps.at[half], *taps_scratch[half], taps_flat[half])
            background.append(then(job, functools.partial(keep_taps, half)))

    def point_part(part):
        width = channels // len(one_grad)
        lanes = slice(part * width, (part + 1) * width)
        one_grad[part][...] = dot_split(read_pair(ut_pair), (dh_pair[0][:, lanes], dh_pair[1][:, lanes]))
        job = reduce_all_job(net, one_grad[part], *one_scratch[part], grad_one[part])
        background.append(then(job, lambda: loads.leave(grad_one[part], one_out.at[:, pl.ds(part * width, width)])))

    early = blocks // 2
    for index in range(blocks):
        block_taps(index)
        if 1 <= index <= early:
            block_back(index - 1)
        if index == early and len(one_grad) == 2:
            point_part(0)
        progress()
    for index in range(early, blocks):
        block_back(index)
        progress()
    point_part(len(one_grad) - 1)
    progress()

    def last_sums(index, carry):
        where = pl.ds(aligned(index * TILE, TILE), TILE)
        dy = dot_split(read_pair(dh_pair, where), read_pair(point_pair), NT) * valid(where)
        du[where, :] = dy
        return carry[0] + column_sum(dy), carry[1] + column_sum(dy * xhat[where, :])

    zero = jnp.zeros((1, channels), F32)
    write_sums(sums_own, *lax.fori_loop(0, pixels // TILE, last_sums, (zero, zero)))
    sums = all_sum_job(net, sums_own, total, *sums_slots)
    next(sums)
    next(sums)
    progress()
    finish(sums)
    grad_bias, grad_gain = read_sums(total)
    came_back.wait()

    def last_back(index, carry):
        where = pl.ds(aligned(index * TILE, TILE), TILE)
        field = du[where, :] - grad_bias / count - xhat[where, :] * (grad_gain / count)
        back_three[where, :] += valid(where) * gain * inv * field
        return carry

    lax.fori_loop(0, pixels // TILE, last_back, 0)
    loads.leave(back_three, cells_out)
    while background:
        progress()
    loads.finish()


def gather_pieces_job(net, part, outs):
    core = net.bit(0)
    _, per_shard, size, _ = part.shape
    rows = outs[0].shape[0]
    halvings = [halving(net, order, rows) for order in (net.bits, net.bits[::-1])]

    def lanes(block):
        return pl.ds(aligned((2 * block + core) * LANES, LANES), LANES)

    own = []
    for which, out in enumerate(outs):
        base = halvings[which][1]
        for block in range(per_shard):
            own.append(net.own(part.at[which, block], out.at[pl.ds(aligned(base, 8), size), lanes(block)]))
            own[-1].start()
    for one in own:
        one.wait()
    for back_step in range(1, len(net.bits) + 1):
        moves = []
        for which, out in enumerate(outs):
            bit, base, span = halvings[which][0][-back_step]
            here = pl.ds(aligned(base + net.bit(bit) * (span // 2), 8), span // 2)
            for block in range(per_shard):
                piece = out.at[here, lanes(block)]
                moves.append(net.copy(piece, piece, net.across(bit)))
                moves[-1].start()
        yield
        for one in moves:
            one.wait()
    moves = []
    for out in outs:
        for block in range(per_shard):
            piece = out.at[:, lanes(block)]
            moves.append(net.copy(piece, piece, net.across(0)))
            moves[-1].start()
    yield
    for one in moves:
        one.wait()


def last(mesh, tables, dconv, xf, kf, mask, x, hidden, point_one, params, total_one, back_three, part, point_grad):
    dp, rows = mesh
    lines, _, channels = dconv.shape
    pixels = lines * SLOTS
    blocks = channels // LANES
    unit = 8 * dp * rows
    tap_rows = -(-SPAN * SPAN // unit) * unit
    constants = [
        jnp.asarray(split_constant(slots_to_freq(), 2)),
        jnp.asarray(split_constant(freq_to_slots(), 2)),
        jnp.asarray(split_constant(freq_to_taps(), 3)),
    ]

    def pair(*dims):
        return [pltpu.VMEM(dims, BF16)] * 2

    halves = 2 if channels // (dp * rows) % 8 == 0 else 1
    one_part = [pltpu.VMEM((channels, channels // halves), F32)] * halves
    field = pltpu.VMEM((pixels, channels), F32)
    square = pltpu.VMEM((channels, channels), F32)
    scratch = [
        pltpu.VMEM(dconv.shape, F32),
        pltpu.VMEM(mask.shape, F32),
        field,
        field,
        square,
        field,
        pltpu.VMEM(part.shape, F32),
        square,
        pltpu.SemaphoreType.DMA((16,)),
        pltpu.VMEM((8, LANES), F32),
        sum_scratch(mesh, 8),
        pltpu.SemaphoreType.DMA((4,)),
        pltpu.VMEM((blocks, WINDOW_PAD, SLOTS, LANES), F32),
        pltpu.VMEM((blocks, WINDOW_PAD, FREQ, LANES), F32),
        [pltpu.VMEM((ZERO_ROW + 1, FREQ, LANES), F32)] * 2,
        [pltpu.VMEM((TAP_ROWS, FREQ, LANES), F32)] * 2,
        pltpu.VMEM((SPAN, FREQ, LANES), F32),
        pltpu.VMEM((lines, FREQ, LANES), F32),
        pltpu.VMEM((blocks // 2, tap_rows, 2 * LANES), F32),
        [pltpu.VMEM((tap_rows, 2 * LANES), F32)] * (blocks // 2),
        pltpu.VMEM((SPAN, SPAN, channels), F32),
        pair(channels, pixels),
        pair(channels, channels),
        pair(pixels, channels),
        field,
        one_part,
        one_part,
        square,
        square,
        square,
        all_scratch(mesh, channels, channels),
        [all_scratch(mesh, channels, channels // halves)] * halves,
        [all_scratch(mesh, tap_rows, 2 * LANES)] * (blocks // 2),
    ]
    smem = pl.BlockSpec(memory_space=pltpu.SMEM)
    return exchange(
        "last",
        3,
        mesh,
        last_kernel,
        (*tables, dconv, xf, kf, mask, x, hidden, point_one, params, total_one, back_three, part, point_grad, *constants),
        [smem] * 2 + [HBM] * 7 + [VMEM] * 2 + [HBM] * 3 + [VMEM] * 3,
        [shape(pixels, channels), shape(8, LANES)] + [shape(channels, channels)] * 4 + [shape(SPAN, SPAN, channels)],
        [HBM, VMEM] + [HBM] * 5,
        scratch,
        60,
        late=True,
    )


def first_kernel(
    net,
    value,
    names,
    x_in,
    up_in,
    down_in,
    point_in,
    big_in,
    small,
    mask_in,
    params,
    to_freq,
    taps_freq,
    to_slots,
    hidden_out,
    wall,
    xf_out,
    kf_out,
    conv_out,
    conv_sums,
    total,
    row_table,
    tap_table,
    x,
    up,
    down,
    point_one,
    big,
    taps,
    mask,
    load_sem,
    sums_slots,
    got_names,
    name_rows,
    u_pair,
    point_pair,
    hidden,
    act,
    window,
    xf,
    kf,
    yf,
    conv,
):
    rows, _, channels = act.shape
    pixels = rows * SLOTS
    blocks = channels // LANES
    gain, bias = params[0:1, :], params[1:2, :]
    loads = Loads(load_sem)
    came_up = loads.start(up_in, up)
    came_down = loads.start(down_in, down)
    came_x = loads.start(x_in, x)
    came_point = loads.start(point_in, point_one)
    came_mask = loads.start(mask_in, mask)
    came_taps = loads.start(big_in, big)
    net.ready()
    sums = all_sum_job(net, value, total, *sums_slots)
    next(sums)
    below, above = net.z < net.rows - 1, net.z > 0
    name_moves = [
        (net.copy(names.at[1], got_names.at[0], net.line(1)), below, above),
        (net.copy(names.at[2], got_names.at[1], net.line(net.rows - 1)), above, below),
    ]
    for one, goes, _ in name_moves:
        pl.when(goes)(one.start)

    @pl.when(net.z == 0)
    def _():
        got_names[0] = jnp.zeros(got_names.shape[1:], jnp.int32)

    @pl.when(net.z == net.rows - 1)
    def _():
        got_names[1] = jnp.zeros(got_names.shape[1:], jnp.int32)

    came_up.wait()
    came_down.wait()

    background = [weights_line_job(net, up, down, wall, range(1, net.rows - 1))]

    def progress():
        background[:] = [job for job in background if next(job, StopIteration) is not StopIteration]

    progress()
    next(sums)
    came_point.wait()
    store_split(point_pair, Ellipsis, point_one[...])
    came_x.wait()
    came_mask.wait()
    finish(sums)
    mean, inv = norm_terms(total, read_count(total))

    def first_norm(index, carry):
        where = pl.ds(aligned(index * LANES, LANES), LANES)
        m = jnp.concatenate([mask[where, :]] * blocks, axis=1)
        store_split(u_pair, where, ((x[where, :] - mean) * inv * gain + bias) * m)
        return carry

    lax.fori_loop(0, pixels // LANES, first_norm, 0)
    waits = []
    for half in range(blocks // 2):
        lanes = slice(half * 2 * LANES, (half + 1) * 2 * LANES)
        for tile in range(pixels // TILE):
            where = slice(tile * TILE, (tile + 1) * TILE)
            pre = dot_split(
                (u_pair[0][where, :], u_pair[1][where, :]), (point_pair[0][:, lanes], point_pair[1][:, lanes])
            )
            hidden[where, lanes] = pre
            act[where.start // SLOTS : where.stop // SLOTS, :, lanes] = gelu_parts(pre)[0].reshape(
                TILE // SLOTS, SLOTS, 2 * LANES
            )
        waits += [start_halo(net, act, window, index) for index in (2 * half, 2 * half + 1)]
    progress()
    near = weights_layer_job(net, wall, (1,))
    next(near)
    loads.leave(hidden, hidden_out)
    came_taps.wait()
    taps[...] = jnp.zeros(taps.shape, F32)
    taps[:SPAN, :SPAN, :] = big[...]
    small_span = small.shape[0]
    middle_taps = slice(REACH - small_span // 2, REACH + small_span // 2 + 1)
    taps[middle_taps, middle_taps, :] = big[middle_taps, middle_taps, :] + small[...]
    group = taps_freq.shape[0] // FREQ
    for index in range(blocks):
        for first in range(0, taps.shape[0], group):
            part = taps[first : first + group, :, index * LANES : (index + 1) * LANES]
            freq = product_split(taps_freq, part.reshape(group * SPAN_PAD, LANES))
            kf[index][first : first + group] = freq.reshape(group, FREQ, LANES)
        loads.leave(kf[index], kf_out.at[index])
    for one, goes, comes in name_moves:
        pl.when(comes)(one.wait_recv)
        pl.when(goes)(one.wait_send)
    moved = [loads.start(src, name_rows.at[k]) for k, src in enumerate((names.at[0], got_names.at[0], got_names.at[1]))]
    for one in moved:
        one.wait()
    list_rows(rows, name_rows, row_table, tap_table)
    next(near, None)
    sums = [jnp.zeros((1, LANES), F32)] * 2 * blocks
    for index in range(blocks):
        lanes = slice(index * LANES, (index + 1) * LANES)
        waits[index]()
        transform(window.at[index], to_freq, xf[index], to_freq.shape[0] // FREQ)
        loads.leave(xf[index].at[pl.ds(0, ZERO_ROW + 1)], xf_out.at[index])
        sum_table(row_table, rows, xf[index], kf[index], yf, False)
        group = to_slots.shape[0] // SLOTS
        for first in range(0, rows, group):
            where = slice(first * SLOTS, (first + group) * SLOTS)
            cells = product_split(to_slots, yf[first : first + group].reshape(group * FREQ, LANES)) * mask[where, :]
            conv[where, lanes] = cells
            sums[2 * index] = sums[2 * index] + column_sum(cells)
            sums[2 * index + 1] = sums[2 * index + 1] + column_sum(cells * cells)
    loads.leave(conv, conv_out)
    for index in range(blocks):
        conv_sums[index : index + 1, :] = sums[2 * index]
        conv_sums[4 + index : 5 + index, :] = sums[2 * index + 1]
    finish(near)
    while background:
        progress()
    loads.finish()


def list_rows(rows, names, row_table, tap_table):
    for side in range(2):

        def name(w):
            return names[0, side, w] + names[1, side, w] + names[2, side, w]

        def one_row(row, carry):
            at = row + REACH
            own = name(at)

            def count(first):
                same = jnp.int32(0)
                for k in range(REACH):
                    same = same + jnp.where(name(first + k) == own, 1, 0)
                return same

            low = at - count(row)
            high = jnp.where(own > 0, at + 1 + count(at + 1), low)
            for tap in range(LEFT_TAPS):
                row_table[side * rows + row, tap] = jnp.where(low + tap < high, low + tap, ZERO_ROW)
            for tap in range(SPAN):
                w = row + tap
                tap_table[side * SPAN + tap, row] = jnp.where((w >= low) & (w < high), w, ZERO_ROW)
            return carry

        lax.fori_loop(0, rows, one_row, 0)


def read_count(total):
    return jnp.concatenate([total[8 + row : 9 + row, :] for row in range(4)], axis=1)


def first(mesh, value, names, x, up, down, point_one, big, small, mask, params):
    dp, devices = mesh
    pixels, channels = x.shape
    lines = pixels // SLOTS
    blocks = channels // LANES
    constants = [
        jnp.asarray(split_constant(slots_to_freq(), 2)),
        jnp.asarray(split_constant(taps_to_freq(), 4)),
        jnp.asarray(split_constant(freq_to_slots(), 2)),
    ]

    def pair(*dims):
        return [pltpu.VMEM(dims, BF16)] * 2

    field = pltpu.VMEM((pixels, channels), F32)
    scratch = [
        field,
        pltpu.VMEM(up.shape, F32),
        pltpu.VMEM(down.shape, F32),
        pltpu.VMEM(point_one.shape, F32),
        pltpu.VMEM(big.shape, F32),
        pltpu.VMEM((TAP_ROWS, SPAN_PAD, channels), F32),
        pltpu.VMEM(mask.shape, F32),
        pltpu.SemaphoreType.DMA((24,)),
        sum_scratch(mesh, value.shape[0]),
        pltpu.VMEM((2, 8, LANES), jnp.int32),
        pltpu.SMEM((3, 8, LANES), jnp.int32),
        pair(pixels, channels),
        pair(channels, channels),
        field,
        pltpu.VMEM((lines, SLOTS, channels), F32),
        pltpu.VMEM((blocks, WINDOW_PAD, SLOTS, LANES), F32),
        [pltpu.VMEM((WINDOW_PAD, FREQ, LANES), F32)] * blocks,
        [pltpu.VMEM((TAP_ROWS, FREQ, LANES), F32)] * blocks,
        pltpu.VMEM((lines, FREQ, LANES), F32),
        field,
    ]
    smem = pl.BlockSpec(memory_space=pltpu.SMEM)
    return exchange(
        "first",
        0,
        mesh,
        first_kernel,
        (value, names, x, up, down, point_one, big, small, mask, params, *constants),
        [VMEM, VMEM] + [HBM] * 5 + [VMEM, HBM] + [VMEM] * 4,
        [
            shape(pixels, channels),
            shape(devices, 2, *up.shape),
            shape(blocks, ZERO_ROW + 1, FREQ, LANES),
            shape(blocks, TAP_ROWS, FREQ, LANES),
            shape(pixels, channels),
            shape(8, LANES),
            shape(*value.shape),
            jax.ShapeDtypeStruct((2 * lines, LANES), jnp.int32),
            jax.ShapeDtypeStruct((2 * SPAN, LANES), jnp.int32),
        ],
        [HBM] * 5 + [VMEM] * 2 + [smem] * 2,
        scratch,
        60,
        late=True,
    )


def begin_kernel(place, id_lanes, inputs, grads, x, gy, mask, value):
    rows = x.shape[0] // SLOTS
    columns = id_lanes.shape[0] // rows
    blocks = x.shape[1] // LANES

    def one_row(row, sums):
        sums = list(sums)
        for side, (start, width) in enumerate(((0, LEFT), (LEFT, RIGHT))):
            name, at = place[2 * side, row], place[2 * side + 1, row]
            pixel = row * columns + at
            slots = pl.ds(row * SLOTS + start, width)
            own = jnp.where(name < 0, -9, name).astype(F32)
            m = jnp.where(id_lanes[pl.ds(pixel, width), :] == own, 1.0, 0.0)
            mask[slots, :] = m
            sums[-1] = sums[-1] + column_sum(m)
            for block in range(blocks):
                lanes = slice(block * LANES, (block + 1) * LANES)
                cells = pl.ds(pixel * blocks + block, width, stride=blocks)
                v = inputs[cells, :] * m
                x[slots, lanes] = v
                gy[slots, lanes] = grads[cells, :] * m
                sums[block] = sums[block] + column_sum(v)
                sums[blocks + block] = sums[blocks + block] + column_sum(v * v)
        return tuple(sums)

    sums = lax.fori_loop(0, rows, one_row, (jnp.zeros((1, LANES), F32),) * (2 * blocks + 1))
    for row in range(2 * blocks):
        value[row : row + 1, :] = sums[row]
    for row in range(blocks):
        value[2 * blocks + row : 2 * blocks + row + 1, :] = sums[-1]
    value[3 * blocks :, :] = jnp.zeros((value.shape[0] - 3 * blocks, LANES), F32)


def begin(place, id_lanes, inputs, grads, rows, channels):
    return pl.pallas_call(
        begin_kernel,
        out_shape=[
            shape(rows * SLOTS, channels),
            shape(rows * SLOTS, channels),
            shape(rows * SLOTS, LANES),
            shape(16, LANES),
        ],
        in_specs=[pl.BlockSpec(memory_space=pltpu.SMEM)] + [VMEM] * 3,
        out_specs=[VMEM] * 4,
        compiler_params=pltpu.CompilerParams(vmem_limit_bytes=16 << 20),
        name="begin",
    )(place, id_lanes, inputs, grads)


def finish_kernel(
    place,
    inputs,
    grads,
    delta_in,
    cells_in,
    one_in,
    two_in,
    up_in,
    down_in,
    cube_in,
    total_three,
    total_two,
    total_one,
    output,
    grad_input,
    one_out,
    two_out,
    up_out,
    down_out,
    cube_out,
    small,
    *rest,
):
    vectors, (field, field_back, delta, cells, squares, cube, sems) = rest[:6], rest[6:]
    rows = delta.shape[0] // SLOTS
    blocks = delta.shape[1] // LANES
    columns = field.shape[0] // rows // blocks
    loads = Loads(sems)
    came = [[loads.start(inputs, field), loads.start(delta_in, delta)], [loads.start(grads, field_back), loads.start(cells_in, cells)]]
    through = [
        (loads.start(src, middle), middle, out)
        for src, middle, out in zip(
            (one_in, two_in, up_in, down_in, cube_in), (*squares, cube), (one_out, two_out, up_out, down_out, cube_out)
        )
    ]
    for copies, whole, part, out in zip(came, (field, field_back), (delta, cells), (output, grad_input)):
        for one in copies:
            one.wait()

        def one_row(row, carry):
            for side, (start, width) in enumerate(((0, LEFT), (LEFT, RIGHT))):
                pixel = row * columns + place[2 * side + 1, row]
                slots = pl.ds(row * SLOTS + start, width)
                for block in range(blocks):
                    where = pl.ds(pixel * blocks + block, width, stride=blocks)
                    whole[where, :] = whole[where, :] + part[slots, block * LANES : (block + 1) * LANES]
            return carry

        lax.fori_loop(0, rows, one_row, 0)
        loads.leave(whole, out)
    for one, middle, out in through:
        one.wait()
        loads.leave(middle, out)
    first = REACH - small.shape[0] // 2
    last = first + small.shape[0]
    small[...] = cube[first:last, first:last, :]
    for which, total in enumerate((total_one, total_two, total_three)):
        for out, value in zip(vectors[2 * which : 2 * which + 2], read_sums(total)):
            out[...] = value
    loads.finish()


def place_results(place, inputs, grads, delta, cells, squares, cube, totals, small_span):
    channels = delta.shape[1]
    square = pltpu.VMEM((channels, channels), F32)
    return pl.pallas_call(
        finish_kernel,
        out_shape=[shape(*inputs.shape)] * 2
        + [shape(channels, channels)] * 4
        + [shape(*cube.shape), shape(small_span, small_span, channels)]
        + [shape(1, channels)] * 6,
        in_specs=[pl.BlockSpec(memory_space=pltpu.SMEM)] + [HBM] * 9 + [VMEM] * 3,
        out_specs=[HBM] * 7 + [VMEM] * 7,
        scratch_shapes=[
            pltpu.VMEM(inputs.shape, F32),
            pltpu.VMEM(inputs.shape, F32),
            pltpu.VMEM(delta.shape, F32),
            pltpu.VMEM(delta.shape, F32),
            [square] * 4,
            pltpu.VMEM(cube.shape, F32),
            pltpu.SemaphoreType.DMA((16,)),
        ],
        compiler_params=pltpu.CompilerParams(vmem_limit_bytes=60 << 20),
        name="finish",
    )(place, inputs, grads, delta, cells, *squares, cube, *totals)


def shards(
    dp,
    devices_rows,
    inputs,
    image_ids,
    first_norm_gain,
    first_norm_bias,
    point_one,
    kernel_big,
    kernel_small,
    second_norm_gain,
    second_norm_bias,
    point_two,
    feedforward_norm_gain,
    feedforward_norm_bias,
    w_up,
    w_down,
    out_grad,
):
    rows, canvases, columns, channels = inputs.shape
    assert canvases == 1 and kernel_big.shape[0] == SPAN
    pixels = rows * SLOTS
    ids = image_ids[:, 0]
    mesh = (dp, devices_rows)

    place = jnp.arange(columns, dtype=jnp.int32)[None, :]
    is_left = (ids >= 0) & (ids < LEFT_IDS)
    is_right = ids >= LEFT_IDS

    def side(member, width):
        name = jnp.max(jnp.where(member, ids, -1), axis=1)
        first = jnp.min(jnp.where(member, place, columns), axis=1)
        return name, jnp.minimum(first, columns - width)

    left_id, left_at = side(is_left, LEFT)
    right_id, right_at = side(is_right, RIGHT)
    spot = jnp.stack([left_id, left_at, right_id, right_at])
    lines = (rows * columns * channels // LANES, LANES)
    id_lanes = jnp.broadcast_to(ids.reshape(rows * columns, 1).astype(F32), (rows * columns, LANES))
    x, gy, mask_lanes, value = begin(spot, id_lanes, inputs.reshape(lines), out_grad.reshape(lines), rows, channels)
    names = jnp.stack([left_id, right_id]) + 1

    def name_tile(first, last, lane):
        return jnp.pad(names[:, first:last], ((0, 6), (lane, LANES - lane - (last - first))))

    names = jnp.stack(
        [
            name_tile(0, rows, REACH),
            name_tile(rows - REACH, rows, 0),
            name_tile(0, REACH, REACH + rows),
        ]
    )
    vectors = [
        first_norm_gain,
        first_norm_bias,
        second_norm_gain,
        second_norm_bias,
        feedforward_norm_gain,
        feedforward_norm_bias,
    ]
    params = jnp.stack(vectors + [jnp.zeros((channels,), F32)] * 2)
    hidden, wall, xf, kf, conv, conv_sums, total_one, *tables = first(
        mesh,
        value,
        names,
        x,
        w_up,
        w_down,
        point_one,
        kernel_big,
        kernel_small,
        mask_lanes,
        params,
    )
    delta, back_three, total_four, total_five, dconv, point_grad, part, _ = middle(
        mesh, conv, conv_sums, x, gy, mask_lanes, params, total_one, point_two, wall
    )
    cells, total, grad_point_one, grad_point_two, grad_up, grad_down, grad_kernel = last(
        mesh,
        tables,
        dconv,
        xf,
        kf,
        mask_lanes,
        x,
        hidden,
        point_one,
        params,
        total_one,
        back_three,
        part,
        point_grad,
    )
    squares = (grad_point_one, grad_point_two, grad_up, grad_down)
    output, grad_input, grad_point_one, grad_point_two, grad_up, grad_down, grad_kernel, grad_small, *vectors = place_results(
        spot,
        inputs.reshape(lines),
        out_grad.reshape(lines),
        delta,
        cells,
        squares,
        grad_kernel,
        (total_four, total_five, total),
        kernel_small.shape[0],
    )
    vectors = [vector.reshape(channels) for vector in vectors]
    grad_bias_one, grad_gain_one, grad_bias_two, grad_gain_two, grad_bias_three, grad_gain_three = vectors
    return (
        output.reshape(inputs.shape),
        grad_input.reshape(inputs.shape),
        grad_gain_one,
        grad_bias_one,
        grad_point_one,
        grad_kernel,
        grad_small,
        grad_gain_two,
        grad_bias_two,
        grad_point_two,
        grad_gain_three,
        grad_bias_three,
        grad_up,
        grad_down,
    )


def solution(mesh):
    field = P("rows", "dp", None, None)
    everywhere = P()
    up, down = P(None, "rows"), P("rows", None)
    return jax.shard_map(
        functools.partial(shards, mesh.shape["dp"], mesh.shape["rows"]),
        mesh=mesh,
        in_specs=(field, P("rows", "dp", None)) + (everywhere,) * 10 + (up, down, field),
        out_specs=(field, field) + (everywhere,) * 10 + (up, down),
        check_vma=False,
    )
```
